32 devices in a mesh: grp: 1, seq: 32 (over z, y, x, core).
Axes of the slice: x: 2, y: 2, z: 4, core: 2. Of those that a mesh axis runs over, the one named last changes fastest.
Arguments:
- queries: bfloat16 [256, 1792], P(('grp', 'seq')), may hold values from -6 to 6
- stretch_keys: bfloat16 [256, 256], P(('grp', 'seq')), may hold values from -6 to 6
- stretch_values: bfloat16 [256, 256], P(('grp', 'seq')), may hold values from -6 to 6
- cache_keys: bfloat16 [32768, 256], P(('grp', 'seq')), may hold values from -6 to 6
- cache_values: bfloat16 [32768, 256], P(('grp', 'seq')), may hold values from -6 to 6
- chosen: int32 [32, 14, 3], P(('grp', 'seq')), may hold values from 0 to 7, all different within a row; in each aligned block of 7 rows (0 to 6, 7 to 13, ..., all dimensions but the last counted through in order) at most 4 rows name the same one
- out_weight: bfloat16 [1792, 1792], replicated, may hold values from -0.5 to 0.5
Outputs:
- attended: bfloat16 [256, 1792], P(('grp', 'seq'))
The draws below stay inside these ranges and needn't reach their ends.
Inputs may be any that keep to these rules, and one draw needn't show every extreme that they name: Each head's 3 chosen blocks differ. Among the 7 heads that share one key-value head, in one query block, no key block is chosen by more than 4 heads.
All inputs are finite; a program needn't handle non-finite values.
Results may differ from the reference program's by a relative error of at most 0.005.
Values may be sent and summed in bfloat16 or wider, within the bound.
No kernel may reach another device: no remote copies, remote signals or barrier semaphores. Data moves between devices by JAX's collectives and lax.ppermute only.
A program may use at most 64 MiB of HBM per device.

```python
import math
import jax
import jax.numpy as jnp
import numpy as np
from jax import lax

H = 14
KVH = 2
HD = 128
D = 1792
BLK = 4096
TOPK = 3
CTX_DEV = 1024
Q_DEV = 8
GROUP = 7
QB = 32
QT = 256
CTX = 32768
NB = 8
MOST = 4
N_SEQ = 32


def draw_queries(key, part):
    inner = jax.random.fold_in(key, 1)
    base = 1.6 * jax.random.truncated_normal(inner, -3.5, 3.5, (QT, H * HD), jnp.float32)
    return base.astype(jnp.bfloat16)


def draw_stretch_keys(key, part):
    inner = jax.random.fold_in(key, 2)
    base = 1.6 * jax.random.truncated_normal(inner, -3.5, 3.5, (QT, KVH * HD), jnp.float32)
    return base.astype(jnp.bfloat16)


def block_levels(own_key, dims, cuts, smallest, largest):
    level = 1.0
    for position, shards_of in cuts:
        heights = jax.random.uniform(jax.random.fold_in(jax.random.fold_in(own_key, 6), position), (shards_of,), jnp.float32, smallest / len(cuts), largest / len(cuts))
        level = level * jnp.repeat(jnp.exp(heights), dims[position] // shards_of).reshape((-1,) + (1,) * (len(dims) - 1 - position))
    return level


def routed_block(rng, own, number, rows, number_of, top, reach, skew):
    order = jax.random.permutation(rng, number_of)
    crowded, common = load_shares(number_of, rows * top, reach, skew, True), load_shares(number_of, rows * top, reach, skew, False)
    places = jnp.arange(number_of)

    def named(lengths, turn):
        used = int((lengths > 0).sum())
        fixed = max(1, used // 4)
        shifted = fixed + (places - fixed + turn * (used - fixed)) % max(1, number_of - fixed)
        return jnp.zeros((number_of,), jnp.int32).at[order[jnp.where(places < fixed, places, shifted)]].set(jnp.asarray(lengths, jnp.int32))

    lengths = jnp.where(number % 4 == 0, named(crowded, number // 4), named(common, number - number // 4 - 1))
    mixed = jax.random.permutation(jax.random.fold_in(own, 3), number_of)
    donor, receiver = mixed[0:number_of // 2 * 2:2], mixed[1:number_of // 2 * 2:2]
    slack = jnp.minimum(lengths[donor] - 1, reach - lengths[receiver]) // 2
    slack = jnp.where((donor == order[0]) | (receiver == order[0]) | (lengths[receiver] == 0), 0, jnp.maximum(slack, 0))
    shifted = jax.random.randint(jax.random.fold_in(own, 4), (number_of // 2,), 0, 1 << 20) % (slack + 1)
    lengths = lengths.at[donor].add(-shifted).at[receiver].add(shifted)
    labels = jnp.searchsorted(jnp.cumsum(lengths), jnp.arange(rows * top), side="right").astype(jnp.int32)
    listing = labels.reshape(top, rows).T
    listing = listing[jax.random.permutation(jax.random.fold_in(own, 1), rows)]
    turn = jax.random.randint(jax.random.fold_in(own, 2), (rows, 1), 0, top)
    return jnp.take_along_axis(listing, (jnp.arange(top)[None, :] + turn) % top, axis=1)


def load_shares(number_of, total, bound, lean, full):
    portions = [(1 << 20) // math.isqrt(grade ** lean) + 1 for grade in range(1, number_of + 1)]
    largest = bound if full else min(bound, max(-(-total // number_of), total * portions[0] // sum(portions)))
    least = 1 if total - largest >= number_of - 1 else 0
    given, rest = [largest] + [least] * (number_of - 1), total - largest - least * (number_of - 1)
    while rest > 0:
        free = [i for i in range(1, number_of) if given[i] < largest] or [i for i in range(1, number_of) if given[i] < bound]
        pool, budget = sum([portions[i] for i in free]), rest
        for i in free:
            extra = min(bound - given[i], max(1, budget * portions[i] // pool), rest)
            given[i] = given[i] + extra
            rest = rest - extra
    return np.array(given)


def noise(own_key, shape, deviation, most, cuts=(), kind=jnp.bfloat16):
    drawn = jax.random.normal(own_key, shape, jnp.float32) * deviation
    if len(cuts) > 0:
        drawn = block_levels(own_key, shape, cuts, -0.22, 0.18) * drawn
    return jnp.clip(drawn, min=-most, max=most).astype(kind)


def setup_inputs(seed: int = 0, part: int = 0) -> dict:
    streams_of = jax.random.split(jax.random.key(seed), 8)
    part_splits = jax.random.split(jax.random.fold_in(streams_of[7], part), 8)
    queries = draw_queries(jax.random.fold_in(jax.random.fold_in(streams_of[7], part), 71), part)
    stretch_keys = draw_stretch_keys(jax.random.fold_in(jax.random.fold_in(streams_of[7], part), 71), part)
    stretch_values = noise(part_splits[2], (QT, KVH * HD), 1.0, 6.0, ((0, 32),))
    cache_keys = noise(part_splits[3], (CTX, KVH * HD), 1.6, 6.0, ((0, 32),))
    cache_values = noise(part_splits[4], (CTX, KVH * HD), 1.0, 6.0, ((0, 32),))
    chosen_keys = jax.random.split(jax.random.fold_in(part_splits[5], 1), QB * H // GROUP)
    chosen_turns = jax.random.permutation(jax.random.fold_in(part_splits[5], 3), QB * H // GROUP)
    chosen = jax.vmap(lambda own, number: routed_block(jax.random.fold_in(part_splits[5], 2), own, number, GROUP, NB, TOPK, MOST, 2))(chosen_keys, chosen_turns).reshape((QB, H, TOPK))
    out_weight = noise(streams_of[6], (H * HD, D), (H * HD // 16) ** -0.5, 0.5)
    return dict(queries=queries, stretch_keys=stretch_keys, stretch_values=stretch_values, cache_keys=cache_keys, cache_values=cache_values, chosen=chosen, out_weight=out_weight)


LOW_SCORE = -1e30


def query_block(block_index, query_rows, selection, hist_keys, hist_values, stretch_keys4, stretch_values4):
    group = H // KVH
    score_scale = HD ** -0.5
    highest = lax.Precision.HIGHEST
    query_heads = query_rows.reshape(Q_DEV, KVH, group, HD).astype(jnp.float32)
    head_sel = selection.reshape(KVH, group, TOPK).astype(jnp.int32)
    kv_index = jnp.arange(KVH, dtype=jnp.int32)[:, None, None]
    picked_keys = hist_keys[kv_index, head_sel].astype(jnp.float32)
    picked_values = hist_values[kv_index, head_sel].astype(jnp.float32)
    scores = jnp.einsum("qgrd,grtscd->grtsqc", query_heads, picked_keys, precision=highest) * score_scale
    seg_max = jnp.max(scores, axis=-1)
    seg_weights = jnp.exp(scores - seg_max[..., None]).astype(jnp.bfloat16)
    seg_sum = jnp.sum(seg_weights.astype(jnp.float32), axis=-1)
    seg_out = jnp.einsum("grtsqc,grtscd->grtsqd", seg_weights.astype(jnp.float32), picked_values, precision=highest)

    stretch_scores = jnp.einsum("qgrd,nkgd->grqnk", query_heads, stretch_keys4, precision=highest) * score_scale
    key_pos = jnp.arange(QT, dtype=jnp.int32).reshape(N_SEQ, Q_DEV)
    query_pos = block_index * Q_DEV + jnp.arange(Q_DEV, dtype=jnp.int32)
    visible = (key_pos[None] <= query_pos[:, None, None]) & (key_pos[None] // BLK == query_pos[:, None, None] // BLK)
    visible = visible[None, None]
    masked = jnp.where(visible, stretch_scores, LOW_SCORE)
    stretch_max = jnp.max(masked, axis=-1)
    stretch_weights = jnp.where(visible, jnp.exp(masked - stretch_max[..., None]), 0.0).astype(jnp.bfloat16)
    stretch_sum = jnp.sum(stretch_weights.astype(jnp.float32), axis=-1)
    stretch_out = jnp.einsum("grqnk,nkgd->grqnd", stretch_weights.astype(jnp.float32), stretch_values4, precision=highest)

    row_max = jnp.maximum(jnp.max(seg_max, axis=(2, 3)), jnp.max(stretch_max, axis=-1))
    hist_scale = jnp.exp(seg_max - row_max[:, :, None, None, :])
    stretch_scale = jnp.exp(stretch_max - row_max[..., None])
    denominator = jnp.sum(hist_scale * seg_sum, axis=(2, 3)) + jnp.sum(stretch_scale * stretch_sum, axis=-1)
    numerator = jnp.sum(hist_scale[..., None] * seg_out, axis=(2, 3)) + jnp.sum(stretch_scale[..., None] * stretch_out, axis=3)
    attention = numerator / denominator[..., None]
    attention = attention.transpose(2, 0, 1, 3).reshape(Q_DEV, H * HD).astype(jnp.bfloat16)
    return attention


def reference(queries, stretch_keys, stretch_values, cache_keys, cache_values, chosen, out_weight):
    span = BLK // CTX_DEV
    hist_keys = cache_keys.reshape(NB, span, CTX_DEV, KVH, HD).transpose(3, 0, 1, 2, 4)
    hist_values = cache_values.reshape(NB, span, CTX_DEV, KVH, HD).transpose(3, 0, 1, 2, 4)
    stretch_keys4 = stretch_keys.reshape(N_SEQ, Q_DEV, KVH, HD).astype(jnp.float32)
    stretch_values4 = stretch_values.reshape(N_SEQ, Q_DEV, KVH, HD).astype(jnp.float32)

    def one_block(packed):
        block_index, query_rows, selection = packed
        attention = query_block(block_index, query_rows, selection, hist_keys, hist_values, stretch_keys4, stretch_values4)
        return jnp.dot(attention, out_weight, preferred_element_type=jnp.float32).astype(jnp.bfloat16)

    results = lax.map(one_block, (jnp.arange(N_SEQ, dtype=jnp.int32), queries.reshape(N_SEQ, Q_DEV, H * HD), chosen))
    return results.reshape(QT, D)
```

```python
import functools
import math

import jax
import jax.numpy as jnp
from jax import lax
from jax.experimental import pallas as pl
from jax.experimental.pallas import tpu as pltpu
from jax.sharding import PartitionSpec as P

H = 14
KVH = 2
HD = 128
BLK = 4096
TOPK = 3
GROUP = H // KVH

LOW_SCORE = -1e30
LOG2E = math.log2(math.e)
LANES = 128


def head_rows(q_ref, g):
    q = q_ref[...].astype(jnp.float32)
    return [q[:, h * HD : (h + 1) * HD] for h in range(g * GROUP, (g + 1) * GROUP)]


def slot_match(chosen_ref, g, block, slot, token):
    rows = lax.broadcasted_iota(jnp.int32, block.shape, 0)
    same_token = token == rows
    seen = jnp.zeros(block.shape, jnp.int32)
    found = []
    for h in range(g * GROUP, (g + 1) * GROUP):
        picked = block == chosen_ref[0, h, 0]
        for t in range(1, TOPK):
            picked = picked | (block == chosen_ref[0, h, t])
        found.append(jnp.where(picked & same_token & (seen == slot), 1.0, 0.0))
        seen = seen + picked.astype(jnp.int32)
    return found


def pack_kernel(chips, capacity, chosen_ref, q_ref, k_ref, v_ref, send_ref):
    tokens = q_ref.shape[0]
    per = capacity * tokens
    span = chips * KVH
    key_blocks = send_ref.shape[0] // span
    lane = lax.broadcasted_iota(jnp.int32, (tokens, key_blocks * per), 1)
    block, slot, token = lane // per, lane % per // tokens, lane % tokens
    for g in range(KVH):
        spread = jnp.concatenate(
            slot_match(chosen_ref, g, block, slot, token) + [jnp.zeros(lane.shape, jnp.float32)], axis=0
        )
        rows = head_rows(q_ref, g)
        rows = jnp.concatenate(rows + [jnp.zeros_like(rows[0])], axis=0)
        slots = jnp.dot(
            spread.T.astype(jnp.bfloat16), rows.astype(jnp.bfloat16), preferred_element_type=jnp.float32
        ).astype(jnp.bfloat16)
        cols = slice(g * HD, (g + 1) * HD)
        fresh = jnp.concatenate(
            [k_ref[:, cols].astype(jnp.float32), v_ref[:, cols].astype(jnp.float32)], axis=0
        ).astype(jnp.bfloat16)
        for b in range(key_blocks):
            for chip in range(chips):
                to = b * span + chip * KVH + g
                send_ref[to, :per, :] = slots[b * per : (b + 1) * per]
                send_ref[to, per:, :] = fresh


def attend_kernel(per, core_ref, q_ref, k_ref, v_ref, peer_ref, out_ref, va_ref, vb_ref):
    cols = pl.ds(pl.multiple_of(core_ref[0] * HD, HD), HD)
    ones = jnp.ones((k_ref.shape[0], HD), jnp.bfloat16)
    va_ref[:, :HD] = v_ref[:, cols]
    va_ref[:, HD:] = ones
    vb_ref[:, :HD] = peer_ref[1]
    vb_ref[:, HD:] = ones
    sources = q_ref.shape[0]
    step = 256 // per
    scale = LOG2E * HD**-0.5
    nt = (((1,), (1,)), ((), ()))
    row = lax.broadcasted_iota(jnp.int32, (per, LANES), 0)
    lane = lax.broadcasted_iota(jnp.int32, (per, LANES), 1)
    diagonal = row == lane % per
    piece = lax.broadcasted_iota(jnp.int32, (16, LANES), 0)
    for first in range(0, sources, step):
        q = q_ref[first : first + step, :per, :].reshape(step * per, HD)
        sa = lax.dot_general(q, k_ref[:, cols], nt, preferred_element_type=jnp.float32)
        sb = lax.dot_general(q, peer_ref[0], nt, preferred_element_type=jnp.float32)
        top = jnp.maximum(jnp.max(sa, axis=1, keepdims=True), jnp.max(sb, axis=1, keepdims=True)) * scale
        wa = jnp.exp2(sa * scale - top).astype(jnp.bfloat16)
        wb = jnp.exp2(sb * scale - top).astype(jnp.bfloat16)
        both = jnp.dot(wa, va_ref[...], preferred_element_type=jnp.float32) + jnp.dot(
            wb, vb_ref[...], preferred_element_type=jnp.float32
        )
        total = both[:, HD:]
        out = (both[:, :HD] / total).astype(jnp.bfloat16)
        lse = top + jnp.log(total) * LOG2E
        for s in range(step):
            part = slice(s * per, (s + 1) * per)
            out_ref[first + s, :per, :] = out[part]
            flat = jnp.sum(jnp.where(diagonal, lse[part], 0.0), axis=0, keepdims=True)
            hi = flat.astype(jnp.bfloat16).astype(jnp.float32)
            mid = (flat - hi).astype(jnp.bfloat16).astype(jnp.float32)
            low = flat - hi - mid
            out_ref[first + s, per:, :] = jnp.where(
                piece == 0, hi, jnp.where(piece == 1, mid, jnp.where(piece == 2, low, 0.0))
            ).astype(jnp.bfloat16)


def fresh_kernel(chips, capacity, place_ref, chosen_ref, q_ref, mine_ref, peer_ref, out_ref, lse_ref, match_ref):
    tokens = q_ref.shape[0]
    sources = mine_ref.shape[0]
    per = capacity * tokens
    core, first = place_ref[0], place_ref[1]
    scale = LOG2E * HD**-0.5
    nt = (((1,), (1,)), ((), ()))
    shape = (GROUP * tokens, sources * tokens)
    key_pos = lax.broadcasted_iota(jnp.int32, shape, 1)
    query_pos = first + lax.broadcasted_iota(jnp.int32, shape, 0) % tokens
    visible = (key_pos <= query_pos) & (key_pos // BLK == query_pos // BLK)
    lane = lax.broadcasted_iota(jnp.int32, (tokens, match_ref.shape[2]), 1)
    block, slot, token = lane // (per * chips), lane % per // tokens, lane % tokens
    mine = mine_ref[...].astype(jnp.float32).reshape(sources, 2, tokens, HD)
    peer = peer_ref[...].astype(jnp.float32).reshape(sources, 2, tokens, HD)
    ones = jnp.ones((sources * tokens, HD), jnp.bfloat16)
    for g in range(KVH):
        match_ref[g] = jnp.concatenate(slot_match(chosen_ref, g, block, slot, token), axis=0)
        kv = jnp.where(core == g, mine, peer)
        keys = kv[:, 0].reshape(sources * tokens, HD).astype(jnp.bfloat16)
        values = kv[:, 1].reshape(sources * tokens, HD).astype(jnp.bfloat16)
        q = jnp.concatenate(head_rows(q_ref, g), axis=0).astype(jnp.bfloat16)
        s = lax.dot_general(q, keys, nt, preferred_element_type=jnp.float32) * scale
        s = jnp.where(visible, s, LOW_SCORE)
        top = jnp.max(s, axis=1, keepdims=True)
        w = jnp.where(visible, jnp.exp2(s - top), 0.0).astype(jnp.bfloat16)
        both = jnp.dot(w, jnp.concatenate([values, ones], axis=1), preferred_element_type=jnp.float32)
        total = both[:, HD:]
        out_ref[g] = both[:, :HD] / total
        lse_ref[g] = top + jnp.log(total) * LOG2E


def project_kernel(per, hist_ref, out_ref, lse_ref, match_ref, w_ref, y_ref, att_ref):
    tokens = y_ref.shape[0]
    holders = hist_ref.shape[0]
    fold = LANES // per
    row = lax.broadcasted_iota(jnp.int32, (holders, LANES), 0)
    lane = lax.broadcasted_iota(jnp.int32, (holders, LANES), 1)
    for g in range(KVH):
        outs = hist_ref[:, g, :per, :].reshape(holders * per, HD)
        stats = jnp.sum(hist_ref[:, g, per:, :].astype(jnp.float32), axis=1)
        stats = jnp.where(row % fold == lane // per, stats, 0.0)
        lse = jnp.concatenate(
            [
                jnp.sum(jnp.where(row // fold == m, stats, 0.0), axis=0, keepdims=True)
                for m in range(holders // fold)
            ],
            axis=1,
        )
        match = match_ref[g] > 0.5
        lse = jnp.where(match, lse, LOW_SCORE)
        own = lse_ref[g]
        top = jnp.maximum(jnp.max(lse, axis=1, keepdims=True), own)
        w = jnp.where(match, jnp.exp2(lse - top[:, :1]), 0.0)
        own_w = jnp.exp2(own - top)
        hi = w.astype(jnp.bfloat16)
        low = (w - hi.astype(jnp.float32)).astype(jnp.bfloat16)
        num = (
            jnp.dot(hi, outs, preferred_element_type=jnp.float32)
            + jnp.dot(low, outs, preferred_element_type=jnp.float32)
            + own_w * out_ref[g]
        )
        att = num / (jnp.sum(w, axis=1, keepdims=True) + own_w)
        for r in range(GROUP):
            h = g * GROUP + r
            att_ref[:, h * HD : (h + 1) * HD] = att[r * tokens : (r + 1) * tokens]
    y_ref[...] = jnp.dot(
        att_ref[...].astype(jnp.bfloat16), w_ref[...], preferred_element_type=jnp.float32
    ).astype(jnp.bfloat16)


VMEM = pl.BlockSpec(memory_space=pltpu.VMEM)
SMEM = pl.BlockSpec(memory_space=pltpu.SMEM)


def call(kernel, name, out_shape, specs, *operands, scratch=(), flops=0, moved=0, limit=16):
    outs = jax.tree.map(lambda _: VMEM, out_shape)
    return pl.pallas_call(
        kernel,
        name=name,
        out_shape=out_shape,
        in_specs=specs,
        out_specs=outs,
        scratch_shapes=scratch,
        cost_estimate=pl.CostEstimate(flops=flops, bytes_accessed=moved, transcendentals=0),
        compiler_params=pltpu.CompilerParams(vmem_limit_bytes=limit << 20),
    )(*operands)


def body(queries, stretch_keys, stretch_values, cache_keys, cache_values, chosen, out_weight):
    devices = lax.axis_size("seq")
    device_index = lax.axis_index("seq")
    tokens = queries.shape[0]
    cache_rows = cache_keys.shape[0]
    span = BLK // cache_rows
    chips = span // KVH
    key_blocks = cache_rows * devices // BLK
    capacity = (GROUP * TOPK + key_blocks - 1) // key_blocks + 1
    per = capacity * tokens
    core = device_index % KVH
    swap = [(i, i ^ 1) for i in range(devices)]
    f32, bf16 = jnp.float32, jnp.bfloat16

    send = call(
        functools.partial(pack_kernel, chips, capacity),
        "pack",
        jax.ShapeDtypeStruct((devices, per + 2 * tokens, HD), bf16),
        [SMEM, VMEM, VMEM, VMEM],
        chosen, queries, stretch_keys, stretch_values,
    )
    got = lax.all_to_all(send, "seq", split_axis=0, concat_axis=0, tiled=True)

    away = (1 - core) * HD
    peer_cache = lax.ppermute(
        jnp.stack(
            [
                lax.dynamic_slice_in_dim(cache_keys, away, HD, axis=1),
                lax.dynamic_slice_in_dim(cache_values, away, HD, axis=1),
            ]
        ),
        "seq",
        swap,
    )
    place = jnp.stack([core, device_index * tokens]).astype(jnp.int32)
    rows = devices * per
    back = call(
        functools.partial(attend_kernel, per),
        "attend",
        jax.ShapeDtypeStruct((devices, per + 16, HD), bf16),
        [SMEM, VMEM, VMEM, VMEM, VMEM],
        place, got, cache_keys, cache_values, peer_cache,
        scratch=[pltpu.VMEM((cache_rows, 2 * HD), bf16)] * 2,
        flops=8 * rows * cache_rows * HD,
        moved=4 << 20,
        limit=32,
    )
    hist = lax.all_to_all(back, "seq", split_axis=0, concat_axis=0, tiled=True)

    fresh = got[:, per:, :]
    peer_fresh = lax.ppermute(fresh, "seq", swap)
    holders = devices // KVH
    out, lse, match = call(
        functools.partial(fresh_kernel, chips, capacity),
        "fresh",
        (
            jax.ShapeDtypeStruct((KVH, GROUP * tokens, HD), f32),
            jax.ShapeDtypeStruct((KVH, GROUP * tokens, HD), f32),
            jax.ShapeDtypeStruct((KVH, GROUP * tokens, holders * per), f32),
        ),
        [SMEM, SMEM, VMEM, VMEM, VMEM],
        place, chosen, queries, fresh, peer_fresh,
        flops=8 * H * tokens * devices * tokens * HD,
        moved=2 << 20,
    )
    return call(
        functools.partial(project_kernel, per),
        "project",
        jax.ShapeDtypeStruct((tokens, out_weight.shape[1]), bf16),
        [VMEM] * 5,
        hist.reshape(holders, KVH, per + 16, HD), out, lse, match, out_weight,
        scratch=[pltpu.VMEM((tokens, H * HD), f32)],
        flops=2 * tokens * out_weight.size,
        moved=out_weight.size * 2,
        limit=24,
    )


def solution(mesh):
    seq = ("grp", "seq")
    return jax.shard_map(
        body,
        mesh=mesh,
        in_specs=(
            P(seq, None),
            P(seq, None),
            P(seq, None),
            P(seq, None),
            P(seq, None),
            P(seq, None, None),
            P(),
        ),
        out_specs=P(seq, None),
        check_vma=False,
    )
```

```python
import functools
import math

import jax
import jax.numpy as jnp
from jax import lax
from jax.experimental import pallas as pl
from jax.experimental.pallas import tpu as pltpu
from jax.sharding import PartitionSpec as P

H = 14
KVH = 2
HD = 128
BLK = 4096
TOPK = 3
GROUP = H // KVH

LOW_SCORE = -1e30
LOG2E = math.log2(math.e)
LANES = 128


def head_rows(q_ref, g):
    q = q_ref[...].astype(jnp.float32)
    return [q[:, h * HD : (h + 1) * HD] for h in range(g * GROUP, (g + 1) * GROUP)]


def slot_match(chosen_ref, g, block, slot, token):
    rows = lax.broadcasted_iota(jnp.int32, block.shape, 0)
    same_token = token == rows
    seen = jnp.zeros(block.shape, jnp.int32)
    found = []
    for h in range(g * GROUP, (g + 1) * GROUP):
        picked = block == chosen_ref[0, :, h : h + 1]
        for t in range(1, TOPK):
            picked = picked | (block == chosen_ref[t, :, h : h + 1])
        found.append(jnp.where(picked & same_token & (seen == slot), 1.0, 0.0))
        seen = seen + picked.astype(jnp.int32)
    return found


def fetch(pairs, sems):
    copies = [pltpu.make_async_copy(src, dst, sems.at[i]) for i, (src, dst) in enumerate(pairs)]
    for copy in copies:
        copy.start()
    return copies


def pack_kernel(chips, capacity, chosen_hbm, q_hbm, k_hbm, v_hbm, send_ref, fresh_ref, chosen_ref, q_ref, sems):
    copies = fetch(
        [(chosen_hbm, chosen_ref), (q_hbm, q_ref), (k_hbm, fresh_ref.at[0]), (v_hbm, fresh_ref.at[1])], sems
    )
    tokens = q_ref.shape[0]
    per = capacity * tokens
    span = chips * KVH
    key_blocks = send_ref.shape[0] // span
    lane = lax.broadcasted_iota(jnp.int32, (tokens, key_blocks * per), 1)
    block, slot, token = lane // per, lane % per // tokens, lane % tokens
    for copy in copies:
        copy.wait()
    for g in range(KVH):
        spread = jnp.concatenate(
            slot_match(chosen_ref, g, block, slot, token) + [jnp.zeros(lane.shape, jnp.float32)], axis=0
        )
        rows = head_rows(q_ref, g)
        rows = jnp.concatenate(rows + [jnp.zeros_like(rows[0])], axis=0)
        slots = jnp.dot(
            spread.T.astype(jnp.bfloat16), rows.astype(jnp.bfloat16), preferred_element_type=jnp.float32
        ).astype(jnp.bfloat16)
        for b in range(key_blocks):
            for chip in range(chips):
                send_ref[b * span + chip * KVH + g] = slots[b * per : (b + 1) * per]


def split_kernel(after_ref, k_hbm, v_hbm, own_ref, away_ref, sems):
    core = lax.axis_index("seq") % KVH
    own = pl.ds(pl.multiple_of(core * HD, HD), HD)
    away = pl.ds(pl.multiple_of((1 - core) * HD, HD), HD)
    copies = fetch(
        [
            (k_hbm.at[:, away], away_ref.at[:, :HD]),
            (v_hbm.at[:, away], away_ref.at[:, HD : 2 * HD]),
            (k_hbm.at[:, own], own_ref.at[:, :HD]),
            (v_hbm.at[:, own], own_ref.at[:, HD : 2 * HD]),
        ],
        sems,
    )
    ones = jnp.ones((own_ref.shape[0], HD), jnp.bfloat16)
    own_ref[:, 2 * HD :] = ones
    away_ref[:, 2 * HD :] = ones
    for copy in copies:
        copy.wait()


def attend_kernel(q_ref, own_ref, peer_ref, out_ref):
    sources, per = q_ref.shape[:2]
    step = 256 // per
    scale = LOG2E * HD**-0.5
    nt = (((1,), (1,)), ((), ()))
    row = lax.broadcasted_iota(jnp.int32, (per, LANES), 0)
    lane = lax.broadcasted_iota(jnp.int32, (per, LANES), 1)
    diagonal = row == lane % per
    piece = lax.broadcasted_iota(jnp.int32, (8, LANES), 0)
    for first in range(0, sources, step):
        q = q_ref[first : first + step].reshape(step * per, HD)
        sa = lax.dot_general(q, own_ref[:, :HD], nt, preferred_element_type=jnp.float32)
        sb = lax.dot_general(q, peer_ref[:, :HD], nt, preferred_element_type=jnp.float32)
        top = jnp.maximum(jnp.max(sa, axis=1, keepdims=True), jnp.max(sb, axis=1, keepdims=True)) * scale
        wa = jnp.exp2(sa * scale - top).astype(jnp.bfloat16)
        wb = jnp.exp2(sb * scale - top).astype(jnp.bfloat16)
        both = jnp.dot(wa, own_ref[:, HD:], preferred_element_type=jnp.float32) + jnp.dot(
            wb, peer_ref[:, HD:], preferred_element_type=jnp.float32
        )
        total = both[:, HD:]
        out = (both[:, :HD] / total).astype(jnp.bfloat16)
        lse = top + jnp.log(total) * LOG2E
        for s in range(step):
            part = slice(s * per, (s + 1) * per)
            out_ref[first + s, :per, :] = out[part]
            flat = jnp.sum(jnp.where(diagonal, lse[part], 0.0), axis=0, keepdims=True)
            hi = flat.astype(jnp.bfloat16).astype(jnp.float32)
            mid = (flat - hi).astype(jnp.bfloat16).astype(jnp.float32)
            low = flat - hi - mid
            out_ref[first + s, per:, :] = jnp.where(
                piece == 0, hi, jnp.where(piece == 1, mid, jnp.where(piece == 2, low, 0.0))
            ).astype(jnp.bfloat16)


def fresh_kernel(chips, capacity, after_ref, chosen_hbm, q_hbm, w_hbm, kv_ref, out_ref, lse_ref, match_ref, w_ref, chosen_ref, q_ref, sems):
    copies = fetch([(chosen_hbm, chosen_ref), (q_hbm, q_ref), (w_hbm, w_ref)], sems)
    tokens = q_ref.shape[0]
    sources = kv_ref.shape[0]
    per = capacity * tokens
    place = lax.axis_index("seq")
    scale = LOG2E * HD**-0.5
    nt = (((1,), (1,)), ((), ()))
    column = lax.broadcasted_iota(jnp.int32, (tokens, sources * tokens), 1)
    source, bits = place, sources.bit_length() - 1
    for i in range(bits):
        source = source ^ ((column // (tokens << i) & 1) << (bits - 1 - i))
    key_pos = source * tokens + column % tokens
    query_pos = place * tokens + lax.broadcasted_iota(jnp.int32, column.shape, 0)
    visible = (key_pos <= query_pos) & (key_pos // BLK == query_pos // BLK)
    visible = jnp.concatenate([visible.astype(jnp.int32)] * GROUP, axis=0) > 0
    lane = lax.broadcasted_iota(jnp.int32, (tokens, match_ref.shape[2]), 1)
    block, slot, token = lane // (per * chips), lane % per // tokens, lane % tokens
    ones = jnp.ones((sources * tokens, HD), jnp.bfloat16)
    copies[0].wait()
    copies[1].wait()
    for g in range(KVH):
        match_ref[g] = jnp.concatenate(slot_match(chosen_ref, g, block, slot, token), axis=0)
        keys, values = [
            kv_ref[:, i, :, g * HD : (g + 1) * HD]
            .astype(jnp.float32)
            .reshape(sources * tokens, HD)
            .astype(jnp.bfloat16)
            for i in range(2)
        ]
        q = jnp.concatenate(head_rows(q_ref, g), axis=0).astype(jnp.bfloat16)
        s = lax.dot_general(q, keys, nt, preferred_element_type=jnp.float32) * scale
        s = jnp.where(visible, s, LOW_SCORE)
        top = jnp.max(s, axis=1, keepdims=True)
        w = jnp.where(visible, jnp.exp2(s - top), 0.0).astype(jnp.bfloat16)
        both = jnp.dot(w, jnp.concatenate([values, ones], axis=1), preferred_element_type=jnp.float32)
        total = both[:, HD:]
        out_ref[g] = both[:, :HD] / total
        lse_ref[g] = top + jnp.log(total) * LOG2E
    copies[2].wait()


def project_kernel(per, hist_ref, out_ref, lse_ref, match_ref, w_ref, y_ref, att_ref):
    tokens = y_ref.shape[0]
    holders = hist_ref.shape[0]
    fold = LANES // per
    row = lax.broadcasted_iota(jnp.int32, (holders, LANES), 0)
    lane = lax.broadcasted_iota(jnp.int32, (holders, LANES), 1)
    for g in range(KVH):
        outs = hist_ref[:, g, :per, :].reshape(holders * per, HD)
        stats = jnp.sum(hist_ref[:, g, per:, :].astype(jnp.float32), axis=1)
        stats = jnp.where(row % fold == lane // per, stats, 0.0)
        lse = jnp.concatenate(
            [
                jnp.sum(jnp.where(row // fold == m, stats, 0.0), axis=0, keepdims=True)
                for m in range(holders // fold)
            ],
            axis=1,
        )
        match = match_ref[g] > 0.5
        lse = jnp.where(match, lse, LOW_SCORE)
        own = lse_ref[g]
        top = jnp.maximum(jnp.max(lse, axis=1, keepdims=True), own)
        w = jnp.where(match, jnp.exp2(lse - top[:, :1]), 0.0)
        own_w = jnp.exp2(own - top)
        hi = w.astype(jnp.bfloat16)
        low = (w - hi.astype(jnp.float32)).astype(jnp.bfloat16)
        num = (
            jnp.dot(hi, outs, preferred_element_type=jnp.float32)
            + jnp.dot(low, outs, preferred_element_type=jnp.float32)
            + own_w * out_ref[g]
        )
        att = num / (jnp.sum(w, axis=1, keepdims=True) + own_w)
        for r in range(GROUP):
            h = g * GROUP + r
            att_ref[:, h * HD : (h + 1) * HD] = att[r * tokens : (r + 1) * tokens]
    y_ref[...] = jnp.dot(
        att_ref[...].astype(jnp.bfloat16), w_ref[...], preferred_element_type=jnp.float32
    ).astype(jnp.bfloat16)


VMEM = pl.BlockSpec(memory_space=pltpu.VMEM)
HBM = pl.BlockSpec(memory_space=pltpu.HBM)
ANY = pl.BlockSpec(memory_space=pl.ANY)


def call(kernel, name, out_shape, specs, *operands, scratch=(), flops=0, moved=0, limit=16):
    outs = jax.tree.map(lambda _: VMEM, out_shape)
    return pl.pallas_call(
        kernel,
        name=name,
        out_shape=out_shape,
        in_specs=specs,
        out_specs=outs,
        scratch_shapes=scratch,
        cost_estimate=pl.CostEstimate(flops=flops, bytes_accessed=moved, transcendentals=0),
        compiler_params=pltpu.CompilerParams(vmem_limit_bytes=limit << 20),
    )(*operands)


def body(queries, stretch_keys, stretch_values, cache_keys, cache_values, chosen, out_weight):
    devices = lax.axis_size("seq")
    tokens = queries.shape[0]
    cache_rows = cache_keys.shape[0]
    span = BLK // cache_rows
    chips = span // KVH
    key_blocks = cache_rows * devices // BLK
    capacity = (GROUP * TOPK + key_blocks - 1) // key_blocks + 1
    per = capacity * tokens
    f32, bf16 = jnp.float32, jnp.bfloat16
    picks = chosen.transpose(2, 0, 1)

    def partner(bit):
        return [(i, i ^ bit) for i in range(devices)]

    send, fresh = call(
        functools.partial(pack_kernel, chips, capacity),
        "pack",
        (
            jax.ShapeDtypeStruct((devices, per, HD), bf16),
            jax.ShapeDtypeStruct((2, tokens, KVH * HD), bf16),
        ),
        [HBM] * 4,
        picks, queries, stretch_keys, stretch_values,
        scratch=[
            pltpu.VMEM(picks.shape, jnp.int32),
            pltpu.VMEM(queries.shape, bf16),
            pltpu.SemaphoreType.DMA((4,)),
        ],
        limit=60,
    )
    got = lax.all_to_all(send, "seq", split_axis=0, concat_axis=0, tiled=True)

    side = jax.ShapeDtypeStruct((cache_rows, 3 * HD), bf16)
    own, away = call(
        split_kernel,
        "split",
        (side, side),
        [ANY, HBM, HBM],
        fresh, cache_keys, cache_values,
        scratch=[pltpu.SemaphoreType.DMA((4,))],
        moved=4 << 20,
    )
    peer = lax.ppermute(away, "seq", partner(1))

    gathered = fresh[None]
    bit = devices // 2
    while bit:
        gathered = jnp.concatenate([gathered, lax.ppermute(gathered, "seq", partner(bit))], axis=0)
        bit //= 2
    rows = devices * per
    back = call(
        attend_kernel,
        "attend",
        jax.ShapeDtypeStruct((devices, per + 8, HD), bf16),
        [VMEM] * 3,
        got, own, peer,
        flops=8 * rows * cache_rows * HD,
        moved=4 << 20,
        limit=32,
    )
    hist = lax.all_to_all(back, "seq", split_axis=0, concat_axis=0, tiled=True)

    holders = devices // KVH
    out, lse, match, weight = call(
        functools.partial(fresh_kernel, chips, capacity),
        "fresh",
        (
            jax.ShapeDtypeStruct((KVH, GROUP * tokens, HD), f32),
            jax.ShapeDtypeStruct((KVH, GROUP * tokens, HD), f32),
            jax.ShapeDtypeStruct((KVH, GROUP * tokens, holders * per), f32),
            jax.ShapeDtypeStruct(out_weight.shape, bf16),
        ),
        [ANY, HBM, HBM, HBM, VMEM],
        back, picks, queries, out_weight, gathered,
        scratch=[
            pltpu.VMEM(picks.shape, jnp.int32),
            pltpu.VMEM(queries.shape, bf16),
            pltpu.SemaphoreType.DMA((3,)),
        ],
        flops=8 * H * tokens * devices * tokens * HD,
        moved=8 << 20,
        limit=20,
    )
    return call(
        functools.partial(project_kernel, per),
        "project",
        jax.ShapeDtypeStruct((tokens, out_weight.shape[1]), bf16),
        [VMEM] * 5,
        hist.reshape(holders, KVH, per + 8, HD), out, lse, match, weight,
        scratch=[pltpu.VMEM((tokens, H * HD), f32)],
        flops=2 * tokens * out_weight.size,
        moved=out_weight.size * 2,
        limit=20,
    )


def solution(mesh):
    seq = ("grp", "seq")
    return jax.shard_map(
        body,
        mesh=mesh,
        in_specs=(
            P(seq, None),
            P(seq, None),
            P(seq, None),
            P(seq, None),
            P(seq, None),
            P(seq, None, None),
            P(),
        ),
        out_specs=P(seq, None),
        check_vma=False,
    )
```

```python
import functools
import math

import jax
import jax.numpy as jnp
from jax import lax
from jax.experimental import pallas as pl
from jax.experimental.pallas import tpu as pltpu
from jax.sharding import PartitionSpec as P

H = 14
KVH = 2
HD = 128
BLK = 4096
TOPK = 3
GROUP = H // KVH

LOW_SCORE = -1e30
LOG2E = math.log2(math.e)
LANES = 128


def head_rows(q_ref, g):
    q = q_ref[...].astype(jnp.float32)
    return [q[:, h * HD : (h + 1) * HD] for h in range(g * GROUP, (g + 1) * GROUP)]


def slot_match(chosen_ref, g, block, slot, token):
    rows = lax.broadcasted_iota(jnp.int32, block.shape, 0)
    same_token = token == rows
    seen = jnp.zeros(block.shape, jnp.int32)
    found = []
    for h in range(g * GROUP, (g + 1) * GROUP):
        picked = block == chosen_ref[0, :, h : h + 1]
        for t in range(1, TOPK):
            picked = picked | (block == chosen_ref[t, :, h : h + 1])
        found.append(jnp.where(picked & same_token & (seen == slot), 1.0, 0.0))
        seen = seen + picked.astype(jnp.int32)
    return found


def fetch(pairs, sems):
    copies = [pltpu.make_async_copy(src, dst, sems.at[i]) for i, (src, dst) in enumerate(pairs)]
    for copy in copies:
        copy.start()
    return copies


def pack_kernel(chips, capacity, chosen_hbm, q_hbm, k_hbm, v_hbm, send_ref, chosen_ref, q_ref, k_ref, v_ref, sems):
    copies = fetch([(chosen_hbm, chosen_ref), (q_hbm, q_ref), (k_hbm, k_ref), (v_hbm, v_ref)], sems)
    tokens = q_ref.shape[0]
    per = capacity * tokens
    span = chips * KVH
    key_blocks = send_ref.shape[0] // span
    lane = lax.broadcasted_iota(jnp.int32, (tokens, key_blocks * per), 1)
    block, slot, token = lane // per, lane % per // tokens, lane % tokens
    for copy in copies:
        copy.wait()
    for g in range(KVH):
        spread = jnp.concatenate(
            slot_match(chosen_ref, g, block, slot, token) + [jnp.zeros(lane.shape, jnp.float32)], axis=0
        )
        rows = head_rows(q_ref, g)
        rows = jnp.concatenate(rows + [jnp.zeros_like(rows[0])], axis=0)
        slots = jnp.dot(
            spread.T.astype(jnp.bfloat16), rows.astype(jnp.bfloat16), preferred_element_type=jnp.float32
        ).astype(jnp.bfloat16)
        cols = slice(g * HD, (g + 1) * HD)
        fresh = [k_ref[:, cols], v_ref[:, cols]]
        for b in range(key_blocks):
            for chip in range(chips):
                to = b * span + chip * KVH + g
                send_ref[to, :per, :] = slots[b * per : (b + 1) * per]
                send_ref[to, per:, :] = fresh[chip % 2]


def attend_kernel(per, q_ref, own_ref, peer_ref, out_ref, fresh_ref):
    sources = q_ref.shape[0]
    fresh_ref[...] = q_ref[:, per:, :]
    step = 256 // per
    scale = LOG2E * HD**-0.5
    nt = (((1,), (1,)), ((), ()))
    row = lax.broadcasted_iota(jnp.int32, (per, LANES), 0)
    lane = lax.broadcasted_iota(jnp.int32, (per, LANES), 1)
    diagonal = row == lane % per
    piece = lax.broadcasted_iota(jnp.int32, (8, LANES), 0)
    for first in range(0, sources, step):
        q = q_ref[first : first + step, :per, :].reshape(step * per, HD)
        sa = lax.dot_general(q, own_ref[:, :HD], nt, preferred_element_type=jnp.float32)
        sb = lax.dot_general(q, peer_ref[:, :HD], nt, preferred_element_type=jnp.float32)
        top = jnp.maximum(jnp.max(sa, axis=1, keepdims=True), jnp.max(sb, axis=1, keepdims=True)) * scale
        wa = jnp.exp2(sa * scale - top).astype(jnp.bfloat16)
        wb = jnp.exp2(sb * scale - top).astype(jnp.bfloat16)
        both = jnp.dot(wa, own_ref[:, HD:], preferred_element_type=jnp.float32) + jnp.dot(
            wb, peer_ref[:, HD:], preferred_element_type=jnp.float32
        )
        total = both[:, HD:]
        out = (both[:, :HD] / total).astype(jnp.bfloat16)
        lse = top + jnp.log(total) * LOG2E
        for s in range(step):
            part = slice(s * per, (s + 1) * per)
            out_ref[first + s, :per, :] = out[part]
            flat = jnp.sum(jnp.where(diagonal, lse[part], 0.0), axis=0, keepdims=True)
            hi = flat.astype(jnp.bfloat16).astype(jnp.float32)
            mid = (flat - hi).astype(jnp.bfloat16).astype(jnp.float32)
            low = flat - hi - mid
            out_ref[first + s, per:, :] = jnp.where(
                piece == 0, hi, jnp.where(piece == 1, mid, jnp.where(piece == 2, low, 0.0))
            ).astype(jnp.bfloat16)


def fresh_kernel(chips, capacity, chosen_hbm, q_hbm, kv_ref, kv1_ref, kv2_ref, kv3_ref, out_ref, lse_ref, match_ref, chosen_ref, q_ref, sems):
    copies = fetch([(chosen_hbm, chosen_ref), (q_hbm, q_ref)], sems)
    tokens = q_ref.shape[0]
    sources = kv_ref.shape[0]
    per = capacity * tokens
    place = lax.axis_index("seq")
    core, odd = place % KVH, place // KVH % 2
    scale = LOG2E * HD**-0.5
    nt = (((1,), (1,)), ((), ()))
    column = lax.broadcasted_iota(jnp.int32, (tokens, sources * tokens), 1)
    query_pos = place * tokens + lax.broadcasted_iota(jnp.int32, column.shape, 0)
    visible = (column <= query_pos) & (column // BLK == query_pos // BLK)
    visible = jnp.concatenate([visible.astype(jnp.int32)] * GROUP, axis=0) > 0
    lane = lax.broadcasted_iota(jnp.int32, (tokens, match_ref.shape[2]), 1)
    block, slot, token = lane // (per * chips), lane % per // tokens, lane % tokens
    ones = jnp.ones((sources * tokens, HD), jnp.bfloat16)
    here, near, far, both = [
        ref[...].astype(jnp.float32).reshape(sources * tokens, HD) for ref in (kv_ref, kv1_ref, kv2_ref, kv3_ref)
    ]
    keys = [jnp.where(odd == 0, here, far), jnp.where(odd == 0, near, both)]
    values = [jnp.where(odd == 0, far, here), jnp.where(odd == 0, both, near)]
    for copy in copies:
        copy.wait()
    for g in range(KVH):
        match_ref[g] = jnp.concatenate(slot_match(chosen_ref, g, block, slot, token), axis=0)
        k = jnp.where(core == g, keys[0], keys[1]).astype(jnp.bfloat16)
        v = jnp.where(core == g, values[0], values[1]).astype(jnp.bfloat16)
        q = jnp.concatenate(head_rows(q_ref, g), axis=0).astype(jnp.bfloat16)
        s = lax.dot_general(q, k, nt, preferred_element_type=jnp.float32) * scale
        s = jnp.where(visible, s, LOW_SCORE)
        top = jnp.max(s, axis=1, keepdims=True)
        w = jnp.where(visible, jnp.exp2(s - top), 0.0).astype(jnp.bfloat16)
        total_out = jnp.dot(w, jnp.concatenate([v, ones], axis=1), preferred_element_type=jnp.float32)
        total = total_out[:, HD:]
        out_ref[g] = total_out[:, :HD] / total
        lse_ref[g] = top + jnp.log(total) * LOG2E


def project_kernel(per, hist_ref, out_ref, lse_ref, match_ref, w_hbm, y_ref, att_ref, w_ref, sems):
    depth = w_ref.shape[0] // GROUP
    chunks = [pl.ds(i * depth, depth) for i in range(GROUP)]
    copies = fetch([(w_hbm.at[chunk], w_ref.at[chunk]) for chunk in chunks], sems)
    tokens = y_ref.shape[0]
    holders = hist_ref.shape[0]
    fold = LANES // per
    row = lax.broadcasted_iota(jnp.int32, (holders, LANES), 0)
    lane = lax.broadcasted_iota(jnp.int32, (holders, LANES), 1)
    for g in range(KVH):
        outs = hist_ref[:, g, :per, :].reshape(holders * per, HD)
        stats = jnp.sum(hist_ref[:, g, per:, :].astype(jnp.float32), axis=1)
        stats = jnp.where(row % fold == lane // per, stats, 0.0)
        lse = jnp.concatenate(
            [
                jnp.sum(jnp.where(row // fold == m, stats, 0.0), axis=0, keepdims=True)
                for m in range(holders // fold)
            ],
            axis=1,
        )
        match = match_ref[g] > 0.5
        lse = jnp.where(match, lse, LOW_SCORE)
        own = lse_ref[g]
        top = jnp.maximum(jnp.max(lse, axis=1, keepdims=True), own)
        w = jnp.where(match, jnp.exp2(lse - top[:, :1]), 0.0)
        own_w = jnp.exp2(own - top)
        hi = w.astype(jnp.bfloat16)
        low = (w - hi.astype(jnp.float32)).astype(jnp.bfloat16)
        num = (
            jnp.dot(hi, outs, preferred_element_type=jnp.float32)
            + jnp.dot(low, outs, preferred_element_type=jnp.float32)
            + own_w * out_ref[g]
        )
        att = num / (jnp.sum(w, axis=1, keepdims=True) + own_w)
        for r in range(GROUP):
            h = g * GROUP + r
            att_ref[:, h * HD : (h + 1) * HD] = att[r * tokens : (r + 1) * tokens]
    y = jnp.zeros(y_ref.shape, jnp.float32)
    for chunk, copy in zip(chunks, copies):
        att = att_ref[:, chunk].astype(jnp.bfloat16)
        copy.wait()
        y = y + jnp.dot(att, w_ref[chunk, :], preferred_element_type=jnp.float32)
    y_ref[...] = y.astype(jnp.bfloat16)


VMEM = pl.BlockSpec(memory_space=pltpu.VMEM)
HBM = pl.BlockSpec(memory_space=pltpu.HBM)


def call(kernel, name, out_shape, specs, *operands, scratch=(), flops=0, moved=0, limit=16):
    outs = jax.tree.map(lambda _: VMEM, out_shape)
    return pl.pallas_call(
        kernel,
        name=name,
        out_shape=out_shape,
        in_specs=specs,
        out_specs=outs,
        scratch_shapes=scratch,
        cost_estimate=pl.CostEstimate(flops=flops, bytes_accessed=moved, transcendentals=0),
        compiler_params=pltpu.CompilerParams(vmem_limit_bytes=limit << 20),
    )(*operands)


def body(queries, stretch_keys, stretch_values, cache_keys, cache_values, chosen, out_weight):
    devices = lax.axis_size("seq")
    tokens = queries.shape[0]
    cache_rows = cache_keys.shape[0]
    span = BLK // cache_rows
    chips = span // KVH
    key_blocks = cache_rows * devices // BLK
    capacity = (GROUP * TOPK + key_blocks - 1) // key_blocks + 1
    per = capacity * tokens
    f32, bf16 = jnp.float32, jnp.bfloat16
    picks = chosen.transpose(2, 0, 1)

    def partner(bit):
        return [(i, i ^ bit) for i in range(devices)]

    send = call(
        functools.partial(pack_kernel, chips, capacity),
        "pack",
        jax.ShapeDtypeStruct((devices, per + tokens, HD), bf16),
        [HBM] * 4,
        picks, queries, stretch_keys, stretch_values,
        scratch=[
            pltpu.VMEM(picks.shape, jnp.int32),
            pltpu.VMEM(queries.shape, bf16),
            pltpu.VMEM(stretch_keys.shape, bf16),
            pltpu.VMEM(stretch_values.shape, bf16),
            pltpu.SemaphoreType.DMA((4,)),
        ],
        limit=60,
    )
    got = lax.all_to_all(send, "seq", split_axis=0, concat_axis=0, tiled=True)

    core = lax.axis_index("seq") % KVH
    ones = jnp.ones((cache_rows, HD), bf16)

    def side(head):
        columns = [lax.dynamic_slice_in_dim(x, head * HD, HD, axis=1) for x in (cache_keys, cache_values)]
        return jnp.concatenate(columns + [ones], axis=1)

    own = side(core)
    peer = lax.ppermute(side(1 - core), "seq", partner(1))

    rows = devices * per
    back, fresh = call(
        functools.partial(attend_kernel, per),
        "attend",
        (
            jax.ShapeDtypeStruct((devices, per + 8, HD), bf16),
            jax.ShapeDtypeStruct((devices, tokens, HD), bf16),
        ),
        [VMEM] * 3,
        got, own, peer,
        flops=8 * rows * cache_rows * HD,
        moved=4 << 20,
        limit=32,
    )
    hist = lax.all_to_all(back, "seq", split_axis=0, concat_axis=0, tiled=True)

    holders = devices // KVH
    out, lse, match = call(
        functools.partial(fresh_kernel, chips, capacity),
        "fresh",
        (
            jax.ShapeDtypeStruct((KVH, GROUP * tokens, HD), f32),
            jax.ShapeDtypeStruct((KVH, GROUP * tokens, HD), f32),
            jax.ShapeDtypeStruct((KVH, GROUP * tokens, holders * per), f32),
        ),
        [HBM, HBM, VMEM, VMEM, VMEM, VMEM],
        picks, queries, fresh, *[lax.ppermute(fresh, "seq", partner(bit)) for bit in (1, 2, 3)],
        scratch=[
            pltpu.VMEM(picks.shape, jnp.int32),
            pltpu.VMEM(queries.shape, bf16),
            pltpu.SemaphoreType.DMA((2,)),
        ],
        flops=8 * H * tokens * devices * tokens * HD,
        moved=2 << 20,
        limit=20,
    )
    return call(
        functools.partial(project_kernel, per),
        "project",
        jax.ShapeDtypeStruct((tokens, out_weight.shape[1]), bf16),
        [VMEM] * 4 + [HBM],
        hist.reshape(holders, KVH, per + 8, HD), out, lse, match, out_weight,
        scratch=[
            pltpu.VMEM((tokens, H * HD), f32),
            pltpu.VMEM(out_weight.shape, bf16),
            pltpu.SemaphoreType.DMA((GROUP,)),
        ],
        flops=2 * tokens * out_weight.size,
        moved=out_weight.size * 2,
        limit=58,
    )


def solution(mesh):
    seq = ("grp", "seq")
    return jax.shard_map(
        body,
        mesh=mesh,
        in_specs=(
            P(seq, None),
            P(seq, None),
            P(seq, None),
            P(seq, None),
            P(seq, None),
            P(seq, None, None),
            P(),
        ),
        out_specs=P(seq, None),
        check_vma=False,
    )
```

```python
import functools
import math

import jax
import jax.numpy as jnp
from jax import lax
from jax.experimental import pallas as pl
from jax.experimental.pallas import tpu as pltpu
from jax.sharding import PartitionSpec as P

H = 14
KVH = 2
HD = 128
BLK = 4096
TOPK = 3
GROUP = H // KVH

LOW_SCORE = -1e30
LOG2E = math.log2(math.e)
LANES = 128


def head_rows(q_ref, g):
    q = q_ref[...].astype(jnp.float32)
    return [q[:, h * HD : (h + 1) * HD] for h in range(g * GROUP, (g + 1) * GROUP)]


def slot_match(chosen_ref, g, block, slot, token):
    rows = lax.broadcasted_iota(jnp.int32, block.shape, 0)
    same_token = token == rows
    seen = jnp.zeros(block.shape, jnp.int32)
    found = []
    for h in range(g * GROUP, (g + 1) * GROUP):
        picked = block == chosen_ref[0, :, h : h + 1]
        for t in range(1, TOPK):
            picked = picked | (block == chosen_ref[t, :, h : h + 1])
        found.append(jnp.where(picked & same_token & (seen == slot), 1.0, 0.0))
        seen = seen + picked.astype(jnp.int32)
    return found


def fetch(pairs, sems):
    copies = [pltpu.make_async_copy(src, dst, sems.at[i]) for i, (src, dst) in enumerate(pairs)]
    for copy in copies:
        copy.start()
    return copies


def pack_kernel(chips, capacity, chosen_hbm, q_hbm, k_hbm, v_hbm, send_ref, after_ref, chosen_ref, q_ref, k_ref, v_ref, sems):
    copies = fetch([(chosen_hbm, chosen_ref), (q_hbm, q_ref), (k_hbm, k_ref), (v_hbm, v_ref)], sems)
    tokens = q_ref.shape[0]
    per = capacity * tokens
    span = chips * KVH
    key_blocks = send_ref.shape[0] // span
    lane = lax.broadcasted_iota(jnp.int32, (tokens, key_blocks * per), 1)
    block, slot, token = lane // per, lane % per // tokens, lane % tokens
    for copy in copies:
        copy.wait()
    for g in range(KVH):
        spread = jnp.concatenate(
            slot_match(chosen_ref, g, block, slot, token) + [jnp.zeros(lane.shape, jnp.float32)], axis=0
        )
        rows = head_rows(q_ref, g)
        rows = jnp.concatenate(rows + [jnp.zeros_like(rows[0])], axis=0)
        slots = jnp.dot(
            spread.T.astype(jnp.bfloat16), rows.astype(jnp.bfloat16), preferred_element_type=jnp.float32
        ).astype(jnp.bfloat16)
        cols = slice(g * HD, (g + 1) * HD)
        fresh = [k_ref[:, cols], v_ref[:, cols]]
        for b in range(key_blocks):
            for chip in range(chips):
                to = b * span + chip * KVH + g
                send_ref[to, :per, :] = slots[b * per : (b + 1) * per]
                send_ref[to, per:, :] = fresh[chip % 2]
    after_ref[...] = jnp.zeros_like(after_ref)


def split_kernel(after_ref, k_hbm, v_hbm, own_ref, away_ref, sems):
    core = lax.axis_index("seq") % KVH
    own = pl.ds(pl.multiple_of(core * HD, HD), HD)
    away = pl.ds(pl.multiple_of((1 - core) * HD, HD), HD)
    copies = fetch(
        [
            (k_hbm.at[:, away], away_ref.at[:, :HD]),
            (v_hbm.at[:, away], away_ref.at[:, HD : 2 * HD]),
            (k_hbm.at[:, own], own_ref.at[:, :HD]),
            (v_hbm.at[:, own], own_ref.at[:, HD : 2 * HD]),
        ],
        sems,
    )
    ones = jnp.ones((own_ref.shape[0], HD), jnp.bfloat16)
    own_ref[:, 2 * HD :] = ones
    away_ref[:, 2 * HD :] = ones
    for copy in copies:
        copy.wait()


def attend_kernel(per, q_ref, own_ref, peer_ref, out_ref, fresh_ref):
    sources = q_ref.shape[0]
    fresh_ref[...] = q_ref[:, per:, :]
    step = 256 // per
    scale = LOG2E * HD**-0.5
    nt = (((1,), (1,)), ((), ()))
    row = lax.broadcasted_iota(jnp.int32, (per, LANES), 0)
    lane = lax.broadcasted_iota(jnp.int32, (per, LANES), 1)
    diagonal = row == lane % per
    piece = lax.broadcasted_iota(jnp.int32, (8, LANES), 0)
    for first in range(0, sources, step):
        q = q_ref[first : first + step, :per, :].reshape(step * per, HD)
        sa = lax.dot_general(q, own_ref[:, :HD], nt, preferred_element_type=jnp.float32)
        sb = lax.dot_general(q, peer_ref[:, :HD], nt, preferred_element_type=jnp.float32)
        top = jnp.maximum(jnp.max(sa, axis=1, keepdims=True), jnp.max(sb, axis=1, keepdims=True)) * scale
        wa = jnp.exp2(sa * scale - top).astype(jnp.bfloat16)
        wb = jnp.exp2(sb * scale - top).astype(jnp.bfloat16)
        both = jnp.dot(wa, own_ref[:, HD:], preferred_element_type=jnp.float32) + jnp.dot(
            wb, peer_ref[:, HD:], preferred_element_type=jnp.float32
        )
        total = both[:, HD:]
        out = (both[:, :HD] / total).astype(jnp.bfloat16)
        lse = top + jnp.log(total) * LOG2E
        for s in range(step):
            part = slice(s * per, (s + 1) * per)
            out_ref[first + s, :per, :] = out[part]
            flat = jnp.sum(jnp.where(diagonal, lse[part], 0.0), axis=0, keepdims=True)
            hi = flat.astype(jnp.bfloat16).astype(jnp.float32)
            mid = (flat - hi).astype(jnp.bfloat16).astype(jnp.float32)
            low = flat - hi - mid
            out_ref[first + s, per:, :] = jnp.where(
                piece == 0, hi, jnp.where(piece == 1, mid, jnp.where(piece == 2, low, 0.0))
            ).astype(jnp.bfloat16)


def fresh_kernel(chips, capacity, chosen_hbm, q_hbm, kv_ref, kv1_ref, kv2_ref, kv3_ref, out_ref, lse_ref, match_ref, chosen_ref, q_ref, sems):
    copies = fetch([(chosen_hbm, chosen_ref), (q_hbm, q_ref)], sems)
    tokens = q_ref.shape[0]
    sources = kv_ref.shape[0]
    per = capacity * tokens
    place = lax.axis_index("seq")
    core, odd = place % KVH, place // KVH % 2
    scale = LOG2E * HD**-0.5
    nt = (((1,), (1,)), ((), ()))
    column = lax.broadcasted_iota(jnp.int32, (tokens, sources * tokens), 1)
    query_pos = place * tokens + lax.broadcasted_iota(jnp.int32, column.shape, 0)
    visible = (column <= query_pos) & (column // BLK == query_pos // BLK)
    visible = jnp.concatenate([visible.astype(jnp.int32)] * GROUP, axis=0) > 0
    lane = lax.broadcasted_iota(jnp.int32, (tokens, match_ref.shape[2]), 1)
    block, slot, token = lane // (per * chips), lane % per // tokens, lane % tokens
    ones = jnp.ones((sources * tokens, HD), jnp.bfloat16)
    here, near, far, both = [
        ref[...].astype(jnp.float32).reshape(sources * tokens, HD) for ref in (kv_ref, kv1_ref, kv2_ref, kv3_ref)
    ]
    keys = [jnp.where(odd == 0, here, far), jnp.where(odd == 0, near, both)]
    values = [jnp.where(odd == 0, far, here), jnp.where(odd == 0, both, near)]
    for copy in copies:
        copy.wait()
    for g in range(KVH):
        match_ref[g] = jnp.concatenate(slot_match(chosen_ref, g, block, slot, token), axis=0)
        k = jnp.where(core == g, keys[0], keys[1]).astype(jnp.bfloat16)
        v = jnp.where(core == g, values[0], values[1]).astype(jnp.bfloat16)
        q = jnp.concatenate(head_rows(q_ref, g), axis=0).astype(jnp.bfloat16)
        s = lax.dot_general(q, k, nt, preferred_element_type=jnp.float32) * scale
        s = jnp.where(visible, s, LOW_SCORE)
        top = jnp.max(s, axis=1, keepdims=True)
        w = jnp.where(visible, jnp.exp2(s - top), 0.0).astype(jnp.bfloat16)
        total_out = jnp.dot(w, jnp.concatenate([v, ones], axis=1), preferred_element_type=jnp.float32)
        total = total_out[:, HD:]
        out_ref[g] = total_out[:, :HD] / total
        lse_ref[g] = top + jnp.log(total) * LOG2E


def project_kernel(per, hist_ref, out_ref, lse_ref, match_ref, w_hbm, y_ref, att_ref, w_ref, sems):
    depth = w_ref.shape[0] // GROUP
    chunks = [pl.ds(i * depth, depth) for i in range(GROUP)]
    copies = fetch([(w_hbm.at[chunk], w_ref.at[chunk]) for chunk in chunks], sems)
    tokens = y_ref.shape[0]
    holders = hist_ref.shape[0]
    fold = LANES // per
    row = lax.broadcasted_iota(jnp.int32, (holders, LANES), 0)
    lane = lax.broadcasted_iota(jnp.int32, (holders, LANES), 1)
    for g in range(KVH):
        outs = hist_ref[:, g, :per, :].reshape(holders * per, HD)
        stats = jnp.sum(hist_ref[:, g, per:, :].astype(jnp.float32), axis=1)
        stats = jnp.where(row % fold == lane // per, stats, 0.0)
        lse = jnp.concatenate(
            [
                jnp.sum(jnp.where(row // fold == m, stats, 0.0), axis=0, keepdims=True)
                for m in range(holders // fold)
            ],
            axis=1,
        )
        match = match_ref[g] > 0.5
        lse = jnp.where(match, lse, LOW_SCORE)
        own = lse_ref[g]
        top = jnp.maximum(jnp.max(lse, axis=1, keepdims=True), own)
        w = jnp.where(match, jnp.exp2(lse - top[:, :1]), 0.0)
        own_w = jnp.exp2(own - top)
        hi = w.astype(jnp.bfloat16)
        low = (w - hi.astype(jnp.float32)).astype(jnp.bfloat16)
        num = (
            jnp.dot(hi, outs, preferred_element_type=jnp.float32)
            + jnp.dot(low, outs, preferred_element_type=jnp.float32)
            + own_w * out_ref[g]
        )
        att = num / (jnp.sum(w, axis=1, keepdims=True) + own_w)
        for r in range(GROUP):
            h = g * GROUP + r
            att_ref[:, h * HD : (h + 1) * HD] = att[r * tokens : (r + 1) * tokens]
    y = jnp.zeros(y_ref.shape, jnp.float32)
    for chunk, copy in zip(chunks, copies):
        att = att_ref[:, chunk].astype(jnp.bfloat16)
        copy.wait()
        y = y + jnp.dot(att, w_ref[chunk, :], preferred_element_type=jnp.float32)
    y_ref[...] = y.astype(jnp.bfloat16)


VMEM = pl.BlockSpec(memory_space=pltpu.VMEM)
HBM = pl.BlockSpec(memory_space=pltpu.HBM)


def call(kernel, name, out_shape, specs, *operands, scratch=(), flops=0, moved=0, limit=16):
    outs = jax.tree.map(lambda _: VMEM, out_shape)
    return pl.pallas_call(
        kernel,
        name=name,
        out_shape=out_shape,
        in_specs=specs,
        out_specs=outs,
        scratch_shapes=scratch,
        cost_estimate=pl.CostEstimate(flops=flops, bytes_accessed=moved, transcendentals=0),
        compiler_params=pltpu.CompilerParams(vmem_limit_bytes=limit << 20),
    )(*operands)


def body(queries, stretch_keys, stretch_values, cache_keys, cache_values, chosen, out_weight):
    devices = lax.axis_size("seq")
    tokens = queries.shape[0]
    cache_rows = cache_keys.shape[0]
    span = BLK // cache_rows
    chips = span // KVH
    key_blocks = cache_rows * devices // BLK
    capacity = (GROUP * TOPK + key_blocks - 1) // key_blocks + 1
    per = capacity * tokens
    f32, bf16 = jnp.float32, jnp.bfloat16
    picks = chosen.transpose(2, 0, 1)

    def partner(bit):
        return [(i, i ^ bit) for i in range(devices)]

    send, after = call(
        functools.partial(pack_kernel, chips, capacity),
        "pack",
        (
            jax.ShapeDtypeStruct((devices, per + tokens, HD), bf16),
            jax.ShapeDtypeStruct((8, LANES), f32),
        ),
        [HBM] * 4,
        picks, queries, stretch_keys, stretch_values,
        scratch=[
            pltpu.VMEM(picks.shape, jnp.int32),
            pltpu.VMEM(queries.shape, bf16),
            pltpu.VMEM(stretch_keys.shape, bf16),
            pltpu.VMEM(stretch_values.shape, bf16),
            pltpu.SemaphoreType.DMA((4,)),
        ],
        limit=60,
    )
    got = lax.all_to_all(send, "seq", split_axis=0, concat_axis=0, tiled=True)

    side = jax.ShapeDtypeStruct((cache_rows, 3 * HD), bf16)
    own, away = call(
        split_kernel,
        "split",
        (side, side),
        [VMEM, HBM, HBM],
        after, cache_keys, cache_values,
        scratch=[pltpu.SemaphoreType.DMA((4,))],
    )
    peer = lax.ppermute(away, "seq", partner(1))

    rows = devices * per
    back, fresh = call(
        functools.partial(attend_kernel, per),
        "attend",
        (
            jax.ShapeDtypeStruct((devices, per + 8, HD), bf16),
            jax.ShapeDtypeStruct((devices, tokens, HD), bf16),
        ),
        [VMEM] * 3,
        got, own, peer,
        flops=8 * rows * cache_rows * HD,
        moved=4 << 20,
        limit=32,
    )
    hist = lax.all_to_all(back, "seq", split_axis=0, concat_axis=0, tiled=True)

    holders = devices // KVH
    out, lse, match = call(
        functools.partial(fresh_kernel, chips, capacity),
        "fresh",
        (
            jax.ShapeDtypeStruct((KVH, GROUP * tokens, HD), f32),
            jax.ShapeDtypeStruct((KVH, GROUP * tokens, HD), f32),
            jax.ShapeDtypeStruct((KVH, GROUP * tokens, holders * per), f32),
        ),
        [HBM, HBM, VMEM, VMEM, VMEM, VMEM],
        picks, queries, fresh, *[lax.ppermute(fresh, "seq", partner(bit)) for bit in (1, 2, 3)],
        scratch=[
            pltpu.VMEM(picks.shape, jnp.int32),
            pltpu.VMEM(queries.shape, bf16),
            pltpu.SemaphoreType.DMA((2,)),
        ],
        flops=8 * H * tokens * devices * tokens * HD,
        moved=2 << 20,
        limit=20,
    )
    return call(
        functools.partial(project_kernel, per),
        "project",
        jax.ShapeDtypeStruct((tokens, out_weight.shape[1]), bf16),
        [VMEM] * 4 + [HBM],
        hist.reshape(holders, KVH, per + 8, HD), out, lse, match, out_weight,
        scratch=[
            pltpu.VMEM((tokens, H * HD), f32),
            pltpu.VMEM(out_weight.shape, bf16),
            pltpu.SemaphoreType.DMA((GROUP,)),
        ],
        flops=2 * tokens * out_weight.size,
        moved=out_weight.size * 2,
        limit=50,
    )


def solution(mesh):
    seq = ("grp", "seq")
    return jax.shard_map(
        body,
        mesh=mesh,
        in_specs=(
            P(seq, None),
            P(seq, None),
            P(seq, None),
            P(seq, None),
            P(seq, None),
            P(seq, None, None),
            P(),
        ),
        out_specs=P(seq, None),
        check_vma=False,
    )
```

```python
import functools
import math

import jax
import jax.numpy as jnp
from jax import lax
from jax.experimental import pallas as pl
from jax.experimental.pallas import tpu as pltpu
from jax.sharding import PartitionSpec as P

H = 14
KVH = 2
HD = 128
BLK = 4096
TOPK = 3
GROUP = H // KVH

LOW_SCORE = -1e30
LOG2E = math.log2(math.e)
LANES = 128
EARLY = 3


def head_rows(q_ref, g):
    q = q_ref[...].astype(jnp.float32)
    return [q[:, h * HD : (h + 1) * HD] for h in range(g * GROUP, (g + 1) * GROUP)]


def slot_match(chosen_ref, g, block, slot, token):
    rows = lax.broadcasted_iota(jnp.int32, block.shape, 0)
    same_token = token == rows
    seen = jnp.zeros(block.shape, jnp.int32)
    found = []
    for h in range(g * GROUP, (g + 1) * GROUP):
        picked = block == chosen_ref[0, :, h : h + 1]
        for t in range(1, TOPK):
            picked = picked | (block == chosen_ref[t, :, h : h + 1])
        found.append(jnp.where(picked & same_token & (seen == slot), 1.0, 0.0))
        seen = seen + picked.astype(jnp.int32)
    return found


def fetch(pairs, sems):
    copies = [pltpu.make_async_copy(src, dst, sems.at[i]) for i, (src, dst) in enumerate(pairs)]
    for copy in copies:
        copy.start()
    return copies


def pack_kernel(chips, capacity, chosen_hbm, q_hbm, k_hbm, v_hbm, send_ref, after_ref, chosen_ref, q_ref, k_ref, v_ref, sems):
    copies = fetch([(chosen_hbm, chosen_ref), (q_hbm, q_ref), (k_hbm, k_ref), (v_hbm, v_ref)], sems)
    tokens = q_ref.shape[0]
    per = capacity * tokens
    span = chips * KVH
    key_blocks = send_ref.shape[0] // span
    lane = lax.broadcasted_iota(jnp.int32, (tokens, key_blocks * per), 1)
    block, slot, token = lane // per, lane % per // tokens, lane % tokens
    for copy in copies:
        copy.wait()
    for g in range(KVH):
        spread = jnp.concatenate(
            slot_match(chosen_ref, g, block, slot, token) + [jnp.zeros(lane.shape, jnp.float32)], axis=0
        )
        rows = head_rows(q_ref, g)
        rows = jnp.concatenate(rows + [jnp.zeros_like(rows[0])], axis=0)
        slots = jnp.dot(
            spread.T.astype(jnp.bfloat16), rows.astype(jnp.bfloat16), preferred_element_type=jnp.float32
        ).astype(jnp.bfloat16)
        cols = slice(g * HD, (g + 1) * HD)
        fresh = [k_ref[:, cols], v_ref[:, cols]]
        for b in range(key_blocks):
            for chip in range(chips):
                to = b * span + chip * KVH + g
                send_ref[to, :per, :] = slots[b * per : (b + 1) * per]
                send_ref[to, per:, :] = fresh[chip % 2]
    after_ref[...] = jnp.zeros_like(after_ref)


def split_kernel(
    chips, capacity, after_ref, k_hbm, v_hbm, chosen_hbm, q_hbm, w_hbm,
    k_own, v_own, k_away, v_away, match_ref, rows_ref, w_ref, chosen_ref, q_ref, sems,
):
    core = lax.axis_index("seq") % KVH
    own = pl.ds(pl.multiple_of(core * HD, HD), HD)
    away = pl.ds(pl.multiple_of((1 - core) * HD, HD), HD)
    copies = fetch(
        [
            (k_hbm.at[:, away], k_away),
            (v_hbm.at[:, away], v_away),
            (chosen_hbm, chosen_ref),
            (q_hbm, q_ref),
            (k_hbm.at[:, own], k_own),
            (v_hbm.at[:, own], v_own),
            (w_hbm.at[: w_ref.shape[0]], w_ref),
        ],
        sems,
    )
    tokens = q_ref.shape[0]
    per = capacity * tokens
    lane = lax.broadcasted_iota(jnp.int32, (tokens, match_ref.shape[2]), 1)
    block, slot, token = lane // (per * chips), lane % per // tokens, lane % tokens
    copies[2].wait()
    copies[3].wait()
    for g in range(KVH):
        match_ref[g] = jnp.concatenate(slot_match(chosen_ref, g, block, slot, token), axis=0)
        rows_ref[g] = jnp.concatenate(head_rows(q_ref, g), axis=0)
    for i in (0, 1, 4, 5, 6):
        copies[i].wait()


def attend_kernel(per, q_ref, ka_ref, va_ref, kb_ref, vb_ref, out_ref, fresh_ref):
    sources = q_ref.shape[0]
    fresh_ref[...] = q_ref[:, per:, :]
    step = 256 // per
    scale = LOG2E * HD**-0.5
    nt = (((1,), (1,)), ((), ()))
    row = lax.broadcasted_iota(jnp.int32, (per, LANES), 0)
    lane = lax.broadcasted_iota(jnp.int32, (per, LANES), 1)
    diagonal = row == lane % per
    piece = lax.broadcasted_iota(jnp.int32, (8, LANES), 0)
    ones = jnp.ones(va_ref.shape, jnp.bfloat16)
    for first in range(0, sources, step):
        q = q_ref[first : first + step, :per, :].reshape(step * per, HD)
        sa = lax.dot_general(q, ka_ref[...], nt, preferred_element_type=jnp.float32)
        sb = lax.dot_general(q, kb_ref[...], nt, preferred_element_type=jnp.float32)
        top = jnp.maximum(jnp.max(sa, axis=1, keepdims=True), jnp.max(sb, axis=1, keepdims=True)) * scale
        wa = jnp.exp2(sa * scale - top).astype(jnp.bfloat16)
        wb = jnp.exp2(sb * scale - top).astype(jnp.bfloat16)
        both = jnp.dot(
            wa, jnp.concatenate([va_ref[...], ones], axis=1), preferred_element_type=jnp.float32
        ) + jnp.dot(wb, jnp.concatenate([vb_ref[...], ones], axis=1), preferred_element_type=jnp.float32)
        total = both[:, HD:]
        out = (both[:, :HD] / total).astype(jnp.bfloat16)
        lse = top + jnp.log(total) * LOG2E
        for s in range(step):
            part = slice(s * per, (s + 1) * per)
            out_ref[first + s, :per, :] = out[part]
            flat = jnp.sum(jnp.where(diagonal, lse[part], 0.0), axis=0, keepdims=True)
            hi = flat.astype(jnp.bfloat16).astype(jnp.float32)
            mid = (flat - hi).astype(jnp.bfloat16).astype(jnp.float32)
            low = flat - hi - mid
            out_ref[first + s, per:, :] = jnp.where(
                piece == 0, hi, jnp.where(piece == 1, mid, jnp.where(piece == 2, low, 0.0))
            ).astype(jnp.bfloat16)


def fresh_kernel(tokens, rows_ref, kv_ref, kv1_ref, kv2_ref, kv3_ref, out_ref, lse_ref):
    sources = kv_ref.shape[0]
    place = lax.axis_index("seq")
    core, odd = place % KVH, place // KVH % 2
    scale = LOG2E * HD**-0.5
    nt = (((1,), (1,)), ((), ()))
    column = lax.broadcasted_iota(jnp.int32, (tokens, sources * tokens), 1)
    query_pos = place * tokens + lax.broadcasted_iota(jnp.int32, column.shape, 0)
    visible = (column <= query_pos) & (column // BLK == query_pos // BLK)
    visible = jnp.concatenate([visible.astype(jnp.int32)] * GROUP, axis=0) > 0
    ones = jnp.ones((sources * tokens, HD), jnp.bfloat16)
    here, near, far, both = [
        ref[...].astype(jnp.float32).reshape(sources * tokens, HD) for ref in (kv_ref, kv1_ref, kv2_ref, kv3_ref)
    ]
    keys = [jnp.where(odd == 0, here, far), jnp.where(odd == 0, near, both)]
    values = [jnp.where(odd == 0, far, here), jnp.where(odd == 0, both, near)]
    for g in range(KVH):
        k = jnp.where(core == g, keys[0], keys[1]).astype(jnp.bfloat16)
        v = jnp.where(core == g, values[0], values[1]).astype(jnp.bfloat16)
        q = rows_ref[g].astype(jnp.bfloat16)
        s = lax.dot_general(q, k, nt, preferred_element_type=jnp.float32) * scale
        s = jnp.where(visible, s, LOW_SCORE)
        top = jnp.max(s, axis=1, keepdims=True)
        w = jnp.where(visible, jnp.exp2(s - top), 0.0).astype(jnp.bfloat16)
        total_out = jnp.dot(w, jnp.concatenate([v, ones], axis=1), preferred_element_type=jnp.float32)
        total = total_out[:, HD:]
        out_ref[g] = total_out[:, :HD] / total
        lse_ref[g] = top + jnp.log(total) * LOG2E


def project_kernel(per, hist_ref, out_ref, lse_ref, match_ref, first_ref, w_hbm, y_ref, att_ref, w_ref, sems):
    depth = KVH * HD
    ready = first_ref.shape[0] // depth
    copies = fetch(
        [
            (w_hbm.at[pl.ds((ready + i) * depth, depth)], w_ref.at[pl.ds(i * depth, depth)])
            for i in range(w_ref.shape[0] // depth)
        ],
        sems,
    )
    tokens = y_ref.shape[0]
    holders = hist_ref.shape[0]
    fold = LANES // per
    row = lax.broadcasted_iota(jnp.int32, (holders, LANES), 0)
    lane = lax.broadcasted_iota(jnp.int32, (holders, LANES), 1)
    for g in range(KVH):
        outs = hist_ref[:, g, :per, :].reshape(holders * per, HD)
        stats = jnp.sum(hist_ref[:, g, per:, :].astype(jnp.float32), axis=1)
        stats = jnp.where(row % fold == lane // per, stats, 0.0)
        lse = jnp.concatenate(
            [
                jnp.sum(jnp.where(row // fold == m, stats, 0.0), axis=0, keepdims=True)
                for m in range(holders // fold)
            ],
            axis=1,
        )
        match = match_ref[g] > 0.5
        lse = jnp.where(match, lse, LOW_SCORE)
        own = lse_ref[g]
        top = jnp.maximum(jnp.max(lse, axis=1, keepdims=True), own)
        w = jnp.where(match, jnp.exp2(lse - top[:, :1]), 0.0)
        own_w = jnp.exp2(own - top)
        hi = w.astype(jnp.bfloat16)
        low = (w - hi.astype(jnp.float32)).astype(jnp.bfloat16)
        num = (
            jnp.dot(hi, outs, preferred_element_type=jnp.float32)
            + jnp.dot(low, outs, preferred_element_type=jnp.float32)
            + own_w * out_ref[g]
        )
        att = num / (jnp.sum(w, axis=1, keepdims=True) + own_w)
        for r in range(GROUP):
            h = g * GROUP + r
            att_ref[:, h * HD : (h + 1) * HD] = att[r * tokens : (r + 1) * tokens]
    att = att_ref[...].astype(jnp.bfloat16)
    y = jnp.dot(att[:, : ready * depth], first_ref[...], preferred_element_type=jnp.float32)
    for i, copy in enumerate(copies):
        copy.wait()
        y = y + jnp.dot(
            att[:, (ready + i) * depth : (ready + i + 1) * depth],
            w_ref[i * depth : (i + 1) * depth, :],
            preferred_element_type=jnp.float32,
        )
    y_ref[...] = y.astype(jnp.bfloat16)


VMEM = pl.BlockSpec(memory_space=pltpu.VMEM)
HBM = pl.BlockSpec(memory_space=pltpu.HBM)


def call(kernel, name, out_shape, specs, *operands, scratch=(), flops=0, moved=0, limit=16):
    outs = jax.tree.map(lambda _: VMEM, out_shape)
    return pl.pallas_call(
        kernel,
        name=name,
        out_shape=out_shape,
        in_specs=specs,
        out_specs=outs,
        scratch_shapes=scratch,
        cost_estimate=pl.CostEstimate(flops=flops, bytes_accessed=moved, transcendentals=0),
        compiler_params=pltpu.CompilerParams(vmem_limit_bytes=limit << 20),
    )(*operands)


def body(queries, stretch_keys, stretch_values, cache_keys, cache_values, chosen, out_weight):
    devices = lax.axis_size("seq")
    tokens = queries.shape[0]
    cache_rows = cache_keys.shape[0]
    span = BLK // cache_rows
    chips = span // KVH
    key_blocks = cache_rows * devices // BLK
    capacity = (GROUP * TOPK + key_blocks - 1) // key_blocks + 1
    per = capacity * tokens
    f32, bf16 = jnp.float32, jnp.bfloat16
    picks = chosen.transpose(2, 0, 1)

    def partner(bit):
        return [(i, i ^ bit) for i in range(devices)]

    send, after = call(
        functools.partial(pack_kernel, chips, capacity),
        "pack",
        (
            jax.ShapeDtypeStruct((devices, per + tokens, HD), bf16),
            jax.ShapeDtypeStruct((8, LANES), f32),
        ),
        [HBM] * 4,
        picks, queries, stretch_keys, stretch_values,
        scratch=[
            pltpu.VMEM(picks.shape, jnp.int32),
            pltpu.VMEM(queries.shape, bf16),
            pltpu.VMEM(stretch_keys.shape, bf16),
            pltpu.VMEM(stretch_values.shape, bf16),
            pltpu.SemaphoreType.DMA((4,)),
        ],
        limit=60,
    )
    got = lax.all_to_all(send, "seq", split_axis=0, concat_axis=0, tiled=True)

    holders = devices // KVH
    ready = EARLY * KVH * HD
    side = jax.ShapeDtypeStruct((cache_rows, HD), bf16)
    k_own, v_own, k_away, v_away, match, query_rows, first = call(
        functools.partial(split_kernel, chips, capacity),
        "split",
        (
            side,
            side,
            side,
            side,
            jax.ShapeDtypeStruct((KVH, GROUP * tokens, holders * per), f32),
            jax.ShapeDtypeStruct((KVH, GROUP * tokens, HD), f32),
            jax.ShapeDtypeStruct((ready, out_weight.shape[1]), bf16),
        ),
        [VMEM] + [HBM] * 5,
        after, cache_keys, cache_values, picks, queries, out_weight,
        scratch=[
            pltpu.VMEM(picks.shape, jnp.int32),
            pltpu.VMEM(queries.shape, bf16),
            pltpu.SemaphoreType.DMA((7,)),
        ],
        limit=50,
    )
    k_peer, v_peer = [lax.ppermute(x, "seq", partner(1)) for x in (k_away, v_away)]

    rows = devices * per
    back, fresh = call(
        functools.partial(attend_kernel, per),
        "attend",
        (
            jax.ShapeDtypeStruct((devices, per + 8, HD), bf16),
            jax.ShapeDtypeStruct((devices, tokens, HD), bf16),
        ),
        [VMEM] * 5,
        got, k_own, v_own, k_peer, v_peer,
        flops=8 * rows * cache_rows * HD,
        moved=4 << 20,
        limit=32,
    )
    hist = lax.all_to_all(back, "seq", split_axis=0, concat_axis=0, tiled=True)

    part = jax.ShapeDtypeStruct((KVH, GROUP * tokens, HD), f32)
    out, lse = call(
        functools.partial(fresh_kernel, tokens),
        "fresh",
        (part, part),
        [VMEM] * 5,
        query_rows, fresh, *[lax.ppermute(fresh, "seq", partner(bit)) for bit in (1, 2, 3)],
        flops=8 * H * tokens * devices * tokens * HD,
        moved=1 << 20,
    )
    return call(
        functools.partial(project_kernel, per),
        "project",
        jax.ShapeDtypeStruct((tokens, out_weight.shape[1]), bf16),
        [VMEM] * 5 + [HBM],
        hist.reshape(holders, KVH, per + 8, HD), out, lse, match, first, out_weight,
        scratch=[
            pltpu.VMEM((tokens, H * HD), f32),
            pltpu.VMEM((out_weight.shape[0] - ready, out_weight.shape[1]), bf16),
            pltpu.SemaphoreType.DMA((GROUP - EARLY,)),
        ],
        flops=2 * tokens * out_weight.size,
        moved=out_weight.size * 2,
        limit=50,
    )


def solution(mesh):
    seq = ("grp", "seq")
    return jax.shard_map(
        body,
        mesh=mesh,
        in_specs=(
            P(seq, None),
            P(seq, None),
            P(seq, None),
            P(seq, None),
            P(seq, None),
            P(seq, None, None),
            P(),
        ),
        out_specs=P(seq, None),
        check_vma=False,
    )
```

```python
import functools
import math

import jax
import jax.numpy as jnp
from jax import lax
from jax.experimental import pallas as pl
from jax.experimental.pallas import tpu as pltpu
from jax.sharding import PartitionSpec as P

H = 14
KVH = 2
HD = 128
BLK = 4096
TOPK = 3
GROUP = H // KVH

LOW_SCORE = -1e30
LOG2E = math.log2(math.e)
LANES = 128
EARLY = 3


def head_rows(q_ref, g):
    q = q_ref[...].astype(jnp.float32)
    return [q[:, h * HD : (h + 1) * HD] for h in range(g * GROUP, (g + 1) * GROUP)]


def slot_match(chosen_ref, g, block, slot, token):
    rows = lax.broadcasted_iota(jnp.int32, block.shape, 0)
    same_token = token == rows
    seen = jnp.zeros(block.shape, jnp.int32)
    found = []
    for h in range(g * GROUP, (g + 1) * GROUP):
        picked = block == chosen_ref[0, :, h : h + 1]
        for t in range(1, TOPK):
            picked = picked | (block == chosen_ref[t, :, h : h + 1])
        found.append(jnp.where(picked & same_token & (seen == slot), 1.0, 0.0))
        seen = seen + picked.astype(jnp.int32)
    return found


def fetch(pairs, sems):
    copies = [pltpu.make_async_copy(src, dst, sems.at[i]) for i, (src, dst) in enumerate(pairs)]
    for copy in copies:
        copy.start()
    return copies


def pack_kernel(chips, capacity, chosen_hbm, q_hbm, k_hbm, v_hbm, send_ref, chosen_ref, q_ref, k_ref, v_ref, sems):
    copies = fetch([(chosen_hbm, chosen_ref), (q_hbm, q_ref), (k_hbm, k_ref), (v_hbm, v_ref)], sems)
    tokens = q_ref.shape[0]
    per = capacity * tokens
    span = chips * KVH
    key_blocks = send_ref.shape[0] // span
    lane = lax.broadcasted_iota(jnp.int32, (tokens, key_blocks * per), 1)
    block, slot, token = lane // per, lane % per // tokens, lane % tokens
    for copy in copies:
        copy.wait()
    for g in range(KVH):
        spread = jnp.concatenate(
            slot_match(chosen_ref, g, block, slot, token) + [jnp.zeros(lane.shape, jnp.float32)], axis=0
        )
        rows = head_rows(q_ref, g)
        rows = jnp.concatenate(rows + [jnp.zeros_like(rows[0])], axis=0)
        slots = jnp.dot(
            spread.T.astype(jnp.bfloat16), rows.astype(jnp.bfloat16), preferred_element_type=jnp.float32
        ).astype(jnp.bfloat16)
        cols = slice(g * HD, (g + 1) * HD)
        fresh = [k_ref[:, cols], v_ref[:, cols]]
        for b in range(key_blocks):
            for chip in range(chips):
                to = b * span + chip * KVH + g
                send_ref[to, :per, :] = slots[b * per : (b + 1) * per]
                send_ref[to, per:, :] = fresh[chip % 2]


def masks_kernel(chips, capacity, chosen_ref, q_ref, match_ref, rows_ref):
    tokens = q_ref.shape[0]
    per = capacity * tokens
    lane = lax.broadcasted_iota(jnp.int32, (tokens, match_ref.shape[2]), 1)
    block, slot, token = lane // (per * chips), lane % per // tokens, lane % tokens
    for g in range(KVH):
        match_ref[g] = jnp.concatenate(slot_match(chosen_ref, g, block, slot, token), axis=0)
        rows_ref[g] = jnp.concatenate(head_rows(q_ref, g), axis=0)


def attend_kernel(per, q_ref, ka_ref, va_ref, kb_ref, vb_ref, out_ref, fresh_ref):
    sources = q_ref.shape[0]
    fresh_ref[...] = q_ref[:, per:, :]
    step = 256 // per
    scale = LOG2E * HD**-0.5
    nt = (((1,), (1,)), ((), ()))
    row = lax.broadcasted_iota(jnp.int32, (per, LANES), 0)
    lane = lax.broadcasted_iota(jnp.int32, (per, LANES), 1)
    diagonal = row == lane % per
    piece = lax.broadcasted_iota(jnp.int32, (8, LANES), 0)
    ones = jnp.ones(va_ref.shape, jnp.bfloat16)
    for first in range(0, sources, step):
        q = q_ref[first : first + step, :per, :].reshape(step * per, HD)
        sa = lax.dot_general(q, ka_ref[...], nt, preferred_element_type=jnp.float32)
        sb = lax.dot_general(q, kb_ref[...], nt, preferred_element_type=jnp.float32)
        top = jnp.maximum(jnp.max(sa, axis=1, keepdims=True), jnp.max(sb, axis=1, keepdims=True)) * scale
        wa = jnp.exp2(sa * scale - top).astype(jnp.bfloat16)
        wb = jnp.exp2(sb * scale - top).astype(jnp.bfloat16)
        both = jnp.dot(
            wa, jnp.concatenate([va_ref[...], ones], axis=1), preferred_element_type=jnp.float32
        ) + jnp.dot(wb, jnp.concatenate([vb_ref[...], ones], axis=1), preferred_element_type=jnp.float32)
        total = both[:, HD:]
        out = (both[:, :HD] / total).astype(jnp.bfloat16)
        lse = top + jnp.log(total) * LOG2E
        for s in range(step):
            part = slice(s * per, (s + 1) * per)
            out_ref[first + s, :per, :] = out[part]
            flat = jnp.sum(jnp.where(diagonal, lse[part], 0.0), axis=0, keepdims=True)
            hi = flat.astype(jnp.bfloat16).astype(jnp.float32)
            mid = (flat - hi).astype(jnp.bfloat16).astype(jnp.float32)
            low = flat - hi - mid
            out_ref[first + s, per:, :] = jnp.where(
                piece == 0, hi, jnp.where(piece == 1, mid, jnp.where(piece == 2, low, 0.0))
            ).astype(jnp.bfloat16)


def fresh_kernel(tokens, rows_ref, kv_ref, kv1_ref, kv2_ref, kv3_ref, w_hbm, out_ref, lse_ref, w_ref, sems):
    copies = fetch([(w_hbm.at[: w_ref.shape[0]], w_ref)], sems)
    sources = kv_ref.shape[0]
    place = lax.axis_index("seq")
    core, odd = place % KVH, place // KVH % 2
    scale = LOG2E * HD**-0.5
    nt = (((1,), (1,)), ((), ()))
    column = lax.broadcasted_iota(jnp.int32, (tokens, sources * tokens), 1)
    query_pos = place * tokens + lax.broadcasted_iota(jnp.int32, column.shape, 0)
    visible = (column <= query_pos) & (column // BLK == query_pos // BLK)
    visible = jnp.concatenate([visible.astype(jnp.int32)] * GROUP, axis=0) > 0
    ones = jnp.ones((sources * tokens, HD), jnp.bfloat16)
    here, near, far, both = [
        ref[...].astype(jnp.float32).reshape(sources * tokens, HD) for ref in (kv_ref, kv1_ref, kv2_ref, kv3_ref)
    ]
    keys = [jnp.where(odd == 0, here, far), jnp.where(odd == 0, near, both)]
    values = [jnp.where(odd == 0, far, here), jnp.where(odd == 0, both, near)]
    for g in range(KVH):
        k = jnp.where(core == g, keys[0], keys[1]).astype(jnp.bfloat16)
        v = jnp.where(core == g, values[0], values[1]).astype(jnp.bfloat16)
        q = rows_ref[g].astype(jnp.bfloat16)
        s = lax.dot_general(q, k, nt, preferred_element_type=jnp.float32) * scale
        s = jnp.where(visible, s, LOW_SCORE)
        top = jnp.max(s, axis=1, keepdims=True)
        w = jnp.where(visible, jnp.exp2(s - top), 0.0).astype(jnp.bfloat16)
        total_out = jnp.dot(w, jnp.concatenate([v, ones], axis=1), preferred_element_type=jnp.float32)
        total = total_out[:, HD:]
        out_ref[g] = total_out[:, :HD] / total
        lse_ref[g] = top + jnp.log(total) * LOG2E
    for copy in copies:
        copy.wait()


def project_kernel(per, hist_ref, out_ref, lse_ref, match_ref, first_ref, w_hbm, y_ref, att_ref, w_ref, sems):
    depth = KVH * HD
    ready = first_ref.shape[0] // depth
    copies = fetch(
        [
            (w_hbm.at[pl.ds((ready + i) * depth, depth)], w_ref.at[pl.ds(i * depth, depth)])
            for i in range(w_ref.shape[0] // depth)
        ],
        sems,
    )
    tokens = y_ref.shape[0]
    holders = hist_ref.shape[0]
    fold = LANES // per
    row = lax.broadcasted_iota(jnp.int32, (holders, LANES), 0)
    lane = lax.broadcasted_iota(jnp.int32, (holders, LANES), 1)
    for g in range(KVH):
        outs = hist_ref[:, g, :per, :].reshape(holders * per, HD)
        stats = jnp.sum(hist_ref[:, g, per:, :].astype(jnp.float32), axis=1)
        stats = jnp.where(row % fold == lane // per, stats, 0.0)
        lse = jnp.concatenate(
            [
                jnp.sum(jnp.where(row // fold == m, stats, 0.0), axis=0, keepdims=True)
                for m in range(holders // fold)
            ],
            axis=1,
        )
        match = match_ref[g] > 0.5
        lse = jnp.where(match, lse, LOW_SCORE)
        own = lse_ref[g]
        top = jnp.maximum(jnp.max(lse, axis=1, keepdims=True), own)
        w = jnp.where(match, jnp.exp2(lse - top[:, :1]), 0.0)
        own_w = jnp.exp2(own - top)
        hi = w.astype(jnp.bfloat16)
        low = (w - hi.astype(jnp.float32)).astype(jnp.bfloat16)
        num = (
            jnp.dot(hi, outs, preferred_element_type=jnp.float32)
            + jnp.dot(low, outs, preferred_element_type=jnp.float32)
            + own_w * out_ref[g]
        )
        att = num / (jnp.sum(w, axis=1, keepdims=True) + own_w)
        for r in range(GROUP):
            h = g * GROUP + r
            att_ref[:, h * HD : (h + 1) * HD] = att[r * tokens : (r + 1) * tokens]
    att = att_ref[...].astype(jnp.bfloat16)
    y = jnp.dot(att[:, : ready * depth], first_ref[...], preferred_element_type=jnp.float32)
    for i, copy in enumerate(copies):
        copy.wait()
        y = y + jnp.dot(
            att[:, (ready + i) * depth : (ready + i + 1) * depth],
            w_ref[i * depth : (i + 1) * depth, :],
            preferred_element_type=jnp.float32,
        )
    y_ref[...] = y.astype(jnp.bfloat16)


VMEM = pl.BlockSpec(memory_space=pltpu.VMEM)
HBM = pl.BlockSpec(memory_space=pltpu.HBM)


def call(kernel, name, out_shape, specs, *operands, scratch=(), flops=0, moved=0, limit=16):
    outs = jax.tree.map(lambda _: VMEM, out_shape)
    return pl.pallas_call(
        kernel,
        name=name,
        out_shape=out_shape,
        in_specs=specs,
        out_specs=outs,
        scratch_shapes=scratch,
        cost_estimate=pl.CostEstimate(flops=flops, bytes_accessed=moved, transcendentals=0),
        compiler_params=pltpu.CompilerParams(vmem_limit_bytes=limit << 20),
    )(*operands)


def body(queries, stretch_keys, stretch_values, cache_keys, cache_values, chosen, out_weight):
    devices = lax.axis_size("seq")
    tokens = queries.shape[0]
    cache_rows = cache_keys.shape[0]
    span = BLK // cache_rows
    chips = span // KVH
    key_blocks = cache_rows * devices // BLK
    capacity = (GROUP * TOPK + key_blocks - 1) // key_blocks + 1
    per = capacity * tokens
    f32, bf16 = jnp.float32, jnp.bfloat16
    picks = chosen.transpose(2, 0, 1)

    def partner(bit):
        return [(i, i ^ bit) for i in range(devices)]

    send = call(
        functools.partial(pack_kernel, chips, capacity),
        "pack",
        jax.ShapeDtypeStruct((devices, per + tokens, HD), bf16),
        [HBM] * 4,
        picks, queries, stretch_keys, stretch_values,
        scratch=[
            pltpu.VMEM(picks.shape, jnp.int32),
            pltpu.VMEM(queries.shape, bf16),
            pltpu.VMEM(stretch_keys.shape, bf16),
            pltpu.VMEM(stretch_values.shape, bf16),
            pltpu.SemaphoreType.DMA((4,)),
        ],
        limit=60,
    )
    send, cache_keys, cache_values, picks, queries = lax.optimization_barrier(
        (send, cache_keys, cache_values, picks, queries)
    )
    got = lax.all_to_all(send, "seq", split_axis=0, concat_axis=0, tiled=True)

    core = lax.axis_index("seq") % KVH

    def halves(head):
        return [lax.dynamic_slice_in_dim(x, head * HD, HD, axis=1) for x in (cache_keys, cache_values)]

    k_own, v_own = halves(core)
    k_peer, v_peer = [lax.ppermute(x, "seq", partner(1)) for x in halves(1 - core)]
    holders = devices // KVH
    match, query_rows = call(
        functools.partial(masks_kernel, chips, capacity),
        "masks",
        (
            jax.ShapeDtypeStruct((KVH, GROUP * tokens, holders * per), f32),
            jax.ShapeDtypeStruct((KVH, GROUP * tokens, HD), f32),
        ),
        [VMEM] * 2,
        picks, queries,
    )

    rows = devices * per
    back, fresh = call(
        functools.partial(attend_kernel, per),
        "attend",
        (
            jax.ShapeDtypeStruct((devices, per + 8, HD), bf16),
            jax.ShapeDtypeStruct((devices, tokens, HD), bf16),
        ),
        [VMEM] * 5,
        got, k_own, v_own, k_peer, v_peer,
        flops=8 * rows * cache_rows * HD,
        moved=4 << 20,
        limit=32,
    )
    hist = lax.all_to_all(back, "seq", split_axis=0, concat_axis=0, tiled=True)

    far = lax.ppermute(fresh, "seq", partner(2))
    near, both = [lax.ppermute(x, "seq", partner(1)) for x in (fresh, far)]
    part = jax.ShapeDtypeStruct((KVH, GROUP * tokens, HD), f32)
    ready = EARLY * KVH * HD
    out, lse, first = call(
        functools.partial(fresh_kernel, tokens),
        "fresh",
        (part, part, jax.ShapeDtypeStruct((ready, out_weight.shape[1]), bf16)),
        [VMEM] * 5 + [HBM],
        query_rows, fresh, near, far, both, out_weight,
        scratch=[pltpu.SemaphoreType.DMA((1,))],
        flops=8 * H * tokens * devices * tokens * HD,
        moved=1 << 20,
        limit=50,
    )
    return call(
        functools.partial(project_kernel, per),
        "project",
        jax.ShapeDtypeStruct((tokens, out_weight.shape[1]), bf16),
        [VMEM] * 5 + [HBM],
        hist.reshape(holders, KVH, per + 8, HD), out, lse, match, first, out_weight,
        scratch=[
            pltpu.VMEM((tokens, H * HD), f32),
            pltpu.VMEM((out_weight.shape[0] - ready, out_weight.shape[1]), bf16),
            pltpu.SemaphoreType.DMA((GROUP - EARLY,)),
        ],
        flops=2 * tokens * out_weight.size,
        moved=out_weight.size * 2,
        limit=50,
    )


def solution(mesh):
    seq = ("grp", "seq")
    return jax.shard_map(
        body,
        mesh=mesh,
        in_specs=(
            P(seq, None),
            P(seq, None),
            P(seq, None),
            P(seq, None),
            P(seq, None),
            P(seq, None, None),
            P(),
        ),
        out_specs=P(seq, None),
        check_vma=False,
    )
```

```python
import functools
import math

import jax
import jax.numpy as jnp
from jax import lax
from jax.experimental import pallas as pl
from jax.experimental.pallas import tpu as pltpu
from jax.sharding import PartitionSpec as P

H = 14
KVH = 2
HD = 128
BLK = 4096
TOPK = 3
GROUP = H // KVH

LOW_SCORE = -1e30
LOG2E = math.log2(math.e)
LANES = 128
EARLY = 3
SPAN = 4


def head_rows(q_ref, g):
    q = q_ref[...].astype(jnp.float32)
    return [q[:, h * HD : (h + 1) * HD] for h in range(g * GROUP, (g + 1) * GROUP)]


def slot_match(chosen_ref, g, block, slot, token):
    rows = lax.broadcasted_iota(jnp.int32, block.shape, 0)
    same_token = token == rows
    seen = jnp.zeros(block.shape, jnp.int32)
    found = []
    for h in range(g * GROUP, (g + 1) * GROUP):
        picked = block == chosen_ref[0, :, h : h + 1]
        for t in range(1, TOPK):
            picked = picked | (block == chosen_ref[t, :, h : h + 1])
        found.append(jnp.where(picked & same_token & (seen == slot), 1.0, 0.0))
        seen = seen + picked.astype(jnp.int32)
    return found


def fetch(pairs, sems):
    copies = [pltpu.make_async_copy(src, dst, sems.at[i]) for i, (src, dst) in enumerate(pairs)]
    for copy in copies:
        copy.start()
    return copies


def pack_kernel(capacity, chosen_hbm, q_hbm, k_hbm, v_hbm, send_ref, chosen_ref, q_ref, k_ref, v_ref, sems):
    copies = fetch([(chosen_hbm, chosen_ref), (q_hbm, q_ref), (k_hbm, k_ref), (v_hbm, v_ref)], sems)
    core = lax.axis_index("seq") % KVH
    tokens = q_ref.shape[0]
    per = capacity * tokens
    key_blocks = send_ref.shape[0]
    lane = lax.broadcasted_iota(jnp.int32, (tokens, key_blocks * per), 1)
    block, slot, token = lane // per, lane % per // tokens, lane % tokens
    for copy in copies:
        copy.wait()
    slots = []
    for g in range(KVH):
        spread = jnp.concatenate(
            slot_match(chosen_ref, g, block, slot, token) + [jnp.zeros(lane.shape, jnp.float32)], axis=0
        )
        rows = head_rows(q_ref, g)
        rows = jnp.concatenate(rows + [jnp.zeros_like(rows[0])], axis=0)
        slots.append(
            jnp.dot(
                spread.T.astype(jnp.bfloat16), rows.astype(jnp.bfloat16), preferred_element_type=jnp.float32
            )
        )
    ordered = [
        jnp.where(core == 0, slots[0], slots[1]).astype(jnp.bfloat16),
        jnp.where(core == 0, slots[1], slots[0]).astype(jnp.bfloat16),
    ]
    fresh = jnp.concatenate(
        [
            ref[:, g * HD : (g + 1) * HD].astype(jnp.float32)
            for g in range(KVH)
            for ref in (k_ref, v_ref)
        ],
        axis=0,
    ).astype(jnp.bfloat16)
    for b in range(key_blocks):
        for i in range(KVH):
            send_ref[b, i * per : (i + 1) * per, :] = ordered[i][b * per : (b + 1) * per]
        send_ref[b, KVH * per :, :] = fresh


def masks_kernel(chips, capacity, chosen_ref, q_ref, match_ref, rows_ref):
    tokens = q_ref.shape[0]
    per = capacity * tokens
    lane = lax.broadcasted_iota(jnp.int32, (tokens, match_ref.shape[2]), 1)
    block, slot, token = lane // (per * chips), lane % per // tokens, lane % tokens
    for g in range(KVH):
        match_ref[g] = jnp.concatenate(slot_match(chosen_ref, g, block, slot, token), axis=0)
        rows_ref[g] = jnp.concatenate(head_rows(q_ref, g), axis=0)


def attend_kernel(q0_ref, q1_ref, q2_ref, q3_ref, ka_ref, va_ref, kb_ref, vb_ref, out_ref):
    place = lax.axis_index("seq") % SPAN
    sources, per = q0_ref.shape[:2]
    step = 256 // per
    scale = LOG2E * HD**-0.5
    nt = (((1,), (1,)), ((), ()))
    row = lax.broadcasted_iota(jnp.int32, (per, LANES), 0)
    lane = lax.broadcasted_iota(jnp.int32, (per, LANES), 1)
    diagonal = row == lane % per
    piece = lax.broadcasted_iota(jnp.int32, (8, LANES), 0)
    ones = jnp.ones(va_ref.shape, jnp.bfloat16)
    for apart, q_ref in enumerate((q0_ref, q1_ref, q2_ref, q3_ref)):
        for first in range(0, sources, step):
            q = q_ref[first : first + step].reshape(step * per, HD)
            sa = lax.dot_general(q, ka_ref[...], nt, preferred_element_type=jnp.float32)
            sb = lax.dot_general(q, kb_ref[...], nt, preferred_element_type=jnp.float32)
            top = scale * jnp.maximum(jnp.max(sa, axis=1, keepdims=True), jnp.max(sb, axis=1, keepdims=True))
            wa = jnp.exp2(sa * scale - top).astype(jnp.bfloat16)
            wb = jnp.exp2(sb * scale - top).astype(jnp.bfloat16)
            both = jnp.dot(
                wa, jnp.concatenate([va_ref[...], ones], axis=1), preferred_element_type=jnp.float32
            ) + jnp.dot(wb, jnp.concatenate([vb_ref[...], ones], axis=1), preferred_element_type=jnp.float32)
            total = both[:, HD:]
            out = (both[:, :HD] / total).astype(jnp.bfloat16)
            lse = top + jnp.log(total) * LOG2E
            for s in range(step):
                part = slice(s * per, (s + 1) * per)
                to = (first + s) * SPAN + (place ^ apart)
                out_ref[to, :per, :] = out[part]
                flat = jnp.sum(jnp.where(diagonal, lse[part], 0.0), axis=0, keepdims=True)
                hi = flat.astype(jnp.bfloat16).astype(jnp.float32)
                mid = (flat - hi).astype(jnp.bfloat16).astype(jnp.float32)
                low = flat - hi - mid
                out_ref[to, per:, :] = jnp.where(
                    piece == 0, hi, jnp.where(piece == 1, mid, jnp.where(piece == 2, low, 0.0))
                ).astype(jnp.bfloat16)


def fresh_kernel(tokens, rows_ref, kv0_ref, kv1_ref, kv2_ref, kv3_ref, w_hbm, out_ref, lse_ref, w_ref, sems):
    copies = fetch([(w_hbm.at[: w_ref.shape[0]], w_ref)], sems)
    blocks = kv0_ref.shape[0]
    place = lax.axis_index("seq")
    scale = LOG2E * HD**-0.5
    nt = (((1,), (1,)), ((), ()))
    column = lax.broadcasted_iota(jnp.int32, (tokens, SPAN * blocks * tokens), 1)
    source = column // tokens % blocks * SPAN + (place % SPAN ^ column // (blocks * tokens))
    key_pos = source * tokens + column % tokens
    query_pos = place * tokens + lax.broadcasted_iota(jnp.int32, column.shape, 0)
    visible = (key_pos <= query_pos) & (key_pos // BLK == query_pos // BLK)
    visible = jnp.concatenate([visible.astype(jnp.int32)] * GROUP, axis=0) > 0
    ones = jnp.ones((SPAN * blocks * tokens, HD), jnp.bfloat16)
    kv = [ref[...].astype(jnp.float32) for ref in (kv0_ref, kv1_ref, kv2_ref, kv3_ref)]
    for g in range(KVH):
        k, v = [
            jnp.concatenate(
                [x[:, i * tokens : (i + 1) * tokens].reshape(blocks * tokens, HD) for x in kv], axis=0
            ).astype(jnp.bfloat16)
            for i in (2 * g, 2 * g + 1)
        ]
        q = rows_ref[g].astype(jnp.bfloat16)
        s = lax.dot_general(q, k, nt, preferred_element_type=jnp.float32) * scale
        s = jnp.where(visible, s, LOW_SCORE)
        top = jnp.max(s, axis=1, keepdims=True)
        w = jnp.where(visible, jnp.exp2(s - top), 0.0).astype(jnp.bfloat16)
        total_out = jnp.dot(w, jnp.concatenate([v, ones], axis=1), preferred_element_type=jnp.float32)
        total = total_out[:, HD:]
        out_ref[g] = total_out[:, :HD] / total
        lse_ref[g] = top + jnp.log(total) * LOG2E
    for copy in copies:
        copy.wait()


def project_kernel(per, hist_ref, out_ref, lse_ref, match_ref, first_ref, w_hbm, y_ref, att_ref, w_ref, sems):
    depth = KVH * HD
    ready = first_ref.shape[0] // depth
    copies = fetch(
        [
            (w_hbm.at[pl.ds((ready + i) * depth, depth)], w_ref.at[pl.ds(i * depth, depth)])
            for i in range(w_ref.shape[0] // depth)
        ],
        sems,
    )
    tokens = y_ref.shape[0]
    holders = hist_ref.shape[0]
    fold = LANES // per
    row = lax.broadcasted_iota(jnp.int32, (holders, LANES), 0)
    lane = lax.broadcasted_iota(jnp.int32, (holders, LANES), 1)
    for g in range(KVH):
        outs = hist_ref[:, g, :per, :].reshape(holders * per, HD)
        stats = jnp.sum(hist_ref[:, g, per:, :].astype(jnp.float32), axis=1)
        stats = jnp.where(row % fold == lane // per, stats, 0.0)
        lse = jnp.concatenate(
            [
                jnp.sum(jnp.where(row // fold == m, stats, 0.0), axis=0, keepdims=True)
                for m in range(holders // fold)
            ],
            axis=1,
        )
        match = match_ref[g] > 0.5
        lse = jnp.where(match, lse, LOW_SCORE)
        own = lse_ref[g]
        top = jnp.maximum(jnp.max(lse, axis=1, keepdims=True), own)
        w = jnp.where(match, jnp.exp2(lse - top[:, :1]), 0.0)
        own_w = jnp.exp2(own - top)
        hi = w.astype(jnp.bfloat16)
        low = (w - hi.astype(jnp.float32)).astype(jnp.bfloat16)
        num = (
            jnp.dot(hi, outs, preferred_element_type=jnp.float32)
            + jnp.dot(low, outs, preferred_element_type=jnp.float32)
            + own_w * out_ref[g]
        )
        att = num / (jnp.sum(w, axis=1, keepdims=True) + own_w)
        for r in range(GROUP):
            h = g * GROUP + r
            att_ref[:, h * HD : (h + 1) * HD] = att[r * tokens : (r + 1) * tokens]
    att = att_ref[...].astype(jnp.bfloat16)
    y = jnp.dot(att[:, : ready * depth], first_ref[...], preferred_element_type=jnp.float32)
    for i, copy in enumerate(copies):
        copy.wait()
        y = y + jnp.dot(
            att[:, (ready + i) * depth : (ready + i + 1) * depth],
            w_ref[i * depth : (i + 1) * depth, :],
            preferred_element_type=jnp.float32,
        )
    y_ref[...] = y.astype(jnp.bfloat16)


VMEM = pl.BlockSpec(memory_space=pltpu.VMEM)
HBM = pl.BlockSpec(memory_space=pltpu.HBM)


def call(kernel, name, out_shape, specs, *operands, scratch=(), flops=0, moved=0, limit=16):
    outs = jax.tree.map(lambda _: VMEM, out_shape)
    return pl.pallas_call(
        kernel,
        name=name,
        out_shape=out_shape,
        in_specs=specs,
        out_specs=outs,
        scratch_shapes=scratch,
        cost_estimate=pl.CostEstimate(flops=flops, bytes_accessed=moved, transcendentals=0),
        compiler_params=pltpu.CompilerParams(vmem_limit_bytes=limit << 20),
    )(*operands)


def body(queries, stretch_keys, stretch_values, cache_keys, cache_values, chosen, out_weight):
    devices = lax.axis_size("seq")
    tokens = queries.shape[0]
    cache_rows = cache_keys.shape[0]
    chips = SPAN // KVH
    key_blocks = cache_rows * devices // BLK
    capacity = (GROUP * TOPK + key_blocks - 1) // key_blocks + 1
    per = capacity * tokens
    f32, bf16 = jnp.float32, jnp.bfloat16
    picks = chosen.transpose(2, 0, 1)

    def partner(bit):
        return [(i, i ^ bit) for i in range(devices)]

    send = call(
        functools.partial(pack_kernel, capacity),
        "pack",
        jax.ShapeDtypeStruct((key_blocks, KVH * per + 2 * KVH * tokens, HD), bf16),
        [HBM] * 4,
        picks, queries, stretch_keys, stretch_values,
        scratch=[
            pltpu.VMEM(picks.shape, jnp.int32),
            pltpu.VMEM(queries.shape, bf16),
            pltpu.VMEM(stretch_keys.shape, bf16),
            pltpu.VMEM(stretch_values.shape, bf16),
            pltpu.SemaphoreType.DMA((4,)),
        ],
        limit=60,
    )
    send, cache_keys, cache_values, picks, queries = lax.optimization_barrier(
        (send, cache_keys, cache_values, picks, queries)
    )
    columns = [[b * SPAN + i for b in range(key_blocks)] for i in range(SPAN)]
    got = lax.all_to_all(
        send, "seq", split_axis=0, concat_axis=0, axis_index_groups=columns, tiled=True
    )
    same, other, fresh = got[:, :per], got[:, per : KVH * per], got[:, KVH * per :]
    slots = [same] + [lax.ppermute(x, "seq", partner(i)) for i, x in ((1, other), (2, same), (3, other))]

    core = lax.axis_index("seq") % KVH

    def halves(head):
        return [lax.dynamic_slice_in_dim(x, head * HD, HD, axis=1) for x in (cache_keys, cache_values)]

    k_own, v_own = halves(core)
    k_peer, v_peer = [lax.ppermute(x, "seq", partner(1)) for x in halves(1 - core)]
    holders = devices // KVH
    match, query_rows = call(
        functools.partial(masks_kernel, chips, capacity),
        "masks",
        (
            jax.ShapeDtypeStruct((KVH, GROUP * tokens, holders * per), f32),
            jax.ShapeDtypeStruct((KVH, GROUP * tokens, HD), f32),
        ),
        [VMEM] * 2,
        picks, queries,
    )

    rows = devices * per
    back = call(
        attend_kernel,
        "attend",
        jax.ShapeDtypeStruct((devices, per + 8, HD), bf16),
        [VMEM] * 8,
        *slots, k_own, v_own, k_peer, v_peer,
        flops=8 * rows * cache_rows * HD,
        moved=4 << 20,
        limit=32,
    )
    hist = lax.all_to_all(back, "seq", split_axis=0, concat_axis=0, tiled=True)

    back, fresh = lax.optimization_barrier((back, fresh))
    spread = [fresh] + [lax.ppermute(fresh, "seq", partner(i)) for i in (1, 2, 3)]
    part = jax.ShapeDtypeStruct((KVH, GROUP * tokens, HD), f32)
    ready = EARLY * KVH * HD
    out, lse, first = call(
        functools.partial(fresh_kernel, tokens),
        "fresh",
        (part, part, jax.ShapeDtypeStruct((ready, out_weight.shape[1]), bf16)),
        [VMEM] * 5 + [HBM],
        query_rows, *spread, out_weight,
        scratch=[pltpu.SemaphoreType.DMA((1,))],
        flops=8 * H * tokens * devices * tokens * HD,
        moved=1 << 20,
        limit=50,
    )
    return call(
        functools.partial(project_kernel, per),
        "project",
        jax.ShapeDtypeStruct((tokens, out_weight.shape[1]), bf16),
        [VMEM] * 5 + [HBM],
        hist.reshape(holders, KVH, per + 8, HD), out, lse, match, first, out_weight,
        scratch=[
            pltpu.VMEM((tokens, H * HD), f32),
            pltpu.VMEM((out_weight.shape[0] - ready, out_weight.shape[1]), bf16),
            pltpu.SemaphoreType.DMA((GROUP - EARLY,)),
        ],
        flops=2 * tokens * out_weight.size,
        moved=out_weight.size * 2,
        limit=50,
    )


def solution(mesh):
    seq = ("grp", "seq")
    return jax.shard_map(
        body,
        mesh=mesh,
        in_specs=(
            P(seq, None),
            P(seq, None),
            P(seq, None),
            P(seq, None),
            P(seq, None),
            P(seq, None, None),
            P(),
        ),
        out_specs=P(seq, None),
        check_vma=False,
    )
```

```python
import functools
import math

import jax
import jax.numpy as jnp
from jax import lax
from jax.experimental import pallas as pl
from jax.experimental.pallas import tpu as pltpu
from jax.sharding import PartitionSpec as P

H = 14
KVH = 2
HD = 128
BLK = 4096
TOPK = 3
GROUP = H // KVH

LOW_SCORE = -1e30
LOG2E = math.log2(math.e)
LANES = 128
EARLY = 3
SPAN = 4


def head_rows(q_ref, g):
    q = q_ref[...].astype(jnp.float32)
    return [q[:, h * HD : (h + 1) * HD] for h in range(g * GROUP, (g + 1) * GROUP)]


def slot_match(chosen_ref, g, block, slot, token):
    rows = lax.broadcasted_iota(jnp.int32, block.shape, 0)
    same_token = token == rows
    seen = jnp.zeros(block.shape, jnp.int32)
    found = []
    for h in range(g * GROUP, (g + 1) * GROUP):
        picked = block == chosen_ref[0, :, h : h + 1]
        for t in range(1, TOPK):
            picked = picked | (block == chosen_ref[t, :, h : h + 1])
        found.append(jnp.where(picked & same_token & (seen == slot), 1.0, 0.0))
        seen = seen + picked.astype(jnp.int32)
    return found


def fetch(pairs, sems):
    copies = [pltpu.make_async_copy(src, dst, sems.at[i]) for i, (src, dst) in enumerate(pairs)]
    for copy in copies:
        copy.start()
    return copies


def pack_kernel(capacity, chosen_hbm, q_hbm, k_hbm, v_hbm, *refs):
    *send_refs, chosen_ref, q_ref, k_ref, v_ref, slots_ref, sems = refs
    copies = fetch([(chosen_hbm, chosen_ref), (q_hbm, q_ref), (k_hbm, k_ref), (v_hbm, v_ref)], sems)
    place = lax.axis_index("seq")
    core, home = place % KVH, place // SPAN
    tokens = q_ref.shape[0]
    per = capacity * tokens
    key_blocks = len(send_refs)
    lane = lax.broadcasted_iota(jnp.int32, (tokens, key_blocks * per), 1)
    block, slot, token = lane // per, lane % per // tokens, lane % tokens
    for copy in copies:
        copy.wait()
    for g in range(KVH):
        spread = jnp.concatenate(
            slot_match(chosen_ref, g, block, slot, token) + [jnp.zeros(lane.shape, jnp.float32)], axis=0
        )
        rows = head_rows(q_ref, g)
        rows = jnp.concatenate(rows + [jnp.zeros_like(rows[0])], axis=0)
        slots = jnp.dot(
            spread.T.astype(jnp.bfloat16), rows.astype(jnp.bfloat16), preferred_element_type=jnp.float32
        )
        slots_ref[core ^ g] = slots.astype(jnp.bfloat16).reshape(key_blocks, per, HD)
    fresh = jnp.concatenate(
        [
            ref[:, g * HD : (g + 1) * HD].astype(jnp.float32)
            for g in range(KVH)
            for ref in (k_ref, v_ref)
        ],
        axis=0,
    ).astype(jnp.bfloat16)
    for apart, send_ref in enumerate(send_refs):
        for i in range(KVH):
            send_ref[i * per : (i + 1) * per, :] = slots_ref[i, home ^ apart]
        send_ref[KVH * per :, :] = fresh


def gather_kernel(*refs):
    *got_refs, same_ref, other_ref, fresh_ref = refs
    per = same_ref.shape[1]
    for i, ref in enumerate(got_refs):
        same_ref[i] = ref[:per, :]
        other_ref[i] = ref[per : KVH * per, :]
        fresh_ref[i] = ref[KVH * per :, :]


def masks_kernel(chips, capacity, chosen_ref, q_ref, match_ref, rows_ref):
    tokens = q_ref.shape[0]
    per = capacity * tokens
    lane = lax.broadcasted_iota(jnp.int32, (tokens, match_ref.shape[2]), 1)
    block, slot, token = lane // (per * chips), lane % per // tokens, lane % tokens
    for g in range(KVH):
        match_ref[g] = jnp.concatenate(slot_match(chosen_ref, g, block, slot, token), axis=0)
        rows_ref[g] = jnp.concatenate(head_rows(q_ref, g), axis=0)


def attend_kernel(q0_ref, q1_ref, q2_ref, q3_ref, ka_ref, va_ref, kb_ref, vb_ref, out_ref):
    place = lax.axis_index("seq")
    sources, per = q0_ref.shape[:2]
    step = 256 // per
    scale = LOG2E * HD**-0.5
    nt = (((1,), (1,)), ((), ()))
    row = lax.broadcasted_iota(jnp.int32, (per, LANES), 0)
    lane = lax.broadcasted_iota(jnp.int32, (per, LANES), 1)
    diagonal = row == lane % per
    piece = lax.broadcasted_iota(jnp.int32, (8, LANES), 0)
    ones = jnp.ones(va_ref.shape, jnp.bfloat16)
    for apart, q_ref in enumerate((q0_ref, q1_ref, q2_ref, q3_ref)):
        for first in range(0, sources, step):
            q = q_ref[first : first + step].reshape(step * per, HD)
            sa = lax.dot_general(q, ka_ref[...], nt, preferred_element_type=jnp.float32)
            sb = lax.dot_general(q, kb_ref[...], nt, preferred_element_type=jnp.float32)
            top = scale * jnp.maximum(jnp.max(sa, axis=1, keepdims=True), jnp.max(sb, axis=1, keepdims=True))
            wa = jnp.exp2(sa * scale - top).astype(jnp.bfloat16)
            wb = jnp.exp2(sb * scale - top).astype(jnp.bfloat16)
            both = jnp.dot(
                wa, jnp.concatenate([va_ref[...], ones], axis=1), preferred_element_type=jnp.float32
            ) + jnp.dot(wb, jnp.concatenate([vb_ref[...], ones], axis=1), preferred_element_type=jnp.float32)
            total = both[:, HD:]
            out = (both[:, :HD] / total).astype(jnp.bfloat16)
            lse = top + jnp.log(total) * LOG2E
            for s in range(step):
                part = slice(s * per, (s + 1) * per)
                to = place ^ (apart + (first + s) * SPAN)
                out_ref[to, :per, :] = out[part]
                flat = jnp.sum(jnp.where(diagonal, lse[part], 0.0), axis=0, keepdims=True)
                hi = flat.astype(jnp.bfloat16).astype(jnp.float32)
                mid = (flat - hi).astype(jnp.bfloat16).astype(jnp.float32)
                low = flat - hi - mid
                out_ref[to, per:, :] = jnp.where(
                    piece == 0, hi, jnp.where(piece == 1, mid, jnp.where(piece == 2, low, 0.0))
                ).astype(jnp.bfloat16)


def fresh_kernel(tokens, rows_ref, kv0_ref, kv1_ref, kv2_ref, kv3_ref, w_hbm, out_ref, lse_ref, w_ref, sems):
    copies = fetch([(w_hbm.at[: w_ref.shape[0]], w_ref)], sems)
    blocks = kv0_ref.shape[0]
    place = lax.axis_index("seq")
    scale = LOG2E * HD**-0.5
    nt = (((1,), (1,)), ((), ()))
    column = lax.broadcasted_iota(jnp.int32, (tokens, SPAN * blocks * tokens), 1)
    source = place ^ (column // tokens % blocks * SPAN + column // (blocks * tokens))
    key_pos = source * tokens + column % tokens
    query_pos = place * tokens + lax.broadcasted_iota(jnp.int32, column.shape, 0)
    visible = (key_pos <= query_pos) & (key_pos // BLK == query_pos // BLK)
    visible = jnp.concatenate([visible.astype(jnp.int32)] * GROUP, axis=0) > 0
    ones = jnp.ones((SPAN * blocks * tokens, HD), jnp.bfloat16)
    kv = [ref[...].astype(jnp.float32) for ref in (kv0_ref, kv1_ref, kv2_ref, kv3_ref)]
    for g in range(KVH):
        k, v = [
            jnp.concatenate(
                [x[:, i * tokens : (i + 1) * tokens].reshape(blocks * tokens, HD) for x in kv], axis=0
            ).astype(jnp.bfloat16)
            for i in (2 * g, 2 * g + 1)
        ]
        q = rows_ref[g].astype(jnp.bfloat16)
        s = lax.dot_general(q, k, nt, preferred_element_type=jnp.float32) * scale
        s = jnp.where(visible, s, LOW_SCORE)
        top = jnp.max(s, axis=1, keepdims=True)
        w = jnp.where(visible, jnp.exp2(s - top), 0.0).astype(jnp.bfloat16)
        total_out = jnp.dot(w, jnp.concatenate([v, ones], axis=1), preferred_element_type=jnp.float32)
        total = total_out[:, HD:]
        out_ref[g] = total_out[:, :HD] / total
        lse_ref[g] = top + jnp.log(total) * LOG2E
    for copy in copies:
        copy.wait()


def project_kernel(per, hist_ref, out_ref, lse_ref, match_ref, first_ref, w_hbm, y_ref, att_ref, w_ref, sems):
    depth = KVH * HD
    ready = first_ref.shape[0] // depth
    copies = fetch(
        [
            (w_hbm.at[pl.ds((ready + i) * depth, depth)], w_ref.at[pl.ds(i * depth, depth)])
            for i in range(w_ref.shape[0] // depth)
        ],
        sems,
    )
    tokens = y_ref.shape[0]
    holders = hist_ref.shape[0]
    fold = LANES // per
    row = lax.broadcasted_iota(jnp.int32, (holders, LANES), 0)
    lane = lax.broadcasted_iota(jnp.int32, (holders, LANES), 1)
    for g in range(KVH):
        outs = hist_ref[:, g, :per, :].reshape(holders * per, HD)
        stats = jnp.sum(hist_ref[:, g, per:, :].astype(jnp.float32), axis=1)
        stats = jnp.where(row % fold == lane // per, stats, 0.0)
        lse = jnp.concatenate(
            [
                jnp.sum(jnp.where(row // fold == m, stats, 0.0), axis=0, keepdims=True)
                for m in range(holders // fold)
            ],
            axis=1,
        )
        match = match_ref[g] > 0.5
        lse = jnp.where(match, lse, LOW_SCORE)
        own = lse_ref[g]
        top = jnp.maximum(jnp.max(lse, axis=1, keepdims=True), own)
        w = jnp.where(match, jnp.exp2(lse - top[:, :1]), 0.0)
        own_w = jnp.exp2(own - top)
        hi = w.astype(jnp.bfloat16)
        low = (w - hi.astype(jnp.float32)).astype(jnp.bfloat16)
        num = (
            jnp.dot(hi, outs, preferred_element_type=jnp.float32)
            + jnp.dot(low, outs, preferred_element_type=jnp.float32)
            + own_w * out_ref[g]
        )
        att = num / (jnp.sum(w, axis=1, keepdims=True) + own_w)
        for r in range(GROUP):
            h = g * GROUP + r
            att_ref[:, h * HD : (h + 1) * HD] = att[r * tokens : (r + 1) * tokens]
    att = att_ref[...].astype(jnp.bfloat16)
    y = jnp.dot(att[:, : ready * depth], first_ref[...], preferred_element_type=jnp.float32)
    for i, copy in enumerate(copies):
        copy.wait()
        y = y + jnp.dot(
            att[:, (ready + i) * depth : (ready + i + 1) * depth],
            w_ref[i * depth : (i + 1) * depth, :],
            preferred_element_type=jnp.float32,
        )
    y_ref[...] = y.astype(jnp.bfloat16)


VMEM = pl.BlockSpec(memory_space=pltpu.VMEM)
HBM = pl.BlockSpec(memory_space=pltpu.HBM)


def call(kernel, name, out_shape, specs, *operands, scratch=(), flops=0, moved=0, limit=16):
    outs = jax.tree.map(lambda _: VMEM, out_shape)
    return pl.pallas_call(
        kernel,
        name=name,
        out_shape=out_shape,
        in_specs=specs,
        out_specs=outs,
        scratch_shapes=scratch,
        cost_estimate=pl.CostEstimate(flops=flops, bytes_accessed=moved, transcendentals=0),
        compiler_params=pltpu.CompilerParams(vmem_limit_bytes=limit << 20),
    )(*operands)


def body(queries, stretch_keys, stretch_values, cache_keys, cache_values, chosen, out_weight):
    devices = lax.axis_size("seq")
    tokens = queries.shape[0]
    cache_rows = cache_keys.shape[0]
    chips = SPAN // KVH
    key_blocks = cache_rows * devices // BLK
    capacity = (GROUP * TOPK + key_blocks - 1) // key_blocks + 1
    per = capacity * tokens
    f32, bf16 = jnp.float32, jnp.bfloat16
    picks = chosen.transpose(2, 0, 1)

    def partner(bit):
        return [(i, i ^ bit) for i in range(devices)]

    send = call(
        functools.partial(pack_kernel, capacity),
        "pack",
        (jax.ShapeDtypeStruct((KVH * per + 2 * KVH * tokens, HD), bf16),) * key_blocks,
        [HBM] * 4,
        picks, queries, stretch_keys, stretch_values,
        scratch=[
            pltpu.VMEM(picks.shape, jnp.int32),
            pltpu.VMEM(queries.shape, bf16),
            pltpu.VMEM(stretch_keys.shape, bf16),
            pltpu.VMEM(stretch_values.shape, bf16),
            pltpu.VMEM((KVH, key_blocks, per, HD), bf16),
            pltpu.SemaphoreType.DMA((4,)),
        ],
        limit=60,
    )
    got = [send[0]] + [lax.ppermute(x, "seq", partner(SPAN * m)) for m, x in enumerate(send) if m]
    got[1], cache_keys, cache_values, picks, queries = lax.optimization_barrier(
        (got[1], cache_keys, cache_values, picks, queries)
    )
    same, other, fresh = call(
        gather_kernel,
        "gather",
        (
            jax.ShapeDtypeStruct((key_blocks, per, HD), bf16),
            jax.ShapeDtypeStruct((key_blocks, per, HD), bf16),
            jax.ShapeDtypeStruct((key_blocks, 2 * KVH * tokens, HD), bf16),
        ),
        [VMEM] * key_blocks,
        *got,
    )
    slots = [same] + [lax.ppermute(x, "seq", partner(i)) for i, x in ((1, other), (2, same), (3, other))]

    core = lax.axis_index("seq") % KVH

    def halves(head):
        return [lax.dynamic_slice_in_dim(x, head * HD, HD, axis=1) for x in (cache_keys, cache_values)]

    k_own, v_own = halves(core)
    k_peer, v_peer = [lax.ppermute(x, "seq", partner(1)) for x in halves(1 - core)]
    holders = devices // KVH
    match, query_rows = call(
        functools.partial(masks_kernel, chips, capacity),
        "masks",
        (
            jax.ShapeDtypeStruct((KVH, GROUP * tokens, holders * per), f32),
            jax.ShapeDtypeStruct((KVH, GROUP * tokens, HD), f32),
        ),
        [VMEM] * 2,
        picks, queries,
    )

    rows = devices * per
    back = call(
        attend_kernel,
        "attend",
        jax.ShapeDtypeStruct((devices, per + 8, HD), bf16),
        [VMEM] * 8,
        *slots, k_own, v_own, k_peer, v_peer,
        flops=8 * rows * cache_rows * HD,
        moved=4 << 20,
        limit=32,
    )
    hist = lax.all_to_all(back, "seq", split_axis=0, concat_axis=0, tiled=True)

    back, fresh = lax.optimization_barrier((back, fresh))
    spread = [fresh] + [lax.ppermute(fresh, "seq", partner(i)) for i in (1, 2, 3)]
    part = jax.ShapeDtypeStruct((KVH, GROUP * tokens, HD), f32)
    ready = EARLY * KVH * HD
    out, lse, first = call(
        functools.partial(fresh_kernel, tokens),
        "fresh",
        (part, part, jax.ShapeDtypeStruct((ready, out_weight.shape[1]), bf16)),
        [VMEM] * 5 + [HBM],
        query_rows, *spread, out_weight,
        scratch=[pltpu.SemaphoreType.DMA((1,))],
        flops=8 * H * tokens * devices * tokens * HD,
        moved=1 << 20,
        limit=50,
    )
    return call(
        functools.partial(project_kernel, per),
        "project",
        jax.ShapeDtypeStruct((tokens, out_weight.shape[1]), bf16),
        [VMEM] * 5 + [HBM],
        hist.reshape(holders, KVH, per + 8, HD), out, lse, match, first, out_weight,
        scratch=[
            pltpu.VMEM((tokens, H * HD), f32),
            pltpu.VMEM((out_weight.shape[0] - ready, out_weight.shape[1]), bf16),
            pltpu.SemaphoreType.DMA((GROUP - EARLY,)),
        ],
        flops=2 * tokens * out_weight.size,
        moved=out_weight.size * 2,
        limit=50,
    )


def solution(mesh):
    seq = ("grp", "seq")
    return jax.shard_map(
        body,
        mesh=mesh,
        in_specs=(
            P(seq, None),
            P(seq, None),
            P(seq, None),
            P(seq, None),
            P(seq, None),
            P(seq, None, None),
            P(),
        ),
        out_specs=P(seq, None),
        check_vma=False,
    )
```

```python
import functools
import math

import jax
import jax.numpy as jnp
from jax import lax
from jax.experimental import pallas as pl
from jax.experimental.pallas import tpu as pltpu
from jax.sharding import PartitionSpec as P

H = 14
KVH = 2
HD = 128
BLK = 4096
TOPK = 3
GROUP = H // KVH

LOW_SCORE = -1e30
LOG2E = math.log2(math.e)
LANES = 128
EARLY = 3


def head_rows(q_ref, g):
    q = q_ref[...].astype(jnp.float32)
    return [q[:, h * HD : (h + 1) * HD] for h in range(g * GROUP, (g + 1) * GROUP)]


def slot_match(chosen_ref, g, block, slot, token):
    rows = lax.broadcasted_iota(jnp.int32, block.shape, 0)
    same_token = token == rows
    seen = jnp.zeros(block.shape, jnp.int32)
    found = []
    for h in range(g * GROUP, (g + 1) * GROUP):
        picked = block == chosen_ref[0, :, h : h + 1]
        for t in range(1, TOPK):
            picked = picked | (block == chosen_ref[t, :, h : h + 1])
        found.append(jnp.where(picked & same_token & (seen == slot), 1.0, 0.0))
        seen = seen + picked.astype(jnp.int32)
    return found


def fetch(pairs, sems):
    copies = [pltpu.make_async_copy(src, dst, sems.at[i]) for i, (src, dst) in enumerate(pairs)]
    for copy in copies:
        copy.start()
    return copies


def pack_kernel(capacity, chosen_hbm, q_hbm, k_hbm, v_hbm, send_hbm, chosen_ref, q_ref, k_ref, v_ref, send_ref, sems):
    copies = fetch([(chosen_hbm, chosen_ref), (q_hbm, q_ref), (k_hbm, k_ref), (v_hbm, v_ref)], sems)
    tokens = q_ref.shape[0]
    per = capacity * tokens
    key_blocks, chips = send_ref.shape[1:3]
    lane = lax.broadcasted_iota(jnp.int32, (tokens, key_blocks * per), 1)
    block, slot, token = lane // per, lane % per // tokens, lane % tokens
    copies[0].wait()
    spread = [
        jnp.concatenate(
            slot_match(chosen_ref, g, block, slot, token) + [jnp.zeros(lane.shape, jnp.float32)], axis=0
        ).T.astype(jnp.bfloat16)
        for g in range(KVH)
    ]
    for copy in copies[1:]:
        copy.wait()
    sent = []
    for g in range(KVH):
        rows = head_rows(q_ref, g)
        rows = jnp.concatenate(rows + [jnp.zeros_like(rows[0])], axis=0).astype(jnp.bfloat16)
        slots = jnp.dot(spread[g], rows, preferred_element_type=jnp.float32).astype(jnp.bfloat16)
        cols = slice(g * HD, (g + 1) * HD)
        fresh = [k_ref[:, cols], v_ref[:, cols]]
        for b in range(key_blocks):
            for chip in range(chips):
                send_ref[g, b, chip, :per, :] = slots[b * per : (b + 1) * per]
                send_ref[g, b, chip, per:, :] = fresh[chip % 2]
        sent.append(pltpu.make_async_copy(send_ref.at[g], send_hbm.at[:, :, g], sems.at[4 + g]))
        sent[g].start()
    for copy in sent:
        copy.wait()


def masks_kernel(chips, capacity, chosen_ref, q_ref, w_hbm, match_ref, rows_ref, w_ref, sems):
    copies = fetch([(w_hbm.at[: w_ref.shape[0]], w_ref)], sems)
    tokens = q_ref.shape[0]
    per = capacity * tokens
    lane = lax.broadcasted_iota(jnp.int32, (tokens, match_ref.shape[2]), 1)
    block, slot, token = lane // (per * chips), lane % per // tokens, lane % tokens
    for g in range(KVH):
        match_ref[g] = jnp.concatenate(slot_match(chosen_ref, g, block, slot, token), axis=0)
        rows_ref[g] = jnp.concatenate(head_rows(q_ref, g), axis=0)
    for copy in copies:
        copy.wait()


def attend_kernel(per, q_ref, ka_ref, va_ref, kb_ref, vb_ref, out_hbm, fresh_ref, out_ref, sems):
    sources = q_ref.shape[0]
    sent = []
    fresh_ref[...] = q_ref[:, per:, :]
    step = 512 // per
    scale = LOG2E * HD**-0.5
    nt = (((1,), (1,)), ((), ()))
    row = lax.broadcasted_iota(jnp.int32, (per, LANES), 0)
    lane = lax.broadcasted_iota(jnp.int32, (per, LANES), 1)
    diagonal = row == lane % per
    piece = lax.broadcasted_iota(jnp.int32, (8, LANES), 0)
    ones = jnp.ones(va_ref.shape, jnp.bfloat16)
    for first in range(0, sources, step):
        q = q_ref[first : first + step, :per, :].reshape(step * per, HD)
        sa = lax.dot_general(q, ka_ref[...], nt, preferred_element_type=jnp.float32)
        sb = lax.dot_general(q, kb_ref[...], nt, preferred_element_type=jnp.float32)
        top = jnp.maximum(jnp.max(sa, axis=1, keepdims=True), jnp.max(sb, axis=1, keepdims=True)) * scale
        wa = jnp.exp2(sa * scale - top).astype(jnp.bfloat16)
        wb = jnp.exp2(sb * scale - top).astype(jnp.bfloat16)
        both = jnp.dot(
            wa, jnp.concatenate([va_ref[...], ones], axis=1), preferred_element_type=jnp.float32
        ) + jnp.dot(wb, jnp.concatenate([vb_ref[...], ones], axis=1), preferred_element_type=jnp.float32)
        total = both[:, HD:]
        out = (both[:, :HD] / total).astype(jnp.bfloat16)
        lse = top + jnp.log(total) * LOG2E
        for s in range(step):
            part = slice(s * per, (s + 1) * per)
            out_ref[first + s, :per, :] = out[part]
            flat = jnp.sum(jnp.where(diagonal, lse[part], 0.0), axis=0, keepdims=True)
            hi = flat.astype(jnp.bfloat16).astype(jnp.float32)
            mid = (flat - hi).astype(jnp.bfloat16).astype(jnp.float32)
            low = flat - hi - mid
            out_ref[first + s, per:, :] = jnp.where(
                piece == 0, hi, jnp.where(piece == 1, mid, jnp.where(piece == 2, low, 0.0))
            ).astype(jnp.bfloat16)
        done = pl.ds(first, step)
        sent.append(pltpu.make_async_copy(out_ref.at[done], out_hbm.at[done], sems.at[first // step]))
        sent[-1].start()
    for copy in sent:
        copy.wait()


def fresh_kernel(tokens, rows_ref, kv_ref, kv1_ref, kv2_ref, kv3_ref, out_ref, lse_ref):
    sources = kv_ref.shape[0]
    place = lax.axis_index("seq")
    core, odd = place % KVH, place // KVH % 2
    scale = LOG2E * HD**-0.5
    nt = (((1,), (1,)), ((), ()))
    column = lax.broadcasted_iota(jnp.int32, (tokens, sources * tokens), 1)
    query_pos = place * tokens + lax.broadcasted_iota(jnp.int32, column.shape, 0)
    visible = (column <= query_pos) & (column // BLK == query_pos // BLK)
    visible = jnp.concatenate([visible.astype(jnp.int32)] * GROUP, axis=0) > 0
    ones = jnp.ones((sources * tokens, HD), jnp.bfloat16)
    here, near, far, both = [
        ref[...].astype(jnp.float32).reshape(sources * tokens, HD) for ref in (kv_ref, kv1_ref, kv2_ref, kv3_ref)
    ]
    keys = [jnp.where(odd == 0, here, far), jnp.where(odd == 0, near, both)]
    values = [jnp.where(odd == 0, far, here), jnp.where(odd == 0, both, near)]
    for g in range(KVH):
        k = jnp.where(core == g, keys[0], keys[1]).astype(jnp.bfloat16)
        v = jnp.where(core == g, values[0], values[1]).astype(jnp.bfloat16)
        q = rows_ref[g].astype(jnp.bfloat16)
        s = lax.dot_general(q, k, nt, preferred_element_type=jnp.float32) * scale
        s = jnp.where(visible, s, LOW_SCORE)
        top = jnp.max(s, axis=1, keepdims=True)
        w = jnp.where(visible, jnp.exp2(s - top), 0.0).astype(jnp.bfloat16)
        total_out = jnp.dot(w, jnp.concatenate([v, ones], axis=1), preferred_element_type=jnp.float32)
        total = total_out[:, HD:]
        out_ref[g] = total_out[:, :HD] / total
        lse_ref[g] = top + jnp.log(total) * LOG2E


def project_kernel(per, hist_ref, out_ref, lse_ref, match_ref, first_ref, w_hbm, y_ref, w_ref, sems):
    depth = KVH * HD
    ready = first_ref.shape[0] // depth
    copies = fetch(
        [
            (w_hbm.at[pl.ds((ready + i) * depth, depth)], w_ref.at[pl.ds(i * depth, depth)])
            for i in range(w_ref.shape[0] // depth)
        ],
        sems,
    )
    tokens = y_ref.shape[0]
    holders = hist_ref.shape[0]
    fold = LANES // per
    row = lax.broadcasted_iota(jnp.int32, (holders, LANES), 0)
    lane = lax.broadcasted_iota(jnp.int32, (holders, LANES), 1)

    def times(heads, weights):
        lhs = jnp.concatenate(heads, axis=1).astype(jnp.bfloat16)
        return jnp.dot(lhs, weights, preferred_element_type=jnp.float32)

    heads = []
    for g in range(KVH):
        outs = hist_ref[:, g, :per, :].reshape(holders * per, HD)
        stats = jnp.sum(hist_ref[:, g, per:, :].astype(jnp.float32), axis=1)
        stats = jnp.where(row % fold == lane // per, stats, 0.0)
        lse = jnp.concatenate(
            [
                jnp.sum(jnp.where(row // fold == m, stats, 0.0), axis=0, keepdims=True)
                for m in range(holders // fold)
            ],
            axis=1,
        )
        match = match_ref[g] > 0.5
        lse = jnp.where(match, lse, LOW_SCORE)
        own = lse_ref[g]
        top = jnp.maximum(jnp.max(lse, axis=1, keepdims=True), own)
        w = jnp.where(match, jnp.exp2(lse - top[:, :1]), 0.0)
        own_w = jnp.exp2(own - top)
        hi = w.astype(jnp.bfloat16)
        low = (w - hi.astype(jnp.float32)).astype(jnp.bfloat16)
        num = (
            jnp.dot(hi, outs, preferred_element_type=jnp.float32)
            + jnp.dot(low, outs, preferred_element_type=jnp.float32)
            + own_w * out_ref[g]
        )
        att = num / (jnp.sum(w, axis=1, keepdims=True) + own_w)
        heads = heads + [att[r * tokens : (r + 1) * tokens] for r in range(GROUP)]
        if g == 0:
            y = times(heads[: ready * KVH], first_ref[...])
    for i, copy in enumerate(copies):
        copy.wait()
        y = y + times(heads[(ready + i) * KVH : (ready + i + 1) * KVH], w_ref[i * depth : (i + 1) * depth, :])
    y_ref[...] = y.astype(jnp.bfloat16)


VMEM = pl.BlockSpec(memory_space=pltpu.VMEM)
HBM = pl.BlockSpec(memory_space=pltpu.HBM)
ANY = pl.BlockSpec(memory_space=pl.ANY)


def call(kernel, name, out_shape, specs, *operands, outs=None, scratch=(), flops=0, moved=0, limit=16):
    outs = outs or jax.tree.map(lambda _: VMEM, out_shape)
    return pl.pallas_call(
        kernel,
        name=name,
        out_shape=out_shape,
        in_specs=specs,
        out_specs=outs,
        scratch_shapes=scratch,
        cost_estimate=pl.CostEstimate(flops=flops, bytes_accessed=moved, transcendentals=0),
        compiler_params=pltpu.CompilerParams(vmem_limit_bytes=limit << 20),
    )(*operands)


def body(queries, stretch_keys, stretch_values, cache_keys, cache_values, chosen, out_weight):
    devices = lax.axis_size("seq")
    tokens = queries.shape[0]
    cache_rows = cache_keys.shape[0]
    span = BLK // cache_rows
    chips = span // KVH
    key_blocks = cache_rows * devices // BLK
    capacity = (GROUP * TOPK + key_blocks - 1) // key_blocks + 1
    per = capacity * tokens
    f32, bf16 = jnp.float32, jnp.bfloat16
    picks = chosen.transpose(2, 0, 1)

    def partner(bit):
        return [(i, i ^ bit) for i in range(devices)]

    send = call(
        functools.partial(pack_kernel, capacity),
        "pack",
        jax.ShapeDtypeStruct((key_blocks, chips, KVH, per + tokens, HD), bf16),
        [HBM] * 4,
        picks, queries, stretch_keys, stretch_values,
        outs=ANY,
        scratch=[
            pltpu.VMEM(picks.shape, jnp.int32),
            pltpu.VMEM(queries.shape, bf16),
            pltpu.VMEM(stretch_keys.shape, bf16),
            pltpu.VMEM(stretch_values.shape, bf16),
            pltpu.VMEM((KVH, key_blocks, chips, per + tokens, HD), bf16),
            pltpu.SemaphoreType.DMA((4 + KVH,)),
        ],
        limit=60,
    )
    send, cache_keys, cache_values, picks, queries = lax.optimization_barrier(
        (send, cache_keys, cache_values, picks, queries)
    )
    send = send.reshape(devices, per + tokens, HD)
    got = lax.all_to_all(send, "seq", split_axis=0, concat_axis=0, tiled=True)

    core = lax.axis_index("seq") % KVH

    def halves(head):
        return [lax.dynamic_slice_in_dim(x, head * HD, HD, axis=1) for x in (cache_keys, cache_values)]

    k_own, v_own = halves(core)
    k_peer, v_peer = [lax.ppermute(x, "seq", partner(1)) for x in halves(1 - core)]
    holders = devices // KVH
    rows = devices * per
    back, fresh = call(
        functools.partial(attend_kernel, per),
        "attend",
        (
            jax.ShapeDtypeStruct((devices, per + 8, HD), bf16),
            jax.ShapeDtypeStruct((devices, tokens, HD), bf16),
        ),
        [VMEM] * 5,
        got, k_own, v_own, k_peer, v_peer,
        outs=(ANY, VMEM),
        scratch=[
            pltpu.VMEM((devices, per + 8, HD), bf16),
            pltpu.SemaphoreType.DMA((rows // 512,)),
        ],
        flops=8 * rows * cache_rows * HD,
        moved=4 << 20,
        limit=32,
    )
    back, picks, queries, out_weight = lax.optimization_barrier((back, picks, queries, out_weight))
    hist = lax.all_to_all(back, "seq", split_axis=0, concat_axis=0, tiled=True)

    ready = EARLY * KVH * HD
    match, query_rows, first = call(
        functools.partial(masks_kernel, chips, capacity),
        "masks",
        (
            jax.ShapeDtypeStruct((KVH, GROUP * tokens, holders * per), f32),
            jax.ShapeDtypeStruct((KVH, GROUP * tokens, HD), f32),
            jax.ShapeDtypeStruct((ready, out_weight.shape[1]), bf16),
        ),
        [VMEM, VMEM, HBM],
        picks, queries, out_weight,
        scratch=[pltpu.SemaphoreType.DMA((1,))],
        limit=50,
    )

    far = lax.ppermute(fresh, "seq", partner(2))
    near, both = [lax.ppermute(x, "seq", partner(1)) for x in (fresh, far)]
    part = jax.ShapeDtypeStruct((KVH, GROUP * tokens, HD), f32)
    out, lse = call(
        functools.partial(fresh_kernel, tokens),
        "fresh",
        (part, part),
        [VMEM] * 5,
        query_rows, fresh, near, far, both,
        flops=8 * H * tokens * devices * tokens * HD,
        moved=1 << 20,
    )
    return call(
        functools.partial(project_kernel, per),
        "project",
        jax.ShapeDtypeStruct((tokens, out_weight.shape[1]), bf16),
        [VMEM] * 5 + [HBM],
        hist.reshape(holders, KVH, per + 8, HD), out, lse, match, first, out_weight,
        scratch=[
            pltpu.VMEM((out_weight.shape[0] - ready, out_weight.shape[1]), bf16),
            pltpu.SemaphoreType.DMA((GROUP - EARLY,)),
        ],
        flops=2 * tokens * out_weight.size,
        moved=out_weight.size * 2,
        limit=50,
    )


def solution(mesh):
    seq = ("grp", "seq")
    return jax.shard_map(
        body,
        mesh=mesh,
        in_specs=(
            P(seq, None),
            P(seq, None),
            P(seq, None),
            P(seq, None),
            P(seq, None),
            P(seq, None, None),
            P(),
        ),
        out_specs=P(seq, None),
        check_vma=False,
    )
```

```python
import functools
import math

import jax
import jax.numpy as jnp
from jax import lax
from jax.experimental import pallas as pl
from jax.experimental.pallas import tpu as pltpu
from jax.sharding import PartitionSpec as P

H = 14
KVH = 2
HD = 128
BLK = 4096
TOPK = 3
GROUP = H // KVH

LOW_SCORE = -1e30
LOG2E = math.log2(math.e)
LANES = 128
EARLY = 3
STEP = 128


def head_rows(q_ref, g):
    q = q_ref[...].astype(jnp.float32)
    return [q[:, h * HD : (h + 1) * HD] for h in range(g * GROUP, (g + 1) * GROUP)]


def slot_match(chosen_ref, g, block, slot, token):
    rows = lax.broadcasted_iota(jnp.int32, block.shape, 0)
    same_token = token == rows
    seen = jnp.zeros(block.shape, jnp.int32)
    found = []
    for h in range(g * GROUP, (g + 1) * GROUP):
        picked = block == chosen_ref[0, :, h : h + 1]
        for t in range(1, TOPK):
            picked = picked | (block == chosen_ref[t, :, h : h + 1])
        found.append(jnp.where(picked & same_token & (seen == slot), 1.0, 0.0))
        seen = seen + picked.astype(jnp.int32)
    return found


def fetch(pairs, sems):
    copies = [pltpu.make_async_copy(src, dst, sems.at[i]) for i, (src, dst) in enumerate(pairs)]
    for copy in copies:
        copy.start()
    return copies


def pack_kernel(capacity, chosen_hbm, q_hbm, k_hbm, v_hbm, send_hbm, chosen_ref, q_ref, k_ref, v_ref, send_ref, sems):
    copies = fetch([(chosen_hbm, chosen_ref), (q_hbm, q_ref), (k_hbm, k_ref), (v_hbm, v_ref)], sems)
    tokens = q_ref.shape[0]
    per = capacity * tokens
    key_blocks, chips = send_ref.shape[1:3]
    lane = lax.broadcasted_iota(jnp.int32, (tokens, key_blocks * per), 1)
    block, slot, token = lane // per, lane % per // tokens, lane % tokens
    copies[0].wait()
    spread = [
        jnp.concatenate(
            slot_match(chosen_ref, g, block, slot, token) + [jnp.zeros(lane.shape, jnp.float32)], axis=0
        ).T.astype(jnp.bfloat16)
        for g in range(KVH)
    ]
    for copy in copies[1:]:
        copy.wait()
    sent = []
    for g in range(KVH):
        rows = head_rows(q_ref, g)
        rows = jnp.concatenate(rows + [jnp.zeros_like(rows[0])], axis=0).astype(jnp.bfloat16)
        slots = jnp.dot(spread[g], rows, preferred_element_type=jnp.float32).astype(jnp.bfloat16)
        cols = slice(g * HD, (g + 1) * HD)
        fresh = [k_ref[:, cols], v_ref[:, cols]]
        for b in range(key_blocks):
            for chip in range(chips):
                send_ref[g, b, chip, :per, :] = slots[b * per : (b + 1) * per]
                send_ref[g, b, chip, per:, :] = fresh[chip % 2]
        sent.append(pltpu.make_async_copy(send_ref.at[g], send_hbm.at[:, :, g], sems.at[4 + g]))
        sent[g].start()
    for copy in sent:
        copy.wait()


def masks_kernel(chips, capacity, chosen_ref, q_ref, w_hbm, match_ref, rows_ref, w_ref, sems):
    copies = fetch([(w_hbm.at[: w_ref.shape[0]], w_ref)], sems)
    tokens = q_ref.shape[0]
    per = capacity * tokens
    lane = lax.broadcasted_iota(jnp.int32, (tokens, match_ref.shape[2]), 1)
    block, slot, token = lane // (per * chips), lane % per // tokens, lane % tokens
    for g in range(KVH):
        match_ref[g] = jnp.concatenate(slot_match(chosen_ref, g, block, slot, token), axis=0)
        rows_ref[g] = jnp.concatenate(head_rows(q_ref, g), axis=0)
    for copy in copies:
        copy.wait()


def attend_kernel(per, q_ref, ka_ref, va_ref, kb_ref, vb_ref, out_hbm, fresh_ref, out_ref, sems):
    sources = q_ref.shape[0]
    sent = []
    step = STEP // per
    scale = LOG2E * HD**-0.5
    nt = (((1,), (1,)), ((), ()))
    row = lax.broadcasted_iota(jnp.int32, (per, LANES), 0)
    lane = lax.broadcasted_iota(jnp.int32, (per, LANES), 1)
    diagonal = row == lane % per
    piece = lax.broadcasted_iota(jnp.int32, (8, LANES), 0)
    ones = jnp.ones(va_ref.shape, jnp.bfloat16)
    fresh_ref[...] = q_ref[:, per:, :]

    def scores(first):
        q = q_ref[first : first + step, :per, :].reshape(step * per, HD)
        return [
            lax.dot_general(q, k_ref[...], nt, preferred_element_type=jnp.float32) for k_ref in (ka_ref, kb_ref)
        ]

    ahead = scores(0)
    for first in range(0, sources, step):
        sa, sb = ahead
        if first + step < sources:
            ahead = scores(first + step)
        top = scale * jnp.maximum(jnp.max(sa, axis=1, keepdims=True), jnp.max(sb, axis=1, keepdims=True))
        wa = jnp.exp2(sa * scale - top).astype(jnp.bfloat16)
        wb = jnp.exp2(sb * scale - top).astype(jnp.bfloat16)
        both = jnp.dot(
            wa, jnp.concatenate([va_ref[...], ones], axis=1), preferred_element_type=jnp.float32
        ) + jnp.dot(wb, jnp.concatenate([vb_ref[...], ones], axis=1), preferred_element_type=jnp.float32)
        total = both[:, HD:]
        out = (both[:, :HD] / total).astype(jnp.bfloat16)
        lse = top + jnp.log(total) * LOG2E
        for s in range(step):
            part = slice(s * per, (s + 1) * per)
            out_ref[first + s, :per, :] = out[part]
            flat = jnp.sum(jnp.where(diagonal, lse[part], 0.0), axis=0, keepdims=True)
            hi = flat.astype(jnp.bfloat16).astype(jnp.float32)
            mid = (flat - hi).astype(jnp.bfloat16).astype(jnp.float32)
            low = flat - hi - mid
            out_ref[first + s, per:, :] = jnp.where(
                piece == 0, hi, jnp.where(piece == 1, mid, jnp.where(piece == 2, low, 0.0))
            ).astype(jnp.bfloat16)
        done = pl.ds(first, step)
        sent.append(pltpu.make_async_copy(out_ref.at[done], out_hbm.at[done], sems.at[first // step]))
        sent[-1].start()
    for copy in sent:
        copy.wait()


def fresh_kernel(tokens, rows_ref, kv_ref, kv1_ref, kv2_ref, kv3_ref, out_ref, lse_ref):
    sources = kv_ref.shape[0]
    place = lax.axis_index("seq")
    core, odd = place % KVH, place // KVH % 2
    scale = LOG2E * HD**-0.5
    nt = (((1,), (1,)), ((), ()))
    column = lax.broadcasted_iota(jnp.int32, (tokens, sources * tokens), 1)
    query_pos = place * tokens + lax.broadcasted_iota(jnp.int32, column.shape, 0)
    visible = (column <= query_pos) & (column // BLK == query_pos // BLK)
    visible = jnp.concatenate([visible.astype(jnp.int32)] * GROUP, axis=0) > 0
    ones = jnp.ones((sources * tokens, HD), jnp.bfloat16)
    here, near, far, both = [
        ref[...].astype(jnp.float32).reshape(sources * tokens, HD) for ref in (kv_ref, kv1_ref, kv2_ref, kv3_ref)
    ]
    keys = [jnp.where(odd == 0, here, far), jnp.where(odd == 0, near, both)]
    values = [jnp.where(odd == 0, far, here), jnp.where(odd == 0, both, near)]
    for g in range(KVH):
        k = jnp.where(core == g, keys[0], keys[1]).astype(jnp.bfloat16)
        v = jnp.where(core == g, values[0], values[1]).astype(jnp.bfloat16)
        q = rows_ref[g].astype(jnp.bfloat16)
        s = lax.dot_general(q, k, nt, preferred_element_type=jnp.float32) * scale
        s = jnp.where(visible, s, LOW_SCORE)
        top = jnp.max(s, axis=1, keepdims=True)
        w = jnp.where(visible, jnp.exp2(s - top), 0.0).astype(jnp.bfloat16)
        total_out = jnp.dot(w, jnp.concatenate([v, ones], axis=1), preferred_element_type=jnp.float32)
        total = total_out[:, HD:]
        out_ref[g] = total_out[:, :HD] / total
        lse_ref[g] = top + jnp.log(total) * LOG2E


def project_kernel(per, hist_ref, out_ref, lse_ref, match_ref, first_ref, w_hbm, y_ref, w_ref, sems):
    depth = KVH * HD
    ready = first_ref.shape[0] // depth
    copies = fetch(
        [
            (w_hbm.at[pl.ds((ready + i) * depth, depth)], w_ref.at[pl.ds(i * depth, depth)])
            for i in range(w_ref.shape[0] // depth)
        ],
        sems,
    )
    tokens = y_ref.shape[0]
    holders = hist_ref.shape[0]
    fold = LANES // per
    row = lax.broadcasted_iota(jnp.int32, (holders, LANES), 0)
    lane = lax.broadcasted_iota(jnp.int32, (holders, LANES), 1)

    def times(heads, weights):
        lhs = jnp.concatenate(heads, axis=1).astype(jnp.bfloat16)
        return jnp.dot(lhs, weights, preferred_element_type=jnp.float32)

    heads = []
    for g in range(KVH):
        outs = hist_ref[:, g, :per, :].reshape(holders * per, HD)
        stats = jnp.sum(hist_ref[:, g, per:, :].astype(jnp.float32), axis=1)
        stats = jnp.where(row % fold == lane // per, stats, 0.0)
        lse = jnp.concatenate(
            [
                jnp.sum(jnp.where(row // fold == m, stats, 0.0), axis=0, keepdims=True)
                for m in range(holders // fold)
            ],
            axis=1,
        )
        match = match_ref[g] > 0.5
        lse = jnp.where(match, lse, LOW_SCORE)
        own = lse_ref[g]
        top = jnp.maximum(jnp.max(lse, axis=1, keepdims=True), own)
        w = jnp.where(match, jnp.exp2(lse - top[:, :1]), 0.0)
        own_w = jnp.exp2(own - top)
        hi = w.astype(jnp.bfloat16)
        low = (w - hi.astype(jnp.float32)).astype(jnp.bfloat16)
        num = (
            jnp.dot(hi, outs, preferred_element_type=jnp.float32)
            + jnp.dot(low, outs, preferred_element_type=jnp.float32)
            + own_w * out_ref[g]
        )
        att = num / (jnp.sum(w, axis=1, keepdims=True) + own_w)
        heads = heads + [att[r * tokens : (r + 1) * tokens] for r in range(GROUP)]
        if g == 0:
            y = times(heads[: ready * KVH], first_ref[...])
    for i, copy in enumerate(copies):
        copy.wait()
        y = y + times(heads[(ready + i) * KVH : (ready + i + 1) * KVH], w_ref[i * depth : (i + 1) * depth, :])
    y_ref[...] = y.astype(jnp.bfloat16)


VMEM = pl.BlockSpec(memory_space=pltpu.VMEM)
HBM = pl.BlockSpec(memory_space=pltpu.HBM)
ANY = pl.BlockSpec(memory_space=pl.ANY)


def call(kernel, name, out_shape, specs, *operands, outs=None, scratch=(), flops=0, moved=0, limit=16):
    outs = outs or jax.tree.map(lambda _: VMEM, out_shape)
    return pl.pallas_call(
        kernel,
        name=name,
        out_shape=out_shape,
        in_specs=specs,
        out_specs=outs,
        scratch_shapes=scratch,
        cost_estimate=pl.CostEstimate(flops=flops, bytes_accessed=moved, transcendentals=0),
        compiler_params=pltpu.CompilerParams(vmem_limit_bytes=limit << 20),
    )(*operands)


def body(queries, stretch_keys, stretch_values, cache_keys, cache_values, chosen, out_weight):
    devices = lax.axis_size("seq")
    tokens = queries.shape[0]
    cache_rows = cache_keys.shape[0]
    span = BLK // cache_rows
    chips = span // KVH
    key_blocks = cache_rows * devices // BLK
    capacity = (GROUP * TOPK + key_blocks - 1) // key_blocks + 1
    per = capacity * tokens
    f32, bf16 = jnp.float32, jnp.bfloat16
    picks = chosen.transpose(2, 0, 1)

    def partner(bit):
        return [(i, i ^ bit) for i in range(devices)]

    send = call(
        functools.partial(pack_kernel, capacity),
        "pack",
        jax.ShapeDtypeStruct((key_blocks, chips, KVH, per + tokens, HD), bf16),
        [HBM] * 4,
        picks, queries, stretch_keys, stretch_values,
        outs=ANY,
        scratch=[
            pltpu.VMEM(picks.shape, jnp.int32),
            pltpu.VMEM(queries.shape, bf16),
            pltpu.VMEM(stretch_keys.shape, bf16),
            pltpu.VMEM(stretch_values.shape, bf16),
            pltpu.VMEM((KVH, key_blocks, chips, per + tokens, HD), bf16),
            pltpu.SemaphoreType.DMA((4 + KVH,)),
        ],
        limit=60,
    )
    send, cache_keys, cache_values, picks, queries = lax.optimization_barrier(
        (send, cache_keys, cache_values, picks, queries)
    )
    send = send.reshape(devices, per + tokens, HD)
    got = lax.all_to_all(send, "seq", split_axis=0, concat_axis=0, tiled=True)

    core = lax.axis_index("seq") % KVH

    def halves(head):
        return [lax.dynamic_slice_in_dim(x, head * HD, HD, axis=1) for x in (cache_keys, cache_values)]

    k_own, v_own = halves(core)
    k_peer, v_peer = [lax.ppermute(x, "seq", partner(1)) for x in halves(1 - core)]
    holders = devices // KVH
    rows = devices * per
    back, fresh = call(
        functools.partial(attend_kernel, per),
        "attend",
        (
            jax.ShapeDtypeStruct((devices, per + 8, HD), bf16),
            jax.ShapeDtypeStruct((devices, tokens, HD), bf16),
        ),
        [VMEM] * 5,
        got, k_own, v_own, k_peer, v_peer,
        outs=(ANY, VMEM),
        scratch=[
            pltpu.VMEM((devices, per + 8, HD), bf16),
            pltpu.SemaphoreType.DMA((rows // STEP,)),
        ],
        flops=8 * rows * cache_rows * HD,
        moved=4 << 20,
        limit=32,
    )
    back, picks, queries, out_weight = lax.optimization_barrier((back, picks, queries, out_weight))
    hist = lax.all_to_all(back, "seq", split_axis=0, concat_axis=0, tiled=True)

    ready = EARLY * KVH * HD
    match, query_rows, first = call(
        functools.partial(masks_kernel, chips, capacity),
        "masks",
        (
            jax.ShapeDtypeStruct((KVH, GROUP * tokens, holders * per), f32),
            jax.ShapeDtypeStruct((KVH, GROUP * tokens, HD), f32),
            jax.ShapeDtypeStruct((ready, out_weight.shape[1]), bf16),
        ),
        [VMEM, VMEM, HBM],
        picks, queries, out_weight,
        scratch=[pltpu.SemaphoreType.DMA((1,))],
        limit=50,
    )

    far = lax.ppermute(fresh, "seq", partner(2))
    near, both = [lax.ppermute(x, "seq", partner(1)) for x in (fresh, far)]
    part = jax.ShapeDtypeStruct((KVH, GROUP * tokens, HD), f32)
    out, lse = call(
        functools.partial(fresh_kernel, tokens),
        "fresh",
        (part, part),
        [VMEM] * 5,
        query_rows, fresh, near, far, both,
        flops=8 * H * tokens * devices * tokens * HD,
        moved=1 << 20,
    )
    return call(
        functools.partial(project_kernel, per),
        "project",
        jax.ShapeDtypeStruct((tokens, out_weight.shape[1]), bf16),
        [VMEM] * 5 + [HBM],
        hist.reshape(holders, KVH, per + 8, HD), out, lse, match, first, out_weight,
        scratch=[
            pltpu.VMEM((out_weight.shape[0] - ready, out_weight.shape[1]), bf16),
            pltpu.SemaphoreType.DMA((GROUP - EARLY,)),
        ],
        flops=2 * tokens * out_weight.size,
        moved=out_weight.size * 2,
        limit=50,
    )


def solution(mesh):
    seq = ("grp", "seq")
    return jax.shard_map(
        body,
        mesh=mesh,
        in_specs=(
            P(seq, None),
            P(seq, None),
            P(seq, None),
            P(seq, None),
            P(seq, None),
            P(seq, None, None),
            P(),
        ),
        out_specs=P(seq, None),
        check_vma=False,
    )
```

```python
import functools
import math

import jax
import jax.numpy as jnp
from jax import lax
from jax.experimental import pallas as pl
from jax.experimental.pallas import tpu as pltpu
from jax.sharding import PartitionSpec as P

H = 14
KVH = 2
HD = 128
BLK = 4096
TOPK = 3
GROUP = H // KVH

LOW_SCORE = -1e30
LOG2E = math.log2(math.e)
LANES = 128
EARLY = 3
PIECES = 4
STEP = 256


def head_rows(q_ref, g):
    q = q_ref[...].astype(jnp.float32)
    return [q[:, h * HD : (h + 1) * HD] for h in range(g * GROUP, (g + 1) * GROUP)]


def slot_match(chosen_ref, g, block, slot, token):
    rows = lax.broadcasted_iota(jnp.int32, block.shape, 0)
    same_token = token == rows
    seen = jnp.zeros(block.shape, jnp.int32)
    found = []
    for h in range(g * GROUP, (g + 1) * GROUP):
        picked = block == chosen_ref[0, :, h : h + 1]
        for t in range(1, TOPK):
            picked = picked | (block == chosen_ref[t, :, h : h + 1])
        found.append(jnp.where(picked & same_token & (seen == slot), 1.0, 0.0))
        seen = seen + picked.astype(jnp.int32)
    return found


def fetch(pairs, sems):
    copies = [pltpu.make_async_copy(src, dst, sems.at[i]) for i, (src, dst) in enumerate(pairs)]
    for copy in copies:
        copy.start()
    return copies


def pack_kernel(capacity, chosen_hbm, q_hbm, k_hbm, v_hbm, send_hbm, chosen_ref, q_ref, k_ref, v_ref, send_ref, sems):
    copies = fetch([(chosen_hbm, chosen_ref), (q_hbm, q_ref), (k_hbm, k_ref), (v_hbm, v_ref)], sems)
    tokens = q_ref.shape[0]
    per = capacity * tokens
    key_blocks, chips = send_ref.shape[1:3]
    lane = lax.broadcasted_iota(jnp.int32, (tokens, key_blocks * per), 1)
    block, slot, token = lane // per, lane % per // tokens, lane % tokens
    copies[0].wait()
    spread = [
        jnp.concatenate(
            slot_match(chosen_ref, g, block, slot, token) + [jnp.zeros(lane.shape, jnp.float32)], axis=0
        ).T.astype(jnp.bfloat16)
        for g in range(KVH)
    ]
    for copy in copies[1:]:
        copy.wait()
    sent = []
    for g in range(KVH):
        rows = head_rows(q_ref, g)
        rows = jnp.concatenate(rows + [jnp.zeros_like(rows[0])], axis=0).astype(jnp.bfloat16)
        slots = jnp.dot(spread[g], rows, preferred_element_type=jnp.float32).astype(jnp.bfloat16)
        cols = slice(g * HD, (g + 1) * HD)
        fresh = [k_ref[:, cols], v_ref[:, cols]]
        for b in range(key_blocks):
            for chip in range(chips):
                send_ref[g, b, chip, :per, :] = slots[b * per : (b + 1) * per]
                send_ref[g, b, chip, per:, :] = fresh[chip % 2]
        sent.append(pltpu.make_async_copy(send_ref.at[g], send_hbm.at[:, :, g], sems.at[4 + g]))
        sent[g].start()
    for copy in sent:
        copy.wait()


def masks_kernel(chips, capacity, chosen_ref, q_ref, w_hbm, match_ref, rows_ref, w_ref, sems):
    copies = fetch([(w_hbm.at[: w_ref.shape[0]], w_ref)], sems)
    tokens = q_ref.shape[0]
    per = capacity * tokens
    lane = lax.broadcasted_iota(jnp.int32, (tokens, match_ref.shape[2]), 1)
    block, slot, token = lane // (per * chips), lane % per // tokens, lane % tokens
    for g in range(KVH):
        match_ref[g] = jnp.concatenate(slot_match(chosen_ref, g, block, slot, token), axis=0)
        rows_ref[g] = jnp.concatenate(head_rows(q_ref, g), axis=0)
    for copy in copies:
        copy.wait()


def attend_kernel(per, q_ref, ka_ref, va_ref, kb_ref, vb_ref, out_hbm, fresh_ref, out_ref, sems):
    sources = q_ref.shape[0]
    sent = []
    step = STEP // per
    scale = LOG2E * HD**-0.5
    nt = (((1,), (1,)), ((), ()))
    row = lax.broadcasted_iota(jnp.int32, (per, LANES), 0)
    lane = lax.broadcasted_iota(jnp.int32, (per, LANES), 1)
    diagonal = row == lane % per
    piece = lax.broadcasted_iota(jnp.int32, (8, LANES), 0)
    ones = jnp.ones(va_ref.shape, jnp.bfloat16)
    fresh_ref[...] = q_ref[:, per:, :]

    def scores(first):
        q = q_ref[first : first + step, :per, :].reshape(step * per, HD)
        return [
            lax.dot_general(q, k_ref[...], nt, preferred_element_type=jnp.float32) for k_ref in (ka_ref, kb_ref)
        ]

    ahead = scores(0)
    for first in range(0, sources, step):
        sa, sb = ahead
        if first + step < sources:
            ahead = scores(first + step)
        top = scale * jnp.maximum(jnp.max(sa, axis=1, keepdims=True), jnp.max(sb, axis=1, keepdims=True))
        wa = jnp.exp2(sa * scale - top).astype(jnp.bfloat16)
        wb = jnp.exp2(sb * scale - top).astype(jnp.bfloat16)
        both = jnp.dot(
            wa, jnp.concatenate([va_ref[...], ones], axis=1), preferred_element_type=jnp.float32
        ) + jnp.dot(wb, jnp.concatenate([vb_ref[...], ones], axis=1), preferred_element_type=jnp.float32)
        total = both[:, HD:]
        out = (both[:, :HD] / total).astype(jnp.bfloat16)
        lse = top + jnp.log(total) * LOG2E
        for s in range(step):
            part = slice(s * per, (s + 1) * per)
            out_ref[first + s, :per, :] = out[part]
            flat = jnp.sum(jnp.where(diagonal, lse[part], 0.0), axis=0, keepdims=True)
            hi = flat.astype(jnp.bfloat16).astype(jnp.float32)
            mid = (flat - hi).astype(jnp.bfloat16).astype(jnp.float32)
            low = flat - hi - mid
            out_ref[first + s, per:, :] = jnp.where(
                piece == 0, hi, jnp.where(piece == 1, mid, jnp.where(piece == 2, low, 0.0))
            ).astype(jnp.bfloat16)
        done = pl.ds(first, step)
        sent.append(pltpu.make_async_copy(out_ref.at[done], out_hbm.at[done], sems.at[first // step]))
        sent[-1].start()
    for copy in sent:
        copy.wait()


def fresh_kernel(tokens, rows_ref, kv_ref, kv1_ref, kv2_ref, kv3_ref, out_ref, lse_ref):
    sources = kv_ref.shape[0]
    place = lax.axis_index("seq")
    core, odd = place % KVH, place // KVH % 2
    scale = LOG2E * HD**-0.5
    nt = (((1,), (1,)), ((), ()))
    column = lax.broadcasted_iota(jnp.int32, (tokens, sources * tokens), 1)
    query_pos = place * tokens + lax.broadcasted_iota(jnp.int32, column.shape, 0)
    visible = (column <= query_pos) & (column // BLK == query_pos // BLK)
    visible = jnp.concatenate([visible.astype(jnp.int32)] * GROUP, axis=0) > 0
    ones = jnp.ones((sources * tokens, HD), jnp.bfloat16)
    here, near, far, both = [
        ref[...].astype(jnp.float32).reshape(sources * tokens, HD) for ref in (kv_ref, kv1_ref, kv2_ref, kv3_ref)
    ]
    keys = [jnp.where(odd == 0, here, far), jnp.where(odd == 0, near, both)]
    values = [jnp.where(odd == 0, far, here), jnp.where(odd == 0, both, near)]
    for g in range(KVH):
        k = jnp.where(core == g, keys[0], keys[1]).astype(jnp.bfloat16)
        v = jnp.where(core == g, values[0], values[1]).astype(jnp.bfloat16)
        q = rows_ref[g].astype(jnp.bfloat16)
        s = lax.dot_general(q, k, nt, preferred_element_type=jnp.float32) * scale
        s = jnp.where(visible, s, LOW_SCORE)
        top = jnp.max(s, axis=1, keepdims=True)
        w = jnp.where(visible, jnp.exp2(s - top), 0.0).astype(jnp.bfloat16)
        total_out = jnp.dot(w, jnp.concatenate([v, ones], axis=1), preferred_element_type=jnp.float32)
        total = total_out[:, HD:]
        out_ref[g] = total_out[:, :HD] / total
        lse_ref[g] = top + jnp.log(total) * LOG2E


def project_kernel(per, hist_ref, out_ref, lse_ref, match_ref, first_ref, w_hbm, y_ref, w_ref, sems):
    depth = KVH * HD
    ready = first_ref.shape[0] // depth
    piece = depth // PIECES
    copies = fetch(
        [
            (w_hbm.at[pl.ds(first_ref.shape[0] + i * piece, piece)], w_ref.at[pl.ds(i * piece, piece)])
            for i in range(w_ref.shape[0] // piece)
        ],
        sems,
    )
    tokens = y_ref.shape[0]
    holders = hist_ref.shape[0]
    fold = LANES // per
    row = lax.broadcasted_iota(jnp.int32, (holders, LANES), 0)
    lane = lax.broadcasted_iota(jnp.int32, (holders, LANES), 1)

    def times(heads, weights):
        lhs = jnp.concatenate(heads, axis=1).astype(jnp.bfloat16)
        return jnp.dot(lhs, weights, preferred_element_type=jnp.float32)

    heads = []
    for g in range(KVH):
        outs = hist_ref[:, g, :per, :].reshape(holders * per, HD)
        stats = jnp.sum(hist_ref[:, g, per:, :].astype(jnp.float32), axis=1)
        stats = jnp.where(row % fold == lane // per, stats, 0.0)
        lse = jnp.concatenate(
            [
                jnp.sum(jnp.where(row // fold == m, stats, 0.0), axis=0, keepdims=True)
                for m in range(holders // fold)
            ],
            axis=1,
        )
        match = match_ref[g] > 0.5
        lse = jnp.where(match, lse, LOW_SCORE)
        own = lse_ref[g]
        top = jnp.maximum(jnp.max(lse, axis=1, keepdims=True), own)
        w = jnp.where(match, jnp.exp2(lse - top[:, :1]), 0.0)
        own_w = jnp.exp2(own - top)
        hi = w.astype(jnp.bfloat16)
        low = (w - hi.astype(jnp.float32)).astype(jnp.bfloat16)
        num = (
            jnp.dot(hi, outs, preferred_element_type=jnp.float32)
            + jnp.dot(low, outs, preferred_element_type=jnp.float32)
            + own_w * out_ref[g]
        )
        att = num / (jnp.sum(w, axis=1, keepdims=True) + own_w)
        heads = heads + [att[r * tokens : (r + 1) * tokens] for r in range(GROUP)]
        if g == 0:
            y = times(heads[: ready * KVH], first_ref[...])
    for i in range(w_ref.shape[0] // depth):
        for copy in copies[i * PIECES : (i + 1) * PIECES]:
            copy.wait()
        y = y + times(heads[(ready + i) * KVH : (ready + i + 1) * KVH], w_ref[i * depth : (i + 1) * depth, :])
    y_ref[...] = y.astype(jnp.bfloat16)


VMEM = pl.BlockSpec(memory_space=pltpu.VMEM)
HBM = pl.BlockSpec(memory_space=pltpu.HBM)
ANY = pl.BlockSpec(memory_space=pl.ANY)


def call(kernel, name, out_shape, specs, *operands, outs=None, scratch=(), flops=0, moved=0, limit=16):
    outs = outs or jax.tree.map(lambda _: VMEM, out_shape)
    return pl.pallas_call(
        kernel,
        name=name,
        out_shape=out_shape,
        in_specs=specs,
        out_specs=outs,
        scratch_shapes=scratch,
        cost_estimate=pl.CostEstimate(flops=flops, bytes_accessed=moved, transcendentals=0),
        compiler_params=pltpu.CompilerParams(vmem_limit_bytes=limit << 20),
    )(*operands)


def body(queries, stretch_keys, stretch_values, cache_keys, cache_values, chosen, out_weight):
    devices = lax.axis_size("seq")
    tokens = queries.shape[0]
    cache_rows = cache_keys.shape[0]
    span = BLK // cache_rows
    chips = span // KVH
    key_blocks = cache_rows * devices // BLK
    capacity = (GROUP * TOPK + key_blocks - 1) // key_blocks + 1
    per = capacity * tokens
    f32, bf16 = jnp.float32, jnp.bfloat16
    picks = chosen.transpose(2, 0, 1)

    def partner(bit):
        return [(i, i ^ bit) for i in range(devices)]

    send = call(
        functools.partial(pack_kernel, capacity),
        "pack",
        jax.ShapeDtypeStruct((key_blocks, chips, KVH, per + tokens, HD), bf16),
        [HBM] * 4,
        picks, queries, stretch_keys, stretch_values,
        outs=ANY,
        scratch=[
            pltpu.VMEM(picks.shape, jnp.int32),
            pltpu.VMEM(queries.shape, bf16),
            pltpu.VMEM(stretch_keys.shape, bf16),
            pltpu.VMEM(stretch_values.shape, bf16),
            pltpu.VMEM((KVH, key_blocks, chips, per + tokens, HD), bf16),
            pltpu.SemaphoreType.DMA((4 + KVH,)),
        ],
        limit=60,
    )
    send, cache_keys, cache_values, picks, queries = lax.optimization_barrier(
        (send, cache_keys, cache_values, picks, queries)
    )
    send = send.reshape(devices, per + tokens, HD)
    got = lax.all_to_all(send, "seq", split_axis=0, concat_axis=0, tiled=True)

    core = lax.axis_index("seq") % KVH

    def halves(head):
        return [lax.dynamic_slice_in_dim(x, head * HD, HD, axis=1) for x in (cache_keys, cache_values)]

    k_own, v_own = halves(core)
    k_peer, v_peer = [lax.ppermute(x, "seq", partner(1)) for x in halves(1 - core)]
    holders = devices // KVH
    rows = devices * per
    back, fresh = call(
        functools.partial(attend_kernel, per),
        "attend",
        (
            jax.ShapeDtypeStruct((devices, per + 8, HD), bf16),
            jax.ShapeDtypeStruct((devices, tokens, HD), bf16),
        ),
        [VMEM] * 5,
        got, k_own, v_own, k_peer, v_peer,
        outs=(ANY, VMEM),
        scratch=[
            pltpu.VMEM((devices, per + 8, HD), bf16),
            pltpu.SemaphoreType.DMA((rows // STEP,)),
        ],
        flops=8 * rows * cache_rows * HD,
        moved=4 << 20,
        limit=32,
    )
    back, picks, queries, out_weight = lax.optimization_barrier((back, picks, queries, out_weight))
    hist = lax.all_to_all(back, "seq", split_axis=0, concat_axis=0, tiled=True)

    ready = EARLY * KVH * HD
    match, query_rows, first = call(
        functools.partial(masks_kernel, chips, capacity),
        "masks",
        (
            jax.ShapeDtypeStruct((KVH, GROUP * tokens, holders * per), f32),
            jax.ShapeDtypeStruct((KVH, GROUP * tokens, HD), f32),
            jax.ShapeDtypeStruct((ready, out_weight.shape[1]), bf16),
        ),
        [VMEM, VMEM, HBM],
        picks, queries, out_weight,
        scratch=[pltpu.SemaphoreType.DMA((1,))],
        limit=50,
    )

    far = lax.ppermute(fresh, "seq", partner(2))
    near, both = [lax.ppermute(x, "seq", partner(1)) for x in (fresh, far)]
    part = jax.ShapeDtypeStruct((KVH, GROUP * tokens, HD), f32)
    out, lse = call(
        functools.partial(fresh_kernel, tokens),
        "fresh",
        (part, part),
        [VMEM] * 5,
        query_rows, fresh, near, far, both,
        flops=8 * H * tokens * devices * tokens * HD,
        moved=1 << 20,
    )
    return call(
        functools.partial(project_kernel, per),
        "project",
        jax.ShapeDtypeStruct((tokens, out_weight.shape[1]), bf16),
        [VMEM] * 5 + [HBM],
        hist.reshape(holders, KVH, per + 8, HD), out, lse, match, first, out_weight,
        scratch=[
            pltpu.VMEM((out_weight.shape[0] - ready, out_weight.shape[1]), bf16),
            pltpu.SemaphoreType.DMA(((GROUP - EARLY) * PIECES,)),
        ],
        flops=2 * tokens * out_weight.size,
        moved=out_weight.size * 2,
        limit=50,
    )


def solution(mesh):
    seq = ("grp", "seq")
    return jax.shard_map(
        body,
        mesh=mesh,
        in_specs=(
            P(seq, None),
            P(seq, None),
            P(seq, None),
            P(seq, None),
            P(seq, None),
            P(seq, None, None),
            P(),
        ),
        out_specs=P(seq, None),
        check_vma=False,
    )
```

```python
import functools
import math

import jax
import jax.numpy as jnp
from jax import lax
from jax.experimental import pallas as pl
from jax.experimental.pallas import tpu as pltpu
from jax.sharding import PartitionSpec as P

H = 14
KVH = 2
HD = 128
BLK = 4096
TOPK = 3
GROUP = H // KVH

LOW_SCORE = -1e30
LOG2E = math.log2(math.e)
LANES = 128
EARLY = 3
STEP = 256


def head_rows(q_ref, g):
    q = q_ref[...].astype(jnp.float32)
    return [q[:, h * HD : (h + 1) * HD] for h in range(g * GROUP, (g + 1) * GROUP)]


def slot_match(chosen_ref, g, block, slot, token):
    rows = lax.broadcasted_iota(jnp.int32, block.shape, 0)
    same_token = token == rows
    seen = jnp.zeros(block.shape, jnp.int32)
    found = []
    for h in range(g * GROUP, (g + 1) * GROUP):
        picked = block == chosen_ref[0, :, h : h + 1]
        for t in range(1, TOPK):
            picked = picked | (block == chosen_ref[t, :, h : h + 1])
        found.append(jnp.where(picked & same_token & (seen == slot), 1.0, 0.0))
        seen = seen + picked.astype(jnp.int32)
    return found


def fetch(pairs, sems):
    copies = [pltpu.make_async_copy(src, dst, sems.at[i]) for i, (src, dst) in enumerate(pairs)]
    for copy in copies:
        copy.start()
    return copies


def pack_kernel(capacity, chosen_hbm, q_hbm, k_hbm, v_hbm, send_hbm, chosen_ref, q_ref, k_ref, v_ref, send_ref, sems):
    copies = fetch([(chosen_hbm, chosen_ref), (q_hbm, q_ref), (k_hbm, k_ref), (v_hbm, v_ref)], sems)
    tokens = q_ref.shape[0]
    per = capacity * tokens
    key_blocks, chips = send_ref.shape[1:3]
    lane = lax.broadcasted_iota(jnp.int32, (tokens, key_blocks * per), 1)
    block, slot, token = lane // per, lane % per // tokens, lane % tokens
    copies[0].wait()
    spread = [
        jnp.concatenate(
            slot_match(chosen_ref, g, block, slot, token) + [jnp.zeros(lane.shape, jnp.float32)], axis=0
        ).T.astype(jnp.bfloat16)
        for g in range(KVH)
    ]
    for copy in copies[1:]:
        copy.wait()
    sent = []
    for g in range(KVH):
        rows = head_rows(q_ref, g)
        rows = jnp.concatenate(rows + [jnp.zeros_like(rows[0])], axis=0).astype(jnp.bfloat16)
        slots = jnp.dot(spread[g], rows, preferred_element_type=jnp.float32).astype(jnp.bfloat16)
        cols = slice(g * HD, (g + 1) * HD)
        fresh = [k_ref[:, cols], v_ref[:, cols]]
        for b in range(key_blocks):
            for chip in range(chips):
                send_ref[g, b, chip, :per, :] = slots[b * per : (b + 1) * per]
                send_ref[g, b, chip, per:, :] = fresh[chip % 2]
        sent.append(pltpu.make_async_copy(send_ref.at[g], send_hbm.at[:, :, g], sems.at[4 + g]))
        sent[g].start()
    for copy in sent:
        copy.wait()


def masks_kernel(chips, capacity, chosen_ref, q_ref, w_hbm, match_ref, rows_ref, w_ref, sems):
    copies = fetch([(w_hbm.at[: w_ref.shape[0]], w_ref)], sems)
    tokens = q_ref.shape[0]
    per = capacity * tokens
    lane = lax.broadcasted_iota(jnp.int32, (tokens, match_ref.shape[2]), 1)
    block, slot, token = lane // (per * chips), lane % per // tokens, lane % tokens
    for g in range(KVH):
        match_ref[g] = jnp.concatenate(slot_match(chosen_ref, g, block, slot, token), axis=0)
        rows_ref[g] = jnp.concatenate(head_rows(q_ref, g), axis=0)
    for copy in copies:
        copy.wait()


def attend_kernel(per, q_ref, ka_ref, va_ref, kb_ref, vb_ref, out_hbm, fresh_ref, out_ref, sems):
    sources = q_ref.shape[0]
    step = STEP // per
    fold = LANES // per
    group = lax.axis_index("seq") // KVH % fold
    scale = LOG2E * HD**-0.5
    nt = (((1,), (1,)), ((), ()))
    piece = lax.broadcasted_iota(jnp.int32, (8, LANES), 0)
    ones = jnp.ones((16, va_ref.shape[1]), jnp.bfloat16)
    fresh_ref[...] = q_ref[:, per:, :]
    sent = []

    def scores(first):
        q = q_ref[first : first + step, :per, :].reshape(STEP, HD)
        return [
            lax.dot_general(k_ref[...], q, nt, preferred_element_type=jnp.float32) for k_ref in (ka_ref, kb_ref)
        ]

    ahead = scores(0)
    for first in range(0, sources, step):
        sa, sb = ahead
        if first + step < sources:
            ahead = scores(first + step)
        top = scale * jnp.maximum(jnp.max(sa, axis=0, keepdims=True), jnp.max(sb, axis=0, keepdims=True))
        wa = jnp.exp2(sa * scale - top).astype(jnp.bfloat16)
        wb = jnp.exp2(sb * scale - top).astype(jnp.bfloat16)
        both = jnp.dot(
            jnp.concatenate([va_ref[...], ones], axis=0), wa, preferred_element_type=jnp.float32
        ) + jnp.dot(jnp.concatenate([vb_ref[...], ones], axis=0), wb, preferred_element_type=jnp.float32)
        total = both[HD : HD + 1]
        out = (both[:HD] / total).T.astype(jnp.bfloat16)
        lse = top + jnp.log(total) * LOG2E
        hi = lse.astype(jnp.bfloat16).astype(jnp.float32)
        mid = (lse - hi).astype(jnp.bfloat16).astype(jnp.float32)
        low = lse - hi - mid
        for s in range(step):
            out_ref[first + s, :per, :] = out[s * per : (s + 1) * per]
        for t in range(step // fold):
            lanes = slice(t * LANES, (t + 1) * LANES)
            parts = jnp.where(
                piece == 0, hi[:, lanes], jnp.where(piece == 1, mid[:, lanes], jnp.where(piece == 2, low[:, lanes], 0.0))
            )
            for i in range(fold):
                turned = pltpu.roll(parts, lax.rem(group - i + fold, fold) * per, 1)
                out_ref[first + t * fold + i, per:, :] = turned.astype(jnp.bfloat16)
        done = pl.ds(first, step)
        sent.append(pltpu.make_async_copy(out_ref.at[done], out_hbm.at[done], sems.at[first // step]))
        sent[-1].start()
    for copy in sent:
        copy.wait()


def fresh_kernel(tokens, rows_ref, kv_ref, kv1_ref, kv2_ref, kv3_ref, out_ref, lse_ref):
    sources = kv_ref.shape[0]
    place = lax.axis_index("seq")
    core, odd = place % KVH, place // KVH % 2
    scale = LOG2E * HD**-0.5
    nt = (((1,), (1,)), ((), ()))
    column = lax.broadcasted_iota(jnp.int32, (tokens, sources * tokens), 1)
    query_pos = place * tokens + lax.broadcasted_iota(jnp.int32, column.shape, 0)
    visible = (column <= query_pos) & (column // BLK == query_pos // BLK)
    visible = jnp.concatenate([visible.astype(jnp.int32)] * GROUP, axis=0) > 0
    ones = jnp.ones((sources * tokens, HD), jnp.bfloat16)
    here, near, far, both = [
        ref[...].astype(jnp.float32).reshape(sources * tokens, HD) for ref in (kv_ref, kv1_ref, kv2_ref, kv3_ref)
    ]
    keys = [jnp.where(odd == 0, here, far), jnp.where(odd == 0, near, both)]
    values = [jnp.where(odd == 0, far, here), jnp.where(odd == 0, both, near)]
    for g in range(KVH):
        k = jnp.where(core == g, keys[0], keys[1]).astype(jnp.bfloat16)
        v = jnp.where(core == g, values[0], values[1]).astype(jnp.bfloat16)
        q = rows_ref[g].astype(jnp.bfloat16)
        s = lax.dot_general(q, k, nt, preferred_element_type=jnp.float32) * scale
        s = jnp.where(visible, s, LOW_SCORE)
        top = jnp.max(s, axis=1, keepdims=True)
        w = jnp.where(visible, jnp.exp2(s - top), 0.0).astype(jnp.bfloat16)
        total_out = jnp.dot(w, jnp.concatenate([v, ones], axis=1), preferred_element_type=jnp.float32)
        total = total_out[:, HD:]
        out_ref[g] = total_out[:, :HD] / total
        lse_ref[g] = top + jnp.log(total) * LOG2E


def project_kernel(per, hist_ref, out_ref, lse_ref, match_ref, first_ref, w_hbm, y_ref, w_ref, sems):
    depth = KVH * HD
    ready = first_ref.shape[0] // depth
    copies = fetch(
        [
            (w_hbm.at[pl.ds((ready + i) * depth, depth)], w_ref.at[pl.ds(i * depth, depth)])
            for i in range(w_ref.shape[0] // depth)
        ],
        sems,
    )
    tokens = y_ref.shape[0]
    holders = hist_ref.shape[0]
    fold = LANES // per
    row = lax.broadcasted_iota(jnp.int32, (holders, LANES), 0)
    lane = lax.broadcasted_iota(jnp.int32, (holders, LANES), 1)

    def times(heads, weights):
        lhs = jnp.concatenate(heads, axis=1).astype(jnp.bfloat16)
        return jnp.dot(lhs, weights, preferred_element_type=jnp.float32)

    heads = []
    for g in range(KVH):
        outs = hist_ref[:, g, :per, :].reshape(holders * per, HD)
        stats = jnp.sum(hist_ref[:, g, per:, :].astype(jnp.float32), axis=1)
        stats = jnp.where(row % fold == lane // per, stats, 0.0)
        lse = jnp.concatenate(
            [
                jnp.sum(jnp.where(row // fold == m, stats, 0.0), axis=0, keepdims=True)
                for m in range(holders // fold)
            ],
            axis=1,
        )
        match = match_ref[g] > 0.5
        lse = jnp.where(match, lse, LOW_SCORE)
        own = lse_ref[g]
        top = jnp.maximum(jnp.max(lse, axis=1, keepdims=True), own)
        w = jnp.where(match, jnp.exp2(lse - top[:, :1]), 0.0)
        own_w = jnp.exp2(own - top)
        hi = w.astype(jnp.bfloat16)
        low = (w - hi.astype(jnp.float32)).astype(jnp.bfloat16)
        num = (
            jnp.dot(hi, outs, preferred_element_type=jnp.float32)
            + jnp.dot(low, outs, preferred_element_type=jnp.float32)
            + own_w * out_ref[g]
        )
        att = num / (jnp.sum(w, axis=1, keepdims=True) + own_w)
        heads = heads + [att[r * tokens : (r + 1) * tokens] for r in range(GROUP)]
        if g == 0:
            y = times(heads[: ready * KVH], first_ref[...])
    for i, copy in enumerate(copies):
        copy.wait()
        y = y + times(heads[(ready + i) * KVH : (ready + i + 1) * KVH], w_ref[i * depth : (i + 1) * depth, :])
    y_ref[...] = y.astype(jnp.bfloat16)


VMEM = pl.BlockSpec(memory_space=pltpu.VMEM)
HBM = pl.BlockSpec(memory_space=pltpu.HBM)
ANY = pl.BlockSpec(memory_space=pl.ANY)


def call(kernel, name, out_shape, specs, *operands, outs=None, scratch=(), flops=0, moved=0, limit=16):
    outs = outs or jax.tree.map(lambda _: VMEM, out_shape)
    return pl.pallas_call(
        kernel,
        name=name,
        out_shape=out_shape,
        in_specs=specs,
        out_specs=outs,
        scratch_shapes=scratch,
        cost_estimate=pl.CostEstimate(flops=flops, bytes_accessed=moved, transcendentals=0),
        compiler_params=pltpu.CompilerParams(vmem_limit_bytes=limit << 20),
    )(*operands)


def body(queries, stretch_keys, stretch_values, cache_keys, cache_values, chosen, out_weight):
    devices = lax.axis_size("seq")
    tokens = queries.shape[0]
    cache_rows = cache_keys.shape[0]
    span = BLK // cache_rows
    chips = span // KVH
    key_blocks = cache_rows * devices // BLK
    capacity = (GROUP * TOPK + key_blocks - 1) // key_blocks + 1
    per = capacity * tokens
    f32, bf16 = jnp.float32, jnp.bfloat16
    picks = chosen.transpose(2, 0, 1)

    def partner(bit):
        return [(i, i ^ bit) for i in range(devices)]

    send = call(
        functools.partial(pack_kernel, capacity),
        "pack",
        jax.ShapeDtypeStruct((key_blocks, chips, KVH, per + tokens, HD), bf16),
        [HBM] * 4,
        picks, queries, stretch_keys, stretch_values,
        outs=ANY,
        scratch=[
            pltpu.VMEM(picks.shape, jnp.int32),
            pltpu.VMEM(queries.shape, bf16),
            pltpu.VMEM(stretch_keys.shape, bf16),
            pltpu.VMEM(stretch_values.shape, bf16),
            pltpu.VMEM((KVH, key_blocks, chips, per + tokens, HD), bf16),
            pltpu.SemaphoreType.DMA((4 + KVH,)),
        ],
        limit=60,
    )
    send, cache_keys, cache_values, picks, queries = lax.optimization_barrier(
        (send, cache_keys, cache_values, picks, queries)
    )
    send = send.reshape(devices, per + tokens, HD)
    got = lax.all_to_all(send, "seq", split_axis=0, concat_axis=0, tiled=True)

    core = lax.axis_index("seq") % KVH

    def halves(head):
        keys, values = [lax.dynamic_slice_in_dim(x, head * HD, HD, axis=1) for x in (cache_keys, cache_values)]
        return keys, values.T

    k_own, v_own = halves(core)
    k_peer, v_peer = [lax.ppermute(x, "seq", partner(1)) for x in halves(1 - core)]
    holders = devices // KVH
    rows = devices * per
    back, fresh = call(
        functools.partial(attend_kernel, per),
        "attend",
        (
            jax.ShapeDtypeStruct((devices, per + 8, HD), bf16),
            jax.ShapeDtypeStruct((devices, tokens, HD), bf16),
        ),
        [VMEM] * 5,
        got, k_own, v_own, k_peer, v_peer,
        outs=(ANY, VMEM),
        scratch=[
            pltpu.VMEM((devices, per + 8, HD), bf16),
            pltpu.SemaphoreType.DMA((rows // STEP,)),
        ],
        flops=8 * rows * cache_rows * HD,
        moved=4 << 20,
        limit=32,
    )
    back, picks, queries, out_weight = lax.optimization_barrier((back, picks, queries, out_weight))
    hist = lax.all_to_all(back, "seq", split_axis=0, concat_axis=0, tiled=True)

    ready = EARLY * KVH * HD
    match, query_rows, first = call(
        functools.partial(masks_kernel, chips, capacity),
        "masks",
        (
            jax.ShapeDtypeStruct((KVH, GROUP * tokens, holders * per), f32),
            jax.ShapeDtypeStruct((KVH, GROUP * tokens, HD), f32),
            jax.ShapeDtypeStruct((ready, out_weight.shape[1]), bf16),
        ),
        [VMEM, VMEM, HBM],
        picks, queries, out_weight,
        scratch=[pltpu.SemaphoreType.DMA((1,))],
        limit=50,
    )

    far = lax.ppermute(fresh, "seq", partner(2))
    near, both = [lax.ppermute(x, "seq", partner(1)) for x in (fresh, far)]
    part = jax.ShapeDtypeStruct((KVH, GROUP * tokens, HD), f32)
    out, lse = call(
        functools.partial(fresh_kernel, tokens),
        "fresh",
        (part, part),
        [VMEM] * 5,
        query_rows, fresh, near, far, both,
        flops=8 * H * tokens * devices * tokens * HD,
        moved=1 << 20,
    )
    return call(
        functools.partial(project_kernel, per),
        "project",
        jax.ShapeDtypeStruct((tokens, out_weight.shape[1]), bf16),
        [VMEM] * 5 + [HBM],
        hist.reshape(holders, KVH, per + 8, HD), out, lse, match, first, out_weight,
        scratch=[
            pltpu.VMEM((out_weight.shape[0] - ready, out_weight.shape[1]), bf16),
            pltpu.SemaphoreType.DMA((GROUP - EARLY,)),
        ],
        flops=2 * tokens * out_weight.size,
        moved=out_weight.size * 2,
        limit=50,
    )


def solution(mesh):
    seq = ("grp", "seq")
    return jax.shard_map(
        body,
        mesh=mesh,
        in_specs=(
            P(seq, None),
            P(seq, None),
            P(seq, None),
            P(seq, None),
            P(seq, None),
            P(seq, None, None),
            P(),
        ),
        out_specs=P(seq, None),
        check_vma=False,
    )
```

```python
import functools
import math

import jax
import jax.numpy as jnp
from jax import lax
from jax.experimental import pallas as pl
from jax.experimental.pallas import tpu as pltpu
from jax.sharding import PartitionSpec as P

H = 14
KVH = 2
HD = 128
BLK = 4096
TOPK = 3
GROUP = H // KVH

LOW_SCORE = -1e30
LOG2E = math.log2(math.e)
LANES = 128
EARLY = 3
STEP = 256


def mirrored(index, count):
    bits = count.bit_length() - 1
    return sum(((index >> i) & 1) << (bits - 1 - i) for i in range(bits))


def head_rows(q_ref, g):
    q = q_ref[...].astype(jnp.float32)
    return [q[:, h * HD : (h + 1) * HD] for h in range(g * GROUP, (g + 1) * GROUP)]


def slot_match(chosen_ref, g, block, slot, token):
    rows = lax.broadcasted_iota(jnp.int32, block.shape, 0)
    same_token = token == rows
    seen = jnp.zeros(block.shape, jnp.int32)
    found = []
    for h in range(g * GROUP, (g + 1) * GROUP):
        picked = block == chosen_ref[0, :, h : h + 1]
        for t in range(1, TOPK):
            picked = picked | (block == chosen_ref[t, :, h : h + 1])
        found.append(jnp.where(picked & same_token & (seen == slot), 1.0, 0.0))
        seen = seen + picked.astype(jnp.int32)
    return found


def fetch(pairs, sems):
    copies = [pltpu.make_async_copy(src, dst, sems.at[i]) for i, (src, dst) in enumerate(pairs)]
    for copy in copies:
        copy.start()
    return copies


def pack_kernel(chips, capacity, chosen_hbm, q_hbm, k_hbm, v_hbm, send_hbm, chosen_ref, q_ref, k_ref, v_ref, send_ref, sems):
    copies = fetch([(chosen_hbm, chosen_ref), (q_hbm, q_ref), (k_hbm, k_ref), (v_hbm, v_ref)], sems)
    tokens = q_ref.shape[0]
    per = capacity * tokens
    devices = send_ref.shape[0]
    key_blocks = devices // (chips * KVH)
    half = devices // KVH
    lane = lax.broadcasted_iota(jnp.int32, (tokens, key_blocks * per), 1)
    block, slot, token = lane // per, lane % per // tokens, lane % tokens
    copies[0].wait()
    spread = [
        jnp.concatenate(
            slot_match(chosen_ref, g, block, slot, token) + [jnp.zeros(lane.shape, jnp.float32)], axis=0
        ).T.astype(jnp.bfloat16)
        for g in range(KVH)
    ]
    for copy in copies[1:]:
        copy.wait()
    sent = []
    for g in range(KVH):
        rows = head_rows(q_ref, g)
        rows = jnp.concatenate(rows + [jnp.zeros_like(rows[0])], axis=0).astype(jnp.bfloat16)
        slots = jnp.dot(spread[g], rows, preferred_element_type=jnp.float32).astype(jnp.bfloat16)
        cols = slice(g * HD, (g + 1) * HD)
        fresh = [k_ref[:, cols], v_ref[:, cols]]
        for b in range(key_blocks):
            for chip in range(chips):
                to = mirrored((b * chips + chip) * KVH + g, devices)
                send_ref[to, :per, :] = slots[b * per : (b + 1) * per]
                send_ref[to, per:, :] = fresh[chip % 2]
        done = pl.ds(g * half, half)
        sent.append(pltpu.make_async_copy(send_ref.at[done], send_hbm.at[done], sems.at[4 + g]))
        sent[g].start()
    for copy in sent:
        copy.wait()


def masks_kernel(chips, capacity, chosen_ref, q_ref, w_hbm, match_ref, rows_ref, w_ref, sems):
    copies = fetch([(w_hbm.at[: w_ref.shape[0]], w_ref)], sems)
    tokens = q_ref.shape[0]
    per = capacity * tokens
    lane = lax.broadcasted_iota(jnp.int32, (tokens, match_ref.shape[2]), 1)
    holder = mirrored(lane // per, match_ref.shape[2] // per)
    block, slot, token = holder // chips, lane % per // tokens, lane % tokens
    for g in range(KVH):
        match_ref[g] = jnp.concatenate(slot_match(chosen_ref, g, block, slot, token), axis=0)
        rows_ref[g] = jnp.concatenate(head_rows(q_ref, g), axis=0)
    for copy in copies:
        copy.wait()


def attend_kernel(per, q_ref, ka_ref, va_ref, kb_ref, vb_ref, out_hbm, fresh_ref, out_ref, sems):
    sources = q_ref.shape[0]
    sent = []
    step = STEP // per
    scale = LOG2E * HD**-0.5
    nt = (((1,), (1,)), ((), ()))
    row = lax.broadcasted_iota(jnp.int32, (per, LANES), 0)
    lane = lax.broadcasted_iota(jnp.int32, (per, LANES), 1)
    diagonal = row == lane % per
    piece = lax.broadcasted_iota(jnp.int32, (8, LANES), 0)
    ones = jnp.ones(va_ref.shape, jnp.bfloat16)
    fresh_ref[...] = q_ref[:, per:, :]

    def scores(first):
        q = q_ref[first : first + step, :per, :].reshape(step * per, HD)
        return [
            lax.dot_general(q, k_ref[...], nt, preferred_element_type=jnp.float32) for k_ref in (ka_ref, kb_ref)
        ]

    ahead = scores(0)
    for first in range(0, sources, step):
        sa, sb = ahead
        if first + step < sources:
            ahead = scores(first + step)
        top = scale * jnp.maximum(jnp.max(sa, axis=1, keepdims=True), jnp.max(sb, axis=1, keepdims=True))
        wa = jnp.exp2(sa * scale - top).astype(jnp.bfloat16)
        wb = jnp.exp2(sb * scale - top).astype(jnp.bfloat16)
        both = jnp.dot(
            wa, jnp.concatenate([va_ref[...], ones], axis=1), preferred_element_type=jnp.float32
        ) + jnp.dot(wb, jnp.concatenate([vb_ref[...], ones], axis=1), preferred_element_type=jnp.float32)
        total = both[:, HD:]
        out = (both[:, :HD] / total).astype(jnp.bfloat16)
        lse = top + jnp.log(total) * LOG2E
        for s in range(step):
            part = slice(s * per, (s + 1) * per)
            out_ref[first + s, :per, :] = out[part]
            flat = jnp.sum(jnp.where(diagonal, lse[part], 0.0), axis=0, keepdims=True)
            hi = flat.astype(jnp.bfloat16).astype(jnp.float32)
            mid = (flat - hi).astype(jnp.bfloat16).astype(jnp.float32)
            low = flat - hi - mid
            out_ref[first + s, per:, :] = jnp.where(
                piece == 0, hi, jnp.where(piece == 1, mid, jnp.where(piece == 2, low, 0.0))
            ).astype(jnp.bfloat16)
        done = pl.ds(first, step)
        sent.append(pltpu.make_async_copy(out_ref.at[done], out_hbm.at[done], sems.at[first // step]))
        sent[-1].start()
    for copy in sent:
        copy.wait()


def fresh_kernel(tokens, rows_ref, kv_ref, kv1_ref, kv2_ref, kv3_ref, out_ref, lse_ref):
    sources = kv_ref.shape[0]
    place = lax.axis_index("seq")
    core, odd = place % KVH, place // KVH % 2
    scale = LOG2E * HD**-0.5
    nt = (((1,), (1,)), ((), ()))
    column = lax.broadcasted_iota(jnp.int32, (tokens, sources * tokens), 1)
    query_pos = place * tokens + lax.broadcasted_iota(jnp.int32, column.shape, 0)
    key_pos = mirrored(column // tokens, sources) * tokens + column % tokens
    visible = (key_pos <= query_pos) & (key_pos // BLK == query_pos // BLK)
    visible = jnp.concatenate([visible.astype(jnp.int32)] * GROUP, axis=0) > 0
    ones = jnp.ones((sources * tokens, HD), jnp.bfloat16)
    here, near, far, both = [
        ref[...].astype(jnp.float32).reshape(sources * tokens, HD) for ref in (kv_ref, kv1_ref, kv2_ref, kv3_ref)
    ]
    keys = [jnp.where(odd == 0, here, far), jnp.where(odd == 0, near, both)]
    values = [jnp.where(odd == 0, far, here), jnp.where(odd == 0, both, near)]
    for g in range(KVH):
        k = jnp.where(core == g, keys[0], keys[1]).astype(jnp.bfloat16)
        v = jnp.where(core == g, values[0], values[1]).astype(jnp.bfloat16)
        q = rows_ref[g].astype(jnp.bfloat16)
        s = lax.dot_general(q, k, nt, preferred_element_type=jnp.float32) * scale
        s = jnp.where(visible, s, LOW_SCORE)
        top = jnp.max(s, axis=1, keepdims=True)
        w = jnp.where(visible, jnp.exp2(s - top), 0.0).astype(jnp.bfloat16)
        total_out = jnp.dot(w, jnp.concatenate([v, ones], axis=1), preferred_element_type=jnp.float32)
        total = total_out[:, HD:]
        out_ref[g] = total_out[:, :HD] / total
        lse_ref[g] = top + jnp.log(total) * LOG2E


def project_kernel(per, hist_ref, out_ref, lse_ref, match_ref, first_ref, w_hbm, y_ref, w_ref, sems):
    depth = KVH * HD
    ready = first_ref.shape[0] // depth
    copies = fetch(
        [
            (w_hbm.at[pl.ds((ready + i) * depth, depth)], w_ref.at[pl.ds(i * depth, depth)])
            for i in range(w_ref.shape[0] // depth)
        ],
        sems,
    )
    tokens = y_ref.shape[0]
    holders = hist_ref.shape[1]
    fold = LANES // per
    row = lax.broadcasted_iota(jnp.int32, (holders, LANES), 0)
    lane = lax.broadcasted_iota(jnp.int32, (holders, LANES), 1)

    def times(heads, weights):
        lhs = jnp.concatenate(heads, axis=1).astype(jnp.bfloat16)
        return jnp.dot(lhs, weights, preferred_element_type=jnp.float32)

    heads = []
    for g in range(KVH):
        outs = hist_ref[g, :, :per, :].reshape(holders * per, HD)
        stats = jnp.sum(hist_ref[g, :, per:, :].astype(jnp.float32), axis=1)
        stats = jnp.where(row % fold == lane // per, stats, 0.0)
        lse = jnp.concatenate(
            [
                jnp.sum(jnp.where(row // fold == m, stats, 0.0), axis=0, keepdims=True)
                for m in range(holders // fold)
            ],
            axis=1,
        )
        match = match_ref[g] > 0.5
        lse = jnp.where(match, lse, LOW_SCORE)
        own = lse_ref[g]
        top = jnp.maximum(jnp.max(lse, axis=1, keepdims=True), own)
        w = jnp.where(match, jnp.exp2(lse - top[:, :1]), 0.0)
        own_w = jnp.exp2(own - top)
        hi = w.astype(jnp.bfloat16)
        low = (w - hi.astype(jnp.float32)).astype(jnp.bfloat16)
        num = (
            jnp.dot(hi, outs, preferred_element_type=jnp.float32)
            + jnp.dot(low, outs, preferred_element_type=jnp.float32)
            + own_w * out_ref[g]
        )
        att = num / (jnp.sum(w, axis=1, keepdims=True) + own_w)
        heads = heads + [att[r * tokens : (r + 1) * tokens] for r in range(GROUP)]
        if g == 0:
            y = times(heads[: ready * KVH], first_ref[...])
    for i, copy in enumerate(copies):
        copy.wait()
        y = y + times(heads[(ready + i) * KVH : (ready + i + 1) * KVH], w_ref[i * depth : (i + 1) * depth, :])
    y_ref[...] = y.astype(jnp.bfloat16)


VMEM = pl.BlockSpec(memory_space=pltpu.VMEM)
HBM = pl.BlockSpec(memory_space=pltpu.HBM)
ANY = pl.BlockSpec(memory_space=pl.ANY)


def call(kernel, name, out_shape, specs, *operands, outs=None, scratch=(), flops=0, moved=0, limit=16):
    outs = outs or jax.tree.map(lambda _: VMEM, out_shape)
    return pl.pallas_call(
        kernel,
        name=name,
        out_shape=out_shape,
        in_specs=specs,
        out_specs=outs,
        scratch_shapes=scratch,
        cost_estimate=pl.CostEstimate(flops=flops, bytes_accessed=moved, transcendentals=0),
        compiler_params=pltpu.CompilerParams(vmem_limit_bytes=limit << 20),
    )(*operands)


def body(queries, stretch_keys, stretch_values, cache_keys, cache_values, chosen, out_weight):
    devices = lax.axis_size("seq")
    tokens = queries.shape[0]
    cache_rows = cache_keys.shape[0]
    span = BLK // cache_rows
    chips = span // KVH
    key_blocks = cache_rows * devices // BLK
    capacity = (GROUP * TOPK + key_blocks - 1) // key_blocks + 1
    per = capacity * tokens
    f32, bf16 = jnp.float32, jnp.bfloat16
    picks = chosen.transpose(2, 0, 1)

    def partner(bit):
        return [(i, i ^ bit) for i in range(devices)]

    send = call(
        functools.partial(pack_kernel, chips, capacity),
        "pack",
        jax.ShapeDtypeStruct((devices, per + tokens, HD), bf16),
        [HBM] * 4,
        picks, queries, stretch_keys, stretch_values,
        outs=ANY,
        scratch=[
            pltpu.VMEM(picks.shape, jnp.int32),
            pltpu.VMEM(queries.shape, bf16),
            pltpu.VMEM(stretch_keys.shape, bf16),
            pltpu.VMEM(stretch_values.shape, bf16),
            pltpu.VMEM((devices, per + tokens, HD), bf16),
            pltpu.SemaphoreType.DMA((4 + KVH,)),
        ],
        limit=60,
    )
    send, cache_keys, cache_values, picks, queries = lax.optimization_barrier(
        (send, cache_keys, cache_values, picks, queries)
    )

    def exchange(x):
        ranks = [mirrored(i, devices) for i in range(devices)]
        return lax.all_to_all(x, "seq", split_axis=0, concat_axis=0, axis_index_groups=[ranks], tiled=True)

    got = exchange(send)

    core = lax.axis_index("seq") % KVH

    def halves(head):
        return [lax.dynamic_slice_in_dim(x, head * HD, HD, axis=1) for x in (cache_keys, cache_values)]

    k_own, v_own = halves(core)
    k_peer, v_peer = [lax.ppermute(x, "seq", partner(1)) for x in halves(1 - core)]
    holders = devices // KVH
    rows = devices * per
    back, fresh = call(
        functools.partial(attend_kernel, per),
        "attend",
        (
            jax.ShapeDtypeStruct((devices, per + 8, HD), bf16),
            jax.ShapeDtypeStruct((devices, tokens, HD), bf16),
        ),
        [VMEM] * 5,
        got, k_own, v_own, k_peer, v_peer,
        outs=(ANY, VMEM),
        scratch=[
            pltpu.VMEM((devices, per + 8, HD), bf16),
            pltpu.SemaphoreType.DMA((rows // STEP,)),
        ],
        flops=8 * rows * cache_rows * HD,
        moved=4 << 20,
        limit=32,
    )
    back, picks, queries, out_weight = lax.optimization_barrier((back, picks, queries, out_weight))
    hist = exchange(back)

    ready = EARLY * KVH * HD
    match, query_rows, first = call(
        functools.partial(masks_kernel, chips, capacity),
        "masks",
        (
            jax.ShapeDtypeStruct((KVH, GROUP * tokens, holders * per), f32),
            jax.ShapeDtypeStruct((KVH, GROUP * tokens, HD), f32),
            jax.ShapeDtypeStruct((ready, out_weight.shape[1]), bf16),
        ),
        [VMEM, VMEM, HBM],
        picks, queries, out_weight,
        scratch=[pltpu.SemaphoreType.DMA((1,))],
        limit=50,
    )

    far = lax.ppermute(fresh, "seq", partner(2))
    near, both = [lax.ppermute(x, "seq", partner(1)) for x in (fresh, far)]
    part = jax.ShapeDtypeStruct((KVH, GROUP * tokens, HD), f32)
    out, lse = call(
        functools.partial(fresh_kernel, tokens),
        "fresh",
        (part, part),
        [VMEM] * 5,
        query_rows, fresh, near, far, both,
        flops=8 * H * tokens * devices * tokens * HD,
        moved=1 << 20,
    )
    return call(
        functools.partial(project_kernel, per),
        "project",
        jax.ShapeDtypeStruct((tokens, out_weight.shape[1]), bf16),
        [VMEM] * 5 + [HBM],
        hist.reshape(KVH, holders, per + 8, HD), out, lse, match, first, out_weight,
        scratch=[
            pltpu.VMEM((out_weight.shape[0] - ready, out_weight.shape[1]), bf16),
            pltpu.SemaphoreType.DMA((GROUP - EARLY,)),
        ],
        flops=2 * tokens * out_weight.size,
        moved=out_weight.size * 2,
        limit=50,
    )


def solution(mesh):
    seq = ("grp", "seq")
    return jax.shard_map(
        body,
        mesh=mesh,
        in_specs=(
            P(seq, None),
            P(seq, None),
            P(seq, None),
            P(seq, None),
            P(seq, None),
            P(seq, None, None),
            P(),
        ),
        out_specs=P(seq, None),
        check_vma=False,
    )
```

```python
import functools
import math

import jax
import jax.numpy as jnp
from jax import lax
from jax.experimental import pallas as pl
from jax.experimental.pallas import tpu as pltpu
from jax.sharding import PartitionSpec as P

H = 14
KVH = 2
HD = 128
BLK = 4096
TOPK = 3
GROUP = H // KVH

LOW_SCORE = -1e30
LOG2E = math.log2(math.e)
LANES = 128
EARLY = 3
STEP = 256


def head_rows(q_ref, g):
    q = q_ref[...].astype(jnp.float32)
    return [q[:, h * HD : (h + 1) * HD] for h in range(g * GROUP, (g + 1) * GROUP)]


def slot_match(chosen_ref, g, block, slot, token):
    rows = lax.broadcasted_iota(jnp.int32, block.shape, 0)
    same_token = token == rows
    seen = jnp.zeros(block.shape, jnp.int32)
    found = []
    for h in range(g * GROUP, (g + 1) * GROUP):
        picked = block == chosen_ref[0, :, h : h + 1]
        for t in range(1, TOPK):
            picked = picked | (block == chosen_ref[t, :, h : h + 1])
        found.append(jnp.where(picked & same_token & (seen == slot), 1.0, 0.0))
        seen = seen + picked.astype(jnp.int32)
    return found


def fetch(pairs, sems):
    copies = [pltpu.make_async_copy(src, dst, sems.at[i]) for i, (src, dst) in enumerate(pairs)]
    for copy in copies:
        copy.start()
    return copies


def pack_kernel(capacity, chosen_hbm, q_hbm, send_hbm, chosen_ref, q_ref, send_ref, sems):
    copies = fetch([(chosen_hbm, chosen_ref), (q_hbm, q_ref)], sems)
    tokens = q_ref.shape[0]
    per = capacity * tokens
    key_blocks = send_ref.shape[1]
    chips = send_hbm.shape[1]
    lane = lax.broadcasted_iota(jnp.int32, (tokens, key_blocks * per), 1)
    block, slot, token = lane // per, lane % per // tokens, lane % tokens
    copies[0].wait()
    spread = [
        jnp.concatenate(
            slot_match(chosen_ref, g, block, slot, token) + [jnp.zeros(lane.shape, jnp.float32)], axis=0
        ).T.astype(jnp.bfloat16)
        for g in range(KVH)
    ]
    copies[1].wait()
    sent = []
    for g in range(KVH):
        rows = head_rows(q_ref, g)
        rows = jnp.concatenate(rows + [jnp.zeros_like(rows[0])], axis=0).astype(jnp.bfloat16)
        slots = jnp.dot(spread[g], rows, preferred_element_type=jnp.float32).astype(jnp.bfloat16)
        send_ref[g] = slots.reshape(key_blocks, per, HD)
        for chip in range(chips):
            sent.append(pltpu.make_async_copy(send_ref.at[g], send_hbm.at[:, chip, g], sems.at[2 + len(sent)]))
            sent[-1].start()
    for copy in sent:
        copy.wait()


def masks_kernel(chips, capacity, chosen_ref, q_ref, w_hbm, match_ref, rows_ref, w_ref, sems):
    copies = fetch([(w_hbm.at[: w_ref.shape[0]], w_ref)], sems)
    tokens = q_ref.shape[0]
    per = capacity * tokens
    lane = lax.broadcasted_iota(jnp.int32, (tokens, match_ref.shape[2]), 1)
    block, slot, token = lane // (per * chips), lane % per // tokens, lane % tokens
    for g in range(KVH):
        match_ref[g] = jnp.concatenate(slot_match(chosen_ref, g, block, slot, token), axis=0)
        rows_ref[g] = jnp.concatenate(head_rows(q_ref, g), axis=0)
    for copy in copies:
        copy.wait()


def attend_kernel(q_ref, ka_ref, va_ref, kb_ref, vb_ref, out_hbm, out_ref, sems):
    sources, per = q_ref.shape[:2]
    sent = []
    step = STEP // per
    scale = LOG2E * HD**-0.5
    nt = (((1,), (1,)), ((), ()))
    row = lax.broadcasted_iota(jnp.int32, (per, LANES), 0)
    lane = lax.broadcasted_iota(jnp.int32, (per, LANES), 1)
    diagonal = row == lane % per
    piece = lax.broadcasted_iota(jnp.int32, (8, LANES), 0)
    ones = jnp.ones(va_ref.shape, jnp.bfloat16)

    def scores(first):
        q = q_ref[first : first + step].reshape(step * per, HD)
        return [
            lax.dot_general(q, k_ref[...], nt, preferred_element_type=jnp.float32) for k_ref in (ka_ref, kb_ref)
        ]

    ahead = scores(0)
    for first in range(0, sources, step):
        sa, sb = ahead
        if first + step < sources:
            ahead = scores(first + step)
        top = scale * jnp.maximum(jnp.max(sa, axis=1, keepdims=True), jnp.max(sb, axis=1, keepdims=True))
        wa = jnp.exp2(sa * scale - top).astype(jnp.bfloat16)
        wb = jnp.exp2(sb * scale - top).astype(jnp.bfloat16)
        both = jnp.dot(
            wa, jnp.concatenate([va_ref[...], ones], axis=1), preferred_element_type=jnp.float32
        ) + jnp.dot(wb, jnp.concatenate([vb_ref[...], ones], axis=1), preferred_element_type=jnp.float32)
        total = both[:, HD:]
        out = (both[:, :HD] / total).astype(jnp.bfloat16)
        lse = top + jnp.log(total) * LOG2E
        for s in range(step):
            part = slice(s * per, (s + 1) * per)
            out_ref[first + s, :per, :] = out[part]
            flat = jnp.sum(jnp.where(diagonal, lse[part], 0.0), axis=0, keepdims=True)
            hi = flat.astype(jnp.bfloat16).astype(jnp.float32)
            mid = (flat - hi).astype(jnp.bfloat16).astype(jnp.float32)
            low = flat - hi - mid
            out_ref[first + s, per:, :] = jnp.where(
                piece == 0, hi, jnp.where(piece == 1, mid, jnp.where(piece == 2, low, 0.0))
            ).astype(jnp.bfloat16)
        done = pl.ds(first, step)
        sent.append(pltpu.make_async_copy(out_ref.at[done], out_hbm.at[done], sems.at[first // step]))
        sent[-1].start()
    for copy in sent:
        copy.wait()


def fresh_kernel(tokens, rows_ref, kv_ref, kv1_ref, kv2_ref, kv3_ref, out_ref, lse_ref):
    sources = kv_ref.shape[0]
    place = lax.axis_index("seq")
    core, odd = place % KVH, place // KVH % 2
    scale = LOG2E * HD**-0.5
    nt = (((1,), (1,)), ((), ()))
    column = lax.broadcasted_iota(jnp.int32, (tokens, sources * tokens), 1)
    query_pos = place * tokens + lax.broadcasted_iota(jnp.int32, column.shape, 0)
    visible = (column <= query_pos) & (column // BLK == query_pos // BLK)
    visible = jnp.concatenate([visible.astype(jnp.int32)] * GROUP, axis=0) > 0
    ones = jnp.ones((sources * tokens, HD), jnp.bfloat16)
    here, near, far, both = [
        ref[...].astype(jnp.float32).reshape(sources * tokens, HD) for ref in (kv_ref, kv1_ref, kv2_ref, kv3_ref)
    ]
    keys = [jnp.where(odd == 0, here, far), jnp.where(odd == 0, near, both)]
    values = [jnp.where(odd == 0, far, here), jnp.where(odd == 0, both, near)]
    for g in range(KVH):
        k = jnp.where(core == g, keys[0], keys[1]).astype(jnp.bfloat16)
        v = jnp.where(core == g, values[0], values[1]).astype(jnp.bfloat16)
        q = rows_ref[g].astype(jnp.bfloat16)
        s = lax.dot_general(q, k, nt, preferred_element_type=jnp.float32) * scale
        s = jnp.where(visible, s, LOW_SCORE)
        top = jnp.max(s, axis=1, keepdims=True)
        w = jnp.where(visible, jnp.exp2(s - top), 0.0).astype(jnp.bfloat16)
        total_out = jnp.dot(w, jnp.concatenate([v, ones], axis=1), preferred_element_type=jnp.float32)
        total = total_out[:, HD:]
        out_ref[g] = total_out[:, :HD] / total
        lse_ref[g] = top + jnp.log(total) * LOG2E


def project_kernel(per, hist_ref, out_ref, lse_ref, match_ref, first_ref, w_hbm, y_ref, w_ref, sems):
    depth = KVH * HD
    ready = first_ref.shape[0] // depth
    copies = fetch(
        [
            (w_hbm.at[pl.ds((ready + i) * depth, depth)], w_ref.at[pl.ds(i * depth, depth)])
            for i in range(w_ref.shape[0] // depth)
        ],
        sems,
    )
    tokens = y_ref.shape[0]
    holders = hist_ref.shape[0]
    fold = LANES // per
    row = lax.broadcasted_iota(jnp.int32, (holders, LANES), 0)
    lane = lax.broadcasted_iota(jnp.int32, (holders, LANES), 1)

    def times(heads, weights):
        lhs = jnp.concatenate(heads, axis=1).astype(jnp.bfloat16)
        return jnp.dot(lhs, weights, preferred_element_type=jnp.float32)

    heads = []
    for g in range(KVH):
        outs = hist_ref[:, g, :per, :].reshape(holders * per, HD)
        stats = jnp.sum(hist_ref[:, g, per:, :].astype(jnp.float32), axis=1)
        stats = jnp.where(row % fold == lane // per, stats, 0.0)
        lse = jnp.concatenate(
            [
                jnp.sum(jnp.where(row // fold == m, stats, 0.0), axis=0, keepdims=True)
                for m in range(holders // fold)
            ],
            axis=1,
        )
        match = match_ref[g] > 0.5
        lse = jnp.where(match, lse, LOW_SCORE)
        own = lse_ref[g]
        top = jnp.maximum(jnp.max(lse, axis=1, keepdims=True), own)
        w = jnp.where(match, jnp.exp2(lse - top[:, :1]), 0.0)
        own_w = jnp.exp2(own - top)
        hi = w.astype(jnp.bfloat16)
        low = (w - hi.astype(jnp.float32)).astype(jnp.bfloat16)
        num = (
            jnp.dot(hi, outs, preferred_element_type=jnp.float32)
            + jnp.dot(low, outs, preferred_element_type=jnp.float32)
            + own_w * out_ref[g]
        )
        att = num / (jnp.sum(w, axis=1, keepdims=True) + own_w)
        heads = heads + [att[r * tokens : (r + 1) * tokens] for r in range(GROUP)]
        if g == 0:
            y = times(heads[: ready * KVH], first_ref[...])
    for i, copy in enumerate(copies):
        copy.wait()
        y = y + times(heads[(ready + i) * KVH : (ready + i + 1) * KVH], w_ref[i * depth : (i + 1) * depth, :])
    y_ref[...] = y.astype(jnp.bfloat16)


VMEM = pl.BlockSpec(memory_space=pltpu.VMEM)
HBM = pl.BlockSpec(memory_space=pltpu.HBM)
ANY = pl.BlockSpec(memory_space=pl.ANY)


def call(kernel, name, out_shape, specs, *operands, outs=None, scratch=(), flops=0, moved=0, limit=16):
    outs = outs or jax.tree.map(lambda _: VMEM, out_shape)
    return pl.pallas_call(
        kernel,
        name=name,
        out_shape=out_shape,
        in_specs=specs,
        out_specs=outs,
        scratch_shapes=scratch,
        cost_estimate=pl.CostEstimate(flops=flops, bytes_accessed=moved, transcendentals=0),
        compiler_params=pltpu.CompilerParams(vmem_limit_bytes=limit << 20),
    )(*operands)


def body(queries, stretch_keys, stretch_values, cache_keys, cache_values, chosen, out_weight):
    devices = lax.axis_size("seq")
    tokens = queries.shape[0]
    cache_rows = cache_keys.shape[0]
    span = BLK // cache_rows
    chips = span // KVH
    key_blocks = cache_rows * devices // BLK
    capacity = (GROUP * TOPK + key_blocks - 1) // key_blocks + 1
    per = capacity * tokens
    f32, bf16 = jnp.float32, jnp.bfloat16
    picks = chosen.transpose(2, 0, 1)

    def partner(bit):
        return [(i, i ^ bit) for i in range(devices)]

    def exchange(x):
        return lax.all_to_all(x, "seq", split_axis=0, concat_axis=0, tiled=True)

    send = call(
        functools.partial(pack_kernel, capacity),
        "pack",
        jax.ShapeDtypeStruct((key_blocks, chips, KVH, per, HD), bf16),
        [HBM] * 2,
        picks, queries,
        outs=ANY,
        scratch=[
            pltpu.VMEM(picks.shape, jnp.int32),
            pltpu.VMEM(queries.shape, bf16),
            pltpu.VMEM((KVH, key_blocks, per, HD), bf16),
            pltpu.SemaphoreType.DMA((2 + KVH * chips,)),
        ],
        limit=60,
    )
    send, cache_keys, cache_values, picks, queries, stretch_keys, stretch_values = lax.optimization_barrier(
        (send, cache_keys, cache_values, picks, queries, stretch_keys, stretch_values)
    )
    got = exchange(send.reshape(devices, per, HD))
    kinds = jnp.stack([stretch_keys, stretch_values]).reshape(2, tokens, KVH, HD).transpose(0, 2, 1, 3)
    kinds = jnp.broadcast_to(kinds[None], (key_blocks, chips, KVH, tokens, HD))
    fresh = exchange(kinds.reshape(devices, tokens, HD))

    core = lax.axis_index("seq") % KVH

    def halves(head):
        return [lax.dynamic_slice_in_dim(x, head * HD, HD, axis=1) for x in (cache_keys, cache_values)]

    k_own, v_own = halves(core)
    k_peer, v_peer = [lax.ppermute(x, "seq", partner(1)) for x in halves(1 - core)]
    holders = devices // KVH
    rows = devices * per
    back = call(
        attend_kernel,
        "attend",
        jax.ShapeDtypeStruct((devices, per + 8, HD), bf16),
        [VMEM] * 5,
        got, k_own, v_own, k_peer, v_peer,
        outs=ANY,
        scratch=[
            pltpu.VMEM((devices, per + 8, HD), bf16),
            pltpu.SemaphoreType.DMA((rows // STEP,)),
        ],
        limit=32,
    )
    back, picks, queries, out_weight, fresh = lax.optimization_barrier((back, picks, queries, out_weight, fresh))
    hist = exchange(back)

    ready = EARLY * KVH * HD
    match, query_rows, first = call(
        functools.partial(masks_kernel, chips, capacity),
        "masks",
        (
            jax.ShapeDtypeStruct((KVH, GROUP * tokens, holders * per), f32),
            jax.ShapeDtypeStruct((KVH, GROUP * tokens, HD), f32),
            jax.ShapeDtypeStruct((ready, out_weight.shape[1]), bf16),
        ),
        [VMEM, VMEM, HBM],
        picks, queries, out_weight,
        scratch=[pltpu.SemaphoreType.DMA((1,))],
        limit=50,
    )

    far = lax.ppermute(fresh, "seq", partner(2))
    near, both = [lax.ppermute(x, "seq", partner(1)) for x in (fresh, far)]
    part = jax.ShapeDtypeStruct((KVH, GROUP * tokens, HD), f32)
    out, lse = call(
        functools.partial(fresh_kernel, tokens),
        "fresh",
        (part, part),
        [VMEM] * 5,
        query_rows, fresh, near, far, both,
        flops=8 * H * tokens * devices * tokens * HD,
        moved=1 << 20,
    )
    return call(
        functools.partial(project_kernel, per),
        "project",
        jax.ShapeDtypeStruct((tokens, out_weight.shape[1]), bf16),
        [VMEM] * 5 + [HBM],
        hist.reshape(holders, KVH, per + 8, HD), out, lse, match, first, out_weight,
        scratch=[
            pltpu.VMEM((out_weight.shape[0] - ready, out_weight.shape[1]), bf16),
            pltpu.SemaphoreType.DMA((GROUP - EARLY,)),
        ],
        flops=2 * tokens * out_weight.size,
        moved=out_weight.size * 2,
        limit=50,
    )


def solution(mesh):
    seq = ("grp", "seq")
    return jax.shard_map(
        body,
        mesh=mesh,
        in_specs=(
            P(seq, None),
            P(seq, None),
            P(seq, None),
            P(seq, None),
            P(seq, None),
            P(seq, None, None),
            P(),
        ),
        out_specs=P(seq, None),
        check_vma=False,
    )
```

```python
import functools
import math

import jax
import jax.numpy as jnp
from jax import lax
from jax.experimental import pallas as pl
from jax.experimental.pallas import tpu as pltpu
from jax.sharding import PartitionSpec as P

H = 14
KVH = 2
HD = 128
BLK = 4096
TOPK = 3
GROUP = H // KVH

LOW_SCORE = -1e30
LOG2E = math.log2(math.e)
LANES = 128
EARLY = 3
STEP = 256


def head_rows(q_ref, g):
    q = q_ref[...].astype(jnp.float32)
    return [q[:, h * HD : (h + 1) * HD] for h in range(g * GROUP, (g + 1) * GROUP)]


def slot_match(chosen_ref, g, block, slot, token):
    rows = lax.broadcasted_iota(jnp.int32, block.shape, 0)
    same_token = token == rows
    seen = jnp.zeros(block.shape, jnp.int32)
    found = []
    for h in range(g * GROUP, (g + 1) * GROUP):
        picked = block == chosen_ref[0, :, h : h + 1]
        for t in range(1, TOPK):
            picked = picked | (block == chosen_ref[t, :, h : h + 1])
        found.append(jnp.where(picked & same_token & (seen == slot), 1.0, 0.0))
        seen = seen + picked.astype(jnp.int32)
    return found


def fetch(pairs, sems):
    copies = [pltpu.make_async_copy(src, dst, sems.at[i]) for i, (src, dst) in enumerate(pairs)]
    for copy in copies:
        copy.start()
    return copies


def pack_kernel(capacity, chosen_hbm, q_hbm, k_hbm, v_hbm, send_hbm, chosen_ref, q_ref, k_ref, v_ref, send_ref, sems):
    copies = fetch([(chosen_hbm, chosen_ref), (q_hbm, q_ref), (k_hbm, k_ref), (v_hbm, v_ref)], sems)
    tokens = q_ref.shape[0]
    per = capacity * tokens
    key_blocks, chips = send_ref.shape[1:3]
    lane = lax.broadcasted_iota(jnp.int32, (tokens, key_blocks * per), 1)
    block, slot, token = lane // per, lane % per // tokens, lane % tokens
    copies[0].wait()
    spread = [
        jnp.concatenate(
            slot_match(chosen_ref, g, block, slot, token) + [jnp.zeros(lane.shape, jnp.float32)], axis=0
        ).T.astype(jnp.bfloat16)
        for g in range(KVH)
    ]
    for copy in copies[1:]:
        copy.wait()
    sent = []
    for g in range(KVH):
        rows = head_rows(q_ref, g)
        rows = jnp.concatenate(rows + [jnp.zeros_like(rows[0])], axis=0).astype(jnp.bfloat16)
        slots = jnp.dot(spread[g], rows, preferred_element_type=jnp.float32).astype(jnp.bfloat16)
        cols = slice(g * HD, (g + 1) * HD)
        fresh = [k_ref[:, cols], v_ref[:, cols]]
        for b in range(key_blocks):
            for chip in range(chips):
                send_ref[g, b, chip, :per, :] = slots[b * per : (b + 1) * per]
                send_ref[g, b, chip, per:, :] = fresh[chip % 2]
        sent.append(pltpu.make_async_copy(send_ref.at[g], send_hbm.at[:, :, g], sems.at[4 + g]))
        sent[g].start()
    for copy in sent:
        copy.wait()


def masks_kernel(chips, capacity, chosen_ref, q_ref, w_hbm, match_ref, rows_ref, w_ref, sems):
    copies = fetch([(w_hbm.at[: w_ref.shape[0]], w_ref)], sems)
    tokens = q_ref.shape[0]
    per = capacity * tokens
    lane = lax.broadcasted_iota(jnp.int32, (tokens, match_ref.shape[2]), 1)
    block, slot, token = lane // (per * chips), lane % per // tokens, lane % tokens
    for g in range(KVH):
        match_ref[g] = jnp.concatenate(slot_match(chosen_ref, g, block, slot, token), axis=0)
        rows_ref[g] = jnp.concatenate(head_rows(q_ref, g), axis=0)
    for copy in copies:
        copy.wait()


def attend_kernel(per, q_ref, ka_ref, va_ref, kb_ref, vb_ref, out_hbm, fresh_ref, out_ref, sems):
    sources = q_ref.shape[0]
    sent = []
    step = STEP // per
    scale = LOG2E * HD**-0.5
    nt = (((1,), (1,)), ((), ()))
    row = lax.broadcasted_iota(jnp.int32, (per, LANES), 0)
    lane = lax.broadcasted_iota(jnp.int32, (per, LANES), 1)
    diagonal = row == lane % per
    group = lax.broadcasted_iota(jnp.int32, (2, LANES), 1) // per
    second = lax.broadcasted_iota(jnp.int32, (2, LANES), 0)
    ones = jnp.ones(va_ref.shape, jnp.bfloat16)
    fresh_ref[...] = q_ref[:, per:, :]

    def scores(first):
        q = q_ref[first : first + step, :per, :].reshape(step * per, HD)
        return [
            lax.dot_general(q, k_ref[...], nt, preferred_element_type=jnp.float32) for k_ref in (ka_ref, kb_ref)
        ]

    ahead = scores(0)
    for first in range(0, sources, step):
        sa, sb = ahead
        if first + step < sources:
            ahead = scores(first + step)
        top = scale * jnp.maximum(jnp.max(sa, axis=1, keepdims=True), jnp.max(sb, axis=1, keepdims=True))
        wa = jnp.exp2(sa * scale - top).astype(jnp.bfloat16)
        wb = jnp.exp2(sb * scale - top).astype(jnp.bfloat16)
        both = jnp.dot(
            wa, jnp.concatenate([va_ref[...], ones], axis=1), preferred_element_type=jnp.float32
        ) + jnp.dot(wb, jnp.concatenate([vb_ref[...], ones], axis=1), preferred_element_type=jnp.float32)
        total = both[:, HD:]
        out = both[:, :HD] / total
        lse = top + jnp.log(total) * LOG2E
        rows = []
        for s in range(step):
            part = slice(s * per, (s + 1) * per)
            flat = jnp.sum(jnp.where(diagonal, lse[part], 0.0), axis=0, keepdims=True)
            hi = flat.astype(jnp.bfloat16).astype(jnp.float32)
            mid = (flat - hi).astype(jnp.bfloat16).astype(jnp.float32)
            low = flat - hi - mid
            stats = jnp.where(group == 0, hi, jnp.where(group == 1, mid, jnp.where(group == 2, low, 0.0)))
            rows = rows + [out[part], jnp.where(second == 0, stats, 0.0)]
        done = pl.ds(first * (per + 2), step * (per + 2))
        out_ref[done, :] = jnp.concatenate(rows, axis=0).astype(jnp.bfloat16)
        sent.append(pltpu.make_async_copy(out_ref.at[done], out_hbm.at[done], sems.at[first // step]))
        sent[-1].start()
    for copy in sent:
        copy.wait()


def fresh_kernel(tokens, rows_ref, kv_ref, kv1_ref, kv2_ref, kv3_ref, out_ref, lse_ref):
    sources = kv_ref.shape[0]
    place = lax.axis_index("seq")
    core, odd = place % KVH, place // KVH % 2
    scale = LOG2E * HD**-0.5
    nt = (((1,), (1,)), ((), ()))
    column = lax.broadcasted_iota(jnp.int32, (tokens, sources * tokens), 1)
    query_pos = place * tokens + lax.broadcasted_iota(jnp.int32, column.shape, 0)
    visible = (column <= query_pos) & (column // BLK == query_pos // BLK)
    visible = jnp.concatenate([visible.astype(jnp.int32)] * GROUP, axis=0) > 0
    ones = jnp.ones((sources * tokens, HD), jnp.bfloat16)
    here, near, far, both = [
        ref[...].astype(jnp.float32).reshape(sources * tokens, HD) for ref in (kv_ref, kv1_ref, kv2_ref, kv3_ref)
    ]
    keys = [jnp.where(odd == 0, here, far), jnp.where(odd == 0, near, both)]
    values = [jnp.where(odd == 0, far, here), jnp.where(odd == 0, both, near)]
    for g in range(KVH):
        k = jnp.where(core == g, keys[0], keys[1]).astype(jnp.bfloat16)
        v = jnp.where(core == g, values[0], values[1]).astype(jnp.bfloat16)
        q = rows_ref[g].astype(jnp.bfloat16)
        s = lax.dot_general(q, k, nt, preferred_element_type=jnp.float32) * scale
        s = jnp.where(visible, s, LOW_SCORE)
        top = jnp.max(s, axis=1, keepdims=True)
        w = jnp.where(visible, jnp.exp2(s - top), 0.0).astype(jnp.bfloat16)
        total_out = jnp.dot(w, jnp.concatenate([v, ones], axis=1), preferred_element_type=jnp.float32)
        total = total_out[:, HD:]
        out_ref[g] = total_out[:, :HD] / total
        lse_ref[g] = top + jnp.log(total) * LOG2E


def project_kernel(per, hist_ref, out_ref, lse_ref, match_ref, first_ref, w_hbm, y_ref, w_ref, sems):
    depth = KVH * HD
    ready = first_ref.shape[0] // depth
    copies = fetch(
        [
            (w_hbm.at[pl.ds((ready + i) * depth, depth)], w_ref.at[pl.ds(i * depth, depth)])
            for i in range(w_ref.shape[0] // depth)
        ],
        sems,
    )
    tokens = y_ref.shape[0]
    holders = match_ref.shape[2] // per
    stride = KVH * (per + 2)
    hist = hist_ref[...].astype(jnp.float32)
    fold = LANES // per
    row = lax.broadcasted_iota(jnp.int32, (holders, LANES), 0)
    lane = lax.broadcasted_iota(jnp.int32, (holders, LANES), 1)

    def times(heads, weights):
        lhs = jnp.concatenate(heads, axis=1).astype(jnp.bfloat16)
        return jnp.dot(lhs, weights, preferred_element_type=jnp.float32)

    heads = []
    for g in range(KVH):
        starts = [m * stride + g * (per + 2) for m in range(holders)]
        outs = jnp.concatenate([hist[i : i + per] for i in starts], axis=0).astype(jnp.bfloat16)
        stats = jnp.concatenate([hist[i + per : i + per + 1] for i in starts], axis=0)
        shift = LANES // 2
        while shift >= per:
            stats = stats + pltpu.roll(stats, shift, 1)
            shift //= 2
        stats = jnp.where(row % fold == lane // per, stats, 0.0)
        lse = jnp.concatenate(
            [
                jnp.sum(jnp.where(row // fold == m, stats, 0.0), axis=0, keepdims=True)
                for m in range(holders // fold)
            ],
            axis=1,
        )
        match = match_ref[g] > 0.5
        lse = jnp.where(match, lse, LOW_SCORE)
        own = lse_ref[g]
        top = jnp.maximum(jnp.max(lse, axis=1, keepdims=True), own)
        w = jnp.where(match, jnp.exp2(lse - top[:, :1]), 0.0)
        own_w = jnp.exp2(own - top)
        hi = w.astype(jnp.bfloat16)
        low = (w - hi.astype(jnp.float32)).astype(jnp.bfloat16)
        num = (
            jnp.dot(hi, outs, preferred_element_type=jnp.float32)
            + jnp.dot(low, outs, preferred_element_type=jnp.float32)
            + own_w * out_ref[g]
        )
        att = num / (jnp.sum(w, axis=1, keepdims=True) + own_w)
        heads = heads + [att[r * tokens : (r + 1) * tokens] for r in range(GROUP)]
        if g == 0:
            y = times(heads[: ready * KVH], first_ref[...])
    for i, copy in enumerate(copies):
        copy.wait()
        y = y + times(heads[(ready + i) * KVH : (ready + i + 1) * KVH], w_ref[i * depth : (i + 1) * depth, :])
    y_ref[...] = y.astype(jnp.bfloat16)


VMEM = pl.BlockSpec(memory_space=pltpu.VMEM)
HBM = pl.BlockSpec(memory_space=pltpu.HBM)
ANY = pl.BlockSpec(memory_space=pl.ANY)


def call(kernel, name, out_shape, specs, *operands, outs=None, scratch=(), flops=0, moved=0, limit=16):
    outs = outs or jax.tree.map(lambda _: VMEM, out_shape)
    return pl.pallas_call(
        kernel,
        name=name,
        out_shape=out_shape,
        in_specs=specs,
        out_specs=outs,
        scratch_shapes=scratch,
        cost_estimate=pl.CostEstimate(flops=flops, bytes_accessed=moved, transcendentals=0),
        compiler_params=pltpu.CompilerParams(vmem_limit_bytes=limit << 20),
    )(*operands)


def body(queries, stretch_keys, stretch_values, cache_keys, cache_values, chosen, out_weight):
    devices = lax.axis_size("seq")
    tokens = queries.shape[0]
    cache_rows = cache_keys.shape[0]
    span = BLK // cache_rows
    chips = span // KVH
    key_blocks = cache_rows * devices // BLK
    capacity = (GROUP * TOPK + key_blocks - 1) // key_blocks + 1
    per = capacity * tokens
    f32, bf16 = jnp.float32, jnp.bfloat16
    picks = chosen.transpose(2, 0, 1)

    def partner(bit):
        return [(i, i ^ bit) for i in range(devices)]

    send = call(
        functools.partial(pack_kernel, capacity),
        "pack",
        jax.ShapeDtypeStruct((key_blocks, chips, KVH, per + tokens, HD), bf16),
        [HBM] * 4,
        picks, queries, stretch_keys, stretch_values,
        outs=ANY,
        scratch=[
            pltpu.VMEM(picks.shape, jnp.int32),
            pltpu.VMEM(queries.shape, bf16),
            pltpu.VMEM(stretch_keys.shape, bf16),
            pltpu.VMEM(stretch_values.shape, bf16),
            pltpu.VMEM((KVH, key_blocks, chips, per + tokens, HD), bf16),
            pltpu.SemaphoreType.DMA((4 + KVH,)),
        ],
        limit=60,
    )
    send, cache_keys, cache_values, picks, queries = lax.optimization_barrier(
        (send, cache_keys, cache_values, picks, queries)
    )
    send = send.reshape(devices, per + tokens, HD)
    got = lax.all_to_all(send, "seq", split_axis=0, concat_axis=0, tiled=True)

    core = lax.axis_index("seq") % KVH

    def halves(head):
        return [lax.dynamic_slice_in_dim(x, head * HD, HD, axis=1) for x in (cache_keys, cache_values)]

    k_own, v_own = halves(core)
    k_peer, v_peer = [lax.ppermute(x, "seq", partner(1)) for x in halves(1 - core)]
    holders = devices // KVH
    rows = devices * per
    back, fresh = call(
        functools.partial(attend_kernel, per),
        "attend",
        (
            jax.ShapeDtypeStruct((devices * (per + 2), HD), bf16),
            jax.ShapeDtypeStruct((devices, tokens, HD), bf16),
        ),
        [VMEM] * 5,
        got, k_own, v_own, k_peer, v_peer,
        outs=(ANY, VMEM),
        scratch=[
            pltpu.VMEM((devices * (per + 2), HD), bf16),
            pltpu.SemaphoreType.DMA((rows // STEP,)),
        ],
        flops=8 * rows * cache_rows * HD,
        moved=4 << 20,
        limit=32,
    )
    back, picks, queries, out_weight = lax.optimization_barrier((back, picks, queries, out_weight))
    back = back.reshape(devices, (per + 2) // 2, 2, HD)
    hist = lax.all_to_all(back, "seq", split_axis=0, concat_axis=0, tiled=True)

    ready = EARLY * KVH * HD
    match, query_rows, first = call(
        functools.partial(masks_kernel, chips, capacity),
        "masks",
        (
            jax.ShapeDtypeStruct((KVH, GROUP * tokens, holders * per), f32),
            jax.ShapeDtypeStruct((KVH, GROUP * tokens, HD), f32),
            jax.ShapeDtypeStruct((ready, out_weight.shape[1]), bf16),
        ),
        [VMEM, VMEM, HBM],
        picks, queries, out_weight,
        scratch=[pltpu.SemaphoreType.DMA((1,))],
        limit=50,
    )

    far = lax.ppermute(fresh, "seq", partner(2))
    near, both = [lax.ppermute(x, "seq", partner(1)) for x in (fresh, far)]
    part = jax.ShapeDtypeStruct((KVH, GROUP * tokens, HD), f32)
    out, lse = call(
        functools.partial(fresh_kernel, tokens),
        "fresh",
        (part, part),
        [VMEM] * 5,
        query_rows, fresh, near, far, both,
        flops=8 * H * tokens * devices * tokens * HD,
        moved=1 << 20,
    )
    return call(
        functools.partial(project_kernel, per),
        "project",
        jax.ShapeDtypeStruct((tokens, out_weight.shape[1]), bf16),
        [VMEM] * 5 + [HBM],
        hist.reshape(devices * (per + 2), HD), out, lse, match, first, out_weight,
        scratch=[
            pltpu.VMEM((out_weight.shape[0] - ready, out_weight.shape[1]), bf16),
            pltpu.SemaphoreType.DMA((GROUP - EARLY,)),
        ],
        flops=2 * tokens * out_weight.size,
        moved=out_weight.size * 2,
        limit=50,
    )


def solution(mesh):
    seq = ("grp", "seq")
    return jax.shard_map(
        body,
        mesh=mesh,
        in_specs=(
            P(seq, None),
            P(seq, None),
            P(seq, None),
            P(seq, None),
            P(seq, None),
            P(seq, None, None),
            P(),
        ),
        out_specs=P(seq, None),
        check_vma=False,
    )
```

```python
import functools
import math

import jax
import jax.numpy as jnp
from jax import lax
from jax.experimental import pallas as pl
from jax.experimental.pallas import tpu as pltpu
from jax.sharding import PartitionSpec as P

H = 14
KVH = 2
HD = 128
BLK = 4096
TOPK = 3
GROUP = H // KVH

LOW_SCORE = -1e30
LOG2E = math.log2(math.e)
LANES = 128
EARLY = 3
STEP = 256


def head_rows(q_ref, g):
    q = q_ref[...].astype(jnp.float32)
    return [q[:, h * HD : (h + 1) * HD] for h in range(g * GROUP, (g + 1) * GROUP)]


def slot_match(chosen_ref, g, block, slot, token):
    rows = lax.broadcasted_iota(jnp.int32, block.shape, 0)
    same_token = token == rows
    seen = jnp.zeros(block.shape, jnp.int32)
    found = []
    for h in range(g * GROUP, (g + 1) * GROUP):
        picked = block == chosen_ref[0, :, h : h + 1]
        for t in range(1, TOPK):
            picked = picked | (block == chosen_ref[t, :, h : h + 1])
        found.append(jnp.where(picked & same_token & (seen == slot), 1.0, 0.0))
        seen = seen + picked.astype(jnp.int32)
    return found


def fetch(pairs, sems):
    copies = [pltpu.make_async_copy(src, dst, sems.at[i]) for i, (src, dst) in enumerate(pairs)]
    for i, copy in enumerate(copies):
        copy.start(priority=i % 2)
    return copies


def pack_kernel(capacity, chosen_hbm, q_hbm, k_hbm, v_hbm, send_hbm, chosen_ref, q_ref, k_ref, v_ref, send_ref, sems):
    copies = fetch([(chosen_hbm, chosen_ref), (q_hbm, q_ref), (k_hbm, k_ref), (v_hbm, v_ref)], sems)
    tokens = q_ref.shape[0]
    per = capacity * tokens
    key_blocks, chips = send_ref.shape[1:3]
    lane = lax.broadcasted_iota(jnp.int32, (tokens, key_blocks * per), 1)
    block, slot, token = lane // per, lane % per // tokens, lane % tokens
    copies[0].wait()
    spread = [
        jnp.concatenate(
            slot_match(chosen_ref, g, block, slot, token) + [jnp.zeros(lane.shape, jnp.float32)], axis=0
        ).T.astype(jnp.bfloat16)
        for g in range(KVH)
    ]
    for copy in copies[1:]:
        copy.wait()
    sent = []
    for g in range(KVH):
        rows = head_rows(q_ref, g)
        rows = jnp.concatenate(rows + [jnp.zeros_like(rows[0])], axis=0).astype(jnp.bfloat16)
        slots = jnp.dot(spread[g], rows, preferred_element_type=jnp.float32).astype(jnp.bfloat16)
        cols = slice(g * HD, (g + 1) * HD)
        fresh = [k_ref[:, cols], v_ref[:, cols]]
        for b in range(key_blocks):
            for chip in range(chips):
                send_ref[g, b, chip, :per, :] = slots[b * per : (b + 1) * per]
                send_ref[g, b, chip, per:, :] = fresh[chip % 2]
        sent.append(pltpu.make_async_copy(send_ref.at[g], send_hbm.at[:, :, g], sems.at[4 + g]))
        sent[g].start()
    for copy in sent:
        copy.wait()


def masks_kernel(chips, capacity, chosen_ref, q_ref, w_hbm, match_ref, rows_ref, w_ref, sems):
    half = w_ref.shape[0] // 2
    copies = fetch([(w_hbm.at[pl.ds(i * half, half)], w_ref.at[pl.ds(i * half, half)]) for i in range(2)], sems)
    tokens = q_ref.shape[0]
    per = capacity * tokens
    lane = lax.broadcasted_iota(jnp.int32, (tokens, match_ref.shape[2]), 1)
    block, slot, token = lane // (per * chips), lane % per // tokens, lane % tokens
    for g in range(KVH):
        match_ref[g] = jnp.concatenate(slot_match(chosen_ref, g, block, slot, token), axis=0)
        rows_ref[g] = jnp.concatenate(head_rows(q_ref, g), axis=0)
    for copy in copies:
        copy.wait()


def attend_kernel(per, q_ref, ka_ref, va_ref, kb_ref, vb_ref, out_hbm, fresh_ref, out_ref, sems):
    sources = q_ref.shape[0]
    sent = []
    step = STEP // per
    scale = LOG2E * HD**-0.5
    nt = (((1,), (1,)), ((), ()))
    row = lax.broadcasted_iota(jnp.int32, (per, LANES), 0)
    lane = lax.broadcasted_iota(jnp.int32, (per, LANES), 1)
    diagonal = row == lane % per
    group = lax.broadcasted_iota(jnp.int32, (2, LANES), 1) // per
    second = lax.broadcasted_iota(jnp.int32, (2, LANES), 0)
    ones = jnp.ones(va_ref.shape, jnp.bfloat16)
    fresh_ref[...] = q_ref[:, per:, :]

    def scores(first, k_ref):
        q = q_ref[first : first + step, :per, :].reshape(step * per, HD)
        return lax.dot_general(q, k_ref[...], nt, preferred_element_type=jnp.float32)

    sides = [(ka_ref, va_ref), (kb_ref, vb_ref)]
    turns = [(first, side) for first in range(0, sources, step) for side in range(2)]
    ahead = scores(0, ka_ref)
    for turn, (first, side) in enumerate(turns):
        s = ahead
        if turn + 1 < len(turns):
            ahead = scores(turns[turn + 1][0], sides[turns[turn + 1][1]][0])
        most = scale * jnp.max(s, axis=1, keepdims=True)
        w = jnp.exp2(s * scale - most).astype(jnp.bfloat16)
        part_out = jnp.dot(
            w, jnp.concatenate([sides[side][1][...], ones], axis=1), preferred_element_type=jnp.float32
        )
        if side == 0:
            before, before_most = part_out, most
            continue
        top = jnp.maximum(before_most, most)
        both = before * jnp.exp2(before_most - top) + part_out * jnp.exp2(most - top)
        total = both[:, HD:]
        out = both[:, :HD] / total
        lse = top + jnp.log(total) * LOG2E
        rows = []
        for s in range(step):
            part = slice(s * per, (s + 1) * per)
            flat = jnp.sum(jnp.where(diagonal, lse[part], 0.0), axis=0, keepdims=True)
            hi = flat.astype(jnp.bfloat16).astype(jnp.float32)
            mid = (flat - hi).astype(jnp.bfloat16).astype(jnp.float32)
            low = flat - hi - mid
            stats = jnp.where(group == 0, hi, jnp.where(group == 1, mid, jnp.where(group == 2, low, 0.0)))
            rows = rows + [out[part], jnp.where(second == 0, stats, 0.0)]
        done = pl.ds(first * (per + 2), step * (per + 2))
        out_ref[done, :] = jnp.concatenate(rows, axis=0).astype(jnp.bfloat16)
        sent.append(pltpu.make_async_copy(out_ref.at[done], out_hbm.at[done], sems.at[first // step]))
        sent[-1].start()
    for copy in sent:
        copy.wait()


def fresh_kernel(tokens, rows_ref, kv_ref, kv1_ref, kv2_ref, kv3_ref, out_ref, lse_ref):
    sources = kv_ref.shape[0]
    place = lax.axis_index("seq")
    core, odd = place % KVH, place // KVH % 2
    scale = LOG2E * HD**-0.5
    nt = (((1,), (1,)), ((), ()))
    column = lax.broadcasted_iota(jnp.int32, (tokens, sources * tokens), 1)
    query_pos = place * tokens + lax.broadcasted_iota(jnp.int32, column.shape, 0)
    visible = (column <= query_pos) & (column // BLK == query_pos // BLK)
    visible = jnp.concatenate([visible.astype(jnp.int32)] * GROUP, axis=0) > 0
    ones = jnp.ones((sources * tokens, HD), jnp.bfloat16)
    here, near, far, both = [
        ref[...].astype(jnp.float32).reshape(sources * tokens, HD) for ref in (kv_ref, kv1_ref, kv2_ref, kv3_ref)
    ]
    keys = [jnp.where(odd == 0, here, far), jnp.where(odd == 0, near, both)]
    values = [jnp.where(odd == 0, far, here), jnp.where(odd == 0, both, near)]
    for g in range(KVH):
        k = jnp.where(core == g, keys[0], keys[1]).astype(jnp.bfloat16)
        v = jnp.where(core == g, values[0], values[1]).astype(jnp.bfloat16)
        q = rows_ref[g].astype(jnp.bfloat16)
        s = lax.dot_general(q, k, nt, preferred_element_type=jnp.float32) * scale
        s = jnp.where(visible, s, LOW_SCORE)
        top = jnp.max(s, axis=1, keepdims=True)
        w = jnp.where(visible, jnp.exp2(s - top), 0.0).astype(jnp.bfloat16)
        total_out = jnp.dot(w, jnp.concatenate([v, ones], axis=1), preferred_element_type=jnp.float32)
        total = total_out[:, HD:]
        out_ref[g] = total_out[:, :HD] / total
        lse_ref[g] = top + jnp.log(total) * LOG2E


def project_kernel(per, hist_ref, out_ref, lse_ref, match_ref, first_ref, w_hbm, y_ref, w_ref, sems):
    depth = KVH * HD
    ready = first_ref.shape[0] // depth
    copies = fetch(
        [
            (w_hbm.at[pl.ds((ready + i) * depth, depth)], w_ref.at[pl.ds(i * depth, depth)])
            for i in range(w_ref.shape[0] // depth)
        ],
        sems,
    )
    tokens = y_ref.shape[0]
    holders = match_ref.shape[2] // per
    stride = KVH * (per + 2)
    hist = hist_ref[...].astype(jnp.float32)
    fold = LANES // per
    row = lax.broadcasted_iota(jnp.int32, (holders, LANES), 0)
    lane = lax.broadcasted_iota(jnp.int32, (holders, LANES), 1)

    def times(heads, weights):
        lhs = jnp.concatenate(heads, axis=1).astype(jnp.bfloat16)
        return jnp.dot(lhs, weights, preferred_element_type=jnp.float32)

    heads = []
    for g in range(KVH):
        starts = [m * stride + g * (per + 2) for m in range(holders)]
        outs = jnp.concatenate([hist[i : i + per] for i in starts], axis=0).astype(jnp.bfloat16)
        stats = jnp.concatenate([hist[i + per : i + per + 1] for i in starts], axis=0)
        shift = LANES // 2
        while shift >= per:
            stats = stats + pltpu.roll(stats, shift, 1)
            shift //= 2
        stats = jnp.where(row % fold == lane // per, stats, 0.0)
        lse = jnp.concatenate(
            [
                jnp.sum(jnp.where(row // fold == m, stats, 0.0), axis=0, keepdims=True)
                for m in range(holders // fold)
            ],
            axis=1,
        )
        match = match_ref[g] > 0.5
        lse = jnp.where(match, lse, LOW_SCORE)
        own = lse_ref[g]
        top = jnp.maximum(jnp.max(lse, axis=1, keepdims=True), own)
        w = jnp.where(match, jnp.exp2(lse - top[:, :1]), 0.0)
        own_w = jnp.exp2(own - top)
        hi = w.astype(jnp.bfloat16)
        low = (w - hi.astype(jnp.float32)).astype(jnp.bfloat16)
        num = (
            jnp.dot(hi, outs, preferred_element_type=jnp.float32)
            + jnp.dot(low, outs, preferred_element_type=jnp.float32)
            + own_w * out_ref[g]
        )
        att = num / (jnp.sum(w, axis=1, keepdims=True) + own_w)
        heads = heads + [att[r * tokens : (r + 1) * tokens] for r in range(GROUP)]
        if g == 0:
            y = times(heads[: ready * KVH], first_ref[...])
    for i, copy in enumerate(copies):
        copy.wait()
        y = y + times(heads[(ready + i) * KVH : (ready + i + 1) * KVH], w_ref[i * depth : (i + 1) * depth, :])
    y_ref[...] = y.astype(jnp.bfloat16)


VMEM = pl.BlockSpec(memory_space=pltpu.VMEM)
HBM = pl.BlockSpec(memory_space=pltpu.HBM)
ANY = pl.BlockSpec(memory_space=pl.ANY)


def call(kernel, name, out_shape, specs, *operands, outs=None, scratch=(), flops=0, moved=0, limit=16):
    outs = outs or jax.tree.map(lambda _: VMEM, out_shape)
    return pl.pallas_call(
        kernel,
        name=name,
        out_shape=out_shape,
        in_specs=specs,
        out_specs=outs,
        scratch_shapes=scratch,
        cost_estimate=pl.CostEstimate(flops=flops, bytes_accessed=moved, transcendentals=0),
        compiler_params=pltpu.CompilerParams(vmem_limit_bytes=limit << 20),
    )(*operands)


def body(queries, stretch_keys, stretch_values, cache_keys, cache_values, chosen, out_weight):
    devices = lax.axis_size("seq")
    tokens = queries.shape[0]
    cache_rows = cache_keys.shape[0]
    span = BLK // cache_rows
    chips = span // KVH
    key_blocks = cache_rows * devices // BLK
    capacity = (GROUP * TOPK + key_blocks - 1) // key_blocks + 1
    per = capacity * tokens
    f32, bf16 = jnp.float32, jnp.bfloat16
    picks = chosen.transpose(2, 0, 1)

    def partner(bit):
        return [(i, i ^ bit) for i in range(devices)]

    send = call(
        functools.partial(pack_kernel, capacity),
        "pack",
        jax.ShapeDtypeStruct((key_blocks, chips, KVH, per + tokens, HD), bf16),
        [HBM] * 4,
        picks, queries, stretch_keys, stretch_values,
        outs=ANY,
        scratch=[
            pltpu.VMEM(picks.shape, jnp.int32),
            pltpu.VMEM(queries.shape, bf16),
            pltpu.VMEM(stretch_keys.shape, bf16),
            pltpu.VMEM(stretch_values.shape, bf16),
            pltpu.VMEM((KVH, key_blocks, chips, per + tokens, HD), bf16),
            pltpu.SemaphoreType.DMA((4 + KVH,)),
        ],
        limit=60,
    )
    send, cache_keys, cache_values, picks, queries = lax.optimization_barrier(
        (send, cache_keys, cache_values, picks, queries)
    )
    send = send.reshape(devices, per + tokens, HD)
    got = lax.all_to_all(send, "seq", split_axis=0, concat_axis=0, tiled=True)

    core = lax.axis_index("seq") % KVH

    def halves(head):
        return [lax.dynamic_slice_in_dim(x, head * HD, HD, axis=1) for x in (cache_keys, cache_values)]

    k_own, v_own = halves(core)
    k_peer, v_peer = [lax.ppermute(x, "seq", partner(1)) for x in halves(1 - core)]
    holders = devices // KVH
    rows = devices * per
    back, fresh = call(
        functools.partial(attend_kernel, per),
        "attend",
        (
            jax.ShapeDtypeStruct((devices * (per + 2), HD), bf16),
            jax.ShapeDtypeStruct((devices, tokens, HD), bf16),
        ),
        [VMEM] * 5,
        got, k_own, v_own, k_peer, v_peer,
        outs=(ANY, VMEM),
        scratch=[
            pltpu.VMEM((devices * (per + 2), HD), bf16),
            pltpu.SemaphoreType.DMA((rows // STEP,)),
        ],
        flops=8 * rows * cache_rows * HD,
        moved=4 << 20,
        limit=32,
    )
    back, picks, queries, out_weight = lax.optimization_barrier((back, picks, queries, out_weight))
    back = back.reshape(devices, (per + 2) // 2, 2, HD)
    hist = lax.all_to_all(back, "seq", split_axis=0, concat_axis=0, tiled=True)

    ready = EARLY * KVH * HD
    match, query_rows, first = call(
        functools.partial(masks_kernel, chips, capacity),
        "masks",
        (
            jax.ShapeDtypeStruct((KVH, GROUP * tokens, holders * per), f32),
            jax.ShapeDtypeStruct((KVH, GROUP * tokens, HD), f32),
            jax.ShapeDtypeStruct((ready, out_weight.shape[1]), bf16),
        ),
        [VMEM, VMEM, HBM],
        picks, queries, out_weight,
        scratch=[pltpu.SemaphoreType.DMA((2,))],
        limit=50,
    )

    far = lax.ppermute(fresh, "seq", partner(2))
    near, both = [lax.ppermute(x, "seq", partner(1)) for x in (fresh, far)]
    part = jax.ShapeDtypeStruct((KVH, GROUP * tokens, HD), f32)
    out, lse = call(
        functools.partial(fresh_kernel, tokens),
        "fresh",
        (part, part),
        [VMEM] * 5,
        query_rows, fresh, near, far, both,
        flops=8 * H * tokens * devices * tokens * HD,
        moved=1 << 20,
    )
    return call(
        functools.partial(project_kernel, per),
        "project",
        jax.ShapeDtypeStruct((tokens, out_weight.shape[1]), bf16),
        [VMEM] * 5 + [HBM],
        hist.reshape(devices * (per + 2), HD), out, lse, match, first, out_weight,
        scratch=[
            pltpu.VMEM((out_weight.shape[0] - ready, out_weight.shape[1]), bf16),
            pltpu.SemaphoreType.DMA((GROUP - EARLY,)),
        ],
        flops=2 * tokens * out_weight.size,
        moved=out_weight.size * 2,
        limit=50,
    )


def solution(mesh):
    seq = ("grp", "seq")
    return jax.shard_map(
        body,
        mesh=mesh,
        in_specs=(
            P(seq, None),
            P(seq, None),
            P(seq, None),
            P(seq, None),
            P(seq, None),
            P(seq, None, None),
            P(),
        ),
        out_specs=P(seq, None),
        check_vma=False,
    )
```

```python
import functools
import math

import jax
import jax.numpy as jnp
from jax import lax
from jax.experimental import pallas as pl
from jax.experimental.pallas import tpu as pltpu
from jax.sharding import PartitionSpec as P

H = 14
KVH = 2
HD = 128
BLK = 4096
TOPK = 3
GROUP = H // KVH

LOW_SCORE = -1e30
LOG2E = math.log2(math.e)
LANES = 128
EARLY = 3
STEP = 256


def head_rows(q_ref, g):
    q = q_ref[...].astype(jnp.float32)
    return [q[:, h * HD : (h + 1) * HD] for h in range(g * GROUP, (g + 1) * GROUP)]


def slot_match(chosen_ref, g, block, slot, token):
    rows = lax.broadcasted_iota(jnp.int32, block.shape, 0)
    same_token = token == rows
    seen = jnp.zeros(block.shape, jnp.int32)
    found = []
    for h in range(g * GROUP, (g + 1) * GROUP):
        picked = block == chosen_ref[0, :, h : h + 1]
        for t in range(1, TOPK):
            picked = picked | (block == chosen_ref[t, :, h : h + 1])
        found.append(jnp.where(picked & same_token & (seen == slot), 1.0, 0.0))
        seen = seen + picked.astype(jnp.int32)
    return found


def fetch(pairs, sems):
    copies = [pltpu.make_async_copy(src, dst, sems.at[i]) for i, (src, dst) in enumerate(pairs)]
    for copy in copies:
        copy.start()
    return copies


def pack_kernel(capacity, chosen_hbm, q_hbm, k_hbm, v_hbm, send_hbm, chosen_ref, q_ref, k_ref, v_ref, send_ref, sems):
    copies = fetch([(chosen_hbm, chosen_ref), (q_hbm, q_ref), (k_hbm, k_ref), (v_hbm, v_ref)], sems)
    tokens = q_ref.shape[0]
    per = capacity * tokens
    key_blocks, chips = send_ref.shape[1:3]
    lane = lax.broadcasted_iota(jnp.int32, (tokens, key_blocks * per), 1)
    block, slot, token = lane // per, lane % per // tokens, lane % tokens
    copies[0].wait()
    spread = [
        jnp.concatenate(
            slot_match(chosen_ref, g, block, slot, token) + [jnp.zeros(lane.shape, jnp.float32)], axis=0
        ).T.astype(jnp.bfloat16)
        for g in range(KVH)
    ]
    for copy in copies[1:]:
        copy.wait()
    sent = []
    for g in range(KVH):
        rows = head_rows(q_ref, g)
        rows = jnp.concatenate(rows + [jnp.zeros_like(rows[0])], axis=0).astype(jnp.bfloat16)
        slots = jnp.dot(spread[g], rows, preferred_element_type=jnp.float32).astype(jnp.bfloat16)
        cols = slice(g * HD, (g + 1) * HD)
        fresh = [k_ref[:, cols], v_ref[:, cols]]
        for b in range(key_blocks):
            for chip in range(chips):
                send_ref[g, b, chip, :per, :] = slots[b * per : (b + 1) * per]
                send_ref[g, b, chip, per:, :] = fresh[chip % 2]
        sent.append(pltpu.make_async_copy(send_ref.at[g], send_hbm.at[:, :, g], sems.at[4 + g]))
        sent[g].start()
    for copy in sent:
        copy.wait()


def masks_kernel(chips, capacity, chosen_ref, q_ref, w_hbm, match_ref, rows_ref, w_ref, sems):
    copies = fetch([(w_hbm.at[: w_ref.shape[0]], w_ref)], sems)
    tokens = q_ref.shape[0]
    per = capacity * tokens
    lane = lax.broadcasted_iota(jnp.int32, (tokens, match_ref.shape[2]), 1)
    block, slot, token = lane // (per * chips), lane % per // tokens, lane % tokens
    for g in range(KVH):
        match_ref[g] = jnp.concatenate(slot_match(chosen_ref, g, block, slot, token), axis=0)
        rows_ref[g] = jnp.concatenate(head_rows(q_ref, g), axis=0)
    for copy in copies:
        copy.wait()


def attend_kernel(per, q_ref, ka_ref, va_ref, kb_ref, vb_ref, out_hbm, fresh_ref, out_ref, sems):
    sources = q_ref.shape[0]
    sent = []
    step = STEP // per
    scale = LOG2E * HD**-0.5
    nt = (((1,), (1,)), ((), ()))
    row = lax.broadcasted_iota(jnp.int32, (per, LANES), 0)
    lane = lax.broadcasted_iota(jnp.int32, (per, LANES), 1)
    diagonal = row == lane % per
    group = lax.broadcasted_iota(jnp.int32, (2, LANES), 1) // per
    second = lax.broadcasted_iota(jnp.int32, (2, LANES), 0)
    ones = jnp.ones(va_ref.shape, jnp.bfloat16)
    fresh_ref[...] = q_ref[:, per:, :]

    def scores(first):
        q = q_ref[first : first + step, :per, :].reshape(step * per, HD).astype(jnp.float32) * scale
        high = q.astype(jnp.bfloat16)
        low = (q - high.astype(jnp.float32)).astype(jnp.bfloat16)
        q = jnp.concatenate([high, low], axis=1)
        return [
            lax.dot_general(
                q, jnp.concatenate([k_ref[...]] * 2, axis=1), nt, preferred_element_type=jnp.float32
            )
            for k_ref in (ka_ref, kb_ref)
        ]

    ahead = scores(0)
    for first in range(0, sources, step):
        sa, sb = ahead
        if first + step < sources:
            ahead = scores(first + step)
        top = jnp.maximum(jnp.max(sa, axis=1, keepdims=True), jnp.max(sb, axis=1, keepdims=True))
        wa = jnp.exp2(sa - top).astype(jnp.bfloat16)
        wb = jnp.exp2(sb - top).astype(jnp.bfloat16)
        both = jnp.dot(
            wa, jnp.concatenate([va_ref[...], ones], axis=1), preferred_element_type=jnp.float32
        ) + jnp.dot(wb, jnp.concatenate([vb_ref[...], ones], axis=1), preferred_element_type=jnp.float32)
        total = both[:, HD:]
        out = both[:, :HD] / total
        lse = top + jnp.log(total) * LOG2E
        rows = []
        for s in range(step):
            part = slice(s * per, (s + 1) * per)
            flat = jnp.sum(jnp.where(diagonal, lse[part], 0.0), axis=0, keepdims=True)
            hi = flat.astype(jnp.bfloat16).astype(jnp.float32)
            mid = (flat - hi).astype(jnp.bfloat16).astype(jnp.float32)
            low = flat - hi - mid
            stats = jnp.where(group == 0, hi, jnp.where(group == 1, mid, jnp.where(group == 2, low, 0.0)))
            rows = rows + [out[part], jnp.where(second == 0, stats, 0.0)]
        done = pl.ds(first * (per + 2), step * (per + 2))
        out_ref[done, :] = jnp.concatenate(rows, axis=0).astype(jnp.bfloat16)
        sent.append(pltpu.make_async_copy(out_ref.at[done], out_hbm.at[done], sems.at[first // step]))
        sent[-1].start()
    for copy in sent:
        copy.wait()


def fresh_kernel(tokens, rows_ref, kv_ref, kv1_ref, kv2_ref, kv3_ref, out_ref, lse_ref):
    sources = kv_ref.shape[0]
    place = lax.axis_index("seq")
    core, odd = place % KVH, place // KVH % 2
    scale = LOG2E * HD**-0.5
    nt = (((1,), (1,)), ((), ()))
    column = lax.broadcasted_iota(jnp.int32, (tokens, sources * tokens), 1)
    query_pos = place * tokens + lax.broadcasted_iota(jnp.int32, column.shape, 0)
    visible = (column <= query_pos) & (column // BLK == query_pos // BLK)
    visible = jnp.concatenate([visible.astype(jnp.int32)] * GROUP, axis=0) > 0
    ones = jnp.ones((sources * tokens, HD), jnp.bfloat16)
    here, near, far, both = [
        ref[...].astype(jnp.float32).reshape(sources * tokens, HD) for ref in (kv_ref, kv1_ref, kv2_ref, kv3_ref)
    ]
    keys = [jnp.where(odd == 0, here, far), jnp.where(odd == 0, near, both)]
    values = [jnp.where(odd == 0, far, here), jnp.where(odd == 0, both, near)]
    for g in range(KVH):
        k = jnp.where(core == g, keys[0], keys[1]).astype(jnp.bfloat16)
        v = jnp.where(core == g, values[0], values[1]).astype(jnp.bfloat16)
        q = rows_ref[g].astype(jnp.bfloat16)
        s = lax.dot_general(q, k, nt, preferred_element_type=jnp.float32) * scale
        s = jnp.where(visible, s, LOW_SCORE)
        top = jnp.max(s, axis=1, keepdims=True)
        w = jnp.where(visible, jnp.exp2(s - top), 0.0).astype(jnp.bfloat16)
        total_out = jnp.dot(w, jnp.concatenate([v, ones], axis=1), preferred_element_type=jnp.float32)
        total = total_out[:, HD:]
        out_ref[g] = total_out[:, :HD] / total
        lse_ref[g] = top + jnp.log(total) * LOG2E


def project_kernel(per, hist_ref, out_ref, lse_ref, match_ref, first_ref, w_hbm, y_ref, w_ref, sems):
    depth = KVH * HD
    ready = first_ref.shape[0] // depth
    copies = fetch(
        [
            (w_hbm.at[pl.ds((ready + i) * depth, depth)], w_ref.at[pl.ds(i * depth, depth)])
            for i in range(w_ref.shape[0] // depth)
        ],
        sems,
    )
    tokens = y_ref.shape[0]
    holders = match_ref.shape[2] // per
    stride = KVH * (per + 2)
    hist = hist_ref[...].astype(jnp.float32)
    fold = LANES // per
    row = lax.broadcasted_iota(jnp.int32, (holders, LANES), 0)
    lane = lax.broadcasted_iota(jnp.int32, (holders, LANES), 1)

    def times(heads, weights):
        lhs = jnp.concatenate(heads, axis=1).astype(jnp.bfloat16)
        return jnp.dot(lhs, weights, preferred_element_type=jnp.float32)

    heads = []
    for g in range(KVH):
        starts = [m * stride + g * (per + 2) for m in range(holders)]
        outs = jnp.concatenate([hist[i : i + per] for i in starts], axis=0).astype(jnp.bfloat16)
        stats = jnp.concatenate([hist[i + per : i + per + 1] for i in starts], axis=0)
        shift = LANES // 2
        while shift >= per:
            stats = stats + pltpu.roll(stats, shift, 1)
            shift //= 2
        stats = jnp.where(row % fold == lane // per, stats, 0.0)
        lse = jnp.concatenate(
            [
                jnp.sum(jnp.where(row // fold == m, stats, 0.0), axis=0, keepdims=True)
                for m in range(holders // fold)
            ],
            axis=1,
        )
        match = match_ref[g] > 0.5
        lse = jnp.where(match, lse, LOW_SCORE)
        own = lse_ref[g]
        top = jnp.maximum(jnp.max(lse, axis=1, keepdims=True), own)
        w = jnp.where(match, jnp.exp2(lse - top[:, :1]), 0.0)
        own_w = jnp.exp2(own - top)
        hi = w.astype(jnp.bfloat16)
        low = (w - hi.astype(jnp.float32)).astype(jnp.bfloat16)
        num = (
            jnp.dot(hi, outs, preferred_element_type=jnp.float32)
            + jnp.dot(low, outs, preferred_element_type=jnp.float32)
            + own_w * out_ref[g]
        )
        att = num / (jnp.sum(w, axis=1, keepdims=True) + own_w)
        heads = heads + [att[r * tokens : (r + 1) * tokens] for r in range(GROUP)]
        if g == 0:
            y = times(heads[: ready * KVH], first_ref[...])
    for i, copy in enumerate(copies):
        copy.wait()
        y = y + times(heads[(ready + i) * KVH : (ready + i + 1) * KVH], w_ref[i * depth : (i + 1) * depth, :])
    y_ref[...] = y.astype(jnp.bfloat16)


VMEM = pl.BlockSpec(memory_space=pltpu.VMEM)
HBM = pl.BlockSpec(memory_space=pltpu.HBM)
ANY = pl.BlockSpec(memory_space=pl.ANY)


def call(kernel, name, out_shape, specs, *operands, outs=None, scratch=(), flops=0, moved=0, limit=16):
    outs = outs or jax.tree.map(lambda _: VMEM, out_shape)
    return pl.pallas_call(
        kernel,
        name=name,
        out_shape=out_shape,
        in_specs=specs,
        out_specs=outs,
        scratch_shapes=scratch,
        cost_estimate=pl.CostEstimate(flops=flops, bytes_accessed=moved, transcendentals=0),
        compiler_params=pltpu.CompilerParams(vmem_limit_bytes=limit << 20),
    )(*operands)


def body(queries, stretch_keys, stretch_values, cache_keys, cache_values, chosen, out_weight):
    devices = lax.axis_size("seq")
    tokens = queries.shape[0]
    cache_rows = cache_keys.shape[0]
    span = BLK // cache_rows
    chips = span // KVH
    key_blocks = cache_rows * devices // BLK
    capacity = (GROUP * TOPK + key_blocks - 1) // key_blocks + 1
    per = capacity * tokens
    f32, bf16 = jnp.float32, jnp.bfloat16
    picks = chosen.transpose(2, 0, 1)

    def partner(bit):
        return [(i, i ^ bit) for i in range(devices)]

    send = call(
        functools.partial(pack_kernel, capacity),
        "pack",
        jax.ShapeDtypeStruct((key_blocks, chips, KVH, per + tokens, HD), bf16),
        [HBM] * 4,
        picks, queries, stretch_keys, stretch_values,
        outs=ANY,
        scratch=[
            pltpu.VMEM(picks.shape, jnp.int32),
            pltpu.VMEM(queries.shape, bf16),
            pltpu.VMEM(stretch_keys.shape, bf16),
            pltpu.VMEM(stretch_values.shape, bf16),
            pltpu.VMEM((KVH, key_blocks, chips, per + tokens, HD), bf16),
            pltpu.SemaphoreType.DMA((4 + KVH,)),
        ],
        limit=60,
    )
    send, cache_keys, cache_values, picks, queries = lax.optimization_barrier(
        (send, cache_keys, cache_values, picks, queries)
    )
    send = send.reshape(devices, per + tokens, HD)
    got = lax.all_to_all(send, "seq", split_axis=0, concat_axis=0, tiled=True)

    core = lax.axis_index("seq") % KVH

    def halves(head):
        return [lax.dynamic_slice_in_dim(x, head * HD, HD, axis=1) for x in (cache_keys, cache_values)]

    k_own, v_own = halves(core)
    k_peer, v_peer = [lax.ppermute(x, "seq", partner(1)) for x in halves(1 - core)]
    holders = devices // KVH
    rows = devices * per
    back, fresh = call(
        functools.partial(attend_kernel, per),
        "attend",
        (
            jax.ShapeDtypeStruct((devices * (per + 2), HD), bf16),
            jax.ShapeDtypeStruct((devices, tokens, HD), bf16),
        ),
        [VMEM] * 5,
        got, k_own, v_own, k_peer, v_peer,
        outs=(ANY, VMEM),
        scratch=[
            pltpu.VMEM((devices * (per + 2), HD), bf16),
            pltpu.SemaphoreType.DMA((rows // STEP,)),
        ],
        flops=8 * rows * cache_rows * HD,
        moved=4 << 20,
        limit=32,
    )
    back, picks, queries, out_weight = lax.optimization_barrier((back, picks, queries, out_weight))
    back = back.reshape(devices, (per + 2) // 2, 2, HD)
    hist = lax.all_to_all(back, "seq", split_axis=0, concat_axis=0, tiled=True)

    ready = EARLY * KVH * HD
    match, query_rows, first = call(
        functools.partial(masks_kernel, chips, capacity),
        "masks",
        (
            jax.ShapeDtypeStruct((KVH, GROUP * tokens, holders * per), f32),
            jax.ShapeDtypeStruct((KVH, GROUP * tokens, HD), f32),
            jax.ShapeDtypeStruct((ready, out_weight.shape[1]), bf16),
        ),
        [VMEM, VMEM, HBM],
        picks, queries, out_weight,
        scratch=[pltpu.SemaphoreType.DMA((1,))],
        limit=50,
    )

    far = lax.ppermute(fresh, "seq", partner(2))
    near, both = [lax.ppermute(x, "seq", partner(1)) for x in (fresh, far)]
    part = jax.ShapeDtypeStruct((KVH, GROUP * tokens, HD), f32)
    out, lse = call(
        functools.partial(fresh_kernel, tokens),
        "fresh",
        (part, part),
        [VMEM] * 5,
        query_rows, fresh, near, far, both,
        flops=8 * H * tokens * devices * tokens * HD,
        moved=1 << 20,
    )
    return call(
        functools.partial(project_kernel, per),
        "project",
        jax.ShapeDtypeStruct((tokens, out_weight.shape[1]), bf16),
        [VMEM] * 5 + [HBM],
        hist.reshape(devices * (per + 2), HD), out, lse, match, first, out_weight,
        scratch=[
            pltpu.VMEM((out_weight.shape[0] - ready, out_weight.shape[1]), bf16),
            pltpu.SemaphoreType.DMA((GROUP - EARLY,)),
        ],
        flops=2 * tokens * out_weight.size,
        moved=out_weight.size * 2,
        limit=50,
    )


def solution(mesh):
    seq = ("grp", "seq")
    return jax.shard_map(
        body,
        mesh=mesh,
        in_specs=(
            P(seq, None),
            P(seq, None),
            P(seq, None),
            P(seq, None),
            P(seq, None),
            P(seq, None, None),
            P(),
        ),
        out_specs=P(seq, None),
        check_vma=False,
    )
```

```python
import functools
import math

import jax
import jax.numpy as jnp
from jax import lax
from jax.experimental import pallas as pl
from jax.experimental.pallas import tpu as pltpu
from jax.sharding import PartitionSpec as P

H = 14
KVH = 2
HD = 128
BLK = 4096
TOPK = 3
GROUP = H // KVH

LOW_SCORE = -1e30
LOG2E = math.log2(math.e)
LANES = 128
EARLY = 3
STEP = 256


def head_rows(q_ref, g):
    q = q_ref[...].astype(jnp.float32)
    return [q[:, h * HD : (h + 1) * HD] for h in range(g * GROUP, (g + 1) * GROUP)]


def slot_match(chosen_ref, g, block, slot, token):
    rows = lax.broadcasted_iota(jnp.int32, block.shape, 0)
    same_token = token == rows
    seen = jnp.zeros(block.shape, jnp.int32)
    found = []
    for h in range(g * GROUP, (g + 1) * GROUP):
        picked = block == chosen_ref[0, :, h : h + 1]
        for t in range(1, TOPK):
            picked = picked | (block == chosen_ref[t, :, h : h + 1])
        found.append(jnp.where(picked & same_token & (seen == slot), 1.0, 0.0))
        seen = seen + picked.astype(jnp.int32)
    return found


def fetch(pairs, sems):
    copies = [pltpu.make_async_copy(src, dst, sems.at[i]) for i, (src, dst) in enumerate(pairs)]
    for copy in copies:
        copy.start()
    return copies


def slot_spread(chosen_ref, g, capacity, tokens, key_blocks):
    lane = lax.broadcasted_iota(jnp.int32, (tokens, LANES), 1)
    head = lane // tokens
    same_token = (lane % tokens == lax.broadcasted_iota(jnp.int32, lane.shape, 0)) & (head < GROUP)
    picks = [[chosen_ref[t, 0, g * GROUP + r] for r in range(GROUP)] for t in range(TOPK)]
    places = []
    for t in range(TOPK):
        block = jnp.zeros(lane.shape, jnp.int32)
        for r in range(GROUP):
            block = jnp.where(head == r, picks[t][r], block)
        rank = jnp.zeros(lane.shape, jnp.int32)
        for r in range(GROUP - 1):
            taken = block == picks[0][r]
            for other in range(1, TOPK):
                taken = taken | (block == picks[other][r])
            rank = rank + jnp.where(taken & (head > r), 1, 0)
        places.append(jnp.where(same_token, block * capacity + rank, -1))
    rows = []
    for place in range(key_blocks * capacity):
        found = places[0] == place
        for t in range(1, TOPK):
            found = found | (places[t] == place)
        rows.append(jnp.where(found, 1.0, 0.0))
    return jnp.concatenate(rows, axis=0).astype(jnp.bfloat16)


def pack_kernel(capacity, chosen_hbm, q_hbm, k_hbm, v_hbm, send_hbm, chosen_ref, q_ref, k_ref, v_ref, send_ref, sems):
    copies = fetch([(chosen_hbm, chosen_ref), (q_hbm, q_ref), (k_hbm, k_ref), (v_hbm, v_ref)], sems)
    tokens = q_ref.shape[0]
    per = capacity * tokens
    key_blocks, chips = send_ref.shape[1:3]
    copies[0].wait()
    spread = [slot_spread(chosen_ref, g, capacity, tokens, key_blocks) for g in range(KVH)]
    for copy in copies[1:]:
        copy.wait()
    sent = []
    for g in range(KVH):
        rows = head_rows(q_ref, g)
        rows = rows + [jnp.zeros_like(rows[0])] * (LANES // tokens - GROUP)
        rows = jnp.concatenate(rows, axis=0).astype(jnp.bfloat16)
        slots = jnp.dot(spread[g], rows, preferred_element_type=jnp.float32).astype(jnp.bfloat16)
        cols = slice(g * HD, (g + 1) * HD)
        fresh = [k_ref[:, cols], v_ref[:, cols]]
        for b in range(key_blocks):
            for chip in range(chips):
                send_ref[g, b, chip, :per, :] = slots[b * per : (b + 1) * per]
                send_ref[g, b, chip, per:, :] = fresh[chip % 2]
        sent.append(pltpu.make_async_copy(send_ref.at[g], send_hbm.at[:, :, g], sems.at[4 + g]))
        sent[g].start()
    for copy in sent:
        copy.wait()


def masks_kernel(chips, capacity, chosen_ref, q_ref, w_hbm, match_ref, rows_ref, w_ref, sems):
    copies = fetch([(w_hbm.at[: w_ref.shape[0]], w_ref)], sems)
    tokens = q_ref.shape[0]
    per = capacity * tokens
    lane = lax.broadcasted_iota(jnp.int32, (tokens, match_ref.shape[2]), 1)
    block, slot, token = lane // (per * chips), lane % per // tokens, lane % tokens
    for g in range(KVH):
        match_ref[g] = jnp.concatenate(slot_match(chosen_ref, g, block, slot, token), axis=0)
        rows_ref[g] = jnp.concatenate(head_rows(q_ref, g), axis=0)
    for copy in copies:
        copy.wait()


def attend_kernel(per, q_ref, ka_ref, va_ref, kb_ref, vb_ref, out_hbm, fresh_ref, out_ref, sems):
    sources = q_ref.shape[0]
    sent = []
    step = STEP // per
    scale = LOG2E * HD**-0.5
    nt = (((1,), (1,)), ((), ()))
    row = lax.broadcasted_iota(jnp.int32, (per, LANES), 0)
    lane = lax.broadcasted_iota(jnp.int32, (per, LANES), 1)
    diagonal = row == lane % per
    group = lax.broadcasted_iota(jnp.int32, (2, LANES), 1) // per
    second = lax.broadcasted_iota(jnp.int32, (2, LANES), 0)
    ones = jnp.ones(va_ref.shape, jnp.bfloat16)
    fresh_ref[...] = q_ref[:, per:, :]

    def scores(first):
        q = q_ref[first : first + step, :per, :].reshape(step * per, HD)
        return [
            lax.dot_general(q, k_ref[...], nt, preferred_element_type=jnp.float32) for k_ref in (ka_ref, kb_ref)
        ]

    ahead = scores(0)
    for first in range(0, sources, step):
        sa, sb = ahead
        if first + step < sources:
            ahead = scores(first + step)
        top = scale * jnp.maximum(jnp.max(sa, axis=1, keepdims=True), jnp.max(sb, axis=1, keepdims=True))
        wa = jnp.exp2((sa * scale - top).astype(jnp.bfloat16))
        wb = jnp.exp2((sb * scale - top).astype(jnp.bfloat16))
        both = jnp.dot(
            wa, jnp.concatenate([va_ref[...], ones], axis=1), preferred_element_type=jnp.float32
        ) + jnp.dot(wb, jnp.concatenate([vb_ref[...], ones], axis=1), preferred_element_type=jnp.float32)
        total = both[:, HD:]
        out = both[:, :HD] / total
        lse = top + jnp.log(total) * LOG2E
        rows = []
        for s in range(step):
            part = slice(s * per, (s + 1) * per)
            flat = jnp.sum(jnp.where(diagonal, lse[part], 0.0), axis=0, keepdims=True)
            hi = flat.astype(jnp.bfloat16).astype(jnp.float32)
            mid = (flat - hi).astype(jnp.bfloat16).astype(jnp.float32)
            low = flat - hi - mid
            stats = jnp.where(group == 0, hi, jnp.where(group == 1, mid, jnp.where(group == 2, low, 0.0)))
            rows = rows + [out[part], jnp.where(second == 0, stats, 0.0)]
        done = pl.ds(first * (per + 2), step * (per + 2))
        out_ref[done, :] = jnp.concatenate(rows, axis=0).astype(jnp.bfloat16)
        sent.append(pltpu.make_async_copy(out_ref.at[done], out_hbm.at[done], sems.at[first // step]))
        sent[-1].start()
    for copy in sent:
        copy.wait()


def fresh_kernel(tokens, rows_ref, kv_ref, kv1_ref, kv2_ref, kv3_ref, out_ref, lse_ref):
    sources = kv_ref.shape[0]
    place = lax.axis_index("seq")
    core, odd = place % KVH, place // KVH % 2
    scale = LOG2E * HD**-0.5
    nt = (((1,), (1,)), ((), ()))
    column = lax.broadcasted_iota(jnp.int32, (tokens, sources * tokens), 1)
    query_pos = place * tokens + lax.broadcasted_iota(jnp.int32, column.shape, 0)
    visible = (column <= query_pos) & (column // BLK == query_pos // BLK)
    visible = jnp.concatenate([visible.astype(jnp.int32)] * GROUP, axis=0) > 0
    ones = jnp.ones((sources * tokens, HD), jnp.bfloat16)
    here, near, far, both = [
        ref[...].astype(jnp.float32).reshape(sources * tokens, HD) for ref in (kv_ref, kv1_ref, kv2_ref, kv3_ref)
    ]
    keys = [jnp.where(odd == 0, here, far), jnp.where(odd == 0, near, both)]
    values = [jnp.where(odd == 0, far, here), jnp.where(odd == 0, both, near)]
    for g in range(KVH):
        k = jnp.where(core == g, keys[0], keys[1]).astype(jnp.bfloat16)
        v = jnp.where(core == g, values[0], values[1]).astype(jnp.bfloat16)
        q = rows_ref[g].astype(jnp.bfloat16)
        s = lax.dot_general(q, k, nt, preferred_element_type=jnp.float32) * scale
        s = jnp.where(visible, s, LOW_SCORE)
        top = jnp.max(s, axis=1, keepdims=True)
        w = jnp.where(visible, jnp.exp2(s - top), 0.0).astype(jnp.bfloat16)
        total_out = jnp.dot(w, jnp.concatenate([v, ones], axis=1), preferred_element_type=jnp.float32)
        total = total_out[:, HD:]
        out_ref[g] = total_out[:, :HD] / total
        lse_ref[g] = top + jnp.log(total) * LOG2E


def project_kernel(per, hist_ref, out_ref, lse_ref, match_ref, first_ref, w_hbm, y_ref, w_ref, sems):
    depth = KVH * HD
    ready = first_ref.shape[0] // depth
    copies = fetch(
        [
            (w_hbm.at[pl.ds((ready + i) * depth, depth)], w_ref.at[pl.ds(i * depth, depth)])
            for i in range(w_ref.shape[0] // depth)
        ],
        sems,
    )
    tokens = y_ref.shape[0]
    holders = match_ref.shape[2] // per
    stride = KVH * (per + 2)
    hist = hist_ref[...].astype(jnp.float32)
    fold = LANES // per
    row = lax.broadcasted_iota(jnp.int32, (holders, LANES), 0)
    lane = lax.broadcasted_iota(jnp.int32, (holders, LANES), 1)

    def times(heads, weights):
        lhs = jnp.concatenate(heads, axis=1).astype(jnp.bfloat16)
        return jnp.dot(lhs, weights, preferred_element_type=jnp.float32)

    heads = []
    for g in range(KVH):
        starts = [m * stride + g * (per + 2) for m in range(holders)]
        outs = jnp.concatenate([hist[i : i + per] for i in starts], axis=0).astype(jnp.bfloat16)
        stats = jnp.concatenate([hist[i + per : i + per + 1] for i in starts], axis=0)
        shift = LANES // 2
        while shift >= per:
            stats = stats + pltpu.roll(stats, shift, 1)
            shift //= 2
        stats = jnp.where(row % fold == lane // per, stats, 0.0)
        lse = jnp.concatenate(
            [
                jnp.sum(jnp.where(row // fold == m, stats, 0.0), axis=0, keepdims=True)
                for m in range(holders // fold)
            ],
            axis=1,
        )
        match = match_ref[g] > 0.5
        lse = jnp.where(match, lse, LOW_SCORE)
        own = lse_ref[g]
        top = jnp.maximum(jnp.max(lse, axis=1, keepdims=True), own)
        w = jnp.where(match, jnp.exp2(lse - top[:, :1]), 0.0)
        own_w = jnp.exp2(own - top)
        hi = w.astype(jnp.bfloat16)
        low = (w - hi.astype(jnp.float32)).astype(jnp.bfloat16)
        num = (
            jnp.dot(hi, outs, preferred_element_type=jnp.float32)
            + jnp.dot(low, outs, preferred_element_type=jnp.float32)
            + own_w * out_ref[g]
        )
        att = num / (jnp.sum(w, axis=1, keepdims=True) + own_w)
        heads = heads + [att[r * tokens : (r + 1) * tokens] for r in range(GROUP)]
        if g == 0:
            y = times(heads[: ready * KVH], first_ref[...])
    for i, copy in enumerate(copies):
        copy.wait()
        y = y + times(heads[(ready + i) * KVH : (ready + i + 1) * KVH], w_ref[i * depth : (i + 1) * depth, :])
    y_ref[...] = y.astype(jnp.bfloat16)


VMEM = pl.BlockSpec(memory_space=pltpu.VMEM)
HBM = pl.BlockSpec(memory_space=pltpu.HBM)
ANY = pl.BlockSpec(memory_space=pl.ANY)


def call(kernel, name, out_shape, specs, *operands, outs=None, scratch=(), flops=0, moved=0, limit=16):
    outs = outs or jax.tree.map(lambda _: VMEM, out_shape)
    return pl.pallas_call(
        kernel,
        name=name,
        out_shape=out_shape,
        in_specs=specs,
        out_specs=outs,
        scratch_shapes=scratch,
        cost_estimate=pl.CostEstimate(flops=flops, bytes_accessed=moved, transcendentals=0),
        compiler_params=pltpu.CompilerParams(vmem_limit_bytes=limit << 20),
    )(*operands)


def body(queries, stretch_keys, stretch_values, cache_keys, cache_values, chosen, out_weight):
    devices = lax.axis_size("seq")
    tokens = queries.shape[0]
    cache_rows = cache_keys.shape[0]
    span = BLK // cache_rows
    chips = span // KVH
    key_blocks = cache_rows * devices // BLK
    capacity = (GROUP * TOPK + key_blocks - 1) // key_blocks + 1
    per = capacity * tokens
    f32, bf16 = jnp.float32, jnp.bfloat16
    picks = chosen.transpose(2, 0, 1)

    def partner(bit):
        return [(i, i ^ bit) for i in range(devices)]

    send = call(
        functools.partial(pack_kernel, capacity),
        "pack",
        jax.ShapeDtypeStruct((key_blocks, chips, KVH, per + tokens, HD), bf16),
        [HBM] * 4,
        picks, queries, stretch_keys, stretch_values,
        outs=ANY,
        scratch=[
            pltpu.SMEM(picks.shape, jnp.int32),
            pltpu.VMEM(queries.shape, bf16),
            pltpu.VMEM(stretch_keys.shape, bf16),
            pltpu.VMEM(stretch_values.shape, bf16),
            pltpu.VMEM((KVH, key_blocks, chips, per + tokens, HD), bf16),
            pltpu.SemaphoreType.DMA((4 + KVH,)),
        ],
        limit=60,
    )
    send, cache_keys, cache_values, picks, queries = lax.optimization_barrier(
        (send, cache_keys, cache_values, picks, queries)
    )
    send = send.reshape(devices, per + tokens, HD)
    got = lax.all_to_all(send, "seq", split_axis=0, concat_axis=0, tiled=True)

    core = lax.axis_index("seq") % KVH

    def halves(head):
        return [lax.dynamic_slice_in_dim(x, head * HD, HD, axis=1) for x in (cache_keys, cache_values)]

    k_own, v_own = halves(core)
    k_peer, v_peer = [lax.ppermute(x, "seq", partner(1)) for x in halves(1 - core)]
    holders = devices // KVH
    rows = devices * per
    back, fresh = call(
        functools.partial(attend_kernel, per),
        "attend",
        (
            jax.ShapeDtypeStruct((devices * (per + 2), HD), bf16),
            jax.ShapeDtypeStruct((devices, tokens, HD), bf16),
        ),
        [VMEM] * 5,
        got, k_own, v_own, k_peer, v_peer,
        outs=(ANY, VMEM),
        scratch=[
            pltpu.VMEM((devices * (per + 2), HD), bf16),
            pltpu.SemaphoreType.DMA((rows // STEP,)),
        ],
        flops=8 * rows * cache_rows * HD,
        moved=4 << 20,
        limit=32,
    )
    back, picks, queries, out_weight = lax.optimization_barrier((back, picks, queries, out_weight))
    back = back.reshape(devices, (per + 2) // 2, 2, HD)
    hist = lax.all_to_all(back, "seq", split_axis=0, concat_axis=0, tiled=True)

    ready = EARLY * KVH * HD
    match, query_rows, first = call(
        functools.partial(masks_kernel, chips, capacity),
        "masks",
        (
            jax.ShapeDtypeStruct((KVH, GROUP * tokens, holders * per), f32),
            jax.ShapeDtypeStruct((KVH, GROUP * tokens, HD), f32),
            jax.ShapeDtypeStruct((ready, out_weight.shape[1]), bf16),
        ),
        [VMEM, VMEM, HBM],
        picks, queries, out_weight,
        scratch=[pltpu.SemaphoreType.DMA((1,))],
        limit=50,
    )

    far = lax.ppermute(fresh, "seq", partner(2))
    near, both = [lax.ppermute(x, "seq", partner(1)) for x in (fresh, far)]
    part = jax.ShapeDtypeStruct((KVH, GROUP * tokens, HD), f32)
    out, lse = call(
        functools.partial(fresh_kernel, tokens),
        "fresh",
        (part, part),
        [VMEM] * 5,
        query_rows, fresh, near, far, both,
        flops=8 * H * tokens * devices * tokens * HD,
        moved=1 << 20,
    )
    return call(
        functools.partial(project_kernel, per),
        "project",
        jax.ShapeDtypeStruct((tokens, out_weight.shape[1]), bf16),
        [VMEM] * 5 + [HBM],
        hist.reshape(devices * (per + 2), HD), out, lse, match, first, out_weight,
        scratch=[
            pltpu.VMEM((out_weight.shape[0] - ready, out_weight.shape[1]), bf16),
            pltpu.SemaphoreType.DMA((GROUP - EARLY,)),
        ],
        flops=2 * tokens * out_weight.size,
        moved=out_weight.size * 2,
        limit=50,
    )


def solution(mesh):
    seq = ("grp", "seq")
    return jax.shard_map(
        body,
        mesh=mesh,
        in_specs=(
            P(seq, None),
            P(seq, None),
            P(seq, None),
            P(seq, None),
            P(seq, None),
            P(seq, None, None),
            P(),
        ),
        out_specs=P(seq, None),
        check_vma=False,
    )
```

```python
import functools
import math

import jax
import jax.numpy as jnp
from jax import lax
from jax.experimental import pallas as pl
from jax.experimental.pallas import tpu as pltpu
from jax.sharding import PartitionSpec as P

H = 14
KVH = 2
HD = 128
BLK = 4096
TOPK = 3
GROUP = H // KVH

LOW_SCORE = -1e30
LOG2E = math.log2(math.e)
LANES = 128
EARLY = 3
STEP = 256


def head_rows(q_ref, g):
    q = q_ref[...].astype(jnp.float32)
    return [q[:, h * HD : (h + 1) * HD] for h in range(g * GROUP, (g + 1) * GROUP)]


def slot_match(chosen_ref, g, block, slot, token):
    rows = lax.broadcasted_iota(jnp.int32, block.shape, 0)
    same_token = token == rows
    seen = jnp.zeros(block.shape, jnp.int32)
    found = []
    for h in range(g * GROUP, (g + 1) * GROUP):
        picked = block == chosen_ref[0, :, h : h + 1]
        for t in range(1, TOPK):
            picked = picked | (block == chosen_ref[t, :, h : h + 1])
        found.append(jnp.where(picked & same_token & (seen == slot), 1.0, 0.0))
        seen = seen + picked.astype(jnp.int32)
    return found


def fetch(pairs, sems):
    copies = [pltpu.make_async_copy(src, dst, sems.at[i]) for i, (src, dst) in enumerate(pairs)]
    for copy in copies:
        copy.start()
    return copies


def slot_spread(chosen_ref, g, capacity, tokens, key_blocks):
    lane = lax.broadcasted_iota(jnp.int32, (tokens, LANES), 1)
    head = lane // tokens
    same_token = (lane % tokens == lax.broadcasted_iota(jnp.int32, lane.shape, 0)) & (head < GROUP)
    picks = [[chosen_ref[t, 0, g * GROUP + r] for r in range(GROUP)] for t in range(TOPK)]
    places = []
    for t in range(TOPK):
        block = jnp.zeros(lane.shape, jnp.int32)
        for r in range(GROUP):
            block = jnp.where(head == r, picks[t][r], block)
        rank = jnp.zeros(lane.shape, jnp.int32)
        for r in range(GROUP - 1):
            taken = block == picks[0][r]
            for other in range(1, TOPK):
                taken = taken | (block == picks[other][r])
            rank = rank + jnp.where(taken & (head > r), 1, 0)
        places.append(jnp.where(same_token, block * capacity + rank, -1))
    rows = []
    for place in range(key_blocks * capacity):
        found = places[0] == place
        for t in range(1, TOPK):
            found = found | (places[t] == place)
        rows.append(jnp.where(found, 1.0, 0.0))
    return jnp.concatenate(rows, axis=0).astype(jnp.bfloat16)


def pack_kernel(capacity, chosen_hbm, q_hbm, k_hbm, v_hbm, send_hbm, chosen_ref, q_ref, k_ref, v_ref, send_ref, sems):
    copies = fetch([(chosen_hbm, chosen_ref), (q_hbm, q_ref), (k_hbm, k_ref), (v_hbm, v_ref)], sems)
    tokens = q_ref.shape[0]
    per = capacity * tokens
    key_blocks, chips = send_ref.shape[1:3]
    copies[0].wait()
    spread = [slot_spread(chosen_ref, g, capacity, tokens, key_blocks) for g in range(KVH)]
    for copy in copies[1:]:
        copy.wait()
    sent = []
    for g in range(KVH):
        rows = head_rows(q_ref, g)
        rows = rows + [jnp.zeros_like(rows[0])] * (LANES // tokens - GROUP)
        rows = jnp.concatenate(rows, axis=0).astype(jnp.bfloat16)
        slots = jnp.dot(spread[g], rows, preferred_element_type=jnp.float32).astype(jnp.bfloat16)
        cols = slice(g * HD, (g + 1) * HD)
        fresh = [k_ref[:, cols], v_ref[:, cols]]
        for b in range(key_blocks):
            for chip in range(chips):
                send_ref[g, b, chip, :per, :] = slots[b * per : (b + 1) * per]
                send_ref[g, b, chip, per:, :] = fresh[chip % 2]
        sent.append(pltpu.make_async_copy(send_ref.at[g], send_hbm.at[:, :, g], sems.at[4 + g]))
        sent[g].start()
    for copy in sent:
        copy.wait()


def masks_kernel(chips, capacity, chosen_ref, q_ref, w_hbm, match_ref, rows_ref, w_ref, sems):
    copies = fetch([(w_hbm.at[: w_ref.shape[0]], w_ref)], sems)
    tokens = q_ref.shape[0]
    per = capacity * tokens
    lane = lax.broadcasted_iota(jnp.int32, (tokens, match_ref.shape[2]), 1)
    block, slot, token = lane // (per * chips), lane % per // tokens, lane % tokens
    for g in range(KVH):
        match_ref[g] = jnp.concatenate(slot_match(chosen_ref, g, block, slot, token), axis=0)
        rows_ref[g] = jnp.concatenate(head_rows(q_ref, g), axis=0)
    for copy in copies:
        copy.wait()


def attend_kernel(per, q_ref, ka_ref, va_ref, kb_ref, vb_ref, out_hbm, fresh_ref, out_ref, sems):
    sources = q_ref.shape[0]
    sent = []
    step = STEP // per
    scale = LOG2E * HD**-0.5
    row = lax.broadcasted_iota(jnp.int32, (per, LANES), 0)
    lane = lax.broadcasted_iota(jnp.int32, (per, LANES), 1)
    diagonal = row == lane % per
    group = lax.broadcasted_iota(jnp.int32, (2, LANES), 1) // per
    second = lax.broadcasted_iota(jnp.int32, (2, LANES), 0)
    ones = jnp.ones(va_ref.shape, jnp.bfloat16)
    fresh_ref[...] = q_ref[:, per:, :]

    def scores(first):
        q = q_ref[first : first + step, :per, :].reshape(step * per, HD)
        return [jnp.dot(q, k_ref[...], preferred_element_type=jnp.float32) for k_ref in (ka_ref, kb_ref)]

    ahead = scores(0)
    for first in range(0, sources, step):
        sa, sb = ahead
        if first + step < sources:
            ahead = scores(first + step)
        top = scale * jnp.maximum(jnp.max(sa, axis=1, keepdims=True), jnp.max(sb, axis=1, keepdims=True))
        wa = jnp.exp2(sa * scale - top).astype(jnp.bfloat16)
        wb = jnp.exp2(sb * scale - top).astype(jnp.bfloat16)
        both = jnp.dot(
            wa, jnp.concatenate([va_ref[...], ones], axis=1), preferred_element_type=jnp.float32
        ) + jnp.dot(wb, jnp.concatenate([vb_ref[...], ones], axis=1), preferred_element_type=jnp.float32)
        total = both[:, HD:]
        out = both[:, :HD] / total
        lse = top + jnp.log(total) * LOG2E
        rows = []
        for s in range(step):
            part = slice(s * per, (s + 1) * per)
            flat = jnp.sum(jnp.where(diagonal, lse[part], 0.0), axis=0, keepdims=True)
            hi = flat.astype(jnp.bfloat16).astype(jnp.float32)
            mid = (flat - hi).astype(jnp.bfloat16).astype(jnp.float32)
            low = flat - hi - mid
            stats = jnp.where(group == 0, hi, jnp.where(group == 1, mid, jnp.where(group == 2, low, 0.0)))
            rows = rows + [out[part], jnp.where(second == 0, stats, 0.0)]
        done = pl.ds(first * (per + 2), step * (per + 2))
        out_ref[done, :] = jnp.concatenate(rows, axis=0).astype(jnp.bfloat16)
        sent.append(pltpu.make_async_copy(out_ref.at[done], out_hbm.at[done], sems.at[first // step]))
        sent[-1].start()
    for copy in sent:
        copy.wait()


def fresh_kernel(tokens, rows_ref, kv_ref, kv1_ref, kv2_ref, kv3_ref, out_ref, lse_ref):
    sources = kv_ref.shape[0]
    place = lax.axis_index("seq")
    core, odd = place % KVH, place // KVH % 2
    scale = LOG2E * HD**-0.5
    nt = (((1,), (1,)), ((), ()))
    column = lax.broadcasted_iota(jnp.int32, (tokens, sources * tokens), 1)
    query_pos = place * tokens + lax.broadcasted_iota(jnp.int32, column.shape, 0)
    visible = (column <= query_pos) & (column // BLK == query_pos // BLK)
    visible = jnp.concatenate([visible.astype(jnp.int32)] * GROUP, axis=0) > 0
    ones = jnp.ones((sources * tokens, HD), jnp.bfloat16)
    here, near, far, both = [
        ref[...].astype(jnp.float32).reshape(sources * tokens, HD) for ref in (kv_ref, kv1_ref, kv2_ref, kv3_ref)
    ]
    keys = [jnp.where(odd == 0, here, far), jnp.where(odd == 0, near, both)]
    values = [jnp.where(odd == 0, far, here), jnp.where(odd == 0, both, near)]
    for g in range(KVH):
        k = jnp.where(core == g, keys[0], keys[1]).astype(jnp.bfloat16)
        v = jnp.where(core == g, values[0], values[1]).astype(jnp.bfloat16)
        q = rows_ref[g].astype(jnp.bfloat16)
        s = lax.dot_general(q, k, nt, preferred_element_type=jnp.float32) * scale
        s = jnp.where(visible, s, LOW_SCORE)
        top = jnp.max(s, axis=1, keepdims=True)
        w = jnp.where(visible, jnp.exp2(s - top), 0.0).astype(jnp.bfloat16)
        total_out = jnp.dot(w, jnp.concatenate([v, ones], axis=1), preferred_element_type=jnp.float32)
        total = total_out[:, HD:]
        out_ref[g] = total_out[:, :HD] / total
        lse_ref[g] = top + jnp.log(total) * LOG2E


def project_kernel(per, hist_ref, out_ref, lse_ref, match_ref, first_ref, w_hbm, y_ref, w_ref, sems):
    depth = KVH * HD
    ready = first_ref.shape[0] // depth
    copies = fetch(
        [
            (w_hbm.at[pl.ds((ready + i) * depth, depth)], w_ref.at[pl.ds(i * depth, depth)])
            for i in range(w_ref.shape[0] // depth)
        ],
        sems,
    )
    tokens = y_ref.shape[0]
    holders = match_ref.shape[2] // per
    stride = KVH * (per + 2)
    hist = hist_ref[...].astype(jnp.float32)
    fold = LANES // per
    row = lax.broadcasted_iota(jnp.int32, (holders, LANES), 0)
    lane = lax.broadcasted_iota(jnp.int32, (holders, LANES), 1)

    def times(heads, weights):
        lhs = jnp.concatenate(heads, axis=1).astype(jnp.bfloat16)
        return jnp.dot(lhs, weights, preferred_element_type=jnp.float32)

    heads = []
    for g in range(KVH):
        starts = [m * stride + g * (per + 2) for m in range(holders)]
        outs = jnp.concatenate([hist[i : i + per] for i in starts], axis=0).astype(jnp.bfloat16)
        stats = jnp.concatenate([hist[i + per : i + per + 1] for i in starts], axis=0)
        shift = LANES // 2
        while shift >= per:
            stats = stats + pltpu.roll(stats, shift, 1)
            shift //= 2
        stats = jnp.where(row % fold == lane // per, stats, 0.0)
        lse = jnp.concatenate(
            [
                jnp.sum(jnp.where(row // fold == m, stats, 0.0), axis=0, keepdims=True)
                for m in range(holders // fold)
            ],
            axis=1,
        )
        match = match_ref[g] > 0.5
        lse = jnp.where(match, lse, LOW_SCORE)
        own = lse_ref[g]
        top = jnp.maximum(jnp.max(lse, axis=1, keepdims=True), own)
        w = jnp.where(match, jnp.exp2(lse - top[:, :1]), 0.0)
        own_w = jnp.exp2(own - top)
        hi = w.astype(jnp.bfloat16)
        low = (w - hi.astype(jnp.float32)).astype(jnp.bfloat16)
        num = (
            jnp.dot(hi, outs, preferred_element_type=jnp.float32)
            + jnp.dot(low, outs, preferred_element_type=jnp.float32)
            + own_w * out_ref[g]
        )
        att = num / (jnp.sum(w, axis=1, keepdims=True) + own_w)
        heads = heads + [att[r * tokens : (r + 1) * tokens] for r in range(GROUP)]
        if g == 0:
            y = times(heads[: ready * KVH], first_ref[...])
    for i, copy in enumerate(copies):
        copy.wait()
        y = y + times(heads[(ready + i) * KVH : (ready + i + 1) * KVH], w_ref[i * depth : (i + 1) * depth, :])
    y_ref[...] = y.astype(jnp.bfloat16)


VMEM = pl.BlockSpec(memory_space=pltpu.VMEM)
HBM = pl.BlockSpec(memory_space=pltpu.HBM)
ANY = pl.BlockSpec(memory_space=pl.ANY)


def call(kernel, name, out_shape, specs, *operands, outs=None, scratch=(), flops=0, moved=0, limit=16):
    outs = outs or jax.tree.map(lambda _: VMEM, out_shape)
    return pl.pallas_call(
        kernel,
        name=name,
        out_shape=out_shape,
        in_specs=specs,
        out_specs=outs,
        scratch_shapes=scratch,
        cost_estimate=pl.CostEstimate(flops=flops, bytes_accessed=moved, transcendentals=0),
        compiler_params=pltpu.CompilerParams(vmem_limit_bytes=limit << 20),
    )(*operands)


def body(queries, stretch_keys, stretch_values, cache_keys, cache_values, chosen, out_weight):
    devices = lax.axis_size("seq")
    tokens = queries.shape[0]
    cache_rows = cache_keys.shape[0]
    span = BLK // cache_rows
    chips = span // KVH
    key_blocks = cache_rows * devices // BLK
    capacity = (GROUP * TOPK + key_blocks - 1) // key_blocks + 1
    per = capacity * tokens
    f32, bf16 = jnp.float32, jnp.bfloat16
    picks = chosen.transpose(2, 0, 1)

    def partner(bit):
        return [(i, i ^ bit) for i in range(devices)]

    send = call(
        functools.partial(pack_kernel, capacity),
        "pack",
        jax.ShapeDtypeStruct((key_blocks, chips, KVH, per + tokens, HD), bf16),
        [HBM] * 4,
        picks, queries, stretch_keys, stretch_values,
        outs=ANY,
        scratch=[
            pltpu.SMEM(picks.shape, jnp.int32),
            pltpu.VMEM(queries.shape, bf16),
            pltpu.VMEM(stretch_keys.shape, bf16),
            pltpu.VMEM(stretch_values.shape, bf16),
            pltpu.VMEM((KVH, key_blocks, chips, per + tokens, HD), bf16),
            pltpu.SemaphoreType.DMA((4 + KVH,)),
        ],
        limit=60,
    )
    send, cache_keys, cache_values, picks, queries = lax.optimization_barrier(
        (send, cache_keys, cache_values, picks, queries)
    )
    send = send.reshape(devices, per + tokens, HD)
    got = lax.all_to_all(send, "seq", split_axis=0, concat_axis=0, tiled=True)

    core = lax.axis_index("seq") % KVH

    def halves(head):
        keys, values = [lax.dynamic_slice_in_dim(x, head * HD, HD, axis=1) for x in (cache_keys, cache_values)]
        return keys.T, values

    k_own, v_own = halves(core)
    k_peer, v_peer = [lax.ppermute(x, "seq", partner(1)) for x in halves(1 - core)]
    holders = devices // KVH
    rows = devices * per
    back, fresh = call(
        functools.partial(attend_kernel, per),
        "attend",
        (
            jax.ShapeDtypeStruct((devices * (per + 2), HD), bf16),
            jax.ShapeDtypeStruct((devices, tokens, HD), bf16),
        ),
        [VMEM] * 5,
        got, k_own, v_own, k_peer, v_peer,
        outs=(ANY, VMEM),
        scratch=[
            pltpu.VMEM((devices * (per + 2), HD), bf16),
            pltpu.SemaphoreType.DMA((rows // STEP,)),
        ],
        flops=8 * rows * cache_rows * HD,
        moved=4 << 20,
        limit=32,
    )
    back, picks, queries, out_weight = lax.optimization_barrier((back, picks, queries, out_weight))
    back = back.reshape(devices, (per + 2) // 2, 2, HD)
    hist = lax.all_to_all(back, "seq", split_axis=0, concat_axis=0, tiled=True)

    ready = EARLY * KVH * HD
    match, query_rows, first = call(
        functools.partial(masks_kernel, chips, capacity),
        "masks",
        (
            jax.ShapeDtypeStruct((KVH, GROUP * tokens, holders * per), f32),
            jax.ShapeDtypeStruct((KVH, GROUP * tokens, HD), f32),
            jax.ShapeDtypeStruct((ready, out_weight.shape[1]), bf16),
        ),
        [VMEM, VMEM, HBM],
        picks, queries, out_weight,
        scratch=[pltpu.SemaphoreType.DMA((1,))],
        limit=50,
    )

    far = lax.ppermute(fresh, "seq", partner(2))
    near, both = [lax.ppermute(x, "seq", partner(1)) for x in (fresh, far)]
    part = jax.ShapeDtypeStruct((KVH, GROUP * tokens, HD), f32)
    out, lse = call(
        functools.partial(fresh_kernel, tokens),
        "fresh",
        (part, part),
        [VMEM] * 5,
        query_rows, fresh, near, far, both,
        flops=8 * H * tokens * devices * tokens * HD,
        moved=1 << 20,
    )
    return call(
        functools.partial(project_kernel, per),
        "project",
        jax.ShapeDtypeStruct((tokens, out_weight.shape[1]), bf16),
        [VMEM] * 5 + [HBM],
        hist.reshape(devices * (per + 2), HD), out, lse, match, first, out_weight,
        scratch=[
            pltpu.VMEM((out_weight.shape[0] - ready, out_weight.shape[1]), bf16),
            pltpu.SemaphoreType.DMA((GROUP - EARLY,)),
        ],
        flops=2 * tokens * out_weight.size,
        moved=out_weight.size * 2,
        limit=50,
    )


def solution(mesh):
    seq = ("grp", "seq")
    return jax.shard_map(
        body,
        mesh=mesh,
        in_specs=(
            P(seq, None),
            P(seq, None),
            P(seq, None),
            P(seq, None),
            P(seq, None),
            P(seq, None, None),
            P(),
        ),
        out_specs=P(seq, None),
        check_vma=False,
    )
```

```python
import functools
import math

import jax
import jax.numpy as jnp
from jax import lax
from jax.experimental import pallas as pl
from jax.experimental.pallas import tpu as pltpu
from jax.sharding import PartitionSpec as P

H = 14
KVH = 2
HD = 128
BLK = 4096
TOPK = 3
GROUP = H // KVH

LOW_SCORE = -1e30
LOG2E = math.log2(math.e)
LANES = 128
EARLY = 3
STEP = 256


def head_rows(q_ref, g):
    q = q_ref[...].astype(jnp.float32)
    return [q[:, h * HD : (h + 1) * HD] for h in range(g * GROUP, (g + 1) * GROUP)]


def slot_match(chosen_ref, g, block, slot, token):
    rows = lax.broadcasted_iota(jnp.int32, block.shape, 0)
    same_token = token == rows
    seen = jnp.zeros(block.shape, jnp.int32)
    found = []
    for h in range(g * GROUP, (g + 1) * GROUP):
        picked = block == chosen_ref[0, :, h : h + 1]
        for t in range(1, TOPK):
            picked = picked | (block == chosen_ref[t, :, h : h + 1])
        found.append(jnp.where(picked & same_token & (seen == slot), 1.0, 0.0))
        seen = seen + picked.astype(jnp.int32)
    return found


def fetch(pairs, sems):
    copies = [pltpu.make_async_copy(src, dst, sems.at[i]) for i, (src, dst) in enumerate(pairs)]
    for copy in copies:
        copy.start()
    return copies


def slot_spread(chosen_ref, g, capacity, tokens, key_blocks):
    lane = lax.broadcasted_iota(jnp.int32, (tokens, LANES), 1)
    head = lane // tokens
    same_token = (lane % tokens == lax.broadcasted_iota(jnp.int32, lane.shape, 0)) & (head < GROUP)
    picks = [[chosen_ref[t, 0, g * GROUP + r] for r in range(GROUP)] for t in range(TOPK)]
    places = []
    for t in range(TOPK):
        block = jnp.zeros(lane.shape, jnp.int32)
        for r in range(GROUP):
            block = jnp.where(head == r, picks[t][r], block)
        rank = jnp.zeros(lane.shape, jnp.int32)
        for r in range(GROUP - 1):
            taken = block == picks[0][r]
            for other in range(1, TOPK):
                taken = taken | (block == picks[other][r])
            rank = rank + jnp.where(taken & (head > r), 1, 0)
        places.append(jnp.where(same_token, block * capacity + rank, -1))
    rows = []
    for place in range(key_blocks * capacity):
        found = places[0] == place
        for t in range(1, TOPK):
            found = found | (places[t] == place)
        rows.append(jnp.where(found, 1.0, 0.0))
    return jnp.concatenate(rows, axis=0).astype(jnp.bfloat16)


def pack_kernel(capacity, chosen_hbm, q_hbm, k_hbm, v_hbm, send_hbm, chosen_ref, q_ref, k_ref, v_ref, send_ref, sems):
    copies = fetch([(chosen_hbm, chosen_ref), (q_hbm, q_ref), (k_hbm, k_ref), (v_hbm, v_ref)], sems)
    tokens = q_ref.shape[0]
    per = capacity * tokens
    key_blocks, chips = send_ref.shape[1:3]
    copies[0].wait()
    spread = [slot_spread(chosen_ref, g, capacity, tokens, key_blocks) for g in range(KVH)]
    for copy in copies[1:]:
        copy.wait()
    sent = []
    for g in range(KVH):
        rows = head_rows(q_ref, g)
        rows = rows + [jnp.zeros_like(rows[0])] * (LANES // tokens - GROUP)
        rows = jnp.concatenate(rows, axis=0).astype(jnp.bfloat16)
        slots = jnp.dot(spread[g], rows, preferred_element_type=jnp.float32).astype(jnp.bfloat16)
        cols = slice(g * HD, (g + 1) * HD)
        fresh = [k_ref[:, cols], v_ref[:, cols]]
        for b in range(key_blocks):
            for chip in range(chips):
                to = (g, key_blocks - 1 - b, chips - 1 - chip)
                send_ref[(*to, slice(0, per))] = slots[b * per : (b + 1) * per]
                send_ref[(*to, slice(per, None))] = fresh[chip % 2]
        sent.append(pltpu.make_async_copy(send_ref.at[g], send_hbm.at[:, :, KVH - 1 - g], sems.at[4 + g]))
        sent[g].start()
    for copy in sent:
        copy.wait()


def masks_kernel(chips, capacity, chosen_ref, q_ref, w_hbm, match_ref, rows_ref, w_ref, sems):
    copies = fetch([(w_hbm.at[: w_ref.shape[0]], w_ref)], sems)
    tokens = q_ref.shape[0]
    per = capacity * tokens
    lane = lax.broadcasted_iota(jnp.int32, (tokens, match_ref.shape[2]), 1)
    block, slot, token = lane // (per * chips), lane % per // tokens, lane % tokens
    for g in range(KVH):
        match_ref[g] = jnp.concatenate(slot_match(chosen_ref, g, block, slot, token), axis=0)
        rows_ref[g] = jnp.concatenate(head_rows(q_ref, g), axis=0)
    for copy in copies:
        copy.wait()


def attend_kernel(per, q_ref, ka_ref, va_ref, kb_ref, vb_ref, out_hbm, fresh_ref, out_ref, sems):
    sources = q_ref.shape[0]
    sent = []
    step = STEP // per
    scale = LOG2E * HD**-0.5
    row = lax.broadcasted_iota(jnp.int32, (per, LANES), 0)
    lane = lax.broadcasted_iota(jnp.int32, (per, LANES), 1)
    diagonal = row == lane % per
    group = lax.broadcasted_iota(jnp.int32, (2, LANES), 1) // per
    second = lax.broadcasted_iota(jnp.int32, (2, LANES), 0)
    ones = jnp.ones(va_ref.shape, jnp.bfloat16)
    fresh_ref[...] = q_ref[:, per:, :]

    def scores(first):
        q = q_ref[first : first + step, :per, :].reshape(step * per, HD)
        return [jnp.dot(q, k_ref[...], preferred_element_type=jnp.float32) for k_ref in (ka_ref, kb_ref)]

    ahead = scores(0)
    for first in range(0, sources, step):
        sa, sb = ahead
        if first + step < sources:
            ahead = scores(first + step)
        top = scale * jnp.maximum(jnp.max(sa, axis=1, keepdims=True), jnp.max(sb, axis=1, keepdims=True))
        wa = jnp.exp2(sa * scale - top).astype(jnp.bfloat16)
        wb = jnp.exp2(sb * scale - top).astype(jnp.bfloat16)
        both = jnp.dot(
            wa, jnp.concatenate([va_ref[...], ones], axis=1), preferred_element_type=jnp.float32
        ) + jnp.dot(wb, jnp.concatenate([vb_ref[...], ones], axis=1), preferred_element_type=jnp.float32)
        total = both[:, HD:]
        out = both[:, :HD] / total
        lse = top + jnp.log(total) * LOG2E
        rows = []
        for s in range(step):
            part = slice(s * per, (s + 1) * per)
            flat = jnp.sum(jnp.where(diagonal, lse[part], 0.0), axis=0, keepdims=True)
            hi = flat.astype(jnp.bfloat16).astype(jnp.float32)
            mid = (flat - hi).astype(jnp.bfloat16).astype(jnp.float32)
            low = flat - hi - mid
            stats = jnp.where(group == 0, hi, jnp.where(group == 1, mid, jnp.where(group == 2, low, 0.0)))
            rows = rows + [out[part], jnp.where(second == 0, stats, 0.0)]
        done = pl.ds(first * (per + 2), step * (per + 2))
        out_ref[done, :] = jnp.concatenate(rows, axis=0).astype(jnp.bfloat16)
        sent.append(pltpu.make_async_copy(out_ref.at[done], out_hbm.at[done], sems.at[first // step]))
        sent[-1].start()
    for copy in sent:
        copy.wait()


def fresh_kernel(tokens, rows_ref, kv_ref, kv1_ref, kv2_ref, kv3_ref, out_ref, lse_ref):
    sources = kv_ref.shape[0]
    place = lax.axis_index("seq")
    core, odd = place % KVH, place // KVH % 2
    scale = LOG2E * HD**-0.5
    nt = (((1,), (1,)), ((), ()))
    column = lax.broadcasted_iota(jnp.int32, (tokens, sources * tokens), 1)
    query_pos = place * tokens + lax.broadcasted_iota(jnp.int32, column.shape, 0)
    key_pos = (sources - 1 - column // tokens) * tokens + column % tokens
    visible = (key_pos <= query_pos) & (key_pos // BLK == query_pos // BLK)
    visible = jnp.concatenate([visible.astype(jnp.int32)] * GROUP, axis=0) > 0
    ones = jnp.ones((sources * tokens, HD), jnp.bfloat16)
    here, near, far, both = [
        ref[...].astype(jnp.float32).reshape(sources * tokens, HD) for ref in (kv_ref, kv1_ref, kv2_ref, kv3_ref)
    ]
    keys = [jnp.where(odd == 0, here, far), jnp.where(odd == 0, near, both)]
    values = [jnp.where(odd == 0, far, here), jnp.where(odd == 0, both, near)]
    for g in range(KVH):
        k = jnp.where(core == g, keys[0], keys[1]).astype(jnp.bfloat16)
        v = jnp.where(core == g, values[0], values[1]).astype(jnp.bfloat16)
        q = rows_ref[g].astype(jnp.bfloat16)
        s = lax.dot_general(q, k, nt, preferred_element_type=jnp.float32) * scale
        s = jnp.where(visible, s, LOW_SCORE)
        top = jnp.max(s, axis=1, keepdims=True)
        w = jnp.where(visible, jnp.exp2(s - top), 0.0).astype(jnp.bfloat16)
        total_out = jnp.dot(w, jnp.concatenate([v, ones], axis=1), preferred_element_type=jnp.float32)
        total = total_out[:, HD:]
        out_ref[g] = total_out[:, :HD] / total
        lse_ref[g] = top + jnp.log(total) * LOG2E


def project_kernel(per, hist_ref, out_ref, lse_ref, match_ref, first_ref, w_hbm, y_ref, w_ref, sems):
    depth = KVH * HD
    ready = first_ref.shape[0] // depth
    copies = fetch(
        [
            (w_hbm.at[pl.ds((ready + i) * depth, depth)], w_ref.at[pl.ds(i * depth, depth)])
            for i in range(w_ref.shape[0] // depth)
        ],
        sems,
    )
    tokens = y_ref.shape[0]
    holders = match_ref.shape[2] // per
    hist = hist_ref[...].astype(jnp.float32)
    fold = LANES // per
    row = lax.broadcasted_iota(jnp.int32, (holders, LANES), 0)
    lane = lax.broadcasted_iota(jnp.int32, (holders, LANES), 1)

    def times(heads, weights):
        lhs = jnp.concatenate(heads, axis=1).astype(jnp.bfloat16)
        return jnp.dot(lhs, weights, preferred_element_type=jnp.float32)

    heads = []
    for g in range(KVH):
        starts = [(KVH * (holders - m) - 1 - g) * (per + 2) for m in range(holders)]
        outs = jnp.concatenate([hist[i : i + per] for i in starts], axis=0).astype(jnp.bfloat16)
        stats = jnp.concatenate([hist[i + per : i + per + 1] for i in starts], axis=0)
        shift = LANES // 2
        while shift >= per:
            stats = stats + pltpu.roll(stats, shift, 1)
            shift //= 2
        stats = jnp.where(row % fold == lane // per, stats, 0.0)
        lse = jnp.concatenate(
            [
                jnp.sum(jnp.where(row // fold == m, stats, 0.0), axis=0, keepdims=True)
                for m in range(holders // fold)
            ],
            axis=1,
        )
        match = match_ref[g] > 0.5
        lse = jnp.where(match, lse, LOW_SCORE)
        own = lse_ref[g]
        top = jnp.maximum(jnp.max(lse, axis=1, keepdims=True), own)
        w = jnp.where(match, jnp.exp2(lse - top[:, :1]), 0.0)
        own_w = jnp.exp2(own - top)
        hi = w.astype(jnp.bfloat16)
        low = (w - hi.astype(jnp.float32)).astype(jnp.bfloat16)
        num = (
            jnp.dot(hi, outs, preferred_element_type=jnp.float32)
            + jnp.dot(low, outs, preferred_element_type=jnp.float32)
            + own_w * out_ref[g]
        )
        att = num / (jnp.sum(w, axis=1, keepdims=True) + own_w)
        heads = heads + [att[r * tokens : (r + 1) * tokens] for r in range(GROUP)]
        if g == 0:
            y = times(heads[: ready * KVH], first_ref[...])
    for i, copy in enumerate(copies):
        copy.wait()
        y = y + times(heads[(ready + i) * KVH : (ready + i + 1) * KVH], w_ref[i * depth : (i + 1) * depth, :])
    y_ref[...] = y.astype(jnp.bfloat16)


VMEM = pl.BlockSpec(memory_space=pltpu.VMEM)
HBM = pl.BlockSpec(memory_space=pltpu.HBM)
ANY = pl.BlockSpec(memory_space=pl.ANY)


def call(kernel, name, out_shape, specs, *operands, outs=None, scratch=(), flops=0, moved=0, limit=16):
    outs = outs or jax.tree.map(lambda _: VMEM, out_shape)
    return pl.pallas_call(
        kernel,
        name=name,
        out_shape=out_shape,
        in_specs=specs,
        out_specs=outs,
        scratch_shapes=scratch,
        cost_estimate=pl.CostEstimate(flops=flops, bytes_accessed=moved, transcendentals=0),
        compiler_params=pltpu.CompilerParams(vmem_limit_bytes=limit << 20),
    )(*operands)


def body(queries, stretch_keys, stretch_values, cache_keys, cache_values, chosen, out_weight):
    devices = lax.axis_size("seq")
    tokens = queries.shape[0]
    cache_rows = cache_keys.shape[0]
    span = BLK // cache_rows
    chips = span // KVH
    key_blocks = cache_rows * devices // BLK
    capacity = (GROUP * TOPK + key_blocks - 1) // key_blocks + 1
    per = capacity * tokens
    f32, bf16 = jnp.float32, jnp.bfloat16
    picks = chosen.transpose(2, 0, 1)

    def partner(bit):
        return [(i, i ^ bit) for i in range(devices)]

    send = call(
        functools.partial(pack_kernel, capacity),
        "pack",
        jax.ShapeDtypeStruct((key_blocks, chips, KVH, per + tokens, HD), bf16),
        [HBM] * 4,
        picks, queries, stretch_keys, stretch_values,
        outs=ANY,
        scratch=[
            pltpu.SMEM(picks.shape, jnp.int32),
            pltpu.VMEM(queries.shape, bf16),
            pltpu.VMEM(stretch_keys.shape, bf16),
            pltpu.VMEM(stretch_values.shape, bf16),
            pltpu.VMEM((KVH, key_blocks, chips, per + tokens, HD), bf16),
            pltpu.SemaphoreType.DMA((4 + KVH,)),
        ],
        limit=60,
    )
    send, cache_keys, cache_values, picks, queries = lax.optimization_barrier(
        (send, cache_keys, cache_values, picks, queries)
    )

    def exchange(x):
        ranks = [list(range(devices))[::-1]]
        return lax.all_to_all(x, "seq", split_axis=0, concat_axis=0, axis_index_groups=ranks, tiled=True)

    got = exchange(send.reshape(devices, per + tokens, HD))

    core = lax.axis_index("seq") % KVH

    def halves(head):
        keys, values = [lax.dynamic_slice_in_dim(x, head * HD, HD, axis=1) for x in (cache_keys, cache_values)]
        return keys.T, values

    k_own, v_own = halves(core)
    k_peer, v_peer = [lax.ppermute(x, "seq", partner(1)) for x in halves(1 - core)]
    holders = devices // KVH
    rows = devices * per
    back, fresh = call(
        functools.partial(attend_kernel, per),
        "attend",
        (
            jax.ShapeDtypeStruct((devices * (per + 2), HD), bf16),
            jax.ShapeDtypeStruct((devices, tokens, HD), bf16),
        ),
        [VMEM] * 5,
        got, k_own, v_own, k_peer, v_peer,
        outs=(ANY, VMEM),
        scratch=[
            pltpu.VMEM((devices * (per + 2), HD), bf16),
            pltpu.SemaphoreType.DMA((rows // STEP,)),
        ],
        flops=8 * rows * cache_rows * HD,
        moved=4 << 20,
        limit=32,
    )
    back, picks, queries, out_weight = lax.optimization_barrier((back, picks, queries, out_weight))
    hist = exchange(back.reshape(devices, (per + 2) // 2, 2, HD))

    ready = EARLY * KVH * HD
    match, query_rows, first = call(
        functools.partial(masks_kernel, chips, capacity),
        "masks",
        (
            jax.ShapeDtypeStruct((KVH, GROUP * tokens, holders * per), f32),
            jax.ShapeDtypeStruct((KVH, GROUP * tokens, HD), f32),
            jax.ShapeDtypeStruct((ready, out_weight.shape[1]), bf16),
        ),
        [VMEM, VMEM, HBM],
        picks, queries, out_weight,
        scratch=[pltpu.SemaphoreType.DMA((1,))],
        limit=50,
    )

    far = lax.ppermute(fresh, "seq", partner(2))
    near, both = [lax.ppermute(x, "seq", partner(1)) for x in (fresh, far)]
    part = jax.ShapeDtypeStruct((KVH, GROUP * tokens, HD), f32)
    out, lse = call(
        functools.partial(fresh_kernel, tokens),
        "fresh",
        (part, part),
        [VMEM] * 5,
        query_rows, fresh, near, far, both,
        flops=8 * H * tokens * devices * tokens * HD,
        moved=1 << 20,
    )
    return call(
        functools.partial(project_kernel, per),
        "project",
        jax.ShapeDtypeStruct((tokens, out_weight.shape[1]), bf16),
        [VMEM] * 5 + [HBM],
        hist.reshape(devices * (per + 2), HD), out, lse, match, first, out_weight,
        scratch=[
            pltpu.VMEM((out_weight.shape[0] - ready, out_weight.shape[1]), bf16),
            pltpu.SemaphoreType.DMA((GROUP - EARLY,)),
        ],
        flops=2 * tokens * out_weight.size,
        moved=out_weight.size * 2,
        limit=50,
    )


def solution(mesh):
    seq = ("grp", "seq")
    return jax.shard_map(
        body,
        mesh=mesh,
        in_specs=(
            P(seq, None),
            P(seq, None),
            P(seq, None),
            P(seq, None),
            P(seq, None),
            P(seq, None, None),
            P(),
        ),
        out_specs=P(seq, None),
        check_vma=False,
    )
```

```python
import functools
import math

import jax
import jax.numpy as jnp
from jax import lax
from jax.experimental import pallas as pl
from jax.experimental.pallas import tpu as pltpu
from jax.sharding import PartitionSpec as P

H = 14
KVH = 2
HD = 128
BLK = 4096
TOPK = 3
GROUP = H // KVH

LOW_SCORE = -1e30
LOG2E = math.log2(math.e)
LANES = 128
EARLY = 3
STEP = 256


def head_rows(q_ref, g):
    q = q_ref[...].astype(jnp.float32)
    return [q[:, h * HD : (h + 1) * HD] for h in range(g * GROUP, (g + 1) * GROUP)]


def slot_match(chosen_ref, g, block, slot, token):
    rows = lax.broadcasted_iota(jnp.int32, block.shape, 0)
    same_token = token == rows
    seen = jnp.zeros(block.shape, jnp.int32)
    found = []
    for h in range(g * GROUP, (g + 1) * GROUP):
        picked = block == chosen_ref[0, :, h : h + 1]
        for t in range(1, TOPK):
            picked = picked | (block == chosen_ref[t, :, h : h + 1])
        found.append(jnp.where(picked & same_token & (seen == slot), 1.0, 0.0))
        seen = seen + picked.astype(jnp.int32)
    return found


def fetch(pairs, sems):
    copies = [pltpu.make_async_copy(src, dst, sems.at[i]) for i, (src, dst) in enumerate(pairs)]
    for copy in copies:
        copy.start()
    return copies


def slot_spread(chosen_ref, g, capacity, tokens, key_blocks):
    lane = lax.broadcasted_iota(jnp.int32, (tokens, LANES), 1)
    head = lane // tokens
    same_token = (lane % tokens == lax.broadcasted_iota(jnp.int32, lane.shape, 0)) & (head < GROUP)
    picks = [[chosen_ref[t, 0, g * GROUP + r] for r in range(GROUP)] for t in range(TOPK)]
    places = []
    for t in range(TOPK):
        block = jnp.zeros(lane.shape, jnp.int32)
        for r in range(GROUP):
            block = jnp.where(head == r, picks[t][r], block)
        rank = jnp.zeros(lane.shape, jnp.int32)
        for r in range(GROUP - 1):
            taken = block == picks[0][r]
            for other in range(1, TOPK):
                taken = taken | (block == picks[other][r])
            rank = rank + jnp.where(taken & (head > r), 1, 0)
        places.append(jnp.where(same_token, block * capacity + rank, -1))
    rows = []
    for place in range(key_blocks * capacity):
        found = places[0] == place
        for t in range(1, TOPK):
            found = found | (places[t] == place)
        rows.append(jnp.where(found, 1.0, 0.0))
    return jnp.concatenate(rows, axis=0).astype(jnp.bfloat16)


def pack_kernel(capacity, chosen_hbm, q_hbm, k_hbm, v_hbm, send_hbm, chosen_ref, q_ref, k_ref, v_ref, send_ref, sems):
    copies = fetch([(chosen_hbm, chosen_ref), (q_hbm, q_ref), (k_hbm, k_ref), (v_hbm, v_ref)], sems)
    tokens = q_ref.shape[0]
    per = capacity * tokens
    key_blocks, chips = send_ref.shape[1:3]
    copies[0].wait()
    spread = [slot_spread(chosen_ref, g, capacity, tokens, key_blocks) for g in range(KVH)]
    for copy in copies[1:]:
        copy.wait()
    sent = []
    for g in range(KVH):
        rows = head_rows(q_ref, g)
        rows = rows + [jnp.zeros_like(rows[0])] * (LANES // tokens - GROUP)
        rows = jnp.concatenate(rows, axis=0).astype(jnp.bfloat16)
        slots = jnp.dot(spread[g], rows, preferred_element_type=jnp.float32).astype(jnp.bfloat16)
        cols = slice(g * HD, (g + 1) * HD)
        fresh = [k_ref[:, cols], v_ref[:, cols]]
        for b in range(key_blocks):
            for chip in range(chips):
                to = (g, key_blocks - 1 - b, chips - 1 - chip)
                send_ref[(*to, slice(0, per))] = slots[b * per : (b + 1) * per]
                send_ref[(*to, slice(per, None))] = fresh[chip % 2]
        sent.append(pltpu.make_async_copy(send_ref.at[g], send_hbm.at[:, :, KVH - 1 - g], sems.at[4 + g]))
        sent[g].start()
    for copy in sent:
        copy.wait()


def masks_kernel(chips, capacity, chosen_ref, q_ref, w_hbm, match_ref, rows_ref, w_ref, sems):
    copies = fetch([(w_hbm.at[: w_ref.shape[0]], w_ref)], sems)
    tokens = q_ref.shape[0]
    per = capacity * tokens
    lane = lax.broadcasted_iota(jnp.int32, (tokens, match_ref.shape[2]), 1)
    block, slot, token = lane // (per * chips), lane % per // tokens, lane % tokens
    for g in range(KVH):
        match_ref[g] = jnp.concatenate(slot_match(chosen_ref, g, block, slot, token), axis=0)
        rows_ref[g] = jnp.concatenate(head_rows(q_ref, g), axis=0)
    for copy in copies:
        copy.wait()


def attend_kernel(per, q_ref, ka_ref, va_ref, kb_ref, vb_ref, out_hbm, fresh_ref, out_ref, sems):
    sources = q_ref.shape[0]
    step = STEP // per
    scale = LOG2E * HD**-0.5
    row = lax.broadcasted_iota(jnp.int32, (per, LANES), 0)
    lane = lax.broadcasted_iota(jnp.int32, (per, LANES), 1)
    diagonal = row == lane % per
    ones = jnp.ones(va_ref.shape, jnp.bfloat16)
    empty = jnp.zeros((1, LANES), jnp.float32)
    fresh_ref[...] = q_ref[:, per:, :]

    half = step // 2
    turns = [(first, step) for first in range(step, sources - step, step)]
    turns = [(0, half), (half, half)] + turns + [(sources - step, half), (sources - half, half)]

    def scores(first, count):
        q = q_ref[first : first + count, :per, :].reshape(count * per, HD)
        return [jnp.dot(q, k_ref[...], preferred_element_type=jnp.float32) for k_ref in (ka_ref, kb_ref)]

    ahead = scores(*turns[0])
    sent, rows = [], []
    for turn, (first, count) in enumerate(turns):
        sa, sb = ahead
        if turn + 1 < len(turns):
            ahead = scores(*turns[turn + 1])
        top = scale * jnp.maximum(jnp.max(sa, axis=1, keepdims=True), jnp.max(sb, axis=1, keepdims=True))
        wa = jnp.exp2(sa * scale - top).astype(jnp.bfloat16)
        wb = jnp.exp2(sb * scale - top).astype(jnp.bfloat16)
        both = jnp.dot(
            wa, jnp.concatenate([va_ref[...], ones], axis=1), preferred_element_type=jnp.float32
        ) + jnp.dot(wb, jnp.concatenate([vb_ref[...], ones], axis=1), preferred_element_type=jnp.float32)
        total = both[:, HD:]
        out = both[:, :HD] / total
        lse = (top + jnp.log(total) * LOG2E).reshape(count, per, LANES)
        flat = jnp.sum(jnp.where(diagonal[None], lse, 0.0), axis=1)
        hi = flat.astype(jnp.bfloat16).astype(jnp.float32)
        mid = (flat - hi).astype(jnp.bfloat16).astype(jnp.float32)
        low = flat - hi - mid
        group = lax.broadcasted_iota(jnp.int32, flat.shape, 1) // per
        stats = jnp.where(group == 0, hi, jnp.where(group == 1, mid, jnp.where(group == 2, low, 0.0)))
        for s in range(count):
            rows = rows + [out[s * per : (s + 1) * per], stats[s : s + 1], empty]
        if len(rows) == 3 * step:
            done = pl.ds((first + count - step) * (per + 2), step * (per + 2))
            out_ref[done, :] = jnp.concatenate(rows, axis=0).astype(jnp.bfloat16)
            sent.append(pltpu.make_async_copy(out_ref.at[done], out_hbm.at[done], sems.at[len(sent)]))
            sent[-1].start()
            rows = []
    for copy in sent:
        copy.wait()


def fresh_kernel(tokens, rows_ref, kv_ref, kv1_ref, kv2_ref, kv3_ref, out_ref, lse_ref):
    sources = kv_ref.shape[0]
    place = lax.axis_index("seq")
    core, odd = place % KVH, place // KVH % 2
    scale = LOG2E * HD**-0.5
    nt = (((1,), (1,)), ((), ()))
    column = lax.broadcasted_iota(jnp.int32, (tokens, sources * tokens), 1)
    query_pos = place * tokens + lax.broadcasted_iota(jnp.int32, column.shape, 0)
    key_pos = (sources - 1 - column // tokens) * tokens + column % tokens
    visible = (key_pos <= query_pos) & (key_pos // BLK == query_pos // BLK)
    visible = jnp.concatenate([visible.astype(jnp.int32)] * GROUP, axis=0) > 0
    ones = jnp.ones((sources * tokens, HD), jnp.bfloat16)
    here, near, far, both = [
        ref[...].astype(jnp.float32).reshape(sources * tokens, HD) for ref in (kv_ref, kv1_ref, kv2_ref, kv3_ref)
    ]
    keys = [jnp.where(odd == 0, here, far), jnp.where(odd == 0, near, both)]
    values = [jnp.where(odd == 0, far, here), jnp.where(odd == 0, both, near)]
    for g in range(KVH):
        k = jnp.where(core == g, keys[0], keys[1]).astype(jnp.bfloat16)
        v = jnp.where(core == g, values[0], values[1]).astype(jnp.bfloat16)
        q = rows_ref[g].astype(jnp.bfloat16)
        s = lax.dot_general(q, k, nt, preferred_element_type=jnp.float32) * scale
        s = jnp.where(visible, s, LOW_SCORE)
        top = jnp.max(s, axis=1, keepdims=True)
        w = jnp.where(visible, jnp.exp2(s - top), 0.0).astype(jnp.bfloat16)
        total_out = jnp.dot(w, jnp.concatenate([v, ones], axis=1), preferred_element_type=jnp.float32)
        total = total_out[:, HD:]
        out_ref[g] = total_out[:, :HD] / total
        lse_ref[g] = top + jnp.log(total) * LOG2E


def project_kernel(per, hist_ref, out_ref, lse_ref, match_ref, first_ref, w_hbm, y_ref, w_ref, sems):
    depth = KVH * HD
    ready = first_ref.shape[0] // depth
    copies = fetch(
        [
            (w_hbm.at[pl.ds((ready + i) * depth, depth)], w_ref.at[pl.ds(i * depth, depth)])
            for i in range(w_ref.shape[0] // depth)
        ],
        sems,
    )
    tokens = y_ref.shape[0]
    holders = match_ref.shape[2] // per
    hist = hist_ref[...].astype(jnp.float32)
    fold = LANES // per
    row = lax.broadcasted_iota(jnp.int32, (holders, LANES), 0)
    lane = lax.broadcasted_iota(jnp.int32, (holders, LANES), 1)

    def times(heads, weights):
        lhs = jnp.concatenate(heads, axis=1).astype(jnp.bfloat16)
        return jnp.dot(lhs, weights, preferred_element_type=jnp.float32)

    heads = []
    for g in range(KVH):
        starts = [(KVH * (holders - m) - 1 - g) * (per + 2) for m in range(holders)]
        outs = jnp.concatenate([hist[i : i + per] for i in starts], axis=0).astype(jnp.bfloat16)
        stats = jnp.concatenate([hist[i + per : i + per + 1] for i in starts], axis=0)
        shift = LANES // 2
        while shift >= per:
            stats = stats + pltpu.roll(stats, shift, 1)
            shift //= 2
        stats = jnp.where(row % fold == lane // per, stats, 0.0)
        lse = jnp.concatenate(
            [
                jnp.sum(jnp.where(row // fold == m, stats, 0.0), axis=0, keepdims=True)
                for m in range(holders // fold)
            ],
            axis=1,
        )
        match = match_ref[g] > 0.5
        lse = jnp.where(match, lse, LOW_SCORE)
        own = lse_ref[g]
        top = jnp.maximum(jnp.max(lse, axis=1, keepdims=True), own)
        w = jnp.where(match, jnp.exp2(lse - top[:, :1]), 0.0)
        own_w = jnp.exp2(own - top)
        hi = w.astype(jnp.bfloat16)
        low = (w - hi.astype(jnp.float32)).astype(jnp.bfloat16)
        num = (
            jnp.dot(hi, outs, preferred_element_type=jnp.float32)
            + jnp.dot(low, outs, preferred_element_type=jnp.float32)
            + own_w * out_ref[g]
        )
        att = num / (jnp.sum(w, axis=1, keepdims=True) + own_w)
        heads = heads + [att[r * tokens : (r + 1) * tokens] for r in range(GROUP)]
        if g == 0:
            y = times(heads[: ready * KVH], first_ref[...])
    for i, copy in enumerate(copies):
        copy.wait()
        y = y + times(heads[(ready + i) * KVH : (ready + i + 1) * KVH], w_ref[i * depth : (i + 1) * depth, :])
    y_ref[...] = y.astype(jnp.bfloat16)


VMEM = pl.BlockSpec(memory_space=pltpu.VMEM)
HBM = pl.BlockSpec(memory_space=pltpu.HBM)
ANY = pl.BlockSpec(memory_space=pl.ANY)


def call(kernel, name, out_shape, specs, *operands, outs=None, scratch=(), flops=0, moved=0, limit=16):
    outs = outs or jax.tree.map(lambda _: VMEM, out_shape)
    return pl.pallas_call(
        kernel,
        name=name,
        out_shape=out_shape,
        in_specs=specs,
        out_specs=outs,
        scratch_shapes=scratch,
        cost_estimate=pl.CostEstimate(flops=flops, bytes_accessed=moved, transcendentals=0),
        compiler_params=pltpu.CompilerParams(vmem_limit_bytes=limit << 20),
    )(*operands)


def body(queries, stretch_keys, stretch_values, cache_keys, cache_values, chosen, out_weight):
    devices = lax.axis_size("seq")
    tokens = queries.shape[0]
    cache_rows = cache_keys.shape[0]
    span = BLK // cache_rows
    chips = span // KVH
    key_blocks = cache_rows * devices // BLK
    capacity = (GROUP * TOPK + key_blocks - 1) // key_blocks + 1
    per = capacity * tokens
    f32, bf16 = jnp.float32, jnp.bfloat16
    picks = chosen.transpose(2, 0, 1)

    def partner(bit):
        return [(i, i ^ bit) for i in range(devices)]

    send = call(
        functools.partial(pack_kernel, capacity),
        "pack",
        jax.ShapeDtypeStruct((key_blocks, chips, KVH, per + tokens, HD), bf16),
        [HBM] * 4,
        picks, queries, stretch_keys, stretch_values,
        outs=ANY,
        scratch=[
            pltpu.SMEM(picks.shape, jnp.int32),
            pltpu.VMEM(queries.shape, bf16),
            pltpu.VMEM(stretch_keys.shape, bf16),
            pltpu.VMEM(stretch_values.shape, bf16),
            pltpu.VMEM((KVH, key_blocks, chips, per + tokens, HD), bf16),
            pltpu.SemaphoreType.DMA((4 + KVH,)),
        ],
        limit=60,
    )
    send, cache_keys, cache_values, picks, queries = lax.optimization_barrier(
        (send, cache_keys, cache_values, picks, queries)
    )

    def exchange(x):
        ranks = [list(range(devices))[::-1]]
        return lax.all_to_all(x, "seq", split_axis=0, concat_axis=0, axis_index_groups=ranks, tiled=True)

    got = exchange(send.reshape(devices, per + tokens, HD))

    core = lax.axis_index("seq") % KVH

    def halves(head):
        keys, values = [lax.dynamic_slice_in_dim(x, head * HD, HD, axis=1) for x in (cache_keys, cache_values)]
        return keys.T, values

    k_own, v_own = halves(core)
    k_peer, v_peer = [lax.ppermute(x, "seq", partner(1)) for x in halves(1 - core)]
    holders = devices // KVH
    rows = devices * per
    back, fresh = call(
        functools.partial(attend_kernel, per),
        "attend",
        (
            jax.ShapeDtypeStruct((devices * (per + 2), HD), bf16),
            jax.ShapeDtypeStruct((devices, tokens, HD), bf16),
        ),
        [VMEM] * 5,
        got, k_own, v_own, k_peer, v_peer,
        outs=(ANY, VMEM),
        scratch=[
            pltpu.VMEM((devices * (per + 2), HD), bf16),
            pltpu.SemaphoreType.DMA((rows // STEP,)),
        ],
        flops=8 * rows * cache_rows * HD,
        moved=4 << 20,
        limit=32,
    )
    back, picks, queries, out_weight = lax.optimization_barrier((back, picks, queries, out_weight))
    hist = exchange(back.reshape(devices, (per + 2) // 2, 2, HD))

    ready = EARLY * KVH * HD
    match, query_rows, first = call(
        functools.partial(masks_kernel, chips, capacity),
        "masks",
        (
            jax.ShapeDtypeStruct((KVH, GROUP * tokens, holders * per), f32),
            jax.ShapeDtypeStruct((KVH, GROUP * tokens, HD), f32),
            jax.ShapeDtypeStruct((ready, out_weight.shape[1]), bf16),
        ),
        [VMEM, VMEM, HBM],
        picks, queries, out_weight,
        scratch=[pltpu.SemaphoreType.DMA((1,))],
        limit=50,
    )

    far = lax.ppermute(fresh, "seq", partner(2))
    near, both = [lax.ppermute(x, "seq", partner(1)) for x in (fresh, far)]
    part = jax.ShapeDtypeStruct((KVH, GROUP * tokens, HD), f32)
    out, lse = call(
        functools.partial(fresh_kernel, tokens),
        "fresh",
        (part, part),
        [VMEM] * 5,
        query_rows, fresh, near, far, both,
        flops=8 * H * tokens * devices * tokens * HD,
        moved=1 << 20,
    )
    return call(
        functools.partial(project_kernel, per),
        "project",
        jax.ShapeDtypeStruct((tokens, out_weight.shape[1]), bf16),
        [VMEM] * 5 + [HBM],
        hist.reshape(devices * (per + 2), HD), out, lse, match, first, out_weight,
        scratch=[
            pltpu.VMEM((out_weight.shape[0] - ready, out_weight.shape[1]), bf16),
            pltpu.SemaphoreType.DMA((GROUP - EARLY,)),
        ],
        flops=2 * tokens * out_weight.size,
        moved=out_weight.size * 2,
        limit=50,
    )


def solution(mesh):
    seq = ("grp", "seq")
    return jax.shard_map(
        body,
        mesh=mesh,
        in_specs=(
            P(seq, None),
            P(seq, None),
            P(seq, None),
            P(seq, None),
            P(seq, None),
            P(seq, None, None),
            P(),
        ),
        out_specs=P(seq, None),
        check_vma=False,
    )
```

```python
import functools
import math

import jax
import jax.numpy as jnp
from jax import lax
from jax.experimental import pallas as pl
from jax.experimental.pallas import tpu as pltpu
from jax.sharding import PartitionSpec as P

H = 14
KVH = 2
HD = 128
BLK = 4096
TOPK = 3
GROUP = H // KVH

LOW_SCORE = -1e30
LOG2E = math.log2(math.e)
LANES = 128
EARLY = 3
STEP = 256


def head_rows(q_ref, g):
    q = q_ref[...].astype(jnp.float32)
    return [q[:, h * HD : (h + 1) * HD] for h in range(g * GROUP, (g + 1) * GROUP)]


def slot_match(chosen_ref, g, block, slot, token):
    rows = lax.broadcasted_iota(jnp.int32, block.shape, 0)
    same_token = token == rows
    seen = jnp.zeros(block.shape, jnp.int32)
    found = []
    for h in range(g * GROUP, (g + 1) * GROUP):
        picked = block == chosen_ref[0, :, h : h + 1]
        for t in range(1, TOPK):
            picked = picked | (block == chosen_ref[t, :, h : h + 1])
        found.append(jnp.where(picked & same_token & (seen == slot), 1.0, 0.0))
        seen = seen + picked.astype(jnp.int32)
    return found


def fetch(pairs, sems):
    copies = [pltpu.make_async_copy(src, dst, sems.at[i]) for i, (src, dst) in enumerate(pairs)]
    for copy in copies:
        copy.start()
    return copies


def slot_spread(chosen_ref, g, capacity, tokens, key_blocks):
    lane = lax.broadcasted_iota(jnp.int32, (tokens, LANES), 1)
    head = lane // tokens
    same_token = (lane % tokens == lax.broadcasted_iota(jnp.int32, lane.shape, 0)) & (head < GROUP)
    picks = [[chosen_ref[t, 0, g * GROUP + r] for r in range(GROUP)] for t in range(TOPK)]
    places = []
    for t in range(TOPK):
        block = jnp.zeros(lane.shape, jnp.int32)
        for r in range(GROUP):
            block = jnp.where(head == r, picks[t][r], block)
        rank = jnp.zeros(lane.shape, jnp.int32)
        for r in range(GROUP - 1):
            taken = block == picks[0][r]
            for other in range(1, TOPK):
                taken = taken | (block == picks[other][r])
            rank = rank + jnp.where(taken & (head > r), 1, 0)
        places.append(jnp.where(same_token, block * capacity + rank, -1))
    rows = []
    for place in range(key_blocks * capacity):
        found = places[0] == place
        for t in range(1, TOPK):
            found = found | (places[t] == place)
        rows.append(jnp.where(found, 1.0, 0.0))
    return jnp.concatenate(rows, axis=0).astype(jnp.bfloat16)


def pack_kernel(capacity, chosen_hbm, q_hbm, k_hbm, v_hbm, send_hbm, chosen_ref, q_ref, k_ref, v_ref, send_ref, sems):
    copies = fetch([(chosen_hbm, chosen_ref), (q_hbm, q_ref), (k_hbm, k_ref), (v_hbm, v_ref)], sems)
    tokens = q_ref.shape[0]
    per = capacity * tokens
    key_blocks, chips = send_ref.shape[1:3]
    copies[0].wait()
    spread = [slot_spread(chosen_ref, g, capacity, tokens, key_blocks) for g in range(KVH)]
    for copy in copies[1:]:
        copy.wait()
    sent = []
    for g in range(KVH):
        rows = head_rows(q_ref, g)
        rows = rows + [jnp.zeros_like(rows[0])] * (LANES // tokens - GROUP)
        rows = jnp.concatenate(rows, axis=0).astype(jnp.bfloat16)
        slots = jnp.dot(spread[g], rows, preferred_element_type=jnp.float32).astype(jnp.bfloat16)
        cols = slice(g * HD, (g + 1) * HD)
        fresh = [k_ref[:, cols], v_ref[:, cols]]
        for b in range(key_blocks):
            for chip in range(chips):
                to = (g, key_blocks - 1 - b, chips - 1 - chip)
                send_ref[(*to, slice(0, per))] = slots[b * per : (b + 1) * per]
                send_ref[(*to, slice(per, None))] = fresh[chip % 2]
        sent.append(pltpu.make_async_copy(send_ref.at[g], send_hbm.at[:, :, KVH - 1 - g], sems.at[4 + g]))
        sent[g].start()
    for copy in sent:
        copy.wait()


def masks_kernel(chips, capacity, chosen_ref, q_ref, w_hbm, match_ref, rows_ref, w_ref, sems):
    copies = fetch([(w_hbm.at[: w_ref.shape[0]], w_ref)], sems)
    tokens = q_ref.shape[0]
    per = capacity * tokens
    lane = lax.broadcasted_iota(jnp.int32, (tokens, match_ref.shape[2]), 1)
    block, slot, token = lane // (per * chips), lane % per // tokens, lane % tokens
    for g in range(KVH):
        match_ref[g] = jnp.concatenate(slot_match(chosen_ref, g, block, slot, token), axis=0)
        rows_ref[g] = jnp.concatenate(head_rows(q_ref, g), axis=0)
    for copy in copies:
        copy.wait()


def attend_kernel(per, q_ref, k_ref, v_ref, out_hbm, fresh_ref, out_ref, sems):
    sources = q_ref.shape[0]
    sent = []
    step = STEP // per
    scale = LOG2E * HD**-0.5
    row = lax.broadcasted_iota(jnp.int32, (per, LANES), 0)
    lane = lax.broadcasted_iota(jnp.int32, (per, LANES), 1)
    diagonal = row == lane % per
    group = lax.broadcasted_iota(jnp.int32, (2, LANES), 1) // per
    second = lax.broadcasted_iota(jnp.int32, (2, LANES), 0)
    ones = jnp.ones(v_ref.shape, jnp.bfloat16)
    fresh_ref[...] = q_ref[:, per:, :]

    def scores(first):
        q = q_ref[first : first + step, :per, :].reshape(step * per, HD)
        return jnp.dot(q, k_ref[...], preferred_element_type=jnp.float32)

    ahead = scores(0)
    for first in range(0, sources, step):
        score = ahead
        if first + step < sources:
            ahead = scores(first + step)
        top = scale * jnp.max(score, axis=1, keepdims=True)
        weights = jnp.exp2(score * scale - top).astype(jnp.bfloat16)
        both = jnp.dot(
            weights, jnp.concatenate([v_ref[...], ones], axis=1), preferred_element_type=jnp.float32
        )
        total = both[:, HD:]
        out = both[:, :HD] / total
        lse = top + jnp.log(total) * LOG2E
        rows = []
        for s in range(step):
            part = slice(s * per, (s + 1) * per)
            flat = jnp.sum(jnp.where(diagonal, lse[part], 0.0), axis=0, keepdims=True)
            hi = flat.astype(jnp.bfloat16).astype(jnp.float32)
            mid = (flat - hi).astype(jnp.bfloat16).astype(jnp.float32)
            low = flat - hi - mid
            stats = jnp.where(group == 0, hi, jnp.where(group == 1, mid, jnp.where(group == 2, low, 0.0)))
            rows = rows + [out[part], jnp.where(second == 0, stats, 0.0)]
        done = pl.ds(first * (per + 2), step * (per + 2))
        out_ref[done, :] = jnp.concatenate(rows, axis=0).astype(jnp.bfloat16)
        sent.append(pltpu.make_async_copy(out_ref.at[done], out_hbm.at[done], sems.at[first // step]))
        sent[-1].start()
    for copy in sent:
        copy.wait()


def fresh_kernel(tokens, rows_ref, kv_ref, kv1_ref, kv2_ref, kv3_ref, out_ref, lse_ref):
    sources = kv_ref.shape[0]
    place = lax.axis_index("seq")
    core, odd = place % KVH, place // KVH % 2
    scale = LOG2E * HD**-0.5
    nt = (((1,), (1,)), ((), ()))
    column = lax.broadcasted_iota(jnp.int32, (tokens, sources * tokens), 1)
    query_pos = place * tokens + lax.broadcasted_iota(jnp.int32, column.shape, 0)
    key_pos = (sources - 1 - column // tokens) * tokens + column % tokens
    visible = (key_pos <= query_pos) & (key_pos // BLK == query_pos // BLK)
    visible = jnp.concatenate([visible.astype(jnp.int32)] * GROUP, axis=0) > 0
    ones = jnp.ones((sources * tokens, HD), jnp.bfloat16)
    here, near, far, both = [
        ref[...].astype(jnp.float32).reshape(sources * tokens, HD) for ref in (kv_ref, kv1_ref, kv2_ref, kv3_ref)
    ]
    keys = [jnp.where(odd == 0, here, far), jnp.where(odd == 0, near, both)]
    values = [jnp.where(odd == 0, far, here), jnp.where(odd == 0, both, near)]
    for g in range(KVH):
        k = jnp.where(core == g, keys[0], keys[1]).astype(jnp.bfloat16)
        v = jnp.where(core == g, values[0], values[1]).astype(jnp.bfloat16)
        q = rows_ref[g].astype(jnp.bfloat16)
        s = lax.dot_general(q, k, nt, preferred_element_type=jnp.float32) * scale
        s = jnp.where(visible, s, LOW_SCORE)
        top = jnp.max(s, axis=1, keepdims=True)
        w = jnp.where(visible, jnp.exp2(s - top), 0.0).astype(jnp.bfloat16)
        total_out = jnp.dot(w, jnp.concatenate([v, ones], axis=1), preferred_element_type=jnp.float32)
        total = total_out[:, HD:]
        out_ref[g] = total_out[:, :HD] / total
        lse_ref[g] = top + jnp.log(total) * LOG2E


def project_kernel(per, hist_ref, out_ref, lse_ref, match_ref, first_ref, w_hbm, y_ref, w_ref, sems):
    depth = KVH * HD
    ready = first_ref.shape[0] // depth
    copies = fetch(
        [
            (w_hbm.at[pl.ds((ready + i) * depth, depth)], w_ref.at[pl.ds(i * depth, depth)])
            for i in range(w_ref.shape[0] // depth)
        ],
        sems,
    )
    tokens = y_ref.shape[0]
    holders = match_ref.shape[2] // per
    hist = hist_ref[...].astype(jnp.float32)
    fold = LANES // per
    row = lax.broadcasted_iota(jnp.int32, (holders, LANES), 0)
    lane = lax.broadcasted_iota(jnp.int32, (holders, LANES), 1)

    def times(heads, weights):
        lhs = jnp.concatenate(heads, axis=1).astype(jnp.bfloat16)
        return jnp.dot(lhs, weights, preferred_element_type=jnp.float32)

    heads = []
    for g in range(KVH):
        starts = [(KVH * (holders - m) - 1 - g) * (per + 2) for m in range(holders)]
        outs = jnp.concatenate([hist[i : i + per] for i in starts], axis=0).astype(jnp.bfloat16)
        stats = jnp.concatenate([hist[i + per : i + per + 1] for i in starts], axis=0)
        shift = LANES // 2
        while shift >= per:
            stats = stats + pltpu.roll(stats, shift, 1)
            shift //= 2
        stats = jnp.where(row % fold == lane // per, stats, 0.0)
        lse = jnp.concatenate(
            [
                jnp.sum(jnp.where(row // fold == m, stats, 0.0), axis=0, keepdims=True)
                for m in range(holders // fold)
            ],
            axis=1,
        )
        match = match_ref[g] > 0.5
        lse = jnp.where(match, lse, LOW_SCORE)
        own = lse_ref[g]
        top = jnp.maximum(jnp.max(lse, axis=1, keepdims=True), own)
        w = jnp.where(match, jnp.exp2(lse - top[:, :1]), 0.0)
        own_w = jnp.exp2(own - top)
        hi = w.astype(jnp.bfloat16)
        low = (w - hi.astype(jnp.float32)).astype(jnp.bfloat16)
        num = (
            jnp.dot(hi, outs, preferred_element_type=jnp.float32)
            + jnp.dot(low, outs, preferred_element_type=jnp.float32)
            + own_w * out_ref[g]
        )
        att = num / (jnp.sum(w, axis=1, keepdims=True) + own_w)
        heads = heads + [att[r * tokens : (r + 1) * tokens] for r in range(GROUP)]
        if g == 0:
            y = times(heads[: ready * KVH], first_ref[...])
    for i, copy in enumerate(copies):
        copy.wait()
        y = y + times(heads[(ready + i) * KVH : (ready + i + 1) * KVH], w_ref[i * depth : (i + 1) * depth, :])
    y_ref[...] = y.astype(jnp.bfloat16)


VMEM = pl.BlockSpec(memory_space=pltpu.VMEM)
HBM = pl.BlockSpec(memory_space=pltpu.HBM)
ANY = pl.BlockSpec(memory_space=pl.ANY)


def call(kernel, name, out_shape, specs, *operands, outs=None, scratch=(), flops=0, moved=0, limit=16):
    outs = outs or jax.tree.map(lambda _: VMEM, out_shape)
    return pl.pallas_call(
        kernel,
        name=name,
        out_shape=out_shape,
        in_specs=specs,
        out_specs=outs,
        scratch_shapes=scratch,
        cost_estimate=pl.CostEstimate(flops=flops, bytes_accessed=moved, transcendentals=0),
        compiler_params=pltpu.CompilerParams(vmem_limit_bytes=limit << 20),
    )(*operands)


def body(queries, stretch_keys, stretch_values, cache_keys, cache_values, chosen, out_weight):
    devices = lax.axis_size("seq")
    tokens = queries.shape[0]
    cache_rows = cache_keys.shape[0]
    span = BLK // cache_rows
    chips = span // KVH
    key_blocks = cache_rows * devices // BLK
    capacity = (GROUP * TOPK + key_blocks - 1) // key_blocks + 1
    per = capacity * tokens
    f32, bf16 = jnp.float32, jnp.bfloat16
    picks = chosen.transpose(2, 0, 1)

    def partner(bit):
        return [(i, i ^ bit) for i in range(devices)]

    send = call(
        functools.partial(pack_kernel, capacity),
        "pack",
        jax.ShapeDtypeStruct((key_blocks, chips, KVH, per + tokens, HD), bf16),
        [HBM] * 4,
        picks, queries, stretch_keys, stretch_values,
        outs=ANY,
        scratch=[
            pltpu.SMEM(picks.shape, jnp.int32),
            pltpu.VMEM(queries.shape, bf16),
            pltpu.VMEM(stretch_keys.shape, bf16),
            pltpu.VMEM(stretch_values.shape, bf16),
            pltpu.VMEM((KVH, key_blocks, chips, per + tokens, HD), bf16),
            pltpu.SemaphoreType.DMA((4 + KVH,)),
        ],
        limit=60,
    )
    send, cache_keys, cache_values, picks, queries = lax.optimization_barrier(
        (send, cache_keys, cache_values, picks, queries)
    )

    def exchange(x):
        ranks = [list(range(devices))[::-1]]
        return lax.all_to_all(x, "seq", split_axis=0, concat_axis=0, axis_index_groups=ranks, tiled=True)

    got = exchange(send.reshape(devices, per + tokens, HD))

    core = lax.axis_index("seq") % KVH

    def halves(head):
        keys, values = [lax.dynamic_slice_in_dim(x, head * HD, HD, axis=1) for x in (cache_keys, cache_values)]
        return keys.T, values

    k_own, v_own = halves(core)
    k_peer, v_peer = [lax.ppermute(x, "seq", partner(1)) for x in halves(1 - core)]
    holders = devices // KVH
    rows = devices * per
    back, fresh = call(
        functools.partial(attend_kernel, per),
        "attend",
        (
            jax.ShapeDtypeStruct((devices * (per + 2), HD), bf16),
            jax.ShapeDtypeStruct((devices, tokens, HD), bf16),
        ),
        [VMEM] * 3,
        got,
        jnp.concatenate([k_own, k_peer], axis=1),
        jnp.concatenate([v_own, v_peer], axis=0),
        outs=(ANY, VMEM),
        scratch=[
            pltpu.VMEM((devices * (per + 2), HD), bf16),
            pltpu.SemaphoreType.DMA((rows // STEP,)),
        ],
        flops=8 * rows * cache_rows * HD,
        moved=4 << 20,
        limit=32,
    )
    back, picks, queries, out_weight = lax.optimization_barrier((back, picks, queries, out_weight))
    hist = exchange(back.reshape(devices, (per + 2) // 2, 2, HD))

    ready = EARLY * KVH * HD
    match, query_rows, first = call(
        functools.partial(masks_kernel, chips, capacity),
        "masks",
        (
            jax.ShapeDtypeStruct((KVH, GROUP * tokens, holders * per), f32),
            jax.ShapeDtypeStruct((KVH, GROUP * tokens, HD), f32),
            jax.ShapeDtypeStruct((ready, out_weight.shape[1]), bf16),
        ),
        [VMEM, VMEM, HBM],
        picks, queries, out_weight,
        scratch=[pltpu.SemaphoreType.DMA((1,))],
        limit=50,
    )

    far = lax.ppermute(fresh, "seq", partner(2))
    near, both = [lax.ppermute(x, "seq", partner(1)) for x in (fresh, far)]
    part = jax.ShapeDtypeStruct((KVH, GROUP * tokens, HD), f32)
    out, lse = call(
        functools.partial(fresh_kernel, tokens),
        "fresh",
        (part, part),
        [VMEM] * 5,
        query_rows, fresh, near, far, both,
        flops=8 * H * tokens * devices * tokens * HD,
        moved=1 << 20,
    )
    return call(
        functools.partial(project_kernel, per),
        "project",
        jax.ShapeDtypeStruct((tokens, out_weight.shape[1]), bf16),
        [VMEM] * 5 + [HBM],
        hist.reshape(devices * (per + 2), HD), out, lse, match, first, out_weight,
        scratch=[
            pltpu.VMEM((out_weight.shape[0] - ready, out_weight.shape[1]), bf16),
            pltpu.SemaphoreType.DMA((GROUP - EARLY,)),
        ],
        flops=2 * tokens * out_weight.size,
        moved=out_weight.size * 2,
        limit=50,
    )


def solution(mesh):
    seq = ("grp", "seq")
    return jax.shard_map(
        body,
        mesh=mesh,
        in_specs=(
            P(seq, None),
            P(seq, None),
            P(seq, None),
            P(seq, None),
            P(seq, None),
            P(seq, None, None),
            P(),
        ),
        out_specs=P(seq, None),
        check_vma=False,
    )
```

```python
import functools
import math

import jax
import jax.numpy as jnp
from jax import lax
from jax.experimental import pallas as pl
from jax.experimental.pallas import tpu as pltpu
from jax.sharding import PartitionSpec as P

H = 14
KVH = 2
HD = 128
BLK = 4096
TOPK = 3
GROUP = H // KVH

LOW_SCORE = -1e30
LOG2E = math.log2(math.e)
LANES = 128
EARLY = 3
STEP = 256


def head_rows(q_ref, g):
    q = q_ref[...].astype(jnp.float32)
    return [q[:, h * HD : (h + 1) * HD] for h in range(g * GROUP, (g + 1) * GROUP)]


def slot_match(chosen_ref, g, block, slot, token):
    rows = lax.broadcasted_iota(jnp.int32, block.shape, 0)
    same_token = token == rows
    seen = jnp.zeros(block.shape, jnp.int32)
    found = []
    for h in range(g * GROUP, (g + 1) * GROUP):
        picked = block == chosen_ref[0, :, h : h + 1]
        for t in range(1, TOPK):
            picked = picked | (block == chosen_ref[t, :, h : h + 1])
        found.append(jnp.where(picked & same_token & (seen == slot), 1.0, 0.0))
        seen = seen + picked.astype(jnp.int32)
    return found


def fetch(pairs, sems):
    copies = [pltpu.make_async_copy(src, dst, sems.at[i]) for i, (src, dst) in enumerate(pairs)]
    for copy in copies:
        copy.start()
    return copies


def slot_spread(chosen_ref, g, capacity, tokens, key_blocks):
    lane = lax.broadcasted_iota(jnp.int32, (tokens, LANES), 1)
    head = lane // tokens
    same_token = (lane % tokens == lax.broadcasted_iota(jnp.int32, lane.shape, 0)) & (head < GROUP)
    picks = [[chosen_ref[t, 0, g * GROUP + r] for r in range(GROUP)] for t in range(TOPK)]
    places = []
    for t in range(TOPK):
        block = jnp.zeros(lane.shape, jnp.int32)
        for r in range(GROUP):
            block = jnp.where(head == r, picks[t][r], block)
        rank = jnp.zeros(lane.shape, jnp.int32)
        for r in range(GROUP - 1):
            taken = block == picks[0][r]
            for other in range(1, TOPK):
                taken = taken | (block == picks[other][r])
            rank = rank + jnp.where(taken & (head > r), 1, 0)
        places.append(jnp.where(same_token, block * capacity + rank, -1))
    rows = []
    for place in range(key_blocks * capacity):
        found = places[0] == place
        for t in range(1, TOPK):
            found = found | (places[t] == place)
        rows.append(jnp.where(found, 1.0, 0.0))
    return jnp.concatenate(rows, axis=0).astype(jnp.bfloat16)


def pack_kernel(capacity, chosen_hbm, q_hbm, k_hbm, v_hbm, send_hbm, chosen_ref, q_ref, k_ref, v_ref, send_ref, sems):
    copies = fetch([(chosen_hbm, chosen_ref), (q_hbm, q_ref), (k_hbm, k_ref), (v_hbm, v_ref)], sems)
    tokens = q_ref.shape[0]
    per = capacity * tokens
    key_blocks, chips = send_ref.shape[1:3]
    copies[0].wait()
    spread = [slot_spread(chosen_ref, g, capacity, tokens, key_blocks) for g in range(KVH)]
    for copy in copies[1:]:
        copy.wait()
    sent = []
    for g in range(KVH):
        rows = head_rows(q_ref, g)
        rows = rows + [jnp.zeros_like(rows[0])] * (LANES // tokens - GROUP)
        rows = jnp.concatenate(rows, axis=0).astype(jnp.bfloat16)
        slots = jnp.dot(spread[g], rows, preferred_element_type=jnp.float32).astype(jnp.bfloat16)
        cols = slice(g * HD, (g + 1) * HD)
        fresh = [k_ref[:, cols], v_ref[:, cols]]
        for b in range(key_blocks):
            for chip in range(chips):
                to = (g, key_blocks - 1 - b, chips - 1 - chip)
                send_ref[(*to, slice(0, per))] = slots[b * per : (b + 1) * per]
                send_ref[(*to, slice(per, None))] = fresh[chip % 2]
        sent.append(pltpu.make_async_copy(send_ref.at[g], send_hbm.at[:, :, KVH - 1 - g], sems.at[4 + g]))
        sent[g].start()
    for copy in sent:
        copy.wait()


def masks_kernel(chips, capacity, chosen_ref, q_ref, w_hbm, match_ref, rows_ref, w_ref, sems):
    copies = fetch([(w_hbm.at[: w_ref.shape[0]], w_ref)], sems)
    tokens = q_ref.shape[0]
    per = capacity * tokens
    lane = lax.broadcasted_iota(jnp.int32, (tokens, match_ref.shape[2]), 1)
    block, slot, token = lane // (per * chips), lane % per // tokens, lane % tokens
    for g in range(KVH):
        match_ref[g] = jnp.concatenate(slot_match(chosen_ref, g, block, slot, token), axis=0)
        rows_ref[g] = jnp.concatenate(head_rows(q_ref, g), axis=0)
    for copy in copies:
        copy.wait()


def attend_kernel(per, q_ref, ka_ref, va_ref, kb_ref, vb_ref, out_hbm, fresh_ref, out_ref, sems):
    sources = q_ref.shape[0]
    step = STEP // per
    scale = LOG2E * HD**-0.5
    row = lax.broadcasted_iota(jnp.int32, (per, LANES), 0)
    lane = lax.broadcasted_iota(jnp.int32, (per, LANES), 1)
    diagonal = row == lane % per
    group = lax.broadcasted_iota(jnp.int32, (2, LANES), 1) // per
    second = lax.broadcasted_iota(jnp.int32, (2, LANES), 0)
    ones = jnp.ones(va_ref.shape, jnp.bfloat16)
    fresh_ref[...] = q_ref[:, per:, :]

    def scores(first):
        q = q_ref[first : first + step, :per, :].reshape(step * per, HD)
        return [jnp.dot(q, k_ref[...], preferred_element_type=jnp.float32) for k_ref in (ka_ref, kb_ref)]

    sent = []

    def finish(first, wa, wb, top):
        both = jnp.dot(
            wa, jnp.concatenate([va_ref[...], ones], axis=1), preferred_element_type=jnp.float32
        ) + jnp.dot(wb, jnp.concatenate([vb_ref[...], ones], axis=1), preferred_element_type=jnp.float32)
        total = both[:, HD:]
        out = both[:, :HD] / total
        lse = top + jnp.log(total) * LOG2E
        rows = []
        for s in range(step):
            part = slice(s * per, (s + 1) * per)
            flat = jnp.sum(jnp.where(diagonal, lse[part], 0.0), axis=0, keepdims=True)
            hi = flat.astype(jnp.bfloat16).astype(jnp.float32)
            mid = (flat - hi).astype(jnp.bfloat16).astype(jnp.float32)
            low = flat - hi - mid
            stats = jnp.where(group == 0, hi, jnp.where(group == 1, mid, jnp.where(group == 2, low, 0.0)))
            rows = rows + [out[part], jnp.where(second == 0, stats, 0.0)]
        done = pl.ds(first * (per + 2), step * (per + 2))
        out_ref[done, :] = jnp.concatenate(rows, axis=0).astype(jnp.bfloat16)
        sent.append(pltpu.make_async_copy(out_ref.at[done], out_hbm.at[done], sems.at[first // step]))
        sent[-1].start()

    ahead, behind = scores(0), None
    for first in range(0, sources, step):
        sa, sb = ahead
        if first + step < sources:
            ahead = scores(first + step)
        if behind is not None:
            finish(*behind)
        top = scale * jnp.maximum(jnp.max(sa, axis=1, keepdims=True), jnp.max(sb, axis=1, keepdims=True))
        wa = jnp.exp2(sa * scale - top).astype(jnp.bfloat16)
        wb = jnp.exp2(sb * scale - top).astype(jnp.bfloat16)
        behind = (first, wa, wb, top)
    finish(*behind)
    for copy in sent:
        copy.wait()


def fresh_kernel(tokens, rows_ref, kv_ref, kv1_ref, kv2_ref, kv3_ref, out_ref, lse_ref):
    sources = kv_ref.shape[0]
    place = lax.axis_index("seq")
    core, odd = place % KVH, place // KVH % 2
    scale = LOG2E * HD**-0.5
    nt = (((1,), (1,)), ((), ()))
    column = lax.broadcasted_iota(jnp.int32, (tokens, sources * tokens), 1)
    query_pos = place * tokens + lax.broadcasted_iota(jnp.int32, column.shape, 0)
    key_pos = (sources - 1 - column // tokens) * tokens + column % tokens
    visible = (key_pos <= query_pos) & (key_pos // BLK == query_pos // BLK)
    visible = jnp.concatenate([visible.astype(jnp.int32)] * GROUP, axis=0) > 0
    ones = jnp.ones((sources * tokens, HD), jnp.bfloat16)
    here, near, far, both = [
        ref[...].astype(jnp.float32).reshape(sources * tokens, HD) for ref in (kv_ref, kv1_ref, kv2_ref, kv3_ref)
    ]
    keys = [jnp.where(odd == 0, here, far), jnp.where(odd == 0, near, both)]
    values = [jnp.where(odd == 0, far, here), jnp.where(odd == 0, both, near)]
    for g in range(KVH):
        k = jnp.where(core == g, keys[0], keys[1]).astype(jnp.bfloat16)
        v = jnp.where(core == g, values[0], values[1]).astype(jnp.bfloat16)
        q = rows_ref[g].astype(jnp.bfloat16)
        s = lax.dot_general(q, k, nt, preferred_element_type=jnp.float32) * scale
        s = jnp.where(visible, s, LOW_SCORE)
        top = jnp.max(s, axis=1, keepdims=True)
        w = jnp.where(visible, jnp.exp2(s - top), 0.0).astype(jnp.bfloat16)
        total_out = jnp.dot(w, jnp.concatenate([v, ones], axis=1), preferred_element_type=jnp.float32)
        total = total_out[:, HD:]
        out_ref[g] = total_out[:, :HD] / total
        lse_ref[g] = top + jnp.log(total) * LOG2E


def project_kernel(per, hist_ref, out_ref, lse_ref, match_ref, first_ref, w_hbm, y_ref, w_ref, sems):
    depth = KVH * HD
    ready = first_ref.shape[0] // depth
    copies = fetch(
        [
            (w_hbm.at[pl.ds((ready + i) * depth, depth)], w_ref.at[pl.ds(i * depth, depth)])
            for i in range(w_ref.shape[0] // depth)
        ],
        sems,
    )
    tokens = y_ref.shape[0]
    holders = match_ref.shape[2] // per
    hist = hist_ref[...].astype(jnp.float32)
    fold = LANES // per
    row = lax.broadcasted_iota(jnp.int32, (holders, LANES), 0)
    lane = lax.broadcasted_iota(jnp.int32, (holders, LANES), 1)

    def times(heads, weights):
        lhs = jnp.concatenate(heads, axis=1).astype(jnp.bfloat16)
        return jnp.dot(lhs, weights, preferred_element_type=jnp.float32)

    heads = []
    for g in range(KVH):
        starts = [(KVH * (holders - m) - 1 - g) * (per + 2) for m in range(holders)]
        outs = jnp.concatenate([hist[i : i + per] for i in starts], axis=0).astype(jnp.bfloat16)
        stats = jnp.concatenate([hist[i + per : i + per + 1] for i in starts], axis=0)
        shift = LANES // 2
        while shift >= per:
            stats = stats + pltpu.roll(stats, shift, 1)
            shift //= 2
        stats = jnp.where(row % fold == lane // per, stats, 0.0)
        lse = jnp.concatenate(
            [
                jnp.sum(jnp.where(row // fold == m, stats, 0.0), axis=0, keepdims=True)
                for m in range(holders // fold)
            ],
            axis=1,
        )
        match = match_ref[g] > 0.5
        lse = jnp.where(match, lse, LOW_SCORE)
        own = lse_ref[g]
        top = jnp.maximum(jnp.max(lse, axis=1, keepdims=True), own)
        w = jnp.where(match, jnp.exp2(lse - top[:, :1]), 0.0)
        own_w = jnp.exp2(own - top)
        hi = w.astype(jnp.bfloat16)
        low = (w - hi.astype(jnp.float32)).astype(jnp.bfloat16)
        num = (
            jnp.dot(hi, outs, preferred_element_type=jnp.float32)
            + jnp.dot(low, outs, preferred_element_type=jnp.float32)
            + own_w * out_ref[g]
        )
        att = num / (jnp.sum(w, axis=1, keepdims=True) + own_w)
        heads = heads + [att[r * tokens : (r + 1) * tokens] for r in range(GROUP)]
        if g == 0:
            y = times(heads[: ready * KVH], first_ref[...])
    for i, copy in enumerate(copies):
        copy.wait()
        y = y + times(heads[(ready + i) * KVH : (ready + i + 1) * KVH], w_ref[i * depth : (i + 1) * depth, :])
    y_ref[...] = y.astype(jnp.bfloat16)


VMEM = pl.BlockSpec(memory_space=pltpu.VMEM)
HBM = pl.BlockSpec(memory_space=pltpu.HBM)
ANY = pl.BlockSpec(memory_space=pl.ANY)


def call(kernel, name, out_shape, specs, *operands, outs=None, scratch=(), flops=0, moved=0, limit=16):
    outs = outs or jax.tree.map(lambda _: VMEM, out_shape)
    return pl.pallas_call(
        kernel,
        name=name,
        out_shape=out_shape,
        in_specs=specs,
        out_specs=outs,
        scratch_shapes=scratch,
        cost_estimate=pl.CostEstimate(flops=flops, bytes_accessed=moved, transcendentals=0),
        compiler_params=pltpu.CompilerParams(vmem_limit_bytes=limit << 20),
    )(*operands)


def body(queries, stretch_keys, stretch_values, cache_keys, cache_values, chosen, out_weight):
    devices = lax.axis_size("seq")
    tokens = queries.shape[0]
    cache_rows = cache_keys.shape[0]
    span = BLK // cache_rows
    chips = span // KVH
    key_blocks = cache_rows * devices // BLK
    capacity = (GROUP * TOPK + key_blocks - 1) // key_blocks + 1
    per = capacity * tokens
    f32, bf16 = jnp.float32, jnp.bfloat16
    picks = chosen.transpose(2, 0, 1)

    def partner(bit):
        return [(i, i ^ bit) for i in range(devices)]

    send = call(
        functools.partial(pack_kernel, capacity),
        "pack",
        jax.ShapeDtypeStruct((key_blocks, chips, KVH, per + tokens, HD), bf16),
        [HBM] * 4,
        picks, queries, stretch_keys, stretch_values,
        outs=ANY,
        scratch=[
            pltpu.SMEM(picks.shape, jnp.int32),
            pltpu.VMEM(queries.shape, bf16),
            pltpu.VMEM(stretch_keys.shape, bf16),
            pltpu.VMEM(stretch_values.shape, bf16),
            pltpu.VMEM((KVH, key_blocks, chips, per + tokens, HD), bf16),
            pltpu.SemaphoreType.DMA((4 + KVH,)),
        ],
        limit=60,
    )
    send, cache_keys, cache_values, picks, queries = lax.optimization_barrier(
        (send, cache_keys, cache_values, picks, queries)
    )

    def exchange(x):
        ranks = [list(range(devices))[::-1]]
        return lax.all_to_all(x, "seq", split_axis=0, concat_axis=0, axis_index_groups=ranks, tiled=True)

    got = exchange(send.reshape(devices, per + tokens, HD))

    core = lax.axis_index("seq") % KVH

    def halves(head):
        keys, values = [lax.dynamic_slice_in_dim(x, head * HD, HD, axis=1) for x in (cache_keys, cache_values)]
        return keys.T, values

    k_own, v_own = halves(core)
    k_peer, v_peer = [lax.ppermute(x, "seq", partner(1)) for x in halves(1 - core)]
    holders = devices // KVH
    rows = devices * per
    back, fresh = call(
        functools.partial(attend_kernel, per),
        "attend",
        (
            jax.ShapeDtypeStruct((devices * (per + 2), HD), bf16),
            jax.ShapeDtypeStruct((devices, tokens, HD), bf16),
        ),
        [VMEM] * 5,
        got, k_own, v_own, k_peer, v_peer,
        outs=(ANY, VMEM),
        scratch=[
            pltpu.VMEM((devices * (per + 2), HD), bf16),
            pltpu.SemaphoreType.DMA((rows // STEP,)),
        ],
        flops=8 * rows * cache_rows * HD,
        moved=4 << 20,
        limit=32,
    )
    back, picks, queries, out_weight = lax.optimization_barrier((back, picks, queries, out_weight))
    hist = exchange(back.reshape(devices, (per + 2) // 2, 2, HD))

    ready = EARLY * KVH * HD
    match, query_rows, first = call(
        functools.partial(masks_kernel, chips, capacity),
        "masks",
        (
            jax.ShapeDtypeStruct((KVH, GROUP * tokens, holders * per), f32),
            jax.ShapeDtypeStruct((KVH, GROUP * tokens, HD), f32),
            jax.ShapeDtypeStruct((ready, out_weight.shape[1]), bf16),
        ),
        [VMEM, VMEM, HBM],
        picks, queries, out_weight,
        scratch=[pltpu.SemaphoreType.DMA((1,))],
        limit=50,
    )

    far = lax.ppermute(fresh, "seq", partner(2))
    near, both = [lax.ppermute(x, "seq", partner(1)) for x in (fresh, far)]
    part = jax.ShapeDtypeStruct((KVH, GROUP * tokens, HD), f32)
    out, lse = call(
        functools.partial(fresh_kernel, tokens),
        "fresh",
        (part, part),
        [VMEM] * 5,
        query_rows, fresh, near, far, both,
        flops=8 * H * tokens * devices * tokens * HD,
        moved=1 << 20,
    )
    return call(
        functools.partial(project_kernel, per),
        "project",
        jax.ShapeDtypeStruct((tokens, out_weight.shape[1]), bf16),
        [VMEM] * 5 + [HBM],
        hist.reshape(devices * (per + 2), HD), out, lse, match, first, out_weight,
        scratch=[
            pltpu.VMEM((out_weight.shape[0] - ready, out_weight.shape[1]), bf16),
            pltpu.SemaphoreType.DMA((GROUP - EARLY,)),
        ],
        flops=2 * tokens * out_weight.size,
        moved=out_weight.size * 2,
        limit=50,
    )


def solution(mesh):
    seq = ("grp", "seq")
    return jax.shard_map(
        body,
        mesh=mesh,
        in_specs=(
            P(seq, None),
            P(seq, None),
            P(seq, None),
            P(seq, None),
            P(seq, None),
            P(seq, None, None),
            P(),
        ),
        out_specs=P(seq, None),
        check_vma=False,
    )
```

```python
import functools
import math

import jax
import jax.numpy as jnp
from jax import lax
from jax.experimental import pallas as pl
from jax.experimental.pallas import tpu as pltpu
from jax.sharding import PartitionSpec as P

H = 14
KVH = 2
HD = 128
BLK = 4096
TOPK = 3
GROUP = H // KVH

LOW_SCORE = -1e30
LOG2E = math.log2(math.e)
LANES = 128
EARLY = 3
STEP = 256


def head_rows(q_ref, g):
    q = q_ref[...].astype(jnp.float32)
    return [q[:, h * HD : (h + 1) * HD] for h in range(g * GROUP, (g + 1) * GROUP)]


def slot_match(chosen_ref, g, block, slot, token):
    rows = lax.broadcasted_iota(jnp.int32, block.shape, 0)
    same_token = token == rows
    seen = jnp.zeros(block.shape, jnp.int32)
    found = []
    for h in range(g * GROUP, (g + 1) * GROUP):
        picked = block == chosen_ref[0, :, h : h + 1]
        for t in range(1, TOPK):
            picked = picked | (block == chosen_ref[t, :, h : h + 1])
        found.append(jnp.where(picked & same_token & (seen == slot), 1.0, 0.0))
        seen = seen + picked.astype(jnp.int32)
    return found


def fetch(pairs, sems):
    copies = [pltpu.make_async_copy(src, dst, sems.at[i]) for i, (src, dst) in enumerate(pairs)]
    for copy in copies:
        copy.start()
    return copies


def slot_spread(chosen_ref, g, capacity, tokens, key_blocks):
    lane = lax.broadcasted_iota(jnp.int32, (tokens, LANES), 1)
    head = lane // tokens
    same_token = (lane % tokens == lax.broadcasted_iota(jnp.int32, lane.shape, 0)) & (head < GROUP)
    picks = [[chosen_ref[t, 0, g * GROUP + r] for r in range(GROUP)] for t in range(TOPK)]
    places = []
    for t in range(TOPK):
        block = jnp.zeros(lane.shape, jnp.int32)
        for r in range(GROUP):
            block = jnp.where(head == r, picks[t][r], block)
        rank = jnp.zeros(lane.shape, jnp.int32)
        for r in range(GROUP - 1):
            taken = block == picks[0][r]
            for other in range(1, TOPK):
                taken = taken | (block == picks[other][r])
            rank = rank + jnp.where(taken & (head > r), 1, 0)
        places.append(jnp.where(same_token, block * capacity + rank, -1))
    rows = []
    for place in range(key_blocks * capacity):
        found = places[0] == place
        for t in range(1, TOPK):
            found = found | (places[t] == place)
        rows.append(jnp.where(found, 1.0, 0.0))
    return jnp.concatenate(rows, axis=0).astype(jnp.bfloat16)


def pack_kernel(capacity, chosen_hbm, q_hbm, k_hbm, v_hbm, send_hbm, chosen_ref, q_ref, k_ref, v_ref, send_ref, sems):
    copies = fetch([(chosen_hbm, chosen_ref), (q_hbm, q_ref), (k_hbm, k_ref), (v_hbm, v_ref)], sems)
    tokens = q_ref.shape[0]
    per = capacity * tokens
    key_blocks, chips = send_ref.shape[1:3]
    copies[0].wait()
    spread = [slot_spread(chosen_ref, g, capacity, tokens, key_blocks) for g in range(KVH)]
    for copy in copies[1:]:
        copy.wait()
    sent = []
    for g in range(KVH):
        rows = head_rows(q_ref, g)
        rows = rows + [jnp.zeros_like(rows[0])] * (LANES // tokens - GROUP)
        rows = jnp.concatenate(rows, axis=0).astype(jnp.bfloat16)
        slots = jnp.dot(spread[g], rows, preferred_element_type=jnp.float32).astype(jnp.bfloat16)
        cols = slice(g * HD, (g + 1) * HD)
        fresh = [k_ref[:, cols], v_ref[:, cols]]
        for b in range(key_blocks):
            for chip in range(chips):
                to = (g, key_blocks - 1 - b, chips - 1 - chip)
                send_ref[(*to, slice(0, per))] = slots[b * per : (b + 1) * per]
                send_ref[(*to, slice(per, None))] = fresh[chip % 2]
        sent.append(pltpu.make_async_copy(send_ref.at[g], send_hbm.at[:, :, KVH - 1 - g], sems.at[4 + g]))
        sent[g].start()
    for copy in sent:
        copy.wait()


def masks_kernel(chips, capacity, chosen_ref, q_ref, w_hbm, match_ref, rows_ref, w_ref, sems):
    copies = fetch([(w_hbm.at[: w_ref.shape[0]], w_ref)], sems)
    tokens = q_ref.shape[0]
    per = capacity * tokens
    lane = lax.broadcasted_iota(jnp.int32, (tokens, match_ref.shape[2]), 1)
    block, slot, token = lane // (per * chips), lane % per // tokens, lane % tokens
    for g in range(KVH):
        match_ref[g] = jnp.concatenate(slot_match(chosen_ref, g, block, slot, token), axis=0)
        rows_ref[g] = jnp.concatenate(head_rows(q_ref, g), axis=0)
    for copy in copies:
        copy.wait()


def attend_kernel(per, q_ref, ka_ref, va_ref, kb_ref, vb_ref, out_hbm, fresh_ref, out_ref, sems):
    sources = q_ref.shape[0]
    sent = []
    step = STEP // per
    scale = LOG2E * HD**-0.5
    row = lax.broadcasted_iota(jnp.int32, (per, LANES), 0)
    lane = lax.broadcasted_iota(jnp.int32, (per, LANES), 1)
    diagonal = row == lane % per
    group = lax.broadcasted_iota(jnp.int32, (2, LANES), 1) // per
    second = lax.broadcasted_iota(jnp.int32, (2, LANES), 0)
    ones = jnp.ones((2 * LANES, LANES), jnp.bfloat16)
    fresh_ref[...] = q_ref[:, per:, :]

    def scores(first):
        q = q_ref[first : first + step, :per, :].reshape(step * per, HD)
        return [jnp.dot(q, k_ref[...], preferred_element_type=jnp.float32) for k_ref in (ka_ref, kb_ref)]

    ahead = scores(0)
    for first in range(0, sources, step):
        sa, sb = ahead
        if first + step < sources:
            ahead = scores(first + step)
        top = scale * jnp.maximum(jnp.max(sa, axis=1, keepdims=True), jnp.max(sb, axis=1, keepdims=True))
        wa = jnp.exp2(sa * scale - top)
        wb = jnp.exp2(sb * scale - top)
        lanes = sum(w[:, i : i + LANES] for w in (wa, wb) for i in range(0, w.shape[1], LANES))
        high = lanes.astype(jnp.bfloat16)
        low = (lanes - high.astype(jnp.float32)).astype(jnp.bfloat16)
        total = jnp.dot(jnp.concatenate([high, low], axis=1), ones, preferred_element_type=jnp.float32)
        both = jnp.dot(
            wa.astype(jnp.bfloat16), va_ref[...], preferred_element_type=jnp.float32
        ) + jnp.dot(wb.astype(jnp.bfloat16), vb_ref[...], preferred_element_type=jnp.float32)
        out = both / total
        lse = top + jnp.log(total) * LOG2E
        rows = []
        for s in range(step):
            part = slice(s * per, (s + 1) * per)
            flat = jnp.sum(jnp.where(diagonal, lse[part], 0.0), axis=0, keepdims=True)
            hi = flat.astype(jnp.bfloat16).astype(jnp.float32)
            mid = (flat - hi).astype(jnp.bfloat16).astype(jnp.float32)
            low = flat - hi - mid
            stats = jnp.where(group == 0, hi, jnp.where(group == 1, mid, jnp.where(group == 2, low, 0.0)))
            rows = rows + [out[part], jnp.where(second == 0, stats, 0.0)]
        done = pl.ds(first * (per + 2), step * (per + 2))
        out_ref[done, :] = jnp.concatenate(rows, axis=0).astype(jnp.bfloat16)
        sent.append(pltpu.make_async_copy(out_ref.at[done], out_hbm.at[done], sems.at[first // step]))
        sent[-1].start()
    for copy in sent:
        copy.wait()


def fresh_kernel(tokens, rows_ref, kv_ref, kv1_ref, kv2_ref, kv3_ref, out_ref, lse_ref):
    sources = kv_ref.shape[0]
    place = lax.axis_index("seq")
    core, odd = place % KVH, place // KVH % 2
    scale = LOG2E * HD**-0.5
    nt = (((1,), (1,)), ((), ()))
    column = lax.broadcasted_iota(jnp.int32, (tokens, sources * tokens), 1)
    query_pos = place * tokens + lax.broadcasted_iota(jnp.int32, column.shape, 0)
    key_pos = (sources - 1 - column // tokens) * tokens + column % tokens
    visible = (key_pos <= query_pos) & (key_pos // BLK == query_pos // BLK)
    visible = jnp.concatenate([visible.astype(jnp.int32)] * GROUP, axis=0) > 0
    ones = jnp.ones((sources * tokens, HD), jnp.bfloat16)
    here, near, far, both = [
        ref[...].astype(jnp.float32).reshape(sources * tokens, HD) for ref in (kv_ref, kv1_ref, kv2_ref, kv3_ref)
    ]
    keys = [jnp.where(odd == 0, here, far), jnp.where(odd == 0, near, both)]
    values = [jnp.where(odd == 0, far, here), jnp.where(odd == 0, both, near)]
    for g in range(KVH):
        k = jnp.where(core == g, keys[0], keys[1]).astype(jnp.bfloat16)
        v = jnp.where(core == g, values[0], values[1]).astype(jnp.bfloat16)
        q = rows_ref[g].astype(jnp.bfloat16)
        s = lax.dot_general(q, k, nt, preferred_element_type=jnp.float32) * scale
        s = jnp.where(visible, s, LOW_SCORE)
        top = jnp.max(s, axis=1, keepdims=True)
        w = jnp.where(visible, jnp.exp2(s - top), 0.0).astype(jnp.bfloat16)
        total_out = jnp.dot(w, jnp.concatenate([v, ones], axis=1), preferred_element_type=jnp.float32)
        total = total_out[:, HD:]
        out_ref[g] = total_out[:, :HD] / total
        lse_ref[g] = top + jnp.log(total) * LOG2E


def project_kernel(per, hist_ref, out_ref, lse_ref, match_ref, first_ref, w_hbm, y_ref, w_ref, sems):
    depth = KVH * HD
    ready = first_ref.shape[0] // depth
    copies = fetch(
        [
            (w_hbm.at[pl.ds((ready + i) * depth, depth)], w_ref.at[pl.ds(i * depth, depth)])
            for i in range(w_ref.shape[0] // depth)
        ],
        sems,
    )
    tokens = y_ref.shape[0]
    holders = match_ref.shape[2] // per
    hist = hist_ref[...].astype(jnp.float32)
    fold = LANES // per
    row = lax.broadcasted_iota(jnp.int32, (holders, LANES), 0)
    lane = lax.broadcasted_iota(jnp.int32, (holders, LANES), 1)

    def times(heads, weights):
        lhs = jnp.concatenate(heads, axis=1).astype(jnp.bfloat16)
        return jnp.dot(lhs, weights, preferred_element_type=jnp.float32)

    heads = []
    for g in range(KVH):
        starts = [(KVH * (holders - m) - 1 - g) * (per + 2) for m in range(holders)]
        outs = jnp.concatenate([hist[i : i + per] for i in starts], axis=0).astype(jnp.bfloat16)
        stats = jnp.concatenate([hist[i + per : i + per + 1] for i in starts], axis=0)
        shift = LANES // 2
        while shift >= per:
            stats = stats + pltpu.roll(stats, shift, 1)
            shift //= 2
        stats = jnp.where(row % fold == lane // per, stats, 0.0)
        lse = jnp.concatenate(
            [
                jnp.sum(jnp.where(row // fold == m, stats, 0.0), axis=0, keepdims=True)
                for m in range(holders // fold)
            ],
            axis=1,
        )
        match = match_ref[g] > 0.5
        lse = jnp.where(match, lse, LOW_SCORE)
        own = lse_ref[g]
        top = jnp.maximum(jnp.max(lse, axis=1, keepdims=True), own)
        w = jnp.where(match, jnp.exp2(lse - top[:, :1]), 0.0)
        own_w = jnp.exp2(own - top)
        hi = w.astype(jnp.bfloat16)
        low = (w - hi.astype(jnp.float32)).astype(jnp.bfloat16)
        num = (
            jnp.dot(hi, outs, preferred_element_type=jnp.float32)
            + jnp.dot(low, outs, preferred_element_type=jnp.float32)
            + own_w * out_ref[g]
        )
        att = num / (jnp.sum(w, axis=1, keepdims=True) + own_w)
        heads = heads + [att[r * tokens : (r + 1) * tokens] for r in range(GROUP)]
        if g == 0:
            y = times(heads[: ready * KVH], first_ref[...])
    for i, copy in enumerate(copies):
        copy.wait()
        y = y + times(heads[(ready + i) * KVH : (ready + i + 1) * KVH], w_ref[i * depth : (i + 1) * depth, :])
    y_ref[...] = y.astype(jnp.bfloat16)


VMEM = pl.BlockSpec(memory_space=pltpu.VMEM)
HBM = pl.BlockSpec(memory_space=pltpu.HBM)
ANY = pl.BlockSpec(memory_space=pl.ANY)


def call(kernel, name, out_shape, specs, *operands, outs=None, scratch=(), flops=0, moved=0, limit=16):
    outs = outs or jax.tree.map(lambda _: VMEM, out_shape)
    return pl.pallas_call(
        kernel,
        name=name,
        out_shape=out_shape,
        in_specs=specs,
        out_specs=outs,
        scratch_shapes=scratch,
        cost_estimate=pl.CostEstimate(flops=flops, bytes_accessed=moved, transcendentals=0),
        compiler_params=pltpu.CompilerParams(vmem_limit_bytes=limit << 20),
    )(*operands)


def body(queries, stretch_keys, stretch_values, cache_keys, cache_values, chosen, out_weight):
    devices = lax.axis_size("seq")
    tokens = queries.shape[0]
    cache_rows = cache_keys.shape[0]
    span = BLK // cache_rows
    chips = span // KVH
    key_blocks = cache_rows * devices // BLK
    capacity = (GROUP * TOPK + key_blocks - 1) // key_blocks + 1
    per = capacity * tokens
    f32, bf16 = jnp.float32, jnp.bfloat16
    picks = chosen.transpose(2, 0, 1)

    def partner(bit):
        return [(i, i ^ bit) for i in range(devices)]

    send = call(
        functools.partial(pack_kernel, capacity),
        "pack",
        jax.ShapeDtypeStruct((key_blocks, chips, KVH, per + tokens, HD), bf16),
        [HBM] * 4,
        picks, queries, stretch_keys, stretch_values,
        outs=ANY,
        scratch=[
            pltpu.SMEM(picks.shape, jnp.int32),
            pltpu.VMEM(queries.shape, bf16),
            pltpu.VMEM(stretch_keys.shape, bf16),
            pltpu.VMEM(stretch_values.shape, bf16),
            pltpu.VMEM((KVH, key_blocks, chips, per + tokens, HD), bf16),
            pltpu.SemaphoreType.DMA((4 + KVH,)),
        ],
        limit=60,
    )
    send, cache_keys, cache_values, picks, queries = lax.optimization_barrier(
        (send, cache_keys, cache_values, picks, queries)
    )

    def exchange(x):
        ranks = [list(range(devices))[::-1]]
        return lax.all_to_all(x, "seq", split_axis=0, concat_axis=0, axis_index_groups=ranks, tiled=True)

    got = exchange(send.reshape(devices, per + tokens, HD))

    core = lax.axis_index("seq") % KVH

    def halves(head):
        keys, values = [lax.dynamic_slice_in_dim(x, head * HD, HD, axis=1) for x in (cache_keys, cache_values)]
        return keys.T, values

    k_own, v_own = halves(core)
    k_peer, v_peer = [lax.ppermute(x, "seq", partner(1)) for x in halves(1 - core)]
    holders = devices // KVH
    rows = devices * per
    back, fresh = call(
        functools.partial(attend_kernel, per),
        "attend",
        (
            jax.ShapeDtypeStruct((devices * (per + 2), HD), bf16),
            jax.ShapeDtypeStruct((devices, tokens, HD), bf16),
        ),
        [VMEM] * 5,
        got, k_own, v_own, k_peer, v_peer,
        outs=(ANY, VMEM),
        scratch=[
            pltpu.VMEM((devices * (per + 2), HD), bf16),
            pltpu.SemaphoreType.DMA((rows // STEP,)),
        ],
        flops=8 * rows * cache_rows * HD,
        moved=4 << 20,
        limit=32,
    )
    back, picks, queries, out_weight = lax.optimization_barrier((back, picks, queries, out_weight))
    hist = exchange(back.reshape(devices, (per + 2) // 2, 2, HD))

    ready = EARLY * KVH * HD
    match, query_rows, first = call(
        functools.partial(masks_kernel, chips, capacity),
        "masks",
        (
            jax.ShapeDtypeStruct((KVH, GROUP * tokens, holders * per), f32),
            jax.ShapeDtypeStruct((KVH, GROUP * tokens, HD), f32),
            jax.ShapeDtypeStruct((ready, out_weight.shape[1]), bf16),
        ),
        [VMEM, VMEM, HBM],
        picks, queries, out_weight,
        scratch=[pltpu.SemaphoreType.DMA((1,))],
        limit=50,
    )

    far = lax.ppermute(fresh, "seq", partner(2))
    near, both = [lax.ppermute(x, "seq", partner(1)) for x in (fresh, far)]
    part = jax.ShapeDtypeStruct((KVH, GROUP * tokens, HD), f32)
    out, lse = call(
        functools.partial(fresh_kernel, tokens),
        "fresh",
        (part, part),
        [VMEM] * 5,
        query_rows, fresh, near, far, both,
        flops=8 * H * tokens * devices * tokens * HD,
        moved=1 << 20,
    )
    return call(
        functools.partial(project_kernel, per),
        "project",
        jax.ShapeDtypeStruct((tokens, out_weight.shape[1]), bf16),
        [VMEM] * 5 + [HBM],
        hist.reshape(devices * (per + 2), HD), out, lse, match, first, out_weight,
        scratch=[
            pltpu.VMEM((out_weight.shape[0] - ready, out_weight.shape[1]), bf16),
            pltpu.SemaphoreType.DMA((GROUP - EARLY,)),
        ],
        flops=2 * tokens * out_weight.size,
        moved=out_weight.size * 2,
        limit=50,
    )


def solution(mesh):
    seq = ("grp", "seq")
    return jax.shard_map(
        body,
        mesh=mesh,
        in_specs=(
            P(seq, None),
            P(seq, None),
            P(seq, None),
            P(seq, None),
            P(seq, None),
            P(seq, None, None),
            P(),
        ),
        out_specs=P(seq, None),
        check_vma=False,
    )
```

```python
import functools
import math

import jax
import jax.numpy as jnp
from jax import lax
from jax.experimental import pallas as pl
from jax.experimental.pallas import tpu as pltpu
from jax.sharding import PartitionSpec as P

H = 14
KVH = 2
HD = 128
BLK = 4096
TOPK = 3
GROUP = H // KVH

LOW_SCORE = -1e30
LOG2E = math.log2(math.e)
LANES = 128
EARLY = 3
STEP = 256


def head_rows(q_ref, g):
    q = q_ref[...].astype(jnp.float32)
    return [q[:, h * HD : (h + 1) * HD] for h in range(g * GROUP, (g + 1) * GROUP)]


def slot_match(chosen_ref, g, block, slot, token):
    rows = lax.broadcasted_iota(jnp.int32, block.shape, 0)
    same_token = token == rows
    seen = jnp.zeros(block.shape, jnp.int32)
    found = []
    for h in range(g * GROUP, (g + 1) * GROUP):
        picked = block == chosen_ref[0, :, h : h + 1]
        for t in range(1, TOPK):
            picked = picked | (block == chosen_ref[t, :, h : h + 1])
        found.append(jnp.where(picked & same_token & (seen == slot), 1.0, 0.0))
        seen = seen + picked.astype(jnp.int32)
    return found


def fetch(pairs, sems):
    copies = [pltpu.make_async_copy(src, dst, sems.at[i]) for i, (src, dst) in enumerate(pairs)]
    for copy in copies:
        copy.start()
    return copies


def slot_spread(chosen_ref, g, capacity, tokens, key_blocks):
    lane = lax.broadcasted_iota(jnp.int32, (tokens, LANES), 1)
    head = lane // tokens
    same_token = (lane % tokens == lax.broadcasted_iota(jnp.int32, lane.shape, 0)) & (head < GROUP)
    picks = [[chosen_ref[t, 0, g * GROUP + r] for r in range(GROUP)] for t in range(TOPK)]
    places = []
    for t in range(TOPK):
        block = jnp.zeros(lane.shape, jnp.int32)
        for r in range(GROUP):
            block = jnp.where(head == r, picks[t][r], block)
        rank = jnp.zeros(lane.shape, jnp.int32)
        for r in range(GROUP - 1):
            taken = block == picks[0][r]
            for other in range(1, TOPK):
                taken = taken | (block == picks[other][r])
            rank = rank + jnp.where(taken & (head > r), 1, 0)
        places.append(jnp.where(same_token, block * capacity + rank, -1))
    rows = []
    for place in range(key_blocks * capacity):
        found = places[0] == place
        for t in range(1, TOPK):
            found = found | (places[t] == place)
        rows.append(jnp.where(found, 1.0, 0.0))
    return jnp.concatenate(rows, axis=0).astype(jnp.bfloat16)


def pack_kernel(capacity, chosen_hbm, q_hbm, k_hbm, v_hbm, send_hbm, chosen_ref, q_ref, k_ref, v_ref, send_ref, sems):
    copies = fetch([(chosen_hbm, chosen_ref), (q_hbm, q_ref), (k_hbm, k_ref), (v_hbm, v_ref)], sems)
    tokens = q_ref.shape[0]
    per = capacity * tokens
    key_blocks, chips = send_ref.shape[1:3]
    copies[0].wait()
    spread = [slot_spread(chosen_ref, g, capacity, tokens, key_blocks) for g in range(KVH)]
    for copy in copies[1:]:
        copy.wait()
    sent = []
    for g in range(KVH):
        rows = head_rows(q_ref, g)
        rows = rows + [jnp.zeros_like(rows[0])] * (LANES // tokens - GROUP)
        rows = jnp.concatenate(rows, axis=0).astype(jnp.bfloat16)
        slots = jnp.dot(spread[g], rows, preferred_element_type=jnp.float32).astype(jnp.bfloat16)
        cols = slice(g * HD, (g + 1) * HD)
        fresh = [k_ref[:, cols], v_ref[:, cols]]
        for b in range(key_blocks):
            for chip in range(chips):
                to = (g, key_blocks - 1 - b, chips - 1 - chip)
                send_ref[(*to, slice(0, per))] = slots[b * per : (b + 1) * per]
                send_ref[(*to, slice(per, None))] = fresh[chip % 2]
        sent.append(pltpu.make_async_copy(send_ref.at[g], send_hbm.at[:, :, KVH - 1 - g], sems.at[4 + g]))
        sent[g].start()
    for copy in sent:
        copy.wait()


def masks_kernel(chips, capacity, chosen_ref, q_ref, w_hbm, match_ref, rows_ref, w_ref, sems):
    copies = fetch([(w_hbm.at[: w_ref.shape[0]], w_ref)], sems)
    tokens = q_ref.shape[0]
    per = capacity * tokens
    lane = lax.broadcasted_iota(jnp.int32, (tokens, match_ref.shape[2]), 1)
    block, slot, token = lane // (per * chips), lane % per // tokens, lane % tokens
    for g in range(KVH):
        match_ref[g] = jnp.concatenate(slot_match(chosen_ref, g, block, slot, token), axis=0)
        rows_ref[g] = jnp.concatenate(head_rows(q_ref, g), axis=0)
    for copy in copies:
        copy.wait()


def attend_kernel(per, q_ref, ka_ref, va_ref, kb_ref, vb_ref, out_hbm, fresh_ref, out_ref, sems):
    sources = q_ref.shape[0]
    sent = []
    step = STEP // per
    scale = LOG2E * HD**-0.5
    row = lax.broadcasted_iota(jnp.int32, (per, LANES), 0)
    lane = lax.broadcasted_iota(jnp.int32, (per, LANES), 1)
    diagonal = row == lane % per
    group = lax.broadcasted_iota(jnp.int32, (2, LANES), 1) // per
    second = lax.broadcasted_iota(jnp.int32, (2, LANES), 0)
    ones = jnp.ones(va_ref.shape, jnp.bfloat16)
    fresh_ref[...] = q_ref[:, per:, :]

    def scores(first, count):
        q = q_ref[first : first + count, :per, :].reshape(count * per, HD)
        return [jnp.dot(q, k_ref[...], preferred_element_type=jnp.float32) for k_ref in (ka_ref, kb_ref)]

    wide = 2 * step
    tops = []
    for first in range(0, sources, wide):
        most = [jnp.max(s, axis=1, keepdims=True) for s in scores(first, wide)]
        tops.append(scale * jnp.maximum(*most))
    for first in range(0, sources, step):
        begin = first % wide * per
        top = tops[first // wide][begin : begin + step * per]
        sa, sb = scores(first, step)
        wa = jnp.exp2(sa * scale - top).astype(jnp.bfloat16)
        wb = jnp.exp2(sb * scale - top).astype(jnp.bfloat16)
        both = jnp.dot(
            wa, jnp.concatenate([va_ref[...], ones], axis=1), preferred_element_type=jnp.float32
        ) + jnp.dot(wb, jnp.concatenate([vb_ref[...], ones], axis=1), preferred_element_type=jnp.float32)
        total = both[:, HD:]
        out = both[:, :HD] / total
        lse = top + jnp.log(total) * LOG2E
        rows = []
        for s in range(step):
            part = slice(s * per, (s + 1) * per)
            flat = jnp.sum(jnp.where(diagonal, lse[part], 0.0), axis=0, keepdims=True)
            hi = flat.astype(jnp.bfloat16).astype(jnp.float32)
            mid = (flat - hi).astype(jnp.bfloat16).astype(jnp.float32)
            low = flat - hi - mid
            stats = jnp.where(group == 0, hi, jnp.where(group == 1, mid, jnp.where(group == 2, low, 0.0)))
            rows = rows + [out[part], jnp.where(second == 0, stats, 0.0)]
        done = pl.ds(first * (per + 2), step * (per + 2))
        out_ref[done, :] = jnp.concatenate(rows, axis=0).astype(jnp.bfloat16)
        sent.append(pltpu.make_async_copy(out_ref.at[done], out_hbm.at[done], sems.at[first // step]))
        sent[-1].start()
    for copy in sent:
        copy.wait()


def fresh_kernel(tokens, rows_ref, kv_ref, kv1_ref, kv2_ref, kv3_ref, out_ref, lse_ref):
    sources = kv_ref.shape[0]
    place = lax.axis_index("seq")
    core, odd = place % KVH, place // KVH % 2
    scale = LOG2E * HD**-0.5
    nt = (((1,), (1,)), ((), ()))
    column = lax.broadcasted_iota(jnp.int32, (tokens, sources * tokens), 1)
    query_pos = place * tokens + lax.broadcasted_iota(jnp.int32, column.shape, 0)
    key_pos = (sources - 1 - column // tokens) * tokens + column % tokens
    visible = (key_pos <= query_pos) & (key_pos // BLK == query_pos // BLK)
    visible = jnp.concatenate([visible.astype(jnp.int32)] * GROUP, axis=0) > 0
    ones = jnp.ones((sources * tokens, HD), jnp.bfloat16)
    here, near, far, both = [
        ref[...].astype(jnp.float32).reshape(sources * tokens, HD) for ref in (kv_ref, kv1_ref, kv2_ref, kv3_ref)
    ]
    keys = [jnp.where(odd == 0, here, far), jnp.where(odd == 0, near, both)]
    values = [jnp.where(odd == 0, far, here), jnp.where(odd == 0, both, near)]
    for g in range(KVH):
        k = jnp.where(core == g, keys[0], keys[1]).astype(jnp.bfloat16)
        v = jnp.where(core == g, values[0], values[1]).astype(jnp.bfloat16)
        q = rows_ref[g].astype(jnp.bfloat16)
        s = lax.dot_general(q, k, nt, preferred_element_type=jnp.float32) * scale
        s = jnp.where(visible, s, LOW_SCORE)
        top = jnp.max(s, axis=1, keepdims=True)
        w = jnp.where(visible, jnp.exp2(s - top), 0.0).astype(jnp.bfloat16)
        total_out = jnp.dot(w, jnp.concatenate([v, ones], axis=1), preferred_element_type=jnp.float32)
        total = total_out[:, HD:]
        out_ref[g] = total_out[:, :HD] / total
        lse_ref[g] = top + jnp.log(total) * LOG2E


def project_kernel(per, hist_ref, out_ref, lse_ref, match_ref, first_ref, w_hbm, y_ref, w_ref, sems):
    depth = KVH * HD
    ready = first_ref.shape[0] // depth
    copies = fetch(
        [
            (w_hbm.at[pl.ds((ready + i) * depth, depth)], w_ref.at[pl.ds(i * depth, depth)])
            for i in range(w_ref.shape[0] // depth)
        ],
        sems,
    )
    tokens = y_ref.shape[0]
    holders = match_ref.shape[2] // per
    hist = hist_ref[...].astype(jnp.float32)
    fold = LANES // per
    row = lax.broadcasted_iota(jnp.int32, (holders, LANES), 0)
    lane = lax.broadcasted_iota(jnp.int32, (holders, LANES), 1)

    def times(heads, weights):
        lhs = jnp.concatenate(heads, axis=1).astype(jnp.bfloat16)
        return jnp.dot(lhs, weights, preferred_element_type=jnp.float32)

    heads = []
    for g in range(KVH):
        starts = [(KVH * (holders - m) - 1 - g) * (per + 2) for m in range(holders)]
        outs = jnp.concatenate([hist[i : i + per] for i in starts], axis=0).astype(jnp.bfloat16)
        stats = jnp.concatenate([hist[i + per : i + per + 1] for i in starts], axis=0)
        shift = LANES // 2
        while shift >= per:
            stats = stats + pltpu.roll(stats, shift, 1)
            shift //= 2
        stats = jnp.where(row % fold == lane // per, stats, 0.0)
        lse = jnp.concatenate(
            [
                jnp.sum(jnp.where(row // fold == m, stats, 0.0), axis=0, keepdims=True)
                for m in range(holders // fold)
            ],
            axis=1,
        )
        match = match_ref[g] > 0.5
        lse = jnp.where(match, lse, LOW_SCORE)
        own = lse_ref[g]
        top = jnp.maximum(jnp.max(lse, axis=1, keepdims=True), own)
        w = jnp.where(match, jnp.exp2(lse - top[:, :1]), 0.0)
        own_w = jnp.exp2(own - top)
        hi = w.astype(jnp.bfloat16)
        low = (w - hi.astype(jnp.float32)).astype(jnp.bfloat16)
        num = (
            jnp.dot(hi, outs, preferred_element_type=jnp.float32)
            + jnp.dot(low, outs, preferred_element_type=jnp.float32)
            + own_w * out_ref[g]
        )
        att = num / (jnp.sum(w, axis=1, keepdims=True) + own_w)
        heads = heads + [att[r * tokens : (r + 1) * tokens] for r in range(GROUP)]
        if g == 0:
            y = times(heads[: ready * KVH], first_ref[...])
    for i, copy in enumerate(copies):
        copy.wait()
        y = y + times(heads[(ready + i) * KVH : (ready + i + 1) * KVH], w_ref[i * depth : (i + 1) * depth, :])
    y_ref[...] = y.astype(jnp.bfloat16)


VMEM = pl.BlockSpec(memory_space=pltpu.VMEM)
HBM = pl.BlockSpec(memory_space=pltpu.HBM)
ANY = pl.BlockSpec(memory_space=pl.ANY)


def call(kernel, name, out_shape, specs, *operands, outs=None, scratch=(), flops=0, moved=0, limit=16):
    outs = outs or jax.tree.map(lambda _: VMEM, out_shape)
    return pl.pallas_call(
        kernel,
        name=name,
        out_shape=out_shape,
        in_specs=specs,
        out_specs=outs,
        scratch_shapes=scratch,
        cost_estimate=pl.CostEstimate(flops=flops, bytes_accessed=moved, transcendentals=0),
        compiler_params=pltpu.CompilerParams(vmem_limit_bytes=limit << 20),
    )(*operands)


def body(queries, stretch_keys, stretch_values, cache_keys, cache_values, chosen, out_weight):
    devices = lax.axis_size("seq")
    tokens = queries.shape[0]
    cache_rows = cache_keys.shape[0]
    span = BLK // cache_rows
    chips = span // KVH
    key_blocks = cache_rows * devices // BLK
    capacity = (GROUP * TOPK + key_blocks - 1) // key_blocks + 1
    per = capacity * tokens
    f32, bf16 = jnp.float32, jnp.bfloat16
    picks = chosen.transpose(2, 0, 1)

    def partner(bit):
        return [(i, i ^ bit) for i in range(devices)]

    send = call(
        functools.partial(pack_kernel, capacity),
        "pack",
        jax.ShapeDtypeStruct((key_blocks, chips, KVH, per + tokens, HD), bf16),
        [HBM] * 4,
        picks, queries, stretch_keys, stretch_values,
        outs=ANY,
        scratch=[
            pltpu.SMEM(picks.shape, jnp.int32),
            pltpu.VMEM(queries.shape, bf16),
            pltpu.VMEM(stretch_keys.shape, bf16),
            pltpu.VMEM(stretch_values.shape, bf16),
            pltpu.VMEM((KVH, key_blocks, chips, per + tokens, HD), bf16),
            pltpu.SemaphoreType.DMA((4 + KVH,)),
        ],
        limit=60,
    )
    send, cache_keys, cache_values, picks, queries = lax.optimization_barrier(
        (send, cache_keys, cache_values, picks, queries)
    )

    def exchange(x):
        ranks = [list(range(devices))[::-1]]
        return lax.all_to_all(x, "seq", split_axis=0, concat_axis=0, axis_index_groups=ranks, tiled=True)

    got = exchange(send.reshape(devices, per + tokens, HD))

    core = lax.axis_index("seq") % KVH

    def halves(head):
        keys, values = [lax.dynamic_slice_in_dim(x, head * HD, HD, axis=1) for x in (cache_keys, cache_values)]
        return keys.T, values

    k_own, v_own = halves(core)
    k_peer, v_peer = [lax.ppermute(x, "seq", partner(1)) for x in halves(1 - core)]
    holders = devices // KVH
    rows = devices * per
    back, fresh = call(
        functools.partial(attend_kernel, per),
        "attend",
        (
            jax.ShapeDtypeStruct((devices * (per + 2), HD), bf16),
            jax.ShapeDtypeStruct((devices, tokens, HD), bf16),
        ),
        [VMEM] * 5,
        got, k_own, v_own, k_peer, v_peer,
        outs=(ANY, VMEM),
        scratch=[
            pltpu.VMEM((devices * (per + 2), HD), bf16),
            pltpu.SemaphoreType.DMA((rows // STEP,)),
        ],
        flops=8 * rows * cache_rows * HD,
        moved=4 << 20,
        limit=32,
    )
    back, picks, queries, out_weight = lax.optimization_barrier((back, picks, queries, out_weight))
    hist = exchange(back.reshape(devices, (per + 2) // 2, 2, HD))

    ready = EARLY * KVH * HD
    match, query_rows, first = call(
        functools.partial(masks_kernel, chips, capacity),
        "masks",
        (
            jax.ShapeDtypeStruct((KVH, GROUP * tokens, holders * per), f32),
            jax.ShapeDtypeStruct((KVH, GROUP * tokens, HD), f32),
            jax.ShapeDtypeStruct((ready, out_weight.shape[1]), bf16),
        ),
        [VMEM, VMEM, HBM],
        picks, queries, out_weight,
        scratch=[pltpu.SemaphoreType.DMA((1,))],
        limit=50,
    )

    far = lax.ppermute(fresh, "seq", partner(2))
    near, both = [lax.ppermute(x, "seq", partner(1)) for x in (fresh, far)]
    part = jax.ShapeDtypeStruct((KVH, GROUP * tokens, HD), f32)
    out, lse = call(
        functools.partial(fresh_kernel, tokens),
        "fresh",
        (part, part),
        [VMEM] * 5,
        query_rows, fresh, near, far, both,
        flops=8 * H * tokens * devices * tokens * HD,
        moved=1 << 20,
    )
    return call(
        functools.partial(project_kernel, per),
        "project",
        jax.ShapeDtypeStruct((tokens, out_weight.shape[1]), bf16),
        [VMEM] * 5 + [HBM],
        hist.reshape(devices * (per + 2), HD), out, lse, match, first, out_weight,
        scratch=[
            pltpu.VMEM((out_weight.shape[0] - ready, out_weight.shape[1]), bf16),
            pltpu.SemaphoreType.DMA((GROUP - EARLY,)),
        ],
        flops=2 * tokens * out_weight.size,
        moved=out_weight.size * 2,
        limit=50,
    )


def solution(mesh):
    seq = ("grp", "seq")
    return jax.shard_map(
        body,
        mesh=mesh,
        in_specs=(
            P(seq, None),
            P(seq, None),
            P(seq, None),
            P(seq, None),
            P(seq, None),
            P(seq, None, None),
            P(),
        ),
        out_specs=P(seq, None),
        check_vma=False,
    )
```

```python
import functools
import math

import jax
import jax.numpy as jnp
from jax import lax
from jax.experimental import pallas as pl
from jax.experimental.pallas import tpu as pltpu
from jax.sharding import PartitionSpec as P

H = 14
KVH = 2
HD = 128
BLK = 4096
TOPK = 3
GROUP = H // KVH

LOW_SCORE = -1e30
LOG2E = math.log2(math.e)
LANES = 128
EARLY = 3
STEP = 256


def head_rows(q_ref, g):
    q = q_ref[...].astype(jnp.float32)
    return [q[:, h * HD : (h + 1) * HD] for h in range(g * GROUP, (g + 1) * GROUP)]


def slot_match(chosen_ref, g, block, slot, token):
    rows = lax.broadcasted_iota(jnp.int32, block.shape, 0)
    same_token = token == rows
    seen = jnp.zeros(block.shape, jnp.int32)
    found = []
    for h in range(g * GROUP, (g + 1) * GROUP):
        picked = block == chosen_ref[0, :, h : h + 1]
        for t in range(1, TOPK):
            picked = picked | (block == chosen_ref[t, :, h : h + 1])
        found.append(jnp.where(picked & same_token & (seen == slot), 1.0, 0.0))
        seen = seen + picked.astype(jnp.int32)
    return found


def fetch(pairs, sems):
    copies = [pltpu.make_async_copy(src, dst, sems.at[i]) for i, (src, dst) in enumerate(pairs)]
    for copy in copies:
        copy.start()
    return copies


def slot_spread(chosen_ref, g, capacity, tokens, key_blocks):
    lane = lax.broadcasted_iota(jnp.int32, (tokens, LANES), 1)
    head = lane // tokens
    same_token = (lane % tokens == lax.broadcasted_iota(jnp.int32, lane.shape, 0)) & (head < GROUP)
    picks = [[chosen_ref[t, 0, g * GROUP + r] for r in range(GROUP)] for t in range(TOPK)]
    places = []
    for t in range(TOPK):
        block = jnp.zeros(lane.shape, jnp.int32)
        for r in range(GROUP):
            block = jnp.where(head == r, picks[t][r], block)
        rank = jnp.zeros(lane.shape, jnp.int32)
        for r in range(GROUP - 1):
            taken = block == picks[0][r]
            for other in range(1, TOPK):
                taken = taken | (block == picks[other][r])
            rank = rank + jnp.where(taken & (head > r), 1, 0)
        places.append(jnp.where(same_token, block * capacity + rank, -1))
    rows = []
    for place in range(key_blocks * capacity):
        found = places[0] == place
        for t in range(1, TOPK):
            found = found | (places[t] == place)
        rows.append(jnp.where(found, 1.0, 0.0))
    return jnp.concatenate(rows, axis=0).astype(jnp.bfloat16)


def pack_kernel(capacity, chosen_hbm, q_hbm, k_hbm, v_hbm, send_hbm, chosen_ref, q_ref, k_ref, v_ref, send_ref, sems):
    copies = fetch([(chosen_hbm, chosen_ref), (q_hbm, q_ref), (k_hbm, k_ref), (v_hbm, v_ref)], sems)
    tokens = q_ref.shape[0]
    per = capacity * tokens
    key_blocks, chips = send_ref.shape[1:3]
    copies[0].wait()
    spread = [slot_spread(chosen_ref, g, capacity, tokens, key_blocks) for g in range(KVH)]
    for copy in copies[1:]:
        copy.wait()
    sent = []
    for g in range(KVH):
        rows = head_rows(q_ref, g)
        rows = rows + [jnp.zeros_like(rows[0])] * (LANES // tokens - GROUP)
        rows = jnp.concatenate(rows, axis=0).astype(jnp.bfloat16)
        slots = jnp.dot(spread[g], rows, preferred_element_type=jnp.float32).astype(jnp.bfloat16)
        cols = slice(g * HD, (g + 1) * HD)
        fresh = [k_ref[:, cols], v_ref[:, cols]]
        for b in range(key_blocks):
            for chip in range(chips):
                to = (g, key_blocks - 1 - b, chips - 1 - chip)
                send_ref[(*to, slice(0, per))] = slots[b * per : (b + 1) * per]
                send_ref[(*to, slice(per, None))] = fresh[chip % 2]
        sent.append(pltpu.make_async_copy(send_ref.at[g], send_hbm.at[KVH - 1 - g], sems.at[4 + g]))
        sent[g].start()
    for copy in sent:
        copy.wait()


def masks_kernel(chips, capacity, chosen_ref, q_ref, w_hbm, match_ref, rows_ref, w_ref, sems):
    copies = fetch([(w_hbm.at[: w_ref.shape[0]], w_ref)], sems)
    tokens = q_ref.shape[0]
    per = capacity * tokens
    lane = lax.broadcasted_iota(jnp.int32, (tokens, match_ref.shape[2]), 1)
    block, slot, token = lane // (per * chips), lane % per // tokens, lane % tokens
    for g in range(KVH):
        match_ref[g] = jnp.concatenate(slot_match(chosen_ref, g, block, slot, token), axis=0)
        rows_ref[g] = jnp.concatenate(head_rows(q_ref, g), axis=0)
    for copy in copies:
        copy.wait()


def attend_kernel(per, q_ref, ka_ref, va_ref, kb_ref, vb_ref, out_hbm, fresh_ref, out_ref, sems):
    sources = q_ref.shape[0]
    sent = []
    step = STEP // per
    scale = LOG2E * HD**-0.5
    row = lax.broadcasted_iota(jnp.int32, (per, LANES), 0)
    lane = lax.broadcasted_iota(jnp.int32, (per, LANES), 1)
    diagonal = row == lane % per
    group = lax.broadcasted_iota(jnp.int32, (2, LANES), 1) // per
    second = lax.broadcasted_iota(jnp.int32, (2, LANES), 0)
    ones = jnp.ones(va_ref.shape, jnp.bfloat16)
    fresh_ref[...] = q_ref[:, per:, :]

    def scores(first):
        q = q_ref[first : first + step, :per, :].reshape(step * per, HD)
        return [jnp.dot(q, k_ref[...], preferred_element_type=jnp.float32) for k_ref in (ka_ref, kb_ref)]

    ahead = scores(0)
    for first in range(0, sources, step):
        sa, sb = ahead
        if first + step < sources:
            ahead = scores(first + step)
        top = scale * jnp.maximum(jnp.max(sa, axis=1, keepdims=True), jnp.max(sb, axis=1, keepdims=True))
        wa = jnp.exp2(sa * scale - top).astype(jnp.bfloat16)
        wb = jnp.exp2(sb * scale - top).astype(jnp.bfloat16)
        both = jnp.dot(
            wa, jnp.concatenate([va_ref[...], ones], axis=1), preferred_element_type=jnp.float32
        ) + jnp.dot(wb, jnp.concatenate([vb_ref[...], ones], axis=1), preferred_element_type=jnp.float32)
        total = both[:, HD:]
        out = both[:, :HD] / total
        lse = top + jnp.log(total) * LOG2E
        rows = []
        for s in range(step):
            part = slice(s * per, (s + 1) * per)
            flat = jnp.sum(jnp.where(diagonal, lse[part], 0.0), axis=0, keepdims=True)
            hi = flat.astype(jnp.bfloat16).astype(jnp.float32)
            mid = (flat - hi).astype(jnp.bfloat16).astype(jnp.float32)
            low = flat - hi - mid
            stats = jnp.where(group == 0, hi, jnp.where(group == 1, mid, jnp.where(group == 2, low, 0.0)))
            rows = rows + [out[part], jnp.where(second == 0, stats, 0.0)]
        done = pl.ds(first * (per + 2), step * (per + 2))
        out_ref[done, :] = jnp.concatenate(rows, axis=0).astype(jnp.bfloat16)
        sent.append(pltpu.make_async_copy(out_ref.at[done], out_hbm.at[done], sems.at[first // step]))
        sent[-1].start()
    for copy in sent:
        copy.wait()


def fresh_kernel(tokens, rows_ref, kv_ref, kv1_ref, kv2_ref, kv3_ref, out_ref, lse_ref):
    sources = kv_ref.shape[0]
    place = lax.axis_index("seq")
    core, odd = place % KVH, place // KVH % 2
    scale = LOG2E * HD**-0.5
    nt = (((1,), (1,)), ((), ()))
    column = lax.broadcasted_iota(jnp.int32, (tokens, sources * tokens), 1)
    query_pos = place * tokens + lax.broadcasted_iota(jnp.int32, column.shape, 0)
    rank = column // tokens
    half = sources // KVH
    source = (half - 1 - rank % half) * KVH + KVH - 1 - rank // half
    key_pos = source * tokens + column % tokens
    visible = (key_pos <= query_pos) & (key_pos // BLK == query_pos // BLK)
    visible = jnp.concatenate([visible.astype(jnp.int32)] * GROUP, axis=0) > 0
    ones = jnp.ones((sources * tokens, HD), jnp.bfloat16)
    here, near, far, both = [
        ref[...].astype(jnp.float32).reshape(sources * tokens, HD) for ref in (kv_ref, kv1_ref, kv2_ref, kv3_ref)
    ]
    keys = [jnp.where(odd == 0, here, far), jnp.where(odd == 0, near, both)]
    values = [jnp.where(odd == 0, far, here), jnp.where(odd == 0, both, near)]
    for g in range(KVH):
        k = jnp.where(core == g, keys[0], keys[1]).astype(jnp.bfloat16)
        v = jnp.where(core == g, values[0], values[1]).astype(jnp.bfloat16)
        q = rows_ref[g].astype(jnp.bfloat16)
        s = lax.dot_general(q, k, nt, preferred_element_type=jnp.float32) * scale
        s = jnp.where(visible, s, LOW_SCORE)
        top = jnp.max(s, axis=1, keepdims=True)
        w = jnp.where(visible, jnp.exp2(s - top), 0.0).astype(jnp.bfloat16)
        total_out = jnp.dot(w, jnp.concatenate([v, ones], axis=1), preferred_element_type=jnp.float32)
        total = total_out[:, HD:]
        out_ref[g] = total_out[:, :HD] / total
        lse_ref[g] = top + jnp.log(total) * LOG2E


def project_kernel(per, hist_ref, out_ref, lse_ref, match_ref, first_ref, w_hbm, y_ref, w_ref, sems):
    depth = KVH * HD
    ready = first_ref.shape[0] // depth
    copies = fetch(
        [
            (w_hbm.at[pl.ds((ready + i) * depth, depth)], w_ref.at[pl.ds(i * depth, depth)])
            for i in range(w_ref.shape[0] // depth)
        ],
        sems,
    )
    tokens = y_ref.shape[0]
    holders = match_ref.shape[2] // per
    hist = hist_ref[...].astype(jnp.float32)
    fold = LANES // per
    row = lax.broadcasted_iota(jnp.int32, (holders, LANES), 0)
    lane = lax.broadcasted_iota(jnp.int32, (holders, LANES), 1)

    def times(heads, weights):
        lhs = jnp.concatenate(heads, axis=1).astype(jnp.bfloat16)
        return jnp.dot(lhs, weights, preferred_element_type=jnp.float32)

    heads = []
    for g in range(KVH):
        starts = [((KVH - g) * holders - 1 - m) * (per + 2) for m in range(holders)]
        outs = jnp.concatenate([hist[i : i + per] for i in starts], axis=0).astype(jnp.bfloat16)
        stats = jnp.concatenate([hist[i + per : i + per + 1] for i in starts], axis=0)
        shift = LANES // 2
        while shift >= per:
            stats = stats + pltpu.roll(stats, shift, 1)
            shift //= 2
        stats = jnp.where(row % fold == lane // per, stats, 0.0)
        lse = jnp.concatenate(
            [
                jnp.sum(jnp.where(row // fold == m, stats, 0.0), axis=0, keepdims=True)
                for m in range(holders // fold)
            ],
            axis=1,
        )
        match = match_ref[g] > 0.5
        lse = jnp.where(match, lse, LOW_SCORE)
        own = lse_ref[g]
        top = jnp.maximum(jnp.max(lse, axis=1, keepdims=True), own)
        w = jnp.where(match, jnp.exp2(lse - top[:, :1]), 0.0)
        own_w = jnp.exp2(own - top)
        hi = w.astype(jnp.bfloat16)
        low = (w - hi.astype(jnp.float32)).astype(jnp.bfloat16)
        num = (
            jnp.dot(hi, outs, preferred_element_type=jnp.float32)
            + jnp.dot(low, outs, preferred_element_type=jnp.float32)
            + own_w * out_ref[g]
        )
        att = num / (jnp.sum(w, axis=1, keepdims=True) + own_w)
        heads = heads + [att[r * tokens : (r + 1) * tokens] for r in range(GROUP)]
        if g == 0:
            y = times(heads[: ready * KVH], first_ref[...])
    for i, copy in enumerate(copies):
        copy.wait()
        y = y + times(heads[(ready + i) * KVH : (ready + i + 1) * KVH], w_ref[i * depth : (i + 1) * depth, :])
    y_ref[...] = y.astype(jnp.bfloat16)


VMEM = pl.BlockSpec(memory_space=pltpu.VMEM)
HBM = pl.BlockSpec(memory_space=pltpu.HBM)
ANY = pl.BlockSpec(memory_space=pl.ANY)


def call(kernel, name, out_shape, specs, *operands, outs=None, scratch=(), flops=0, moved=0, limit=16):
    outs = outs or jax.tree.map(lambda _: VMEM, out_shape)
    return pl.pallas_call(
        kernel,
        name=name,
        out_shape=out_shape,
        in_specs=specs,
        out_specs=outs,
        scratch_shapes=scratch,
        cost_estimate=pl.CostEstimate(flops=flops, bytes_accessed=moved, transcendentals=0),
        compiler_params=pltpu.CompilerParams(vmem_limit_bytes=limit << 20),
    )(*operands)


def body(queries, stretch_keys, stretch_values, cache_keys, cache_values, chosen, out_weight):
    devices = lax.axis_size("seq")
    tokens = queries.shape[0]
    cache_rows = cache_keys.shape[0]
    span = BLK // cache_rows
    chips = span // KVH
    key_blocks = cache_rows * devices // BLK
    capacity = (GROUP * TOPK + key_blocks - 1) // key_blocks + 1
    per = capacity * tokens
    f32, bf16 = jnp.float32, jnp.bfloat16
    picks = chosen.transpose(2, 0, 1)

    def partner(bit):
        return [(i, i ^ bit) for i in range(devices)]

    send = call(
        functools.partial(pack_kernel, capacity),
        "pack",
        jax.ShapeDtypeStruct((KVH, key_blocks, chips, per + tokens, HD), bf16),
        [HBM] * 4,
        picks, queries, stretch_keys, stretch_values,
        outs=ANY,
        scratch=[
            pltpu.SMEM(picks.shape, jnp.int32),
            pltpu.VMEM(queries.shape, bf16),
            pltpu.VMEM(stretch_keys.shape, bf16),
            pltpu.VMEM(stretch_values.shape, bf16),
            pltpu.VMEM((KVH, key_blocks, chips, per + tokens, HD), bf16),
            pltpu.SemaphoreType.DMA((4 + KVH,)),
        ],
        limit=60,
    )
    send, cache_keys, cache_values, picks, queries = lax.optimization_barrier(
        (send, cache_keys, cache_values, picks, queries)
    )

    def exchange(x):
        ranks = [i for g in range(KVH) for i in range(g, devices, KVH)][::-1]
        return lax.all_to_all(x, "seq", split_axis=0, concat_axis=0, axis_index_groups=[ranks], tiled=True)

    got = exchange(send.reshape(devices, per + tokens, HD))

    core = lax.axis_index("seq") % KVH

    def halves(head):
        keys, values = [lax.dynamic_slice_in_dim(x, head * HD, HD, axis=1) for x in (cache_keys, cache_values)]
        return keys.T, values

    k_own, v_own = halves(core)
    k_peer, v_peer = [lax.ppermute(x, "seq", partner(1)) for x in halves(1 - core)]
    holders = devices // KVH
    rows = devices * per
    back, fresh = call(
        functools.partial(attend_kernel, per),
        "attend",
        (
            jax.ShapeDtypeStruct((devices * (per + 2), HD), bf16),
            jax.ShapeDtypeStruct((devices, tokens, HD), bf16),
        ),
        [VMEM] * 5,
        got, k_own, v_own, k_peer, v_peer,
        outs=(ANY, VMEM),
        scratch=[
            pltpu.VMEM((devices * (per + 2), HD), bf16),
            pltpu.SemaphoreType.DMA((rows // STEP,)),
        ],
        flops=8 * rows * cache_rows * HD,
        moved=4 << 20,
        limit=32,
    )
    back, picks, queries, out_weight = lax.optimization_barrier((back, picks, queries, out_weight))
    hist = exchange(back.reshape(devices, (per + 2) // 2, 2, HD))

    ready = EARLY * KVH * HD
    match, query_rows, first = call(
        functools.partial(masks_kernel, chips, capacity),
        "masks",
        (
            jax.ShapeDtypeStruct((KVH, GROUP * tokens, holders * per), f32),
            jax.ShapeDtypeStruct((KVH, GROUP * tokens, HD), f32),
            jax.ShapeDtypeStruct((ready, out_weight.shape[1]), bf16),
        ),
        [VMEM, VMEM, HBM],
        picks, queries, out_weight,
        scratch=[pltpu.SemaphoreType.DMA((1,))],
        limit=50,
    )

    far = lax.ppermute(fresh, "seq", partner(2))
    near, both = [lax.ppermute(x, "seq", partner(1)) for x in (fresh, far)]
    part = jax.ShapeDtypeStruct((KVH, GROUP * tokens, HD), f32)
    out, lse = call(
        functools.partial(fresh_kernel, tokens),
        "fresh",
        (part, part),
        [VMEM] * 5,
        query_rows, fresh, near, far, both,
        flops=8 * H * tokens * devices * tokens * HD,
        moved=1 << 20,
    )
    return call(
        functools.partial(project_kernel, per),
        "project",
        jax.ShapeDtypeStruct((tokens, out_weight.shape[1]), bf16),
        [VMEM] * 5 + [HBM],
        hist.reshape(devices * (per + 2), HD), out, lse, match, first, out_weight,
        scratch=[
            pltpu.VMEM((out_weight.shape[0] - ready, out_weight.shape[1]), bf16),
            pltpu.SemaphoreType.DMA((GROUP - EARLY,)),
        ],
        flops=2 * tokens * out_weight.size,
        moved=out_weight.size * 2,
        limit=50,
    )


def solution(mesh):
    seq = ("grp", "seq")
    return jax.shard_map(
        body,
        mesh=mesh,
        in_specs=(
            P(seq, None),
            P(seq, None),
            P(seq, None),
            P(seq, None),
            P(seq, None),
            P(seq, None, None),
            P(),
        ),
        out_specs=P(seq, None),
        check_vma=False,
    )
```

```python
import functools
import math

import jax
import jax.numpy as jnp
from jax import lax
from jax.experimental import pallas as pl
from jax.experimental.pallas import tpu as pltpu
from jax.sharding import PartitionSpec as P

H = 14
KVH = 2
HD = 128
BLK = 4096
TOPK = 3
GROUP = H // KVH

LOW_SCORE = -1e30
LOG2E = math.log2(math.e)
LANES = 128
EARLY = 3
STEP = 256


def head_rows(q_ref, g):
    q = q_ref[...].astype(jnp.float32)
    return [q[:, h * HD : (h + 1) * HD] for h in range(g * GROUP, (g + 1) * GROUP)]


def slot_match(chosen_ref, g, block, slot, token):
    rows = lax.broadcasted_iota(jnp.int32, block.shape, 0)
    same_token = token == rows
    seen = jnp.zeros(block.shape, jnp.int32)
    found = []
    for h in range(g * GROUP, (g + 1) * GROUP):
        picked = block == chosen_ref[0, :, h : h + 1]
        for t in range(1, TOPK):
            picked = picked | (block == chosen_ref[t, :, h : h + 1])
        found.append(jnp.where(picked & same_token & (seen == slot), 1.0, 0.0))
        seen = seen + picked.astype(jnp.int32)
    return found


def fetch(pairs, sems):
    copies = [pltpu.make_async_copy(src, dst, sems.at[i]) for i, (src, dst) in enumerate(pairs)]
    for copy in copies:
        copy.start()
    return copies


def slot_spread(chosen_ref, g, capacity, tokens, key_blocks):
    lane = lax.broadcasted_iota(jnp.int32, (tokens, LANES), 1)
    head = lane // tokens
    same_token = (lane % tokens == lax.broadcasted_iota(jnp.int32, lane.shape, 0)) & (head < GROUP)
    picks = [[chosen_ref[t, 0, g * GROUP + r] for r in range(GROUP)] for t in range(TOPK)]
    places = []
    for t in range(TOPK):
        block = jnp.zeros(lane.shape, jnp.int32)
        for r in range(GROUP):
            block = jnp.where(head == r, picks[t][r], block)
        rank = jnp.zeros(lane.shape, jnp.int32)
        for r in range(GROUP - 1):
            taken = block == picks[0][r]
            for other in range(1, TOPK):
                taken = taken | (block == picks[other][r])
            rank = rank + jnp.where(taken & (head > r), 1, 0)
        places.append(jnp.where(same_token, block * capacity + rank, -1))
    rows = []
    for place in range(key_blocks * capacity):
        found = places[0] == place
        for t in range(1, TOPK):
            found = found | (places[t] == place)
        rows.append(jnp.where(found, 1.0, 0.0))
    return jnp.concatenate(rows, axis=0).astype(jnp.bfloat16)


def pack_kernel(capacity, chosen_hbm, q_hbm, k_hbm, v_hbm, send_hbm, chosen_ref, q_ref, k_ref, v_ref, send_ref, sems):
    copies = fetch([(chosen_hbm, chosen_ref), (q_hbm, q_ref), (k_hbm, k_ref), (v_hbm, v_ref)], sems)
    tokens = q_ref.shape[0]
    per = capacity * tokens
    key_blocks, chips = send_ref.shape[1:3]
    copies[0].wait()
    spread = [slot_spread(chosen_ref, g, capacity, tokens, key_blocks) for g in range(KVH)]
    for copy in copies[1:]:
        copy.wait()
    sent = []
    for g in range(KVH):
        rows = head_rows(q_ref, g)
        rows = rows + [jnp.zeros_like(rows[0])] * (LANES // tokens - GROUP)
        rows = jnp.concatenate(rows, axis=0).astype(jnp.bfloat16)
        slots = jnp.dot(spread[g], rows, preferred_element_type=jnp.float32).astype(jnp.bfloat16)
        cols = slice(g * HD, (g + 1) * HD)
        fresh = [k_ref[:, cols], v_ref[:, cols]]
        for b in range(key_blocks):
            for chip in range(chips):
                to = (g, key_blocks - 1 - b, chips - 1 - chip)
                send_ref[(*to, slice(0, per))] = slots[b * per : (b + 1) * per]
                send_ref[(*to, slice(per, None))] = fresh[chip % 2]
        sent.append(pltpu.make_async_copy(send_ref.at[g], send_hbm.at[KVH - 1 - g], sems.at[4 + g]))
        sent[g].start()
    for copy in sent:
        copy.wait()


def masks_kernel(chips, capacity, chosen_ref, q_ref, w_hbm, match_ref, rows_ref, w_ref, sems):
    copies = fetch([(w_hbm.at[: w_ref.shape[0]], w_ref)], sems)
    tokens = q_ref.shape[0]
    per = capacity * tokens
    lane = lax.broadcasted_iota(jnp.int32, (tokens, match_ref.shape[2]), 1)
    holders = match_ref.shape[2] // (per + 2)
    rank = sum((lane >= i * (per + 2)).astype(jnp.int32) for i in range(1, holders))
    place = lane - rank * (per + 2)
    block, slot, token = (holders - 1 - rank) // chips, place // tokens, place % tokens
    for g in range(KVH):
        match_ref[g] = jnp.concatenate(slot_match(chosen_ref, g, block, slot, token), axis=0)
        rows_ref[g] = jnp.concatenate(head_rows(q_ref, g), axis=0)
    for copy in copies:
        copy.wait()


def attend_kernel(per, q_ref, ka_ref, va_ref, kb_ref, vb_ref, out_hbm, fresh_ref, out_ref, sems):
    sources = q_ref.shape[0]
    sent = []
    step = STEP // per
    scale = LOG2E * HD**-0.5
    row = lax.broadcasted_iota(jnp.int32, (per, LANES), 0)
    lane = lax.broadcasted_iota(jnp.int32, (per, LANES), 1)
    diagonal = row == lane % per
    group = lax.broadcasted_iota(jnp.int32, (2, LANES), 1) // per
    second = lax.broadcasted_iota(jnp.int32, (2, LANES), 0)
    ones = jnp.ones(va_ref.shape, jnp.bfloat16)
    fresh_ref[...] = q_ref[:, per:, :]

    def scores(first):
        q = q_ref[first : first + step, :per, :].reshape(step * per, HD)
        return [jnp.dot(q, k_ref[...], preferred_element_type=jnp.float32) for k_ref in (ka_ref, kb_ref)]

    ahead = scores(0)
    for first in range(0, sources, step):
        sa, sb = ahead
        if first + step < sources:
            ahead = scores(first + step)
        top = scale * jnp.maximum(jnp.max(sa, axis=1, keepdims=True), jnp.max(sb, axis=1, keepdims=True))
        wa = jnp.exp2(sa * scale - top).astype(jnp.bfloat16)
        wb = jnp.exp2(sb * scale - top).astype(jnp.bfloat16)
        both = jnp.dot(
            wa, jnp.concatenate([va_ref[...], ones], axis=1), preferred_element_type=jnp.float32
        ) + jnp.dot(wb, jnp.concatenate([vb_ref[...], ones], axis=1), preferred_element_type=jnp.float32)
        total = both[:, HD:]
        out = both[:, :HD] / total
        lse = top + jnp.log(total) * LOG2E
        rows = []
        for s in range(step):
            part = slice(s * per, (s + 1) * per)
            flat = jnp.sum(jnp.where(diagonal, lse[part], 0.0), axis=0, keepdims=True)
            hi = flat.astype(jnp.bfloat16).astype(jnp.float32)
            mid = (flat - hi).astype(jnp.bfloat16).astype(jnp.float32)
            low = flat - hi - mid
            stats = jnp.where(group == 0, hi, jnp.where(group == 1, mid, jnp.where(group == 2, low, 0.0)))
            rows = rows + [out[part], jnp.where(second == 0, stats, 0.0)]
        done = pl.ds(first * (per + 2), step * (per + 2))
        out_ref[done, :] = jnp.concatenate(rows, axis=0).astype(jnp.bfloat16)
        sent.append(pltpu.make_async_copy(out_ref.at[done], out_hbm.at[done], sems.at[first // step]))
        sent[-1].start()
    for copy in sent:
        copy.wait()


def fresh_kernel(tokens, rows_ref, kv_ref, kv1_ref, kv2_ref, kv3_ref, out_ref, lse_ref):
    sources = kv_ref.shape[0]
    place = lax.axis_index("seq")
    core, odd = place % KVH, place // KVH % 2
    scale = LOG2E * HD**-0.5
    nt = (((1,), (1,)), ((), ()))
    column = lax.broadcasted_iota(jnp.int32, (tokens, sources * tokens), 1)
    query_pos = place * tokens + lax.broadcasted_iota(jnp.int32, column.shape, 0)
    rank = column // tokens
    half = sources // KVH
    source = (half - 1 - rank % half) * KVH + KVH - 1 - rank // half
    key_pos = source * tokens + column % tokens
    visible = (key_pos <= query_pos) & (key_pos // BLK == query_pos // BLK)
    visible = jnp.concatenate([visible.astype(jnp.int32)] * GROUP, axis=0) > 0
    ones = jnp.ones((sources * tokens, HD), jnp.bfloat16)
    here, near, far, both = [
        ref[...].astype(jnp.float32).reshape(sources * tokens, HD) for ref in (kv_ref, kv1_ref, kv2_ref, kv3_ref)
    ]
    keys = [jnp.where(odd == 0, here, far), jnp.where(odd == 0, near, both)]
    values = [jnp.where(odd == 0, far, here), jnp.where(odd == 0, both, near)]
    for g in range(KVH):
        k = jnp.where(core == g, keys[0], keys[1]).astype(jnp.bfloat16)
        v = jnp.where(core == g, values[0], values[1]).astype(jnp.bfloat16)
        q = rows_ref[g].astype(jnp.bfloat16)
        s = lax.dot_general(q, k, nt, preferred_element_type=jnp.float32) * scale
        s = jnp.where(visible, s, LOW_SCORE)
        top = jnp.max(s, axis=1, keepdims=True)
        w = jnp.where(visible, jnp.exp2(s - top), 0.0).astype(jnp.bfloat16)
        total_out = jnp.dot(w, jnp.concatenate([v, ones], axis=1), preferred_element_type=jnp.float32)
        total = total_out[:, HD:]
        out_ref[g] = total_out[:, :HD] / total
        lse_ref[g] = top + jnp.log(total) * LOG2E


def project_kernel(per, hist_ref, out_ref, lse_ref, match_ref, first_ref, w_hbm, y_ref, w_ref, sems):
    depth = KVH * HD
    ready = first_ref.shape[0] // depth
    copies = fetch(
        [
            (w_hbm.at[pl.ds((ready + i) * depth, depth)], w_ref.at[pl.ds(i * depth, depth)])
            for i in range(w_ref.shape[0] // depth)
        ],
        sems,
    )
    tokens = y_ref.shape[0]
    stride = per + 2
    count = match_ref.shape[2]
    holders = count // stride
    picked = lax.broadcasted_iota(jnp.int32, (holders, count), 1) - per == stride * lax.broadcasted_iota(
        jnp.int32, (holders, count), 0
    )
    picked = jnp.where(picked, 1.0, 0.0).astype(jnp.bfloat16)
    lane = lax.broadcasted_iota(jnp.int32, (holders, LANES), 1)
    begin = stride * lax.broadcasted_iota(jnp.int32, (holders, LANES), 0)

    def times(heads, weights):
        lhs = jnp.concatenate(heads, axis=1).astype(jnp.bfloat16)
        return jnp.dot(lhs, weights, preferred_element_type=jnp.float32)

    heads = []
    for g in range(KVH):
        outs = hist_ref[(KVH - 1 - g) * count : (KVH - g) * count, :]
        stats = jnp.dot(picked, outs, preferred_element_type=jnp.float32)
        shift = LANES // 2
        while shift >= per:
            stats = stats + pltpu.roll(stats, shift, 1)
            shift //= 2
        stats = pltpu.roll(stats, 0, 1, stride=2, stride_axis=0)
        tiles = []
        for first in range(0, count, LANES):
            inside = (lane + first >= begin) & (lane + first < begin + stride)
            tiles.append(jnp.sum(jnp.where(inside, stats, 0.0), axis=0, keepdims=True))
        lse = jnp.concatenate(tiles, axis=1)[:, :count]
        match = match_ref[g] > 0.5
        lse = jnp.where(match, lse, LOW_SCORE)
        own = lse_ref[g]
        top = jnp.maximum(jnp.max(lse, axis=1, keepdims=True), own)
        w = jnp.where(match, jnp.exp2(lse - top[:, :1]), 0.0)
        own_w = jnp.exp2(own - top)
        hi = w.astype(jnp.bfloat16)
        low = (w - hi.astype(jnp.float32)).astype(jnp.bfloat16)
        num = (
            jnp.dot(hi, outs, preferred_element_type=jnp.float32)
            + jnp.dot(low, outs, preferred_element_type=jnp.float32)
            + own_w * out_ref[g]
        )
        att = num / (jnp.sum(w, axis=1, keepdims=True) + own_w)
        heads = heads + [att[r * tokens : (r + 1) * tokens] for r in range(GROUP)]
        if g == 0:
            y = times(heads[: ready * KVH], first_ref[...])
    for i, copy in enumerate(copies):
        copy.wait()
        y = y + times(heads[(ready + i) * KVH : (ready + i + 1) * KVH], w_ref[i * depth : (i + 1) * depth, :])
    y_ref[...] = y.astype(jnp.bfloat16)


VMEM = pl.BlockSpec(memory_space=pltpu.VMEM)
HBM = pl.BlockSpec(memory_space=pltpu.HBM)
ANY = pl.BlockSpec(memory_space=pl.ANY)


def call(kernel, name, out_shape, specs, *operands, outs=None, scratch=(), flops=0, moved=0, limit=16):
    outs = outs or jax.tree.map(lambda _: VMEM, out_shape)
    return pl.pallas_call(
        kernel,
        name=name,
        out_shape=out_shape,
        in_specs=specs,
        out_specs=outs,
        scratch_shapes=scratch,
        cost_estimate=pl.CostEstimate(flops=flops, bytes_accessed=moved, transcendentals=0),
        compiler_params=pltpu.CompilerParams(vmem_limit_bytes=limit << 20),
    )(*operands)


def body(queries, stretch_keys, stretch_values, cache_keys, cache_values, chosen, out_weight):
    devices = lax.axis_size("seq")
    tokens = queries.shape[0]
    cache_rows = cache_keys.shape[0]
    span = BLK // cache_rows
    chips = span // KVH
    key_blocks = cache_rows * devices // BLK
    capacity = (GROUP * TOPK + key_blocks - 1) // key_blocks + 1
    per = capacity * tokens
    f32, bf16 = jnp.float32, jnp.bfloat16
    picks = chosen.transpose(2, 0, 1)

    def partner(bit):
        return [(i, i ^ bit) for i in range(devices)]

    send = call(
        functools.partial(pack_kernel, capacity),
        "pack",
        jax.ShapeDtypeStruct((KVH, key_blocks, chips, per + tokens, HD), bf16),
        [HBM] * 4,
        picks, queries, stretch_keys, stretch_values,
        outs=ANY,
        scratch=[
            pltpu.SMEM(picks.shape, jnp.int32),
            pltpu.VMEM(queries.shape, bf16),
            pltpu.VMEM(stretch_keys.shape, bf16),
            pltpu.VMEM(stretch_values.shape, bf16),
            pltpu.VMEM((KVH, key_blocks, chips, per + tokens, HD), bf16),
            pltpu.SemaphoreType.DMA((4 + KVH,)),
        ],
        limit=60,
    )
    send, cache_keys, cache_values, picks, queries = lax.optimization_barrier(
        (send, cache_keys, cache_values, picks, queries)
    )

    def exchange(x):
        ranks = [i for g in range(KVH) for i in range(g, devices, KVH)][::-1]
        return lax.all_to_all(x, "seq", split_axis=0, concat_axis=0, axis_index_groups=[ranks], tiled=True)

    got = exchange(send.reshape(devices, per + tokens, HD))

    core = lax.axis_index("seq") % KVH

    def halves(head):
        keys, values = [lax.dynamic_slice_in_dim(x, head * HD, HD, axis=1) for x in (cache_keys, cache_values)]
        return keys.T, values

    k_own, v_own = halves(core)
    k_peer, v_peer = [lax.ppermute(x, "seq", partner(1)) for x in halves(1 - core)]
    holders = devices // KVH
    rows = devices * per
    back, fresh = call(
        functools.partial(attend_kernel, per),
        "attend",
        (
            jax.ShapeDtypeStruct((devices * (per + 2), HD), bf16),
            jax.ShapeDtypeStruct((devices, tokens, HD), bf16),
        ),
        [VMEM] * 5,
        got, k_own, v_own, k_peer, v_peer,
        outs=(ANY, VMEM),
        scratch=[
            pltpu.VMEM((devices * (per + 2), HD), bf16),
            pltpu.SemaphoreType.DMA((rows // STEP,)),
        ],
        flops=8 * rows * cache_rows * HD,
        moved=4 << 20,
        limit=32,
    )
    back, picks, queries, out_weight = lax.optimization_barrier((back, picks, queries, out_weight))
    hist = exchange(back.reshape(devices, (per + 2) // 2, 2, HD))

    ready = EARLY * KVH * HD
    match, query_rows, first = call(
        functools.partial(masks_kernel, chips, capacity),
        "masks",
        (
            jax.ShapeDtypeStruct((KVH, GROUP * tokens, holders * (per + 2)), f32),
            jax.ShapeDtypeStruct((KVH, GROUP * tokens, HD), f32),
            jax.ShapeDtypeStruct((ready, out_weight.shape[1]), bf16),
        ),
        [VMEM, VMEM, HBM],
        picks, queries, out_weight,
        scratch=[pltpu.SemaphoreType.DMA((1,))],
        limit=50,
    )

    far = lax.ppermute(fresh, "seq", partner(2))
    near, both = [lax.ppermute(x, "seq", partner(1)) for x in (fresh, far)]
    part = jax.ShapeDtypeStruct((KVH, GROUP * tokens, HD), f32)
    out, lse = call(
        functools.partial(fresh_kernel, tokens),
        "fresh",
        (part, part),
        [VMEM] * 5,
        query_rows, fresh, near, far, both,
        flops=8 * H * tokens * devices * tokens * HD,
        moved=1 << 20,
    )
    return call(
        functools.partial(project_kernel, per),
        "project",
        jax.ShapeDtypeStruct((tokens, out_weight.shape[1]), bf16),
        [VMEM] * 5 + [HBM],
        hist.reshape(devices * (per + 2), HD), out, lse, match, first, out_weight,
        scratch=[
            pltpu.VMEM((out_weight.shape[0] - ready, out_weight.shape[1]), bf16),
            pltpu.SemaphoreType.DMA((GROUP - EARLY,)),
        ],
        flops=2 * tokens * out_weight.size,
        moved=out_weight.size * 2,
        limit=50,
    )


def solution(mesh):
    seq = ("grp", "seq")
    return jax.shard_map(
        body,
        mesh=mesh,
        in_specs=(
            P(seq, None),
            P(seq, None),
            P(seq, None),
            P(seq, None),
            P(seq, None),
            P(seq, None, None),
            P(),
        ),
        out_specs=P(seq, None),
        check_vma=False,
    )
```

```python
import functools
import math

import jax
import jax.numpy as jnp
from jax import lax
from jax.experimental import pallas as pl
from jax.experimental.pallas import tpu as pltpu
from jax.sharding import PartitionSpec as P

H = 14
KVH = 2
HD = 128
BLK = 4096
TOPK = 3
GROUP = H // KVH

LOW_SCORE = -1e30
LOG2E = math.log2(math.e)
LANES = 128
EARLY = 3
STEP = 256


def head_rows(q_ref, g):
    q = q_ref[...].astype(jnp.float32)
    return [q[:, h * HD : (h + 1) * HD] for h in range(g * GROUP, (g + 1) * GROUP)]


def slot_match(chosen_ref, g, block, slot, token):
    rows = lax.broadcasted_iota(jnp.int32, block.shape, 0)
    same_token = token == rows
    seen = jnp.zeros(block.shape, jnp.int32)
    found = []
    for h in range(g * GROUP, (g + 1) * GROUP):
        picked = block == chosen_ref[0, :, h : h + 1]
        for t in range(1, TOPK):
            picked = picked | (block == chosen_ref[t, :, h : h + 1])
        found.append(jnp.where(picked & same_token & (seen == slot), 1.0, 0.0))
        seen = seen + picked.astype(jnp.int32)
    return found


def fetch(pairs, sems):
    copies = [pltpu.make_async_copy(src, dst, sems.at[i]) for i, (src, dst) in enumerate(pairs)]
    for copy in copies:
        copy.start()
    return copies


def slot_spread(chosen_ref, g, capacity, tokens, key_blocks):
    lane = lax.broadcasted_iota(jnp.int32, (tokens, LANES), 1)
    head = lane // tokens
    same_token = (lane % tokens == lax.broadcasted_iota(jnp.int32, lane.shape, 0)) & (head < GROUP)
    picks = [[chosen_ref[t, 0, g * GROUP + r] for r in range(GROUP)] for t in range(TOPK)]
    places = []
    for t in range(TOPK):
        block = jnp.zeros(lane.shape, jnp.int32)
        for r in range(GROUP):
            block = jnp.where(head == r, picks[t][r], block)
        rank = jnp.zeros(lane.shape, jnp.int32)
        for r in range(GROUP - 1):
            taken = block == picks[0][r]
            for other in range(1, TOPK):
                taken = taken | (block == picks[other][r])
            rank = rank + jnp.where(taken & (head > r), 1, 0)
        places.append(jnp.where(same_token, block * capacity + rank, -1))
    rows = []
    for place in range(key_blocks * capacity):
        found = places[0] == place
        for t in range(1, TOPK):
            found = found | (places[t] == place)
        rows.append(jnp.where(found, 1.0, 0.0))
    return jnp.concatenate(rows, axis=0).astype(jnp.bfloat16)


def pack_kernel(capacity, chosen_hbm, q_hbm, k_hbm, v_hbm, send_hbm, chosen_ref, q_ref, k_ref, v_ref, send_ref, sems):
    copies = fetch([(chosen_hbm, chosen_ref), (q_hbm, q_ref), (k_hbm, k_ref), (v_hbm, v_ref)], sems)
    tokens = q_ref.shape[0]
    per = capacity * tokens
    key_blocks, chips = send_ref.shape[1:3]
    copies[0].wait()
    spread = [slot_spread(chosen_ref, g, capacity, tokens, key_blocks) for g in range(KVH)]
    for copy in copies[1:]:
        copy.wait()
    sent = []
    for g in range(KVH):
        rows = head_rows(q_ref, g)
        rows = rows + [jnp.zeros_like(rows[0])] * (LANES // tokens - GROUP)
        rows = jnp.concatenate(rows, axis=0).astype(jnp.bfloat16)
        slots = jnp.dot(spread[g], rows, preferred_element_type=jnp.float32).astype(jnp.bfloat16)
        cols = slice(g * HD, (g + 1) * HD)
        fresh = [k_ref[:, cols], v_ref[:, cols]]
        for b in range(key_blocks):
            for chip in range(chips):
                to = (g, key_blocks - 1 - b, chips - 1 - chip)
                send_ref[(*to, slice(0, per))] = slots[b * per : (b + 1) * per]
                send_ref[(*to, slice(per, None))] = fresh[chip % 2]
        sent.append(pltpu.make_async_copy(send_ref.at[g], send_hbm.at[KVH - 1 - g], sems.at[4 + g]))
        sent[g].start()
    for copy in sent:
        copy.wait()


def masks_kernel(chips, capacity, chosen_ref, q_ref, w_hbm, match_ref, rows_ref, w_ref, sems):
    copies = fetch([(w_hbm.at[: w_ref.shape[0]], w_ref)], sems)
    tokens = q_ref.shape[0]
    per = capacity * tokens
    lane = lax.broadcasted_iota(jnp.int32, (tokens, match_ref.shape[2]), 1)
    block, slot, token = lane // (per * chips), lane % per // tokens, lane % tokens
    for g in range(KVH):
        match_ref[g] = jnp.concatenate(slot_match(chosen_ref, g, block, slot, token), axis=0)
        rows_ref[g] = jnp.concatenate(head_rows(q_ref, g), axis=0)
    for copy in copies:
        copy.wait()


def attend_kernel(per, q_ref, ka_ref, va_ref, kb_ref, vb_ref, out_hbm, fresh_ref, out_ref, sems):
    sources = q_ref.shape[0]
    sent = []
    step = STEP // per
    scale = LOG2E * HD**-0.5
    row = lax.broadcasted_iota(jnp.int32, (per, LANES), 0)
    lane = lax.broadcasted_iota(jnp.int32, (per, LANES), 1)
    diagonal = row == lane % per
    group = lax.broadcasted_iota(jnp.int32, (2, LANES), 1) // per
    second = lax.broadcasted_iota(jnp.int32, (2, LANES), 0)
    ones = jnp.ones(va_ref.shape, jnp.bfloat16)
    fresh_ref[...] = q_ref[:, per:, :]

    def scores(first):
        q = q_ref[first : first + step, :per, :].reshape(step * per, HD)
        return [jnp.dot(q, k_ref[...], preferred_element_type=jnp.float32) for k_ref in (ka_ref, kb_ref)]

    ahead = scores(0)
    for first in range(0, sources, step):
        sa, sb = ahead
        if first + step < sources:
            ahead = scores(first + step)
        top = scale * jnp.maximum(jnp.max(sa, axis=1, keepdims=True), jnp.max(sb, axis=1, keepdims=True))
        wa = jnp.exp2(sa * scale - top).astype(jnp.bfloat16)
        wb = jnp.exp2(sb * scale - top).astype(jnp.bfloat16)
        both = jnp.dot(
            wa, jnp.concatenate([va_ref[...], ones], axis=1), preferred_element_type=jnp.float32
        ) + jnp.dot(wb, jnp.concatenate([vb_ref[...], ones], axis=1), preferred_element_type=jnp.float32)
        total = both[:, HD:]
        out = both[:, :HD] / total
        lse = top + jnp.log(total) * LOG2E
        rows = []
        for s in range(step):
            part = slice(s * per, (s + 1) * per)
            flat = jnp.sum(jnp.where(diagonal, lse[part], 0.0), axis=0, keepdims=True)
            hi = flat.astype(jnp.bfloat16).astype(jnp.float32)
            mid = (flat - hi).astype(jnp.bfloat16).astype(jnp.float32)
            low = flat - hi - mid
            stats = jnp.where(group == 0, hi, jnp.where(group == 1, mid, jnp.where(group == 2, low, 0.0)))
            rows = rows + [out[part], jnp.where(second == 0, stats, 0.0)]
        done = pl.ds(first * (per + 2), step * (per + 2))
        out_ref[done, :] = jnp.concatenate(rows, axis=0).astype(jnp.bfloat16)
        sent.append(pltpu.make_async_copy(out_ref.at[done], out_hbm.at[done], sems.at[first // step]))
        sent[-1].start()
    for copy in sent:
        copy.wait()


def fresh_kernel(tokens, rows_ref, kv_ref, kv1_ref, kv2_ref, kv3_ref, out_ref, lse_ref):
    sources = kv_ref.shape[0]
    place = lax.axis_index("seq")
    core, odd = place % KVH, place // KVH % 2
    scale = LOG2E * HD**-0.5
    nt = (((1,), (1,)), ((), ()))
    column = lax.broadcasted_iota(jnp.int32, (tokens, sources * tokens), 1)
    query_pos = place * tokens + lax.broadcasted_iota(jnp.int32, column.shape, 0)
    rank = column // tokens
    half = sources // KVH
    source = (half - 1 - rank % half) * KVH + KVH - 1 - rank // half
    key_pos = source * tokens + column % tokens
    visible = (key_pos <= query_pos) & (key_pos // BLK == query_pos // BLK)
    visible = jnp.concatenate([visible.astype(jnp.int32)] * GROUP, axis=0) > 0
    ones = jnp.ones((sources * tokens, HD), jnp.bfloat16)
    here, near, far, both = [
        ref[...].astype(jnp.float32).reshape(sources * tokens, HD) for ref in (kv_ref, kv1_ref, kv2_ref, kv3_ref)
    ]
    keys = [jnp.where(odd == 0, here, far), jnp.where(odd == 0, near, both)]
    values = [jnp.where(odd == 0, far, here), jnp.where(odd == 0, both, near)]
    for g in range(KVH):
        k = jnp.where(core == g, keys[0], keys[1]).astype(jnp.bfloat16)
        v = jnp.where(core == g, values[0], values[1]).astype(jnp.bfloat16)
        q = rows_ref[g].astype(jnp.bfloat16)
        s = lax.dot_general(q, k, nt, preferred_element_type=jnp.float32) * scale
        s = jnp.where(visible, s, LOW_SCORE)
        top = jnp.max(s, axis=1, keepdims=True)
        w = jnp.where(visible, jnp.exp2(s - top), 0.0).astype(jnp.bfloat16)
        total_out = jnp.dot(w, jnp.concatenate([v, ones], axis=1), preferred_element_type=jnp.float32)
        total = total_out[:, HD:]
        out_ref[g] = total_out[:, :HD] / total
        lse_ref[g] = top + jnp.log(total) * LOG2E


def project_kernel(per, hist_ref, out_ref, lse_ref, match_ref, first_ref, w_hbm, y_ref, w_ref, rows_ref, sems):
    depth = KVH * HD
    ready = first_ref.shape[0] // depth
    copies = fetch(
        [
            (w_hbm.at[pl.ds((ready + i) * depth, depth)], w_ref.at[pl.ds(i * depth, depth)])
            for i in range(w_ref.shape[0] // depth)
        ],
        sems,
    )
    tokens = y_ref.shape[0]
    holders = match_ref.shape[2] // per
    rows_ref[...] = hist_ref[...].astype(jnp.float32)
    fold = LANES // per
    row = lax.broadcasted_iota(jnp.int32, (holders, LANES), 0)
    lane = lax.broadcasted_iota(jnp.int32, (holders, LANES), 1)

    def times(heads, weights):
        lhs = jnp.concatenate(heads, axis=1).astype(jnp.bfloat16)
        return jnp.dot(lhs, weights, preferred_element_type=jnp.float32)

    heads = []
    for g in range(KVH):
        starts = [((KVH - g) * holders - 1 - m) * (per + 2) for m in range(holders)]
        outs = jnp.concatenate([rows_ref[i : i + per, :] for i in starts], axis=0).astype(jnp.bfloat16)
        stats = jnp.concatenate([rows_ref[i + per : i + per + 1, :] for i in starts], axis=0)
        shift = LANES // 2
        while shift >= per:
            stats = stats + pltpu.roll(stats, shift, 1)
            shift //= 2
        stats = jnp.where(row % fold == lane // per, stats, 0.0)
        lse = jnp.concatenate(
            [
                jnp.sum(jnp.where(row // fold == m, stats, 0.0), axis=0, keepdims=True)
                for m in range(holders // fold)
            ],
            axis=1,
        )
        match = match_ref[g] > 0.5
        lse = jnp.where(match, lse, LOW_SCORE)
        own = lse_ref[g]
        top = jnp.maximum(jnp.max(lse, axis=1, keepdims=True), own)
        w = jnp.where(match, jnp.exp2(lse - top[:, :1]), 0.0)
        own_w = jnp.exp2(own - top)
        hi = w.astype(jnp.bfloat16)
        low = (w - hi.astype(jnp.float32)).astype(jnp.bfloat16)
        num = (
            jnp.dot(hi, outs, preferred_element_type=jnp.float32)
            + jnp.dot(low, outs, preferred_element_type=jnp.float32)
            + own_w * out_ref[g]
        )
        att = num / (jnp.sum(w, axis=1, keepdims=True) + own_w)
        heads = heads + [att[r * tokens : (r + 1) * tokens] for r in range(GROUP)]
        if g == 0:
            y = times(heads[: ready * KVH], first_ref[...])
    for i, copy in enumerate(copies):
        copy.wait()
        y = y + times(heads[(ready + i) * KVH : (ready + i + 1) * KVH], w_ref[i * depth : (i + 1) * depth, :])
    y_ref[...] = y.astype(jnp.bfloat16)


VMEM = pl.BlockSpec(memory_space=pltpu.VMEM)
HBM = pl.BlockSpec(memory_space=pltpu.HBM)
ANY = pl.BlockSpec(memory_space=pl.ANY)


def call(kernel, name, out_shape, specs, *operands, outs=None, scratch=(), flops=0, moved=0, limit=16):
    outs = outs or jax.tree.map(lambda _: VMEM, out_shape)
    return pl.pallas_call(
        kernel,
        name=name,
        out_shape=out_shape,
        in_specs=specs,
        out_specs=outs,
        scratch_shapes=scratch,
        cost_estimate=pl.CostEstimate(flops=flops, bytes_accessed=moved, transcendentals=0),
        compiler_params=pltpu.CompilerParams(vmem_limit_bytes=limit << 20),
    )(*operands)


def body(queries, stretch_keys, stretch_values, cache_keys, cache_values, chosen, out_weight):
    devices = lax.axis_size("seq")
    tokens = queries.shape[0]
    cache_rows = cache_keys.shape[0]
    span = BLK // cache_rows
    chips = span // KVH
    key_blocks = cache_rows * devices // BLK
    capacity = (GROUP * TOPK + key_blocks - 1) // key_blocks + 1
    per = capacity * tokens
    f32, bf16 = jnp.float32, jnp.bfloat16
    picks = chosen.transpose(2, 0, 1)

    def partner(bit):
        return [(i, i ^ bit) for i in range(devices)]

    send = call(
        functools.partial(pack_kernel, capacity),
        "pack",
        jax.ShapeDtypeStruct((KVH, key_blocks, chips, per + tokens, HD), bf16),
        [HBM] * 4,
        picks, queries, stretch_keys, stretch_values,
        outs=ANY,
        scratch=[
            pltpu.SMEM(picks.shape, jnp.int32),
            pltpu.VMEM(queries.shape, bf16),
            pltpu.VMEM(stretch_keys.shape, bf16),
            pltpu.VMEM(stretch_values.shape, bf16),
            pltpu.VMEM((KVH, key_blocks, chips, per + tokens, HD), bf16),
            pltpu.SemaphoreType.DMA((4 + KVH,)),
        ],
        limit=60,
    )
    send, cache_keys, cache_values, picks, queries = lax.optimization_barrier(
        (send, cache_keys, cache_values, picks, queries)
    )

    def exchange(x):
        ranks = [i for g in range(KVH) for i in range(g, devices, KVH)][::-1]
        return lax.all_to_all(x, "seq", split_axis=0, concat_axis=0, axis_index_groups=[ranks], tiled=True)

    got = exchange(send.reshape(devices, per + tokens, HD))

    core = lax.axis_index("seq") % KVH

    def halves(head):
        keys, values = [lax.dynamic_slice_in_dim(x, head * HD, HD, axis=1) for x in (cache_keys, cache_values)]
        return keys.T, values

    k_own, v_own = halves(core)
    k_peer, v_peer = [lax.ppermute(x, "seq", partner(1)) for x in halves(1 - core)]
    holders = devices // KVH
    rows = devices * per
    back, fresh = call(
        functools.partial(attend_kernel, per),
        "attend",
        (
            jax.ShapeDtypeStruct((devices * (per + 2), HD), bf16),
            jax.ShapeDtypeStruct((devices, tokens, HD), bf16),
        ),
        [VMEM] * 5,
        got, k_own, v_own, k_peer, v_peer,
        outs=(ANY, VMEM),
        scratch=[
            pltpu.VMEM((devices * (per + 2), HD), bf16),
            pltpu.SemaphoreType.DMA((rows // STEP,)),
        ],
        flops=8 * rows * cache_rows * HD,
        moved=4 << 20,
        limit=32,
    )
    back, picks, queries, out_weight = lax.optimization_barrier((back, picks, queries, out_weight))
    hist = exchange(back.reshape(devices, (per + 2) // 2, 2, HD))

    ready = EARLY * KVH * HD
    match, query_rows, first = call(
        functools.partial(masks_kernel, chips, capacity),
        "masks",
        (
            jax.ShapeDtypeStruct((KVH, GROUP * tokens, holders * per), f32),
            jax.ShapeDtypeStruct((KVH, GROUP * tokens, HD), f32),
            jax.ShapeDtypeStruct((ready, out_weight.shape[1]), bf16),
        ),
        [VMEM, VMEM, HBM],
        picks, queries, out_weight,
        scratch=[pltpu.SemaphoreType.DMA((1,))],
        limit=50,
    )

    far = lax.ppermute(fresh, "seq", partner(2))
    near, both = [lax.ppermute(x, "seq", partner(1)) for x in (fresh, far)]
    part = jax.ShapeDtypeStruct((KVH, GROUP * tokens, HD), f32)
    out, lse = call(
        functools.partial(fresh_kernel, tokens),
        "fresh",
        (part, part),
        [VMEM] * 5,
        query_rows, fresh, near, far, both,
        flops=8 * H * tokens * devices * tokens * HD,
        moved=1 << 20,
    )
    return call(
        functools.partial(project_kernel, per),
        "project",
        jax.ShapeDtypeStruct((tokens, out_weight.shape[1]), bf16),
        [VMEM] * 5 + [HBM],
        hist.reshape(devices * (per + 2), HD), out, lse, match, first, out_weight,
        scratch=[
            pltpu.VMEM((out_weight.shape[0] - ready, out_weight.shape[1]), bf16),
            pltpu.VMEM((devices * (per + 2), HD), f32),
            pltpu.SemaphoreType.DMA((GROUP - EARLY,)),
        ],
        flops=2 * tokens * out_weight.size,
        moved=out_weight.size * 2,
        limit=50,
    )


def solution(mesh):
    seq = ("grp", "seq")
    return jax.shard_map(
        body,
        mesh=mesh,
        in_specs=(
            P(seq, None),
            P(seq, None),
            P(seq, None),
            P(seq, None),
            P(seq, None),
            P(seq, None, None),
            P(),
        ),
        out_specs=P(seq, None),
        check_vma=False,
    )
```

```python
import functools
import math

import jax
import jax.numpy as jnp
from jax import lax
from jax.experimental import pallas as pl
from jax.experimental.pallas import tpu as pltpu
from jax.sharding import PartitionSpec as P

H = 14
KVH = 2
HD = 128
BLK = 4096
TOPK = 3
GROUP = H // KVH

LOW_SCORE = -1e30
LOG2E = math.log2(math.e)
LANES = 128
EARLY = 3
STEP = 256


def head_rows(q_ref, g):
    q = q_ref[...].astype(jnp.float32)
    return [q[:, h * HD : (h + 1) * HD] for h in range(g * GROUP, (g + 1) * GROUP)]


def slot_match(chosen_ref, g, block, slot, token):
    rows = lax.broadcasted_iota(jnp.int32, block.shape, 0)
    same_token = token == rows
    seen = jnp.zeros(block.shape, jnp.int32)
    found = []
    for h in range(g * GROUP, (g + 1) * GROUP):
        picked = block == chosen_ref[0, :, h : h + 1]
        for t in range(1, TOPK):
            picked = picked | (block == chosen_ref[t, :, h : h + 1])
        found.append(jnp.where(picked & same_token & (seen == slot), 1.0, 0.0))
        seen = seen + picked.astype(jnp.int32)
    return found


def fetch(pairs, sems):
    copies = [pltpu.make_async_copy(src, dst, sems.at[i]) for i, (src, dst) in enumerate(pairs)]
    for copy in copies:
        copy.start()
    return copies


def slot_spread(chosen_ref, g, capacity, tokens, key_blocks):
    lane = lax.broadcasted_iota(jnp.int32, (tokens, LANES), 1)
    head = lane // tokens
    same_token = (lane % tokens == lax.broadcasted_iota(jnp.int32, lane.shape, 0)) & (head < GROUP)
    picks = [[chosen_ref[t, 0, g * GROUP + r] for r in range(GROUP)] for t in range(TOPK)]
    places = []
    for t in range(TOPK):
        block = jnp.zeros(lane.shape, jnp.int32)
        for r in range(GROUP):
            block = jnp.where(head == r, picks[t][r], block)
        rank = jnp.zeros(lane.shape, jnp.int32)
        for r in range(GROUP - 1):
            taken = block == picks[0][r]
            for other in range(1, TOPK):
                taken = taken | (block == picks[other][r])
            rank = rank + jnp.where(taken & (head > r), 1, 0)
        places.append(jnp.where(same_token, block * capacity + rank, -1))
    rows = []
    for place in range(key_blocks * capacity):
        found = places[0] == place
        for t in range(1, TOPK):
            found = found | (places[t] == place)
        rows.append(jnp.where(found, 1.0, 0.0))
    return jnp.concatenate(rows, axis=0).astype(jnp.bfloat16)


def pack_kernel(capacity, chosen_hbm, q_hbm, k_hbm, v_hbm, send_hbm, chosen_ref, q_ref, k_ref, v_ref, send_ref, sems):
    copies = fetch([(chosen_hbm, chosen_ref), (q_hbm, q_ref), (k_hbm, k_ref), (v_hbm, v_ref)], sems)
    tokens = q_ref.shape[0]
    per = capacity * tokens
    key_blocks, chips = send_ref.shape[1:3]
    copies[0].wait()
    spread = [slot_spread(chosen_ref, g, capacity, tokens, key_blocks) for g in range(KVH)]
    for copy in copies[1:]:
        copy.wait()
    sent = []
    for g in range(KVH):
        rows = head_rows(q_ref, g)
        rows = rows + [jnp.zeros_like(rows[0])] * (LANES // tokens - GROUP)
        rows = jnp.concatenate(rows, axis=0).astype(jnp.bfloat16)
        slots = jnp.dot(spread[g], rows, preferred_element_type=jnp.float32).astype(jnp.bfloat16)
        cols = slice(g * HD, (g + 1) * HD)
        fresh = [k_ref[:, cols], v_ref[:, cols]]
        for b in range(key_blocks):
            for chip in range(chips):
                to = (g, key_blocks - 1 - b, chips - 1 - chip)
                send_ref[(*to, slice(0, per))] = slots[b * per : (b + 1) * per]
                send_ref[(*to, slice(per, None))] = fresh[chip % 2]
        sent.append(pltpu.make_async_copy(send_ref.at[g], send_hbm.at[KVH - 1 - g], sems.at[4 + g]))
        sent[g].start()
    for copy in sent:
        copy.wait()


def masks_kernel(chips, capacity, chosen_ref, q_ref, w_hbm, match_ref, rows_ref, w_ref, sems):
    copies = fetch([(w_hbm.at[: w_ref.shape[0]], w_ref)], sems)
    tokens = q_ref.shape[0]
    per = capacity * tokens
    lane = lax.broadcasted_iota(jnp.int32, (tokens, match_ref.shape[2]), 1)
    block, slot, token = lane // (per * chips), lane % per // tokens, lane % tokens
    for g in range(KVH):
        match_ref[g] = jnp.concatenate(slot_match(chosen_ref, g, block, slot, token), axis=0)
        rows_ref[g] = jnp.concatenate(head_rows(q_ref, g), axis=0)
    for copy in copies:
        copy.wait()


def attend_kernel(per, q_ref, ka_ref, va_ref, kb_ref, vb_ref, out_hbm, fresh_ref, out_ref, rows_ref, sems):
    sources = q_ref.shape[0]
    sent = []
    step = STEP // per
    scale = LOG2E * HD**-0.5
    row = lax.broadcasted_iota(jnp.int32, (per, LANES), 0)
    lane = lax.broadcasted_iota(jnp.int32, (per, LANES), 1)
    diagonal = row == lane % per
    group = lax.broadcasted_iota(jnp.int32, (2, LANES), 1) // per
    second = lax.broadcasted_iota(jnp.int32, (2, LANES), 0)
    ones = jnp.ones(va_ref.shape, jnp.bfloat16)
    fresh_ref[...] = q_ref[:, per:, :]

    def scores(first):
        q = q_ref[first : first + step, :per, :].reshape(step * per, HD)
        return [jnp.dot(q, k_ref[...], preferred_element_type=jnp.float32) for k_ref in (ka_ref, kb_ref)]

    ahead = scores(0)
    for first in range(0, sources, step):
        sa, sb = ahead
        if first + step < sources:
            ahead = scores(first + step)
        top = scale * jnp.maximum(jnp.max(sa, axis=1, keepdims=True), jnp.max(sb, axis=1, keepdims=True))
        wa = jnp.exp2(sa * scale - top).astype(jnp.bfloat16)
        wb = jnp.exp2(sb * scale - top).astype(jnp.bfloat16)
        both = jnp.dot(
            wa, jnp.concatenate([va_ref[...], ones], axis=1), preferred_element_type=jnp.float32
        ) + jnp.dot(wb, jnp.concatenate([vb_ref[...], ones], axis=1), preferred_element_type=jnp.float32)
        total = both[:, HD:]
        out = both[:, :HD] / total
        lse = top + jnp.log(total) * LOG2E
        for s in range(step):
            part = slice(s * per, (s + 1) * per)
            flat = jnp.sum(jnp.where(diagonal, lse[part], 0.0), axis=0, keepdims=True)
            hi = flat.astype(jnp.bfloat16).astype(jnp.float32)
            mid = (flat - hi).astype(jnp.bfloat16).astype(jnp.float32)
            low = flat - hi - mid
            stats = jnp.where(group == 0, hi, jnp.where(group == 1, mid, jnp.where(group == 2, low, 0.0)))
            begin = (first + s) * (per + 2)
            rows_ref[begin : begin + per, :] = out[part]
            rows_ref[begin + per : begin + per + 2, :] = jnp.where(second == 0, stats, 0.0)
        done = pl.ds(first * (per + 2), step * (per + 2))
        out_ref[done, :] = rows_ref[done, :].astype(jnp.bfloat16)
        sent.append(pltpu.make_async_copy(out_ref.at[done], out_hbm.at[done], sems.at[first // step]))
        sent[-1].start()
    for copy in sent:
        copy.wait()


def fresh_kernel(tokens, rows_ref, kv_ref, kv1_ref, kv2_ref, kv3_ref, out_ref, lse_ref):
    sources = kv_ref.shape[0]
    place = lax.axis_index("seq")
    core, odd = place % KVH, place // KVH % 2
    scale = LOG2E * HD**-0.5
    nt = (((1,), (1,)), ((), ()))
    column = lax.broadcasted_iota(jnp.int32, (tokens, sources * tokens), 1)
    query_pos = place * tokens + lax.broadcasted_iota(jnp.int32, column.shape, 0)
    rank = column // tokens
    half = sources // KVH
    source = (half - 1 - rank % half) * KVH + KVH - 1 - rank // half
    key_pos = source * tokens + column % tokens
    visible = (key_pos <= query_pos) & (key_pos // BLK == query_pos // BLK)
    visible = jnp.concatenate([visible.astype(jnp.int32)] * GROUP, axis=0) > 0
    ones = jnp.ones((sources * tokens, HD), jnp.bfloat16)
    here, near, far, both = [
        ref[...].astype(jnp.float32).reshape(sources * tokens, HD) for ref in (kv_ref, kv1_ref, kv2_ref, kv3_ref)
    ]
    keys = [jnp.where(odd == 0, here, far), jnp.where(odd == 0, near, both)]
    values = [jnp.where(odd == 0, far, here), jnp.where(odd == 0, both, near)]
    for g in range(KVH):
        k = jnp.where(core == g, keys[0], keys[1]).astype(jnp.bfloat16)
        v = jnp.where(core == g, values[0], values[1]).astype(jnp.bfloat16)
        q = rows_ref[g].astype(jnp.bfloat16)
        s = lax.dot_general(q, k, nt, preferred_element_type=jnp.float32) * scale
        s = jnp.where(visible, s, LOW_SCORE)
        top = jnp.max(s, axis=1, keepdims=True)
        w = jnp.where(visible, jnp.exp2(s - top), 0.0).astype(jnp.bfloat16)
        total_out = jnp.dot(w, jnp.concatenate([v, ones], axis=1), preferred_element_type=jnp.float32)
        total = total_out[:, HD:]
        out_ref[g] = total_out[:, :HD] / total
        lse_ref[g] = top + jnp.log(total) * LOG2E


def project_kernel(per, hist_ref, out_ref, lse_ref, match_ref, first_ref, w_hbm, y_ref, w_ref, rows_ref, sems):
    depth = KVH * HD
    ready = first_ref.shape[0] // depth
    copies = fetch(
        [
            (w_hbm.at[pl.ds((ready + i) * depth, depth)], w_ref.at[pl.ds(i * depth, depth)])
            for i in range(w_ref.shape[0] // depth)
        ],
        sems,
    )
    tokens = y_ref.shape[0]
    holders = match_ref.shape[2] // per
    rows_ref[...] = hist_ref[...].astype(jnp.float32)
    fold = LANES // per
    row = lax.broadcasted_iota(jnp.int32, (holders, LANES), 0)
    lane = lax.broadcasted_iota(jnp.int32, (holders, LANES), 1)

    def times(heads, weights):
        lhs = jnp.concatenate(heads, axis=1).astype(jnp.bfloat16)
        return jnp.dot(lhs, weights, preferred_element_type=jnp.float32)

    heads = []
    for g in range(KVH):
        starts = [((KVH - g) * holders - 1 - m) * (per + 2) for m in range(holders)]
        outs = jnp.concatenate([rows_ref[i : i + per, :] for i in starts], axis=0).astype(jnp.bfloat16)
        stats = jnp.concatenate([rows_ref[i + per : i + per + 1, :] for i in starts], axis=0)
        shift = LANES // 2
        while shift >= per:
            stats = stats + pltpu.roll(stats, shift, 1)
            shift //= 2
        stats = jnp.where(row % fold == lane // per, stats, 0.0)
        lse = jnp.concatenate(
            [
                jnp.sum(jnp.where(row // fold == m, stats, 0.0), axis=0, keepdims=True)
                for m in range(holders // fold)
            ],
            axis=1,
        )
        match = match_ref[g] > 0.5
        lse = jnp.where(match, lse, LOW_SCORE)
        own = lse_ref[g]
        top = jnp.maximum(jnp.max(lse, axis=1, keepdims=True), own)
        w = jnp.where(match, jnp.exp2(lse - top[:, :1]), 0.0)
        own_w = jnp.exp2(own - top)
        hi = w.astype(jnp.bfloat16)
        low = (w - hi.astype(jnp.float32)).astype(jnp.bfloat16)
        num = (
            jnp.dot(hi, outs, preferred_element_type=jnp.float32)
            + jnp.dot(low, outs, preferred_element_type=jnp.float32)
            + own_w * out_ref[g]
        )
        att = num / (jnp.sum(w, axis=1, keepdims=True) + own_w)
        heads = heads + [att[r * tokens : (r + 1) * tokens] for r in range(GROUP)]
        if g == 0:
            y = times(heads[: ready * KVH], first_ref[...])
    for i, copy in enumerate(copies):
        copy.wait()
        y = y + times(heads[(ready + i) * KVH : (ready + i + 1) * KVH], w_ref[i * depth : (i + 1) * depth, :])
    y_ref[...] = y.astype(jnp.bfloat16)


VMEM = pl.BlockSpec(memory_space=pltpu.VMEM)
HBM = pl.BlockSpec(memory_space=pltpu.HBM)
ANY = pl.BlockSpec(memory_space=pl.ANY)


def call(kernel, name, out_shape, specs, *operands, outs=None, scratch=(), flops=0, moved=0, limit=16):
    outs = outs or jax.tree.map(lambda _: VMEM, out_shape)
    return pl.pallas_call(
        kernel,
        name=name,
        out_shape=out_shape,
        in_specs=specs,
        out_specs=outs,
        scratch_shapes=scratch,
        cost_estimate=pl.CostEstimate(flops=flops, bytes_accessed=moved, transcendentals=0),
        compiler_params=pltpu.CompilerParams(vmem_limit_bytes=limit << 20),
    )(*operands)


def body(queries, stretch_keys, stretch_values, cache_keys, cache_values, chosen, out_weight):
    devices = lax.axis_size("seq")
    tokens = queries.shape[0]
    cache_rows = cache_keys.shape[0]
    span = BLK // cache_rows
    chips = span // KVH
    key_blocks = cache_rows * devices // BLK
    capacity = (GROUP * TOPK + key_blocks - 1) // key_blocks + 1
    per = capacity * tokens
    f32, bf16 = jnp.float32, jnp.bfloat16
    picks = chosen.transpose(2, 0, 1)

    def partner(bit):
        return [(i, i ^ bit) for i in range(devices)]

    send = call(
        functools.partial(pack_kernel, capacity),
        "pack",
        jax.ShapeDtypeStruct((KVH, key_blocks, chips, per + tokens, HD), bf16),
        [HBM] * 4,
        picks, queries, stretch_keys, stretch_values,
        outs=ANY,
        scratch=[
            pltpu.SMEM(picks.shape, jnp.int32),
            pltpu.VMEM(queries.shape, bf16),
            pltpu.VMEM(stretch_keys.shape, bf16),
            pltpu.VMEM(stretch_values.shape, bf16),
            pltpu.VMEM((KVH, key_blocks, chips, per + tokens, HD), bf16),
            pltpu.SemaphoreType.DMA((4 + KVH,)),
        ],
        limit=60,
    )
    send, cache_keys, cache_values, picks, queries = lax.optimization_barrier(
        (send, cache_keys, cache_values, picks, queries)
    )

    def exchange(x):
        ranks = [i for g in range(KVH) for i in range(g, devices, KVH)][::-1]
        return lax.all_to_all(x, "seq", split_axis=0, concat_axis=0, axis_index_groups=[ranks], tiled=True)

    got = exchange(send.reshape(devices, per + tokens, HD))

    core = lax.axis_index("seq") % KVH

    def halves(head):
        keys, values = [lax.dynamic_slice_in_dim(x, head * HD, HD, axis=1) for x in (cache_keys, cache_values)]
        return keys.T, values

    k_own, v_own = halves(core)
    k_peer, v_peer = [lax.ppermute(x, "seq", partner(1)) for x in halves(1 - core)]
    holders = devices // KVH
    rows = devices * per
    back, fresh = call(
        functools.partial(attend_kernel, per),
        "attend",
        (
            jax.ShapeDtypeStruct((devices * (per + 2), HD), bf16),
            jax.ShapeDtypeStruct((devices, tokens, HD), bf16),
        ),
        [VMEM] * 5,
        got, k_own, v_own, k_peer, v_peer,
        outs=(ANY, VMEM),
        scratch=[
            pltpu.VMEM((devices * (per + 2), HD), bf16),
            pltpu.VMEM((devices * (per + 2), HD), f32),
            pltpu.SemaphoreType.DMA((rows // STEP,)),
        ],
        flops=8 * rows * cache_rows * HD,
        moved=4 << 20,
        limit=32,
    )
    back, picks, queries, out_weight = lax.optimization_barrier((back, picks, queries, out_weight))
    hist = exchange(back.reshape(devices, (per + 2) // 2, 2, HD))

    ready = EARLY * KVH * HD
    match, query_rows, first = call(
        functools.partial(masks_kernel, chips, capacity),
        "masks",
        (
            jax.ShapeDtypeStruct((KVH, GROUP * tokens, holders * per), f32),
            jax.ShapeDtypeStruct((KVH, GROUP * tokens, HD), f32),
            jax.ShapeDtypeStruct((ready, out_weight.shape[1]), bf16),
        ),
        [VMEM, VMEM, HBM],
        picks, queries, out_weight,
        scratch=[pltpu.SemaphoreType.DMA((1,))],
        limit=50,
    )

    far = lax.ppermute(fresh, "seq", partner(2))
    near, both = [lax.ppermute(x, "seq", partner(1)) for x in (fresh, far)]
    part = jax.ShapeDtypeStruct((KVH, GROUP * tokens, HD), f32)
    out, lse = call(
        functools.partial(fresh_kernel, tokens),
        "fresh",
        (part, part),
        [VMEM] * 5,
        query_rows, fresh, near, far, both,
        flops=8 * H * tokens * devices * tokens * HD,
        moved=1 << 20,
    )
    return call(
        functools.partial(project_kernel, per),
        "project",
        jax.ShapeDtypeStruct((tokens, out_weight.shape[1]), bf16),
        [VMEM] * 5 + [HBM],
        hist.reshape(devices * (per + 2), HD), out, lse, match, first, out_weight,
        scratch=[
            pltpu.VMEM((out_weight.shape[0] - ready, out_weight.shape[1]), bf16),
            pltpu.VMEM((devices * (per + 2), HD), f32),
            pltpu.SemaphoreType.DMA((GROUP - EARLY,)),
        ],
        flops=2 * tokens * out_weight.size,
        moved=out_weight.size * 2,
        limit=50,
    )


def solution(mesh):
    seq = ("grp", "seq")
    return jax.shard_map(
        body,
        mesh=mesh,
        in_specs=(
            P(seq, None),
            P(seq, None),
            P(seq, None),
            P(seq, None),
            P(seq, None),
            P(seq, None, None),
            P(),
        ),
        out_specs=P(seq, None),
        check_vma=False,
    )
```

```python
import functools
import math

import jax
import jax.numpy as jnp
from jax import lax
from jax.experimental import pallas as pl
from jax.experimental.pallas import tpu as pltpu
from jax.sharding import PartitionSpec as P

H = 14
KVH = 2
HD = 128
BLK = 4096
TOPK = 3
GROUP = H // KVH

LOW_SCORE = -1e30
LOG2E = math.log2(math.e)
LANES = 128
EARLY = 3
WIDE = 4
STEP = 256


def head_rows(q_ref, g):
    q = q_ref[...].astype(jnp.float32)
    return [q[:, h * HD : (h + 1) * HD] for h in range(g * GROUP, (g + 1) * GROUP)]


def slot_match(chosen_ref, g, block, slot, token):
    rows = lax.broadcasted_iota(jnp.int32, block.shape, 0)
    same_token = token == rows
    seen = jnp.zeros(block.shape, jnp.int32)
    found = []
    for h in range(g * GROUP, (g + 1) * GROUP):
        picked = block == chosen_ref[0, :, h : h + 1]
        for t in range(1, TOPK):
            picked = picked | (block == chosen_ref[t, :, h : h + 1])
        found.append(jnp.where(picked & same_token & (seen == slot), 1.0, 0.0))
        seen = seen + picked.astype(jnp.int32)
    return found


def fetch(pairs, sems):
    copies = [pltpu.make_async_copy(src, dst, sems.at[i]) for i, (src, dst) in enumerate(pairs)]
    for copy in copies:
        copy.start()
    return copies


def slot_spread(chosen_ref, g, capacity, tokens, key_blocks):
    lane = lax.broadcasted_iota(jnp.int32, (tokens, LANES), 1)
    head = lane // tokens
    same_token = (lane % tokens == lax.broadcasted_iota(jnp.int32, lane.shape, 0)) & (head < GROUP)
    picks = [[chosen_ref[t, 0, g * GROUP + r] for r in range(GROUP)] for t in range(TOPK)]
    places = []
    for t in range(TOPK):
        block = jnp.zeros(lane.shape, jnp.int32)
        for r in range(GROUP):
            block = jnp.where(head == r, picks[t][r], block)
        rank = jnp.zeros(lane.shape, jnp.int32)
        for r in range(GROUP - 1):
            taken = block == picks[0][r]
            for other in range(1, TOPK):
                taken = taken | (block == picks[other][r])
            rank = rank + jnp.where(taken & (head > r), 1, 0)
        places.append(jnp.where(same_token, block * capacity + rank, -1))
    rows = []
    for place in range(key_blocks * capacity):
        found = places[0] == place
        for t in range(1, TOPK):
            found = found | (places[t] == place)
        rows.append(jnp.where(found, 1.0, 0.0))
    return jnp.concatenate(rows, axis=0).astype(jnp.bfloat16)


def pack_kernel(capacity, chosen_hbm, q_hbm, k_hbm, v_hbm, send_hbm, chosen_ref, q_ref, k_ref, v_ref, send_ref, sems):
    copies = fetch([(chosen_hbm, chosen_ref), (q_hbm, q_ref), (k_hbm, k_ref), (v_hbm, v_ref)], sems)
    tokens = q_ref.shape[0]
    per = capacity * tokens
    key_blocks, chips = send_ref.shape[1:3]
    copies[0].wait()
    spread = [slot_spread(chosen_ref, g, capacity, tokens, key_blocks) for g in range(KVH)]
    for copy in copies[1:]:
        copy.wait()
    sent = []
    for g in range(KVH):
        rows = head_rows(q_ref, g)
        rows = rows + [jnp.zeros_like(rows[0])] * (LANES // tokens - GROUP)
        rows = jnp.concatenate(rows, axis=0).astype(jnp.bfloat16)
        slots = jnp.dot(spread[g], rows, preferred_element_type=jnp.float32).astype(jnp.bfloat16)
        cols = slice(g * HD, (g + 1) * HD)
        fresh = [k_ref[:, cols], v_ref[:, cols]]
        for b in range(key_blocks):
            for chip in range(chips):
                to = (g, key_blocks - 1 - b, chips - 1 - chip)
                send_ref[(*to, slice(0, per))] = slots[b * per : (b + 1) * per]
                send_ref[(*to, slice(per, None))] = fresh[chip % 2]
        sent.append(pltpu.make_async_copy(send_ref.at[g], send_hbm.at[KVH - 1 - g], sems.at[4 + g]))
        sent[g].start()
    for copy in sent:
        copy.wait()


def masks_kernel(chips, capacity, chosen_ref, q_ref, w_hbm, match_ref, rows_ref, w_ref, sems):
    copies = fetch([(w_hbm.at[: w_ref.shape[0]], w_ref)], sems)
    tokens = q_ref.shape[0]
    per = capacity * tokens
    lane = lax.broadcasted_iota(jnp.int32, (tokens, match_ref.shape[2]), 1)
    block, slot, token = lane // (per * chips), lane % per // tokens, lane % tokens
    for g in range(KVH):
        match_ref[g] = jnp.concatenate(slot_match(chosen_ref, g, block, slot, token), axis=0)
        rows_ref[g] = jnp.concatenate(head_rows(q_ref, g), axis=0)
    for copy in copies:
        copy.wait()


def attend_kernel(per, q_ref, ka_ref, va_ref, kb_ref, vb_ref, out_hbm, fresh_ref, out_ref, sems):
    sources = q_ref.shape[0]
    sent = []
    step = STEP // per
    scale = LOG2E * HD**-0.5
    row = lax.broadcasted_iota(jnp.int32, (per, LANES), 0)
    lane = lax.broadcasted_iota(jnp.int32, (per, LANES), 1)
    diagonal = row == lane % per
    group = lax.broadcasted_iota(jnp.int32, (2, LANES), 1) // per
    second = lax.broadcasted_iota(jnp.int32, (2, LANES), 0)
    ones = jnp.ones(va_ref.shape, jnp.bfloat16)
    fresh_ref[...] = q_ref[:, per:, :]

    def scores(first):
        q = q_ref[first : first + step, :per, :].reshape(step * per, HD)
        return [jnp.dot(q, k_ref[...], preferred_element_type=jnp.float32) for k_ref in (ka_ref, kb_ref)]

    ahead = scores(0)
    for first in range(0, sources, step):
        sa, sb = ahead
        if first + step < sources:
            ahead = scores(first + step)
        top = scale * jnp.maximum(jnp.max(sa, axis=1, keepdims=True), jnp.max(sb, axis=1, keepdims=True))
        wa = jnp.exp2(sa * scale - top).astype(jnp.bfloat16)
        wb = jnp.exp2(sb * scale - top).astype(jnp.bfloat16)
        both = jnp.dot(
            wa, jnp.concatenate([va_ref[...], ones], axis=1), preferred_element_type=jnp.float32
        ) + jnp.dot(wb, jnp.concatenate([vb_ref[...], ones], axis=1), preferred_element_type=jnp.float32)
        total = both[:, HD:]
        out = both[:, :HD] / total
        lse = top + jnp.log(total) * LOG2E
        rows = []
        for s in range(step):
            part = slice(s * per, (s + 1) * per)
            flat = jnp.sum(jnp.where(diagonal, lse[part], 0.0), axis=0, keepdims=True)
            hi = flat.astype(jnp.bfloat16).astype(jnp.float32)
            mid = (flat - hi).astype(jnp.bfloat16).astype(jnp.float32)
            low = flat - hi - mid
            stats = jnp.where(group == 0, hi, jnp.where(group == 1, mid, jnp.where(group == 2, low, 0.0)))
            rows = rows + [out[part], jnp.where(second == 0, stats, 0.0)]
        done = pl.ds(first * (per + 2), step * (per + 2))
        out_ref[done, :] = jnp.concatenate(rows, axis=0).astype(jnp.bfloat16)
        sent.append(pltpu.make_async_copy(out_ref.at[done], out_hbm.at[done], sems.at[first // step]))
        sent[-1].start()
    for copy in sent:
        copy.wait()


def fresh_kernel(tokens, rows_ref, kv_ref, kv1_ref, kv2_ref, kv3_ref, out_ref, lse_ref):
    sources = kv_ref.shape[0]
    place = lax.axis_index("seq")
    core, odd = place % KVH, place // KVH % 2
    scale = LOG2E * HD**-0.5
    nt = (((1,), (1,)), ((), ()))
    column = lax.broadcasted_iota(jnp.int32, (tokens, sources * tokens), 1)
    query_pos = place * tokens + lax.broadcasted_iota(jnp.int32, column.shape, 0)
    rank = column // tokens
    half = sources // KVH
    source = (half - 1 - rank % half) * KVH + KVH - 1 - rank // half
    key_pos = source * tokens + column % tokens
    visible = (key_pos <= query_pos) & (key_pos // BLK == query_pos // BLK)
    visible = jnp.concatenate([visible.astype(jnp.int32)] * GROUP, axis=0) > 0
    ones = jnp.ones((sources * tokens, HD), jnp.bfloat16)
    here, near, far, both = [
        ref[...].astype(jnp.float32).reshape(sources * tokens, HD) for ref in (kv_ref, kv1_ref, kv2_ref, kv3_ref)
    ]
    keys = [jnp.where(odd == 0, here, far), jnp.where(odd == 0, near, both)]
    values = [jnp.where(odd == 0, far, here), jnp.where(odd == 0, both, near)]
    for g in range(KVH):
        k = jnp.where(core == g, keys[0], keys[1]).astype(jnp.bfloat16)
        v = jnp.where(core == g, values[0], values[1]).astype(jnp.bfloat16)
        q = rows_ref[g].astype(jnp.bfloat16)
        s = lax.dot_general(q, k, nt, preferred_element_type=jnp.float32) * scale
        s = jnp.where(visible, s, LOW_SCORE)
        top = jnp.max(s, axis=1, keepdims=True)
        w = jnp.where(visible, jnp.exp2(s - top), 0.0).astype(jnp.bfloat16)
        total_out = jnp.dot(w, jnp.concatenate([v, ones], axis=1), preferred_element_type=jnp.float32)
        total = total_out[:, HD:]
        out_ref[g] = total_out[:, :HD] / total
        lse_ref[g] = top + jnp.log(total) * LOG2E


def project_kernel(per, hist_ref, out_ref, lse_ref, match_ref, first_ref, w_hbm, y_ref, w_ref, rows_ref, sems):
    depth = WIDE * HD
    ready = first_ref.shape[0] // HD
    copies = fetch(
        [
            (w_hbm.at[pl.ds(ready * HD + i * depth, depth)], w_ref.at[pl.ds(i * depth, depth)])
            for i in range(w_ref.shape[0] // depth)
        ],
        sems,
    )
    tokens = y_ref.shape[0]
    holders = match_ref.shape[2] // per
    rows_ref[...] = hist_ref[...].astype(jnp.float32)
    fold = LANES // per
    row = lax.broadcasted_iota(jnp.int32, (holders, LANES), 0)
    lane = lax.broadcasted_iota(jnp.int32, (holders, LANES), 1)

    def times(heads, weights):
        lhs = jnp.concatenate(heads, axis=1).astype(jnp.bfloat16)
        return jnp.dot(lhs, weights, preferred_element_type=jnp.float32)

    heads = []
    for g in range(KVH):
        starts = [((KVH - g) * holders - 1 - m) * (per + 2) for m in range(holders)]
        outs = jnp.concatenate([rows_ref[i : i + per, :] for i in starts], axis=0).astype(jnp.bfloat16)
        stats = jnp.concatenate([rows_ref[i + per : i + per + 1, :] for i in starts], axis=0)
        shift = LANES // 2
        while shift >= per:
            stats = stats + pltpu.roll(stats, shift, 1)
            shift //= 2
        stats = jnp.where(row % fold == lane // per, stats, 0.0)
        lse = jnp.concatenate(
            [
                jnp.sum(jnp.where(row // fold == m, stats, 0.0), axis=0, keepdims=True)
                for m in range(holders // fold)
            ],
            axis=1,
        )
        match = match_ref[g] > 0.5
        lse = jnp.where(match, lse, LOW_SCORE)
        own = lse_ref[g]
        top = jnp.maximum(jnp.max(lse, axis=1, keepdims=True), own)
        w = jnp.where(match, jnp.exp2(lse - top[:, :1]), 0.0)
        own_w = jnp.exp2(own - top)
        hi = w.astype(jnp.bfloat16)
        low = (w - hi.astype(jnp.float32)).astype(jnp.bfloat16)
        num = (
            jnp.dot(hi, outs, preferred_element_type=jnp.float32)
            + jnp.dot(low, outs, preferred_element_type=jnp.float32)
            + own_w * out_ref[g]
        )
        att = num / (jnp.sum(w, axis=1, keepdims=True) + own_w)
        heads = heads + [att[r * tokens : (r + 1) * tokens] for r in range(GROUP)]
        if g == 0:
            y = times(heads[:ready], first_ref[...])
    for i, copy in enumerate(copies):
        copy.wait()
        y = y + times(heads[ready + i * WIDE : ready + (i + 1) * WIDE], w_ref[i * depth : (i + 1) * depth, :])
    y_ref[...] = y.astype(jnp.bfloat16)


VMEM = pl.BlockSpec(memory_space=pltpu.VMEM)
HBM = pl.BlockSpec(memory_space=pltpu.HBM)
ANY = pl.BlockSpec(memory_space=pl.ANY)


def call(kernel, name, out_shape, specs, *operands, outs=None, scratch=(), flops=0, moved=0, limit=16):
    outs = outs or jax.tree.map(lambda _: VMEM, out_shape)
    return pl.pallas_call(
        kernel,
        name=name,
        out_shape=out_shape,
        in_specs=specs,
        out_specs=outs,
        scratch_shapes=scratch,
        cost_estimate=pl.CostEstimate(flops=flops, bytes_accessed=moved, transcendentals=0),
        compiler_params=pltpu.CompilerParams(vmem_limit_bytes=limit << 20),
    )(*operands)


def body(queries, stretch_keys, stretch_values, cache_keys, cache_values, chosen, out_weight):
    devices = lax.axis_size("seq")
    tokens = queries.shape[0]
    cache_rows = cache_keys.shape[0]
    span = BLK // cache_rows
    chips = span // KVH
    key_blocks = cache_rows * devices // BLK
    capacity = (GROUP * TOPK + key_blocks - 1) // key_blocks + 1
    per = capacity * tokens
    f32, bf16 = jnp.float32, jnp.bfloat16
    picks = chosen.transpose(2, 0, 1)

    def partner(bit):
        return [(i, i ^ bit) for i in range(devices)]

    send = call(
        functools.partial(pack_kernel, capacity),
        "pack",
        jax.ShapeDtypeStruct((KVH, key_blocks, chips, per + tokens, HD), bf16),
        [HBM] * 4,
        picks, queries, stretch_keys, stretch_values,
        outs=ANY,
        scratch=[
            pltpu.SMEM(picks.shape, jnp.int32),
            pltpu.VMEM(queries.shape, bf16),
            pltpu.VMEM(stretch_keys.shape, bf16),
            pltpu.VMEM(stretch_values.shape, bf16),
            pltpu.VMEM((KVH, key_blocks, chips, per + tokens, HD), bf16),
            pltpu.SemaphoreType.DMA((4 + KVH,)),
        ],
        limit=60,
    )
    send, cache_keys, cache_values, picks, queries = lax.optimization_barrier(
        (send, cache_keys, cache_values, picks, queries)
    )

    def exchange(x):
        ranks = [i for g in range(KVH) for i in range(g, devices, KVH)][::-1]
        return lax.all_to_all(x, "seq", split_axis=0, concat_axis=0, axis_index_groups=[ranks], tiled=True)

    got = exchange(send.reshape(devices, per + tokens, HD))

    core = lax.axis_index("seq") % KVH

    def halves(head):
        keys, values = [lax.dynamic_slice_in_dim(x, head * HD, HD, axis=1) for x in (cache_keys, cache_values)]
        return keys.T, values

    k_own, v_own = halves(core)
    k_peer, v_peer = [lax.ppermute(x, "seq", partner(1)) for x in halves(1 - core)]
    holders = devices // KVH
    rows = devices * per
    back, fresh = call(
        functools.partial(attend_kernel, per),
        "attend",
        (
            jax.ShapeDtypeStruct((devices * (per + 2), HD), bf16),
            jax.ShapeDtypeStruct((devices, tokens, HD), bf16),
        ),
        [VMEM] * 5,
        got, k_own, v_own, k_peer, v_peer,
        outs=(ANY, VMEM),
        scratch=[
            pltpu.VMEM((devices * (per + 2), HD), bf16),
            pltpu.SemaphoreType.DMA((rows // STEP,)),
        ],
        flops=8 * rows * cache_rows * HD,
        moved=4 << 20,
        limit=32,
    )
    back, picks, queries, out_weight = lax.optimization_barrier((back, picks, queries, out_weight))
    hist = exchange(back.reshape(devices, (per + 2) // 2, 2, HD))

    ready = EARLY * KVH * HD
    match, query_rows, first = call(
        functools.partial(masks_kernel, chips, capacity),
        "masks",
        (
            jax.ShapeDtypeStruct((KVH, GROUP * tokens, holders * per), f32),
            jax.ShapeDtypeStruct((KVH, GROUP * tokens, HD), f32),
            jax.ShapeDtypeStruct((ready, out_weight.shape[1]), bf16),
        ),
        [VMEM, VMEM, HBM],
        picks, queries, out_weight,
        scratch=[pltpu.SemaphoreType.DMA((1,))],
        limit=50,
    )

    far = lax.ppermute(fresh, "seq", partner(2))
    near, both = [lax.ppermute(x, "seq", partner(1)) for x in (fresh, far)]
    part = jax.ShapeDtypeStruct((KVH, GROUP * tokens, HD), f32)
    out, lse = call(
        functools.partial(fresh_kernel, tokens),
        "fresh",
        (part, part),
        [VMEM] * 5,
        query_rows, fresh, near, far, both,
        flops=8 * H * tokens * devices * tokens * HD,
        moved=1 << 20,
    )
    return call(
        functools.partial(project_kernel, per),
        "project",
        jax.ShapeDtypeStruct((tokens, out_weight.shape[1]), bf16),
        [VMEM] * 5 + [HBM],
        hist.reshape(devices * (per + 2), HD), out, lse, match, first, out_weight,
        scratch=[
            pltpu.VMEM((out_weight.shape[0] - ready, out_weight.shape[1]), bf16),
            pltpu.VMEM((devices * (per + 2), HD), f32),
            pltpu.SemaphoreType.DMA(((GROUP - EARLY) * KVH // WIDE,)),
        ],
        flops=2 * tokens * out_weight.size,
        moved=out_weight.size * 2,
        limit=50,
    )


def solution(mesh):
    seq = ("grp", "seq")
    return jax.shard_map(
        body,
        mesh=mesh,
        in_specs=(
            P(seq, None),
            P(seq, None),
            P(seq, None),
            P(seq, None),
            P(seq, None),
            P(seq, None, None),
            P(),
        ),
        out_specs=P(seq, None),
        check_vma=False,
    )
```
